32 devices in a mesh: groups: 2 (over y), graph: 4 (over z), edge: 4 (over x, core).
Axes of the slice: x: 2, y: 2, z: 4, core: 2. Of those that a mesh axis runs over, the one named last changes fastest.
Arguments:
- atom_embed: bfloat16 [256, 49, 64], P(('groups', 'graph')), parts along dimension 0, may hold values from -6 to 6
- out_cotangent: bfloat16 [256, 49, 64], P(('groups', 'graph')), parts along dimension 0, may hold values from -6 to 6
- send_rows: int32 [8, 4, 4, 4], P(('groups', 'graph'), None, 'edge'), parts along dimension 0, may hold values from 0 to 31, as said below
- recv_rows: int32 [8, 4, 4, 4], P(('groups', 'graph'), None, 'edge'), parts along dimension 0, may hold values from 0 to 31, as said below
- source_slot: int32 [8192], P(('groups', 'graph', 'edge')), parts along dimension 0, may hold values from 0 to 15, as said below
- target_slot: int32 [8192], P(('groups', 'graph', 'edge')), parts along dimension 0, may hold values from 0 to 15, as said below
- rotation: bfloat16 [8192, 235], P(('groups', 'graph', 'edge')), parts along dimension 0, may hold values from -2 to 2
- edge_feats: bfloat16 [8192, 128], P(('groups', 'graph', 'edge')), parts along dimension 0, may hold values from -6 to 6
- edge_bias: float32 [8192, 4], P(('groups', 'graph', 'edge')), parts along dimension 0, may hold values from -4 to 350
- conv_zero: bfloat16 [448, 448], replicated, may hold values from -0.25 to 0.25
- conv_one: bfloat16 [2, 384, 384], replicated, may hold values from -0.21875 to 0.21875
- conv_two: bfloat16 [2, 320, 320], replicated, may hold values from -0.25 to 0.25
- alpha_in: bfloat16 [64, 256], replicated, may hold values from -0.75 to 0.75
- alpha_edge: bfloat16 [128, 256], replicated, may hold values from -0.5 to 0.5
- alpha_dot: bfloat16 [256], replicated, may hold values from -1.5 to 1.5
- out_proj: bfloat16 [7, 64, 64], replicated, may hold values from -0.75 to 0.75
Outputs:
- output: bfloat16 [256, 49, 64], P(('groups', 'graph')), parts along dimension 0
- grad_atom_embed: bfloat16 [256, 49, 64], P(('groups', 'graph')), parts along dimension 0
- grad_conv_zero: bfloat16 [896, 448], P('groups'), parts along dimension 0
- grad_conv_one: bfloat16 [4, 384, 384], P('groups'), parts along dimension 0
- grad_conv_two: bfloat16 [4, 320, 320], P('groups'), parts along dimension 0
- grad_alpha_in: bfloat16 [128, 256], P('groups'), parts along dimension 0
- grad_alpha_edge: bfloat16 [256, 256], P('groups'), parts along dimension 0
- grad_alpha_dot: bfloat16 [512], P('groups'), parts along dimension 0
- grad_out_proj: bfloat16 [14, 64, 64], P('groups'), parts along dimension 0
The draws below stay inside these ranges and needn't reach their ends.
There are 2 independent parts, one for each index of `groups`. The reference program is written for one: setup_inputs(seed, part) draws one part's arguments, and reference() takes and returns one part's arrays. A program takes and returns all parts, laid end to end along the dimension named above; an argument that names none is the same for every part. Nothing has to cross between parts.
Inputs may be any that keep to these rules, and one draw needn't show every extreme that they name: send_rows[p, g, e] lists n distinct atoms of owner p in its entries 0 .. n-1, with n from 2 to 4; later entries hold 0. In every block (g, e) the list of some owner has n = 4. recv_rows[q, g, e] is built as send_rows; every atom is listed in some block. source_slot[f] = p * 4 + c names a listed entry c < n of send_rows[p, g, e] for the edge's block; every listed entry is named by some edge of the block. target_slot[f] = q * 4 + c names a listed entry of recv_rows[q, g, e] for the edge's block; every listed entry is named by some edge of the block, so every atom is the target of some edge.
All inputs are finite; a program needn't handle non-finite values.
Results may differ from the reference program's by a relative error of at most 0.002.
The reference program's roundings to bfloat16 on the way count: a program that leaves them out, or rounds other values in their place, can miss the bound.
Values may be sent and summed in bfloat16 or wider, within the bound.
No kernel may reach another device: no remote copies, remote signals or barrier semaphores. Data moves between devices by JAX's collectives and lax.ppermute only.
A program may use at most 128 MiB of HBM per device.

```python
import jax
import jax.numpy as jnp
from jax import lax

LMAX = 6
MMAX = 2
CH = 64
HEADS = 4
VAL = 16
ALPHA = 64
EDGE_CH = 128
CAP = 4
ATOM_DEV = 32
EDGE_DEV = 256
COEFFS = 49
ROT_ENTRIES = 235
ATOMS = 128
EDGES = 4096
N_GRAPH = 4
N_EDGE = 4


def slot_tables(key):
    subkeys = jax.random.split(key, 5)
    half_cap = CAP // 2
    extra_count = jax.random.randint(subkeys[0], (N_GRAPH, N_GRAPH, N_EDGE), 0, CAP - half_cap + 1)
    full_owner = jax.random.randint(subkeys[1], (1, N_GRAPH, N_EDGE), 0, N_GRAPH)
    owners = jnp.arange(N_GRAPH, dtype=jnp.int32).reshape(N_GRAPH, 1, 1)
    counts = jnp.where(owners == full_owner, CAP, half_cap + extra_count).astype(jnp.int32)
    spare_count = ATOM_DEV - half_cap
    scores = jax.random.randint(subkeys[2], (N_GRAPH, N_GRAPH, N_EDGE, spare_count), 0, 1 << 16) * spare_count + jnp.arange(spare_count, dtype=jnp.int32)
    chosen = jnp.argsort(scores, axis=-1)[..., :CAP - half_cap].astype(jnp.int32) + half_cap
    fixed_part = jnp.broadcast_to(jnp.arange(half_cap, dtype=jnp.int32), (N_GRAPH, N_GRAPH, N_EDGE, half_cap))
    offsets = jnp.concatenate([fixed_part, chosen], axis=-1)
    requester = jnp.arange(N_GRAPH, dtype=jnp.int32).reshape(1, N_GRAPH, 1, 1) * N_EDGE + jnp.arange(N_EDGE, dtype=jnp.int32).reshape(1, 1, N_EDGE, 1)
    row_table = (requester * half_cap + offsets) % ATOM_DEV
    position = jnp.arange(CAP, dtype=jnp.int32)
    row_table = jnp.where(position < counts[..., None], row_table, 0).astype(jnp.int32)
    per_request = jnp.transpose(counts, (1, 2, 0))
    slot_ends = jnp.cumsum(per_request, axis=-1)
    starts = slot_ends - per_request
    used_slots = slot_ends[..., -1:]
    edge_position = jnp.arange(EDGE_DEV, dtype=jnp.int32)
    extra_rank = jax.random.randint(subkeys[3], (N_GRAPH, N_EDGE, EDGE_DEV), 0, 1 << 24) % used_slots
    slot_rank = jnp.where(edge_position < used_slots, edge_position, extra_rank)
    owner_index = jnp.sum((slot_ends[..., None, :] <= slot_rank[..., None]).astype(jnp.int32), axis=-1)
    owner_start = jnp.take_along_axis(starts, owner_index, axis=-1)
    slot_ids = owner_index * CAP + slot_rank - owner_start
    shuffle_scores = jax.random.randint(subkeys[4], (N_GRAPH, N_EDGE, EDGE_DEV), 0, 1 << 16) * EDGE_DEV + edge_position
    shuffle = jnp.argsort(shuffle_scores, axis=-1)
    slot_ids = jnp.take_along_axis(slot_ids, shuffle, axis=-1)
    return (row_table, slot_ids.reshape(-1).astype(jnp.int32))


def draw_send_rows(key, part):
    row_table, slot_ids = slot_tables(jax.random.fold_in(key, 11))
    return row_table


def draw_source_slot(key, part):
    row_table, slot_ids = slot_tables(jax.random.fold_in(key, 11))
    return slot_ids


def draw_recv_rows(key, part):
    row_table, slot_ids = slot_tables(jax.random.fold_in(key, 23))
    return row_table


def draw_target_slot(key, part):
    row_table, slot_ids = slot_tables(jax.random.fold_in(key, 23))
    return slot_ids


def draw_edge_bias(key, part):
    key = jax.random.fold_in(key, 5)
    subkeys = jax.random.split(key, 1)
    return jnp.clip(jax.random.normal(subkeys[0], (EDGES, HEADS), jnp.float32), -4.0, 4.0)


def block_levels(rng, extent, cuts, low, largest):
    def one(axis_at, shards_of):
        heights = jax.random.uniform(jax.random.fold_in(jax.random.fold_in(rng, 6), axis_at), (shards_of,), jnp.float32, low / len(cuts), largest / len(cuts))
        return jnp.repeat(jnp.exp(heights), extent[axis_at] // shards_of).reshape((-1,) + (1,) * (len(extent) - axis_at - 1))

    factor_of = one(*cuts[0])
    for cut in cuts[1:]:
        factor_of = factor_of * one(*cut)
    return factor_of


def centred(rng, extent, scale, most, cuts=(), kind=jnp.bfloat16):
    values = jax.random.normal(rng, extent, jnp.float32) * scale
    if len(cuts) > 0:
        values = block_levels(rng, extent, cuts, -0.22, 0.18) * values
    return jnp.clip(values, min=-most, max=most).astype(kind)


def setup_inputs(seed: int = 0, part: int = 0) -> dict:
    seeds = jax.random.split(jax.random.key(seed), 17)
    own_keys = jax.random.split(jax.random.fold_in(seeds[16], part), 17)
    atom_embed = centred(own_keys[0], (ATOMS, COEFFS, CH), 1.0, 6.0, ((0, 4),))
    out_cotangent = centred(own_keys[1], (ATOMS, COEFFS, CH), 1.0, 6.0, ((0, 4),))
    send_rows = draw_send_rows(jax.random.fold_in(jax.random.fold_in(seeds[16], part), 71), part)
    recv_rows = draw_recv_rows(jax.random.fold_in(jax.random.fold_in(seeds[16], part), 71), part)
    source_slot = draw_source_slot(jax.random.fold_in(jax.random.fold_in(seeds[16], part), 71), part)
    target_slot = draw_target_slot(jax.random.fold_in(jax.random.fold_in(seeds[16], part), 71), part)
    rotation = centred(own_keys[6], (EDGES, ROT_ENTRIES), 0.35, 2.0, ((0, 16),))
    edge_feats = centred(own_keys[7], (EDGES, EDGE_CH), 1.0, 6.0, ((0, 16),))
    edge_bias = draw_edge_bias(jax.random.fold_in(jax.random.fold_in(seeds[16], part), 71), part)
    conv_zero = centred(seeds[9], ((LMAX + 1) * CH, (LMAX + 1) * CH), ((LMAX + 1) * CH) ** -0.5, 0.25)
    conv_one = centred(seeds[10], (2, LMAX * CH, LMAX * CH), (2 * LMAX * CH) ** -0.5, 0.21875)
    conv_two = centred(seeds[11], (2, (LMAX - 1) * CH, (LMAX - 1) * CH), (2 * (LMAX - 1) * CH) ** -0.5, 0.25)
    alpha_in = centred(seeds[12], (CH, HEADS * ALPHA), CH ** -0.5, 0.75)
    alpha_edge = centred(seeds[13], (EDGE_CH, HEADS * ALPHA), EDGE_CH ** -0.5, 0.5)
    alpha_dot = centred(seeds[14], (HEADS * ALPHA,), (ALPHA // 4) ** -0.5, 1.5)
    out_proj = centred(seeds[15], (LMAX + 1, CH, CH), CH ** -0.5, 0.75)
    return {"atom_embed": atom_embed, "out_cotangent": out_cotangent, "send_rows": send_rows, "recv_rows": recv_rows, "source_slot": source_slot, "target_slot": target_slot, "rotation": rotation, "edge_feats": edge_feats, "edge_bias": edge_bias, "conv_zero": conv_zero, "conv_one": conv_one, "conv_two": conv_two, "alpha_in": alpha_in, "alpha_edge": alpha_edge, "alpha_dot": alpha_dot, "out_proj": out_proj}


precise_mode = lax.Precision.HIGHEST
leak_slope = 0.2
floor_value = -1e+30

def matmul(left_side, right_side):
    return jnp.dot(left_side, right_side, preferred_element_type=jnp.float32)

def degree_blocks():
    result = []
    offset = 0
    for degree in range(LMAX + 1):
        centre = min(degree, MMAX)
        row_total = 2 * centre + 1
        col_total = 2 * degree + 1
        result.append((degree, centre, row_total, col_total, offset))
        offset += row_total * col_total
    return result

def rotation_block(rotation, block_info):
    degree, centre, row_total, col_total, offset = block_info
    return rotation[:, offset:offset + row_total * col_total].reshape(-1, row_total, col_total).astype(jnp.float32)

def to_frame(rotation, field_data):
    pieces = []
    for block_info in degree_blocks():
        degree = block_info[0]
        rot_block = rotation_block(rotation, block_info)
        coeffs = field_data[:, degree * degree:(degree + 1) * (degree + 1), :].astype(jnp.float32)
        pieces.append(jnp.einsum('eij,ejc->eic', rot_block, coeffs, precision=precise_mode))
    return pieces

def from_frame(rotation, pieces):
    outputs = []
    for block_info, piece in zip(degree_blocks(), pieces):
        rot_block = rotation_block(rotation, block_info)
        outputs.append(jnp.einsum('eij,eic->ejc', rot_block, piece.astype(jnp.float32), precision=precise_mode))
    return jnp.concatenate(outputs, axis=1)

def split_orders(pieces):
    blocks = degree_blocks()
    order_zero = jnp.stack([pieces[info[0]][:, info[1]] for info in blocks], axis=1)
    upper_one = jnp.stack([pieces[info[0]][:, info[1] + 1] for info in blocks[1:]], axis=1)
    lower_one = jnp.stack([pieces[info[0]][:, info[1] - 1] for info in blocks[1:]], axis=1)
    upper_two = jnp.stack([pieces[info[0]][:, info[1] + 2] for info in blocks[2:]], axis=1)
    lower_two = jnp.stack([pieces[info[0]][:, info[1] - 2] for info in blocks[2:]], axis=1)
    return (order_zero, upper_one, lower_one, upper_two, lower_two)

def join_orders(groups):
    order_zero, upper_one, lower_one, upper_two, lower_two = groups
    pieces = []
    for degree in range(LMAX + 1):
        entries = []
        if degree >= 2:
            entries.append(lower_two[:, degree - 2])
        if degree >= 1:
            entries.append(lower_one[:, degree - 1])
        entries.append(order_zero[:, degree])
        if degree >= 1:
            entries.append(upper_one[:, degree - 1])
        if degree >= 2:
            entries.append(upper_two[:, degree - 2])
        pieces.append(jnp.stack(entries, axis=1))
    return pieces

def flatten_rows(tensor):
    return tensor.reshape(tensor.shape[0], -1)

def convolve(groups, conv_zero, conv_one, conv_two):
    flat_in = [flatten_rows(tensor) for tensor in groups]
    results = [matmul(flat_in[0], conv_zero)]
    for first_index, weights in ((1, conv_one), (3, conv_two)):
        results.append(matmul(flat_in[first_index], weights[0]) - matmul(flat_in[first_index + 1], weights[1]))
        results.append(matmul(flat_in[first_index], weights[1]) + matmul(flat_in[first_index + 1], weights[0]))
    return tuple((tensor.reshape(groups[number].shape[0], groups[number].shape[1], -1) for number, tensor in enumerate(results)))

def convolve_back(groups, grads, conv_zero, conv_one, conv_two):
    flat_in = [flatten_rows(tensor) for tensor in groups]
    flat_grad = [flatten_rows(tensor) for tensor in grads]
    results = [matmul(flat_grad[0], conv_zero.T)]
    for first_index, weights in ((1, conv_one), (3, conv_two)):
        results.append(matmul(flat_grad[first_index], weights[0].T) + matmul(flat_grad[first_index + 1], weights[1].T))
        results.append(matmul(flat_grad[first_index + 1], weights[0].T) - matmul(flat_grad[first_index], weights[1].T))
    shaped = tuple((tensor.reshape(groups[number].shape[0], groups[number].shape[1], -1) for number, tensor in enumerate(results)))
    weight_zero = matmul(flat_in[0].T, flat_grad[0])
    paired = []
    for first_index in (1, 3):
        real_part = matmul(flat_in[first_index].T, flat_grad[first_index]) + matmul(flat_in[first_index + 1].T, flat_grad[first_index + 1])
        imag_part = matmul(flat_in[first_index].T, flat_grad[first_index + 1]) - matmul(flat_in[first_index + 1].T, flat_grad[first_index])
        paired.append(jnp.stack([real_part, imag_part]))
    return (shaped, (weight_zero, paired[0], paired[1]))

def finish_atoms(atom_num, atom_den, cotangent, out_proj):
    row_count = atom_num.shape[0]
    coeff_count = cotangent.shape[1]
    channels = cotangent.shape[2]
    spread = jnp.repeat(atom_den, VAL, axis=1)
    aggregate = atom_num.reshape(row_count, coeff_count, channels) / spread[:, None, :]
    agg_low = aggregate.astype(jnp.bfloat16)
    outputs = []
    agg_grads = []
    for degree in range(LMAX + 1):
        start = degree * degree
        span_width = 2 * degree + 1
        agg_block = agg_low[:, start:start + span_width].reshape(-1, channels)
        outputs.append(matmul(agg_block, out_proj[degree]).reshape(row_count, span_width, channels))
        cot_block = cotangent[:, start:start + span_width].reshape(-1, channels)
        agg_grads.append(matmul(cot_block, out_proj[degree].T).reshape(row_count, span_width, channels))
    output = jnp.concatenate(outputs, axis=1).astype(jnp.bfloat16)
    agg_grad = jnp.concatenate(agg_grads, axis=1)
    num_grad = (agg_grad / spread[:, None, :]).astype(jnp.bfloat16)
    den_grad = (-(agg_grad * aggregate).reshape(row_count, coeff_count, HEADS, VAL).sum(axis=(1, 3)) / atom_den).astype(jnp.bfloat16)
    return (output, num_grad.reshape(row_count, -1), den_grad, agg_low)

def projection_grad(agg_low, cotangent):
    channels = cotangent.shape[2]
    pieces = []
    for degree in range(LMAX + 1):
        start = degree * degree
        span_width = 2 * degree + 1
        agg_block = agg_low[:, start:start + span_width].reshape(-1, channels)
        cot_block = cotangent[:, start:start + span_width].reshape(-1, channels)
        pieces.append(matmul(agg_block.T, cot_block))
    return jnp.stack(pieces)

def reference(atom_embed, out_cotangent, send_rows, recv_rows, source_slot, target_slot, rotation, edge_feats, edge_bias, conv_zero, conv_one, conv_two, alpha_in, alpha_edge, alpha_dot, out_proj):
    position = jnp.arange(EDGES, dtype=jnp.int32)
    block_id = position // EDGE_DEV
    graph_id = block_id // N_EDGE
    lane_id = block_id % N_EDGE
    source_owner = source_slot // CAP
    sources = (source_owner * ATOM_DEV + send_rows[source_owner, graph_id, lane_id, source_slot % CAP]).astype(jnp.int32)
    target_owner = target_slot // CAP
    targets = (target_owner * ATOM_DEV + recv_rows[target_owner, graph_id, lane_id, target_slot % CAP]).astype(jnp.int32)
    invariant = (rotation[:, 0:1].astype(jnp.float32) * atom_embed[sources, 0, :].astype(jnp.float32)).astype(jnp.bfloat16)
    pre_act = matmul(invariant, alpha_in) + matmul(edge_feats, alpha_edge)
    hidden = jnp.where(pre_act > 0, pre_act, leak_slope * pre_act)
    head_dot = alpha_dot.astype(jnp.float32).reshape(HEADS, ALPHA)
    logits = (hidden.reshape(EDGES, HEADS, ALPHA) * head_dot).sum(axis=2) + edge_bias
    peak = jnp.full((ATOMS, HEADS), floor_value, jnp.float32).at[targets].max(logits)
    weight = jnp.exp(logits - peak[targets])
    block_count = N_GRAPH * N_EDGE

    def blocked(tensor):
        return tensor.reshape((block_count, EDGE_DEV) + tensor.shape[1:])

    def edge_pass(rot_part, source_part):
        gathered = atom_embed[source_part]
        groups = tuple((tensor.astype(jnp.bfloat16) for tensor in split_orders(to_frame(rot_part, gathered))))
        message = from_frame(rot_part, join_orders(convolve(groups, conv_zero, conv_one, conv_two)))
        return (groups, message)

    def forward_step(carried, inputs):
        total_num, total_den = carried
        rot_part, source_part, target_part, weight_part = inputs
        groups, message = edge_pass(rot_part, source_part)
        weighted = message.reshape(EDGE_DEV, COEFFS, HEADS, VAL) * weight_part[:, None, :, None]
        total_num = total_num.at[target_part].add(weighted.reshape(EDGE_DEV, COEFFS, CH))
        total_den = total_den.at[target_part].add(weight_part)
        return ((total_num, total_den), None)
    start_state = (jnp.zeros((ATOMS, COEFFS, CH), jnp.float32), jnp.zeros((ATOMS, HEADS), jnp.float32))
    sums, unused = lax.scan(forward_step, start_state, (blocked(rotation), blocked(sources), blocked(targets), blocked(weight)))
    atom_num, atom_den = sums
    output, num_grad, den_grad, agg_low = finish_atoms(atom_num.reshape(ATOMS, -1), atom_den, out_cotangent, out_proj)
    proj_grad = projection_grad(agg_low, out_cotangent)
    num_table = num_grad.reshape(ATOMS, COEFFS, HEADS, VAL)

    def backward_step(carried, inputs):
        embed_grad, weight_zero, weight_one, weight_two, in_grad, feat_grad, dot_grad = carried
        rot_part, source_part, target_part, weight_part, pre_part, hidden_part, invariant_part, feat_part = inputs
        groups, message = edge_pass(rot_part, source_part)
        edge_num = num_table[target_part].astype(jnp.float32)
        edge_den = den_grad[target_part].astype(jnp.float32)
        message_grad = weight_part[:, None, :, None] * edge_num
        weight_grad = (message.reshape(EDGE_DEV, COEFFS, HEADS, VAL) * edge_num).sum(axis=(1, 3)) + edge_den
        logit_grad = weight_grad * weight_part
        value_grads = tuple((tensor.astype(jnp.bfloat16) for tensor in split_orders(to_frame(rot_part, message_grad.reshape(EDGE_DEV, COEFFS, CH)))))
        input_grads, conv_grads = convolve_back(groups, value_grads, conv_zero, conv_one, conv_two)
        hidden_grad = logit_grad[:, :, None] * head_dot
        pre_grad = (hidden_grad.reshape(EDGE_DEV, -1) * jnp.where(pre_part > 0, 1.0, leak_slope)).astype(jnp.bfloat16)
        dot_grad = dot_grad + (logit_grad[:, :, None] * hidden_part.reshape(EDGE_DEV, HEADS, ALPHA)).sum(axis=0).reshape(-1)
        in_grad = in_grad + matmul(invariant_part.T, pre_grad)
        feat_grad = feat_grad + matmul(feat_part.T, pre_grad)
        invariant_grad = matmul(pre_grad, alpha_in.T)
        zero_grad = input_grads[0].at[:, 0].add(invariant_grad)
        rotated_grad = (zero_grad,) + tuple(input_grads[1:])
        source_grad = from_frame(rot_part, join_orders(rotated_grad))
        embed_grad = embed_grad.at[source_part].add(source_grad)
        carried = (embed_grad, weight_zero + conv_grads[0], weight_one + conv_grads[1], weight_two + conv_grads[2], in_grad, feat_grad, dot_grad)
        return (carried, None)
    start_grads = (jnp.zeros((ATOMS, COEFFS, CH), jnp.float32), jnp.zeros(conv_zero.shape, jnp.float32), jnp.zeros(conv_one.shape, jnp.float32), jnp.zeros(conv_two.shape, jnp.float32), jnp.zeros(alpha_in.shape, jnp.float32), jnp.zeros(alpha_edge.shape, jnp.float32), jnp.zeros(alpha_dot.shape, jnp.float32))
    grads, unused = lax.scan(backward_step, start_grads, (blocked(rotation), blocked(sources), blocked(targets), blocked(weight), blocked(pre_act), blocked(hidden), blocked(invariant), blocked(edge_feats)))
    embed_grad, weight_zero, weight_one, weight_two, in_grad, feat_grad, dot_grad = grads
    return (output, embed_grad.astype(jnp.bfloat16), weight_zero.astype(jnp.bfloat16), weight_one.astype(jnp.bfloat16), weight_two.astype(jnp.bfloat16), in_grad.astype(jnp.bfloat16), feat_grad.astype(jnp.bfloat16), dot_grad.astype(jnp.bfloat16), proj_grad.astype(jnp.bfloat16))
```

```python
import jax
import jax.numpy as jnp
import numpy as np
from jax import lax
from jax.experimental import pallas as pl
from jax.experimental.pallas import tpu as pltpu
from jax.sharding import PartitionSpec as P

LMAX = 6
MMAX = 2
CH = 64
HEADS = 4
VAL = 16
ALPHA = 64
COEFFS = (LMAX + 1) * (LMAX + 1)
FLAT = COEFFS * CH
LANES = 128
BLOCKS = (FLAT + LANES - 1) // LANES
COLS = BLOCKS * LANES
WIDE = COLS + LANES
DIM0 = (LMAX + 1) * CH
DIM1 = LMAX * CH
DIM2 = (LMAX - 1) * CH
PANEL = 256

leak_slope = 0.2
floor_value = -1e30
bf16 = jnp.bfloat16
f32 = jnp.float32

VMEM_LIMIT = 56 * 1024 * 1024


def degree_blocks():
    result = []
    offset = 0
    for degree in range(LMAX + 1):
        centre = min(degree, MMAX)
        row_total = 2 * centre + 1
        col_total = 2 * degree + 1
        result.append((degree, centre, row_total, col_total, offset))
        offset += row_total * col_total
    return result


def degree_of(coeff):
    return int(np.sqrt(coeff))


def dot_nn(left, right):
    return jnp.dot(left, right, preferred_element_type=f32)


def dot_nt(left, right):
    return lax.dot_general(left, right, (((1,), (1,)), ((), ())), preferred_element_type=f32)


def dot_tn(left, right):
    return lax.dot_general(left, right, (((0,), (0,)), ((), ())), preferred_element_type=f32)


def iota(shape, dim):
    return lax.broadcasted_iota(jnp.int32, shape, dim)


def split_two(value):
    high = value.astype(bf16)
    return high, (value - high.astype(f32)).astype(bf16)


def to_frame(source, rot, edges, emit):
    def body(half, carry):
        lanes = pl.ds(pl.multiple_of(half * LANES, LANES), LANES)
        for degree, centre, row_total, col_total, offset in degree_blocks():
            sums = [None] * row_total
            for j in range(col_total):
                column = source[pl.ds((degree * degree + j) * CH, CH), lanes]
                for i in range(row_total):
                    term = rot[pl.ds(offset + i * col_total + j, 1), lanes] * column
                    sums[i] = term if j == 0 else sums[i] + term
            for i in range(row_total):
                emit(degree, i - centre, half, sums[i])
        return carry

    lax.fori_loop(0, edges // LANES, body, 0)


def from_frame(load, rot, edges, emit):
    def body(half, carry):
        lanes = pl.ds(pl.multiple_of(half * LANES, LANES), LANES)
        for degree, centre, row_total, col_total, offset in degree_blocks():
            rows = [load(degree, i - centre, half) for i in range(row_total)]
            for j in range(col_total):
                total = None
                for i in range(row_total):
                    term = rot[pl.ds(offset + i * col_total + j, 1), lanes] * rows[i]
                    total = term if i == 0 else total + term
                emit(degree * degree + j, half, total)
        return carry

    lax.fori_loop(0, edges // LANES, body, 0)


def lane_at(half, edges, second):
    return pl.ds(pl.multiple_of(half * LANES + (edges if second else 0), LANES), LANES)


def frame_place(degree, order, refs):
    if order == 0:
        return refs[0], degree * CH, False
    which = abs(order)
    return refs[which], (degree - which) * CH, order < 0


def spread_heads(rows):
    return jnp.concatenate(
        [jnp.broadcast_to(row, (VAL, row.shape[1])) for row in rows], axis=0
    )


def one_hot_rows(slot_ref, slots):
    edges = slot_ref.shape[1]
    return iota((slots, edges), 0) == slot_ref[...]


def mask_to(mask, dtype):
    return jnp.where(mask, 1.0, 0.0).astype(dtype)


def stack_table(table_ref, rows_ref):
    peers, cap, width = table_ref.shape
    for start in range(0, peers * cap, 8):
        parts = [table_ref[g].astype(f32) for g in range(start // cap, (start + 8) // cap)]
        rows_ref[pl.ds(start, 8), :] = jnp.concatenate(parts, axis=0)


def put_rows(out_ref, cols, value):
    peers, cap = out_ref.shape[0], out_ref.shape[1]
    for g in range(peers):
        out_ref[g, :, cols] = value[g * cap : (g + 1) * cap].astype(out_ref.dtype)


def slot_sums(terms, one_hot, out_ref):
    both = jnp.concatenate([one_hot, one_hot], axis=1)
    for start in range(0, COLS, PANEL):
        size = min(PANEL, COLS - start)
        put_rows(out_ref, pl.ds(start, size), dot_nt(both, terms[pl.ds(start, size), :]))


def store_terms(terms, edges):
    def emit(coeff, half, value):
        high, low = split_two(value)
        rows = pl.ds(coeff * CH, CH)
        terms[rows, lane_at(half, edges, False)] = high
        terms[rows, lane_at(half, edges, True)] = low

    return emit


def forward_kernel(
    table, source_slot, target_slot, rot, feats, bias, wzero, wone, wtwo, ain, aedge, adot,
    sums_out, x0, x1, x2, v0, v1, v2, pre_out, logit_out,
    rows, gathered, neg1, neg2, weights, terms,
):
    edges = source_slot.shape[1]
    slots = table.shape[0] * table.shape[1]
    stack_table(table, rows)
    picked = mask_to(one_hot_rows(source_slot, slots), bf16)
    gathered[...] = dot_tn(rows[...].astype(bf16), picked)

    def emit(degree, order, half, value):
        ref, row, second = frame_place(degree, order, (x0, x1, x2))
        value = value.astype(bf16)
        ref[pl.ds(row, CH), lane_at(half, edges, second)] = value
        if order != 0:
            neg = (None, neg1, neg2)[abs(order)]
            swapped = value if order > 0 else -value
            neg[pl.ds(row, CH), lane_at(half, edges, not second)] = swapped

    to_frame(gathered, rot, edges, emit)

    pre = dot_nn(ain[...], x0[pl.ds(0, CH), :]) + dot_nt(aedge[...], feats[...])
    pre_out[...] = pre
    hidden = jnp.where(pre > 0, pre, leak_slope * pre) * adot[...]
    aims = one_hot_rows(target_slot, slots)
    lane = iota((slots, LANES), 1)
    side = jnp.zeros((slots, LANES), f32)
    for h in range(HEADS):
        logit = jnp.sum(hidden[h * ALPHA : (h + 1) * ALPHA], axis=0, keepdims=True)
        logit = logit + bias[pl.ds(h, 1), :]
        logit_out[pl.ds(h, 1), :] = logit
        peak = jnp.max(jnp.where(aims, logit, floor_value), axis=1, keepdims=True)
        of_edge = jnp.sum(jnp.where(aims, peak, 0.0), axis=0, keepdims=True)
        weight = jnp.exp(logit - of_edge)
        weights[pl.ds(h, 1), :] = weight
        den = jnp.sum(jnp.where(aims, weight, 0.0), axis=1, keepdims=True)
        side = jnp.where(lane == h, den, jnp.where(lane == HEADS + h, peak, side))
    put_rows(sums_out, pl.ds(COLS, LANES), side)

    v0[...] = dot_nn(wzero[...], x0[...])
    v1[...] = dot_nn(wone[0], x1[...]) + dot_nn(wone[1], neg1[...])
    v2[...] = dot_nn(wtwo[0], x2[...]) + dot_nn(wtwo[1], neg2[...])

    def load(degree, order, half):
        ref, row, second = frame_place(degree, order, (v0, v1, v2))
        return ref[pl.ds(row, CH), lane_at(half, edges, second)]

    store = store_terms(terms, edges)

    def weigh(coeff, half, value):
        lanes = lane_at(half, edges, False)
        spread = spread_heads([weights[pl.ds(h, 1), lanes] for h in range(HEADS)])
        store(coeff, half, value * spread)

    terms[pl.ds(FLAT, COLS - FLAT), :] = jnp.zeros((COLS - FLAT, 2 * edges), bf16)
    from_frame(load, rot, edges, weigh)
    slot_sums(terms, mask_to(aims, bf16), sums_out)


def lane_heads(values, shape):
    head = (iota(shape, 1) % CH) // VAL
    result = jnp.broadcast_to(values[0], shape)
    for h in range(1, HEADS):
        result = jnp.where(head == h, values[h], result)
    return result


def collect_rows(place, arrivals, rows_ref):
    for k, arrival in enumerate(arrivals):
        peers, cap, width = arrival.shape
        base = (place[0] ^ k) * (peers * cap)
        for start in range(0, peers * cap, 8):
            parts = [arrival[g] for g in range(start // cap, (start + 8) // cap)]
            at = pl.ds(pl.multiple_of(base + start, 8), 8)
            rows_ref[at, :] = jnp.concatenate(parts, axis=0)


def make_finish(lanes_total):
    def finish_kernel(place, index_row, index_col, own_col, cot, pairs, *rest):
        arrivals = rest[:lanes_total]
        out, back, proj, rows, num, num_grad = rest[lanes_total:]
        atoms = cot.shape[0]
        total = index_row.shape[1]
        slots = own_col.shape[0]
        collect_rows(place, arrivals, rows)
        side = rows[:, pl.ds(COLS, LANES)]
        names = iota((total, atoms), 1) == index_col[...]
        picked = mask_to(iota((atoms, total), 0) == index_row[...], bf16)
        own = iota((slots, atoms), 1) == own_col[...]
        eye = iota((atoms, atoms), 0) == iota((atoms, atoms), 1)
        scales, dens, own_peaks = [], [], []
        for h in range(HEADS):
            peak_rows = side[:, HEADS + h : HEADS + h + 1]
            peak = jnp.max(jnp.where(names, peak_rows, floor_value), axis=0, keepdims=True)
            of_row = jnp.sum(jnp.where(names, peak, 0.0), axis=1, keepdims=True)
            scale = jnp.exp(peak_rows - of_row)
            scaled_den = side[:, h : h + 1] * scale
            den = jnp.sum(jnp.where(names, scaled_den, 0.0), axis=0, keepdims=True)
            scales.append(scale)
            dens.append(jnp.sum(jnp.where(eye, den, 0.0), axis=1, keepdims=True))
            own_peaks.append(jnp.sum(jnp.where(own, peak, 0.0), axis=1, keepdims=True))
        scale_full = lane_heads(scales, (total, LANES))
        den_full = lane_heads(dens, (atoms, LANES))
        twice = jnp.concatenate([picked, picked], axis=1)

        def gather_block(block, carry):
            cols = pl.ds(pl.multiple_of(block * LANES, LANES), LANES)
            high, low = split_two(rows[:, cols] * scale_full)
            num[:, cols] = dot_nn(twice, jnp.concatenate([high, low], axis=0))
            return carry

        lax.fori_loop(0, BLOCKS, gather_block, 0)

        den_sum = jnp.zeros((atoms, LANES), f32)
        tops = [None] * (LMAX + 1)
        lows = [None] * (LMAX + 1)
        for block in range(BLOCKS):
            cols = pl.ds(block * LANES, LANES)
            agg = num[:, cols] / den_full
            agg_low = agg.astype(bf16)
            cot_block = cot[:, cols]
            weight = pairs[block]
            out[:, cols] = dot_nn(agg_low, weight).astype(bf16)
            agg_grad = dot_nt(cot_block, weight)
            num_grad[:, cols] = (agg_grad / den_full).astype(bf16)
            den_sum = den_sum + agg_grad * agg
            outer = dot_tn(agg_low, cot_block)
            first = degree_of(2 * block)
            tops[first] = outer[:CH] if tops[first] is None else tops[first] + outer[:CH]
            if 2 * block + 1 < COEFFS:
                second = degree_of(2 * block + 1)
                lows[second] = outer[CH:] if lows[second] is None else lows[second] + outer[CH:]
        for degree in range(LMAX + 1):
            piece = jnp.zeros((CH, CH), f32)
            if tops[degree] is not None:
                piece = piece + tops[degree][:, :CH]
            if lows[degree] is not None:
                piece = piece + lows[degree][:, CH:]
            proj[pl.ds(degree * CH, CH), :] = piece * (1.0 / lanes_total)

        own_low = mask_to(own, bf16)
        put_rows(back, pl.ds(0, COLS), dot_nn(own_low, num_grad[...]))
        head = (iota((atoms, LANES), 1) % CH) // VAL
        lane = iota((slots, LANES), 1)
        extra = jnp.zeros((slots, LANES), f32)
        for h in range(HEADS):
            summed = jnp.sum(jnp.where(head == h, den_sum, 0.0), axis=1, keepdims=True)
            den_grad = (-summed / dens[h]).astype(bf16).astype(f32)
            as_row = jnp.sum(jnp.where(eye, den_grad, 0.0), axis=0, keepdims=True)
            of_row = jnp.sum(jnp.where(own, as_row, 0.0), axis=1, keepdims=True)
            high = own_peaks[h].astype(bf16).astype(f32)
            rest_one = own_peaks[h] - high
            mid = rest_one.astype(bf16).astype(f32)
            for n, value in enumerate((of_row, high, mid, rest_one - mid)):
                extra = jnp.where(lane == n * HEADS + h, value, extra)
        put_rows(back, pl.ds(COLS, LANES), extra)

    return finish_kernel


def gradient_kernel(
    table, target_slot, rot, feats, x0, x1, x2, v0, v1, v2, pre, logits, adot, proj,
    packed, g0, g1, g2, pre_grad_out,
    rows, spread_grad, weights,
):
    edges = target_slot.shape[1]
    slots = table.shape[0] * table.shape[1]
    stack_table(table, rows)
    picked = mask_to(one_hot_rows(target_slot, slots), bf16)
    low_rows = rows[...].astype(bf16)
    spread_grad[...] = dot_tn(low_rows[:, :COLS], picked)
    side = dot_tn(low_rows[:, COLS:], picked)
    for h in range(HEADS):
        peak = (side[HEADS + h : HEADS + h + 1] + side[2 * HEADS + h : 2 * HEADS + h + 1]) + side[
            3 * HEADS + h : 3 * HEADS + h + 1
        ]
        weights[pl.ds(h, 1), :] = jnp.exp(logits[pl.ds(h, 1), :] - peak)

    state = {}

    def emit(degree, order, half, value):
        lanes = lane_at(half, edges, False)
        ref, row, second = frame_place(degree, order, (v0, v1, v2))
        product = value * ref[pl.ds(row, CH), lane_at(half, edges, second)]
        if degree == 0:
            state["sum"] = product
            state["spread"] = spread_heads([weights[pl.ds(h, 1), lanes] for h in range(HEADS)])
        else:
            state["sum"] = state["sum"] + product
        grad = (value * state["spread"]).astype(bf16)
        ref, row, second = frame_place(degree, order, (g0, g1, g2))
        ref[pl.ds(row, CH), lane_at(half, edges, second)] = grad
        if order != 0:
            swapped = grad if order < 0 else -grad
            below = row + (DIM1 if abs(order) == 1 else DIM2)
            ref[pl.ds(below, CH), lane_at(half, edges, not second)] = swapped
        if degree == LMAX and order == MMAX:
            for h in range(HEADS):
                part = state["sum"][h * VAL : (h + 1) * VAL]
                weights[pl.ds(HEADS + h, 1), lanes] = jnp.sum(part, axis=0, keepdims=True)

    to_frame(spread_grad, rot, edges, emit)

    hidden = jnp.where(pre[...] > 0, pre[...], leak_slope * pre[...])
    logit_grads = [
        weights[pl.ds(h, 1), :] * (weights[pl.ds(HEADS + h, 1), :] + side[h : h + 1])
        for h in range(HEADS)
    ]
    tall = jnp.concatenate(
        [jnp.broadcast_to(row, (ALPHA, edges)) for row in logit_grads], axis=0
    )
    slope = jnp.where(pre[...] > 0, 1.0, leak_slope)
    pre_grad = (tall * adot[...] * slope).astype(bf16)
    pre_grad_out[...] = pre_grad
    dot_grad = jnp.sum(tall * hidden, axis=1, keepdims=True)

    row = 0
    for start in range(0, DIM0, PANEL):
        size = min(PANEL, DIM0 - start)
        packed[pl.ds(row, DIM0), pl.ds(0, size)] = dot_nt(x0[...], g0[pl.ds(start, size), :])
        if size < PANEL:
            packed[pl.ds(row, DIM0), pl.ds(size, CH)] = proj[...]
        row += DIM0
    for left, right, dim in ((x1, g1, DIM1), (x2, g2, DIM2)):
        for start in range(0, 2 * dim, PANEL):
            size = min(PANEL, 2 * dim - start)
            packed[pl.ds(row, dim), pl.ds(0, size)] = dot_nt(left[...], right[pl.ds(start, size), :])
            row += dim
    row -= DIM2
    half = pl.ds(LANES, LANES)
    edge_ch = feats.shape[1]
    edge_grad = lax.dot_general(
        feats[...], pre_grad, (((0,), (1,)), ((), ())), preferred_element_type=f32
    )
    packed[pl.ds(row, edge_ch), half] = edge_grad[:, :LANES]
    packed[pl.ds(row + edge_ch, edge_ch), half] = edge_grad[:, LANES:]
    wide_dot = jnp.transpose(jnp.broadcast_to(dot_grad, (HEADS * ALPHA, LANES)))
    spare = DIM2 - 2 * edge_ch
    tail = iota((spare, LANES), 0)
    first = jnp.broadcast_to(wide_dot[:1, :LANES], (spare, LANES))
    second = jnp.broadcast_to(wide_dot[:1, LANES:], (spare, LANES))
    packed[pl.ds(row + 2 * edge_ch, spare), half] = jnp.where(
        tail == 0, first, jnp.where(tail == 1, second, 0.0)
    )
    row += DIM2
    packed[pl.ds(row, CH), :] = dot_nt(x0[pl.ds(0, CH), :], pre_grad)


PACKED_ROWS = 2 * DIM0 + 3 * DIM1 + 3 * DIM2 + CH


def unpack(packed, edge_ch):
    row = 0
    panels = []
    for dim, count in ((DIM0, 2), (DIM1, 3), (DIM2, 3)):
        for _ in range(count):
            panels.append(packed[row : row + dim])
            row += dim
    rest = DIM0 - PANEL
    zero = jnp.concatenate([panels[0], panels[1][:, :rest]], axis=1)
    proj = panels[1][:, rest:].reshape(LMAX + 1, CH, CH)
    one = jnp.concatenate(panels[2:5], axis=1)
    one = jnp.stack([one[:, :DIM1], one[:, DIM1:]])
    two = jnp.concatenate(panels[5:7] + [panels[7][:, :LANES]], axis=1)
    two = jnp.stack([two[:, :DIM2], two[:, DIM2:]])
    half = panels[7][:, LANES:]
    alpha_edge = jnp.concatenate([half[:edge_ch], half[edge_ch : 2 * edge_ch]], axis=1)
    alpha_dot = half[2 * edge_ch : 2 * edge_ch + 2].reshape(-1)
    alpha_in = packed[row : row + CH]
    return zero, one, two, alpha_in, alpha_edge, alpha_dot, proj


def source_kernel(
    source_slot, rot, g0, g1, g2, pre_grad, wzero, wone, wtwo, ain,
    sums_out, d0, d1, d2, terms,
):
    edges = source_slot.shape[1]
    slots = sums_out.shape[0] * sums_out.shape[1]
    d0[...] = dot_nn(wzero[...], g0[...])
    d0[pl.ds(0, CH), :] += dot_nn(ain[...], pre_grad[...])
    d1[...] = dot_nn(wone[0], g1[pl.ds(0, DIM1), :]) + dot_nn(wone[1], g1[pl.ds(DIM1, DIM1), :])
    d2[...] = dot_nn(wtwo[0], g2[pl.ds(0, DIM2), :]) + dot_nn(wtwo[1], g2[pl.ds(DIM2, DIM2), :])

    def load(degree, order, half):
        ref, row, second = frame_place(degree, order, (d0, d1, d2))
        return ref[pl.ds(row, CH), lane_at(half, edges, second)]

    terms[pl.ds(FLAT, COLS - FLAT), :] = jnp.zeros((COLS - FLAT, 2 * edges), bf16)
    from_frame(load, rot, edges, store_terms(terms, edges))
    slot_sums(terms, mask_to(one_hot_rows(source_slot, slots), bf16), sums_out)


def make_collect(lanes_total):
    def collect_kernel(place, index_row, *rest):
        arrivals = rest[:lanes_total]
        out, rows = rest[lanes_total:]
        atoms = out.shape[0]
        total = index_row.shape[1]
        collect_rows(place, arrivals, rows)
        picked = mask_to(iota((atoms, total), 0) == index_row[...], bf16)
        twice = jnp.concatenate([picked, picked], axis=1)

        def gather_block(block, carry):
            cols = pl.ds(pl.multiple_of(block * LANES, LANES), LANES)
            high, low = split_two(rows[:, cols])
            out[:, cols] = dot_nn(twice, jnp.concatenate([high, low], axis=0)).astype(bf16)
            return carry

        lax.fori_loop(0, BLOCKS, gather_block, 0)

    return collect_kernel


vmem = pl.BlockSpec(memory_space=pltpu.VMEM)
smem = pl.BlockSpec(memory_space=pltpu.SMEM)


def call(kernel, outs, scratch, *args, scalar=False):
    specs = [smem if scalar and n == 0 else vmem for n in range(len(args))]
    return pl.pallas_call(
        kernel,
        out_shape=[jax.ShapeDtypeStruct(shape, kind) for shape, kind in outs],
        in_specs=specs,
        out_specs=[vmem] * len(outs),
        scratch_shapes=[pltpu.VMEM(shape, kind) for shape, kind in scratch],
        compiler_params=pltpu.CompilerParams(vmem_limit_bytes=VMEM_LIMIT),
    )(*args)


def swap(value, axis, bit):
    size = lax.axis_size(axis)
    return lax.ppermute(value, axis, [(i, i ^ (1 << bit)) for i in range(size)])


def bits_of(axis):
    return (lax.axis_size(axis) - 1).bit_length()


def gather_lanes(value):
    held = {0: value}
    for bit in reversed(range(bits_of("edge"))):
        held.update({k | (1 << bit): swap(v, "edge", bit) for k, v in list(held.items())})
    return [held[k] for k in range(len(held))]


def own_bit(axis, bit):
    return (lax.axis_index(axis) >> bit) & 1


def sum_all(packed):
    steps = [("edge", n) for n in range(bits_of("edge"))]
    steps += [("graph", n) for n in range(bits_of("graph"))]
    current = packed
    for axis, bit in steps:
        mine = own_bit(axis, bit)
        parts = current.reshape(2, current.shape[0] // 2, -1)
        sent = swap(lax.dynamic_index_in_dim(parts, 1 - mine, 0, False), axis, bit)
        current = lax.dynamic_index_in_dim(parts, mine, 0, False) + sent
    current = current.astype(bf16)
    for axis, bit in reversed(steps):
        mine = own_bit(axis, bit)
        other = swap(current, axis, bit)
        current = jnp.concatenate(
            [jnp.where(mine == 0, current, other), jnp.where(mine == 0, other, current)], axis=0
        )
    return current


def shards(
    atom_embed, out_cotangent, send_rows, recv_rows, source_slot, target_slot, rotation,
    edge_feats, edge_bias, conv_zero, conv_one, conv_two, alpha_in, alpha_edge, alpha_dot,
    out_proj,
):
    peers = lax.axis_size("graph")
    lanes_total = lax.axis_size("edge")
    atoms = atom_embed.shape[0]
    edges = rotation.shape[0]
    send_list = send_rows.reshape(peers, -1)
    recv_list = recv_rows.reshape(peers, -1)
    cap = send_list.shape[1]
    slots = peers * cap

    def exchange(value):
        return lax.all_to_all(value, "graph", split_axis=0, concat_axis=0, tiled=True)

    outgoing = atom_embed[send_list].reshape(peers, cap, FLAT)
    table = exchange(outgoing)

    source_row = source_slot.reshape(1, edges)
    target_row = target_slot.reshape(1, edges)
    rot = rotation.T.astype(f32)
    bias = edge_bias.T
    adot = alpha_dot.astype(f32).reshape(-1, 1)
    cot = jnp.pad(out_cotangent.reshape(atoms, FLAT), ((0, 0), (0, COLS - FLAT)))
    degrees = np.array([degree_of(k) for k in range(COEFFS)] + [LMAX], np.int32)
    blank = jnp.zeros((BLOCKS, CH, CH), bf16)
    pairs = jnp.concatenate(
        [
            jnp.concatenate([out_proj[degrees[0::2]], blank], axis=2),
            jnp.concatenate([blank, out_proj[degrees[1::2]]], axis=2),
        ],
        axis=1,
    )
    lists = lax.all_gather(jnp.stack([send_list.reshape(-1), recv_list.reshape(-1)]), "edge")
    send_all = lists[:, 0].reshape(-1)
    recv_all = lists[:, 1].reshape(-1)
    place = lax.axis_index("edge").astype(jnp.int32).reshape(1)

    sums, x0, x1, x2, v0, v1, v2, pre, logits = call(
        forward_kernel,
        [
            ((peers, cap, WIDE), f32),
            ((DIM0, edges), bf16),
            ((DIM1, 2 * edges), bf16),
            ((DIM2, 2 * edges), bf16),
            ((DIM0, edges), f32),
            ((DIM1, 2 * edges), f32),
            ((DIM2, 2 * edges), f32),
            ((HEADS * ALPHA, edges), f32),
            ((8, edges), f32),
        ],
        [
            ((slots, FLAT), f32),
            ((FLAT, edges), f32),
            ((DIM1, 2 * edges), bf16),
            ((DIM2, 2 * edges), bf16),
            ((8, edges), f32),
            ((COLS, 2 * edges), bf16),
        ],
        table, source_row, target_row, rot, edge_feats, bias,
        conv_zero.T, jnp.swapaxes(conv_one, 1, 2), jnp.swapaxes(conv_two, 1, 2),
        alpha_in.T, alpha_edge.T, adot,
    )

    arrivals = gather_lanes(exchange(sums))
    total = lanes_total * slots
    out, back, proj = call(
        make_finish(lanes_total),
        [((atoms, COLS), bf16), ((peers, cap, WIDE), bf16), (((LMAX + 1) * CH, CH), f32)],
        [((total, WIDE), f32), ((atoms, COLS), f32), ((atoms, COLS), bf16)],
        place, recv_all.reshape(1, -1), recv_all.reshape(-1, 1), recv_list.reshape(-1, 1),
        cot, pairs, *arrivals,
        scalar=True,
    )

    packed, g0, g1, g2, pre_grad = call(
        gradient_kernel,
        [
            ((PACKED_ROWS, PANEL), f32),
            ((DIM0, edges), bf16),
            ((2 * DIM1, 2 * edges), bf16),
            ((2 * DIM2, 2 * edges), bf16),
            ((HEADS * ALPHA, edges), bf16),
        ],
        [((slots, WIDE), f32), ((COLS, edges), f32), ((8, edges), f32)],
        exchange(back), target_row, rot, edge_feats, x0, x1, x2, v0, v1, v2, pre, logits, adot,
        proj,
    )
    grads = sum_all(packed)

    (source_sums,) = call(
        source_kernel,
        [((peers, cap, COLS), f32)],
        [
            ((DIM0, edges), f32),
            ((DIM1, 2 * edges), f32),
            ((DIM2, 2 * edges), f32),
            ((COLS, 2 * edges), bf16),
        ],
        source_row, rot, g0, g1, g2, pre_grad, conv_zero, conv_one, conv_two, alpha_in,
    )
    (embed,) = call(
        make_collect(lanes_total),
        [((atoms, COLS), bf16)],
        [((total, COLS), f32)],
        place, send_all.reshape(1, -1), *gather_lanes(exchange(source_sums)),
        scalar=True,
    )

    def shaped(rows):
        return rows[:, :FLAT].reshape(atoms, COEFFS, CH)

    return (shaped(out), shaped(embed)) + unpack(grads, edge_feats.shape[1])


def solution(mesh):
    in_specs = (
        P(("groups", "graph"), None, None),
        P(("groups", "graph"), None, None),
        P(("groups", "graph"), None, "edge", None),
        P(("groups", "graph"), None, "edge", None),
        P(("groups", "graph", "edge")),
        P(("groups", "graph", "edge")),
        P(("groups", "graph", "edge"), None),
        P(("groups", "graph", "edge"), None),
        P(("groups", "graph", "edge"), None),
        P(),
        P(),
        P(),
        P(),
        P(),
        P(),
        P(),
    )
    out_specs = (
        P(("groups", "graph"), None, None),
        P(("groups", "graph"), None, None),
        P("groups", None),
        P("groups", None, None),
        P("groups", None, None),
        P("groups", None),
        P("groups", None),
        P("groups"),
        P("groups", None, None),
    )
    return jax.shard_map(shards, mesh=mesh, in_specs=in_specs, out_specs=out_specs, check_vma=False)
```

```python
import jax
import jax.numpy as jnp
import numpy as np
from jax import lax
from jax.experimental import pallas as pl
from jax.experimental.pallas import tpu as pltpu
from jax.sharding import PartitionSpec as P

LMAX = 6
MMAX = 2
CH = 64
HEADS = 4
VAL = 16
ALPHA = 64
COEFFS = (LMAX + 1) * (LMAX + 1)
FLAT = COEFFS * CH
LANES = 128
BLOCKS = (FLAT + LANES - 1) // LANES
COLS = BLOCKS * LANES
WIDE = COLS + LANES
DIM0 = (LMAX + 1) * CH
DIM1 = LMAX * CH
DIM2 = (LMAX - 1) * CH
PANEL = 256

leak_slope = 0.2
floor_value = -1e30
bf16 = jnp.bfloat16
f32 = jnp.float32

VMEM_LIMIT = 56 * 1024 * 1024


def degree_blocks():
    result = []
    offset = 0
    for degree in range(LMAX + 1):
        centre = min(degree, MMAX)
        row_total = 2 * centre + 1
        col_total = 2 * degree + 1
        result.append((degree, centre, row_total, col_total, offset))
        offset += row_total * col_total
    return result


def degree_of(coeff):
    return int(np.sqrt(coeff))


def dot_nn(left, right):
    return jnp.dot(left, right, preferred_element_type=f32)


def dot_nt(left, right):
    return lax.dot_general(left, right, (((1,), (1,)), ((), ())), preferred_element_type=f32)


def dot_tn(left, right):
    return lax.dot_general(left, right, (((0,), (0,)), ((), ())), preferred_element_type=f32)


def iota(shape, dim):
    return lax.broadcasted_iota(jnp.int32, shape, dim)


def split_two(value):
    high = value.astype(bf16)
    return high, (value - high.astype(f32)).astype(bf16)


def to_frame(source, rot, edges, emit):
    def body(half, carry):
        lanes = pl.ds(pl.multiple_of(half * LANES, LANES), LANES)
        for degree, centre, row_total, col_total, offset in degree_blocks():
            sums = [None] * row_total
            for j in range(col_total):
                column = source[pl.ds((degree * degree + j) * CH, CH), lanes]
                for i in range(row_total):
                    term = rot[pl.ds(offset + i * col_total + j, 1), lanes] * column
                    sums[i] = term if j == 0 else sums[i] + term
            for i in range(row_total):
                emit(degree, i - centre, half, sums[i])
        return carry

    lax.fori_loop(0, edges // LANES, body, 0)


def from_frame(load, rot, edges, emit):
    def body(half, carry):
        lanes = pl.ds(pl.multiple_of(half * LANES, LANES), LANES)
        for degree, centre, row_total, col_total, offset in degree_blocks():
            rows = [load(degree, i - centre, half) for i in range(row_total)]
            for j in range(col_total):
                total = None
                for i in range(row_total):
                    term = rot[pl.ds(offset + i * col_total + j, 1), lanes] * rows[i]
                    total = term if i == 0 else total + term
                emit(degree * degree + j, half, total)
        return carry

    lax.fori_loop(0, edges // LANES, body, 0)


def lane_at(half, edges, second):
    return pl.ds(pl.multiple_of(half * LANES + (edges if second else 0), LANES), LANES)


def frame_place(degree, order, refs):
    if order == 0:
        return refs[0], degree * CH, False
    which = abs(order)
    return refs[which], (degree - which) * CH, order < 0


def spread_heads(rows):
    return jnp.concatenate(
        [jnp.broadcast_to(row, (VAL, row.shape[1])) for row in rows], axis=0
    )


def one_hot_rows(slot_ref, slots):
    edges = slot_ref.shape[1]
    return iota((slots, edges), 0) == slot_ref[...]


def mask_to(mask, dtype):
    return jnp.where(mask, 1.0, 0.0).astype(dtype)


def stack_table(table_ref, rows_ref):
    peers, cap, width = table_ref.shape
    for start in range(0, peers * cap, 8):
        parts = [table_ref[g].astype(f32) for g in range(start // cap, (start + 8) // cap)]
        rows_ref[pl.ds(start, 8), :] = jnp.concatenate(parts, axis=0)


def put_rows(out_ref, cols, value):
    peers, cap = out_ref.shape[0], out_ref.shape[1]
    for g in range(peers):
        out_ref[g, :, cols] = value[g * cap : (g + 1) * cap].astype(out_ref.dtype)


def slot_sums(terms, one_hot, out_ref):
    both = jnp.concatenate([one_hot, one_hot], axis=1)
    for start in range(0, COLS, PANEL):
        size = min(PANEL, COLS - start)
        put_rows(out_ref, pl.ds(start, size), dot_nt(both, terms[pl.ds(start, size), :]))


def store_terms(terms, edges):
    def emit(coeff, half, value):
        high, low = split_two(value)
        rows = pl.ds(coeff * CH, CH)
        terms[rows, lane_at(half, edges, False)] = high
        terms[rows, lane_at(half, edges, True)] = low

    return emit


def listed_rows(list_ref, shape):
    peers, cap = list_ref.shape[1], list_ref.shape[3]
    row = iota(shape, 0)
    result = jnp.zeros(shape, jnp.int32)
    for slot in range(peers * cap):
        result = jnp.where(row == slot, list_ref[0, slot // cap, 0, slot % cap], result)
    return result


def outgoing_kernel(send, recv, embed, out):
    atoms = embed.shape[0]
    slots = out.shape[0] * out.shape[1]
    sent = listed_rows(send, (slots, LANES))
    received = listed_rows(recv, (slots, LANES))
    picked = mask_to(iota((slots, atoms), 1) == sent[:, :atoms], bf16)
    put_rows(out, pl.ds(0, FLAT), dot_nn(picked, embed[...]))
    lane = iota((slots, LANES), 1)
    put_rows(out, pl.ds(FLAT, COLS - FLAT), jnp.zeros((slots, COLS - FLAT), f32))
    side = jnp.where(lane == 0, received, jnp.where(lane == 1, sent, 0))
    put_rows(out, pl.ds(COLS, LANES), side.astype(f32))


def swapped_halves(value, edges):
    return jnp.concatenate([-value[:, edges:], value[:, :edges]], axis=1)


def forward_kernel(
    table, source_slot, target_slot, rot, feats, bias, wzero, wone, wtwo, ain, aedge, adot,
    sums_out, x0, x1, x2, v0, v1, v2, pre_out, logit_out, lists_out,
    rows, gathered, weights, terms,
):
    edges = source_slot.shape[1]
    slots = table.shape[0] * table.shape[1]
    stack_table(table, rows)
    picked = mask_to(one_hot_rows(source_slot, slots), bf16)
    gathered[...] = dot_tn(rows[:, pl.ds(0, FLAT)].astype(bf16), picked)
    lists = rows[:, pl.ds(COLS, LANES)]
    lists_out[...] = lists

    def emit(degree, order, half, value):
        ref, row, second = frame_place(degree, order, (x0, x1, x2))
        ref[pl.ds(row, CH), lane_at(half, edges, second)] = value.astype(bf16)

    to_frame(gathered, rot, edges, emit)

    pre = dot_nn(ain[...], x0[pl.ds(0, CH), :]) + dot_nt(aedge[...], feats[...])
    pre_out[...] = pre
    hidden = jnp.where(pre > 0, pre, leak_slope * pre) * adot[...]
    aims = one_hot_rows(target_slot, slots)
    lane = iota((slots, LANES), 1)
    side = jnp.where(lane == 2 * HEADS, lists[:, :1], 0.0)
    for h in range(HEADS):
        logit = jnp.sum(hidden[h * ALPHA : (h + 1) * ALPHA], axis=0, keepdims=True)
        logit = logit + bias[pl.ds(h, 1), :]
        logit_out[pl.ds(h, 1), :] = logit
        peak = jnp.max(jnp.where(aims, logit, floor_value), axis=1, keepdims=True)
        of_edge = jnp.sum(jnp.where(aims, peak, 0.0), axis=0, keepdims=True)
        weight = jnp.exp(logit - of_edge)
        weights[pl.ds(h, 1), :] = weight
        den = jnp.sum(jnp.where(aims, weight, 0.0), axis=1, keepdims=True)
        side = jnp.where(lane == h, den, jnp.where(lane == HEADS + h, peak, side))
    put_rows(sums_out, pl.ds(COLS, LANES), side)

    v0[...] = dot_nn(wzero[...], x0[...])
    for out, weight, value in ((v1, wone, x1[...]), (v2, wtwo, x2[...])):
        out[...] = dot_nn(weight[0], value) + swapped_halves(dot_nn(weight[1], value), edges)

    def load(degree, order, half):
        ref, row, second = frame_place(degree, order, (v0, v1, v2))
        return ref[pl.ds(row, CH), lane_at(half, edges, second)]

    store = store_terms(terms, edges)

    def weigh(coeff, half, value):
        lanes = lane_at(half, edges, False)
        spread = spread_heads([weights[pl.ds(h, 1), lanes] for h in range(HEADS)])
        store(coeff, half, value * spread)

    terms[pl.ds(FLAT, COLS - FLAT), :] = jnp.zeros((COLS - FLAT, 2 * edges), bf16)
    from_frame(load, rot, edges, weigh)
    slot_sums(terms, mask_to(aims, bf16), sums_out)


def lane_heads(values, shape):
    head = (iota(shape, 1) % CH) // VAL
    result = jnp.broadcast_to(values[0], shape)
    for h in range(1, HEADS):
        result = jnp.where(head == h, values[h], result)
    return result


def collect_rows(place, arrivals, rows_ref):
    for k, arrival in enumerate(arrivals):
        peers, cap, width = arrival.shape
        base = (place[0] ^ k) * (peers * cap)
        for start in range(0, peers * cap, 8):
            parts = [arrival[g] for g in range(start // cap, (start + 8) // cap)]
            at = pl.ds(pl.multiple_of(base + start, 8), 8)
            rows_ref[at, :] = jnp.concatenate(parts, axis=0)


def pair_weight(out_proj, block):
    first = out_proj[degree_of(2 * block)]
    if 2 * block + 1 >= COEFFS:
        return first
    second = out_proj[degree_of(2 * block + 1)]
    blank = jnp.zeros((CH, CH), f32)
    top = jnp.concatenate([first.astype(f32), blank], axis=1)
    low = jnp.concatenate([blank, second.astype(f32)], axis=1)
    return jnp.concatenate([top, low], axis=0).astype(bf16)


def pair_key(block):
    return degree_of(2 * block), min(degree_of(min(2 * block + 1, COEFFS)), LMAX)


def block_cols(block):
    return pl.ds(block * LANES, min(LANES, FLAT - block * LANES))


def make_finish(lanes_total):
    def finish_kernel(place, cot, out_proj, *rest):
        arrivals = rest[:lanes_total]
        agg_out, back, rows, terms, num_grad = rest[lanes_total:]
        atoms = cot.shape[0]
        slots = back.shape[0] * back.shape[1]
        total = lanes_total * slots
        collect_rows(place, arrivals, rows)
        side = rows[:, pl.ds(COLS, LANES)]
        at_atom = iota((total, atoms), 1).astype(f32)
        names = at_atom == side[:, 2 * HEADS : 2 * HEADS + 1]
        own_side = jnp.concatenate([arrivals[0][g][:, COLS:] for g in range(back.shape[0])], axis=0)
        own = at_atom[:slots] == own_side[:, 2 * HEADS : 2 * HEADS + 1]
        eye = iota((atoms, atoms), 0) == iota((atoms, atoms), 1)
        scales, dens, own_peaks = [], [], []
        for h in range(HEADS):
            peak_rows = side[:, HEADS + h : HEADS + h + 1]
            peak = jnp.max(jnp.where(names, peak_rows, floor_value), axis=0, keepdims=True)
            of_row = jnp.sum(jnp.where(names, peak, 0.0), axis=1, keepdims=True)
            scale = jnp.exp(peak_rows - of_row)
            scaled_den = side[:, h : h + 1] * scale
            den = jnp.sum(jnp.where(names, scaled_den, 0.0), axis=0, keepdims=True)
            scales.append(scale)
            dens.append(jnp.sum(jnp.where(eye, den, 0.0), axis=1, keepdims=True))
            own_peaks.append(jnp.sum(jnp.where(own, peak, 0.0), axis=1, keepdims=True))
        scale_full = lane_heads(scales, (total, LANES))
        den_full = lane_heads(dens, (atoms, LANES))
        picked = mask_to(names, bf16)
        twice = jnp.concatenate([picked, picked], axis=0)
        for block in range(BLOCKS):
            cols = pl.ds(block * LANES, LANES)
            high, low = split_two(rows[:, cols] * scale_full)
            terms[pl.ds(0, total), cols] = high
            terms[pl.ds(total, total), cols] = low

        den_sum = jnp.zeros((atoms, LANES), f32)
        weights = {}
        for block in range(BLOCKS):
            cols = block_cols(block)
            width = cols.size
            agg = dot_tn(twice, terms[:, cols]) / den_full[:, :width]
            agg_out[:, cols] = agg.astype(bf16)
            key = pair_key(block)
            if key not in weights:
                weights = {key: pair_weight(out_proj, block)}
            weight = weights[key] if width == LANES else out_proj[LMAX]
            agg_grad = dot_nt(cot[:, cols], weight)
            num_grad[:, cols] = (agg_grad / den_full[:, :width]).astype(bf16)
            product = agg_grad * agg
            if width < LANES:
                product = jnp.concatenate([product, jnp.zeros_like(product)], axis=1)
            den_sum = den_sum + product

        own_low = mask_to(own, bf16)
        put_rows(back, pl.ds(0, FLAT), dot_nn(own_low, num_grad[...]))
        put_rows(back, pl.ds(FLAT, COLS - FLAT), jnp.zeros((slots, COLS - FLAT), f32))
        head = (iota((atoms, LANES), 1) % CH) // VAL
        lane = iota((slots, LANES), 1)
        extra = jnp.zeros((slots, LANES), f32)
        for h in range(HEADS):
            summed = jnp.sum(jnp.where(head == h, den_sum, 0.0), axis=1, keepdims=True)
            den_grad = (-summed / dens[h]).astype(bf16).astype(f32)
            as_row = jnp.sum(jnp.where(eye, den_grad, 0.0), axis=0, keepdims=True)
            of_row = jnp.sum(jnp.where(own, as_row, 0.0), axis=1, keepdims=True)
            high = own_peaks[h].astype(bf16).astype(f32)
            rest_one = own_peaks[h] - high
            mid = rest_one.astype(bf16).astype(f32)
            for n, value in enumerate((of_row, high, mid, rest_one - mid)):
                extra = jnp.where(lane == n * HEADS + h, value, extra)
        put_rows(back, pl.ds(COLS, LANES), extra)

    return finish_kernel


def make_project(lanes_total):
    def project_kernel(agg_low, cot, out_proj, out, proj):
        tops = [None] * (LMAX + 1)
        lows = [None] * (LMAX + 1)
        weights = {}
        for block in range(BLOCKS):
            cols = block_cols(block)
            width = cols.size
            left, right = agg_low[:, cols], cot[:, cols]
            key = pair_key(block)
            if key not in weights:
                weights = {key: pair_weight(out_proj, block)}
            weight = weights[key] if width == LANES else out_proj[LMAX]
            out[:, cols] = dot_nn(left, weight).astype(bf16)
            outer = dot_tn(left, right)
            first = degree_of(2 * block)
            top = outer[:CH, :CH]
            tops[first] = top if tops[first] is None else tops[first] + top
            if width == LANES:
                second = degree_of(2 * block + 1)
                low = outer[CH:]
                lows[second] = low if lows[second] is None else lows[second] + low
        for degree in range(LMAX + 1):
            piece = jnp.zeros((CH, CH), f32)
            if tops[degree] is not None:
                piece = piece + tops[degree]
            if lows[degree] is not None:
                piece = piece + lows[degree][:, CH:]
            proj[pl.ds(degree * CH, CH), :] = piece * (1.0 / lanes_total)

    return project_kernel


def gradient_kernel(
    place, table, target_slot, rot, feats, x0, x1, x2, v0, v1, v2, pre, logits, adot, proj,
    g0, top1, top2, pre_grad_out, kept0, sent0, kept1, sent1, kept2, sent2,
    rows, spread_grad, weights, g1, g2, packed, semaphores,
):
    edges = target_slot.shape[1]
    slots = table.shape[0] * table.shape[1]
    stack_table(table, rows)
    picked = mask_to(one_hot_rows(target_slot, slots), bf16)
    low_rows = rows[...].astype(bf16)
    spread_grad[...] = dot_tn(low_rows[:, :COLS], picked)
    side = dot_tn(low_rows[:, COLS:], picked)
    for h in range(HEADS):
        peak = (side[HEADS + h : HEADS + h + 1] + side[2 * HEADS + h : 2 * HEADS + h + 1]) + side[
            3 * HEADS + h : 3 * HEADS + h + 1
        ]
        weights[pl.ds(h, 1), :] = jnp.exp(logits[pl.ds(h, 1), :] - peak)

    state = {}

    def emit(degree, order, half, value):
        lanes = lane_at(half, edges, False)
        ref, row, second = frame_place(degree, order, (v0, v1, v2))
        product = value * ref[pl.ds(row, CH), lane_at(half, edges, second)]
        if degree == 0:
            state["sum"] = product
            state["spread"] = spread_heads([weights[pl.ds(h, 1), lanes] for h in range(HEADS)])
        else:
            state["sum"] = state["sum"] + product
        grad = (value * state["spread"]).astype(bf16)
        ref, row, second = frame_place(degree, order, (g0, g1, g2))
        ref[pl.ds(row, CH), lane_at(half, edges, second)] = grad
        if order != 0:
            swapped = grad if order < 0 else -grad
            below = row + (DIM1 if abs(order) == 1 else DIM2)
            ref[pl.ds(below, CH), lane_at(half, edges, not second)] = swapped
        if degree == LMAX and order == MMAX:
            for h in range(HEADS):
                part = state["sum"][h * VAL : (h + 1) * VAL]
                weights[pl.ds(HEADS + h, 1), lanes] = jnp.sum(part, axis=0, keepdims=True)

    to_frame(spread_grad, rot, edges, emit)

    hidden = jnp.where(pre[...] > 0, pre[...], leak_slope * pre[...])
    logit_grads = [
        weights[pl.ds(h, 1), :] * (weights[pl.ds(HEADS + h, 1), :] + side[h : h + 1])
        for h in range(HEADS)
    ]
    tall = jnp.concatenate(
        [jnp.broadcast_to(row, (ALPHA, edges)) for row in logit_grads], axis=0
    )
    slope = jnp.where(pre[...] > 0, 1.0, leak_slope)
    pre_grad = (tall * adot[...] * slope).astype(bf16)
    pre_grad_out[...] = pre_grad
    dot_grad = jnp.sum(tall * hidden, axis=1, keepdims=True)

    top1[...] = g1[pl.ds(0, DIM1), :]
    top2[...] = g2[pl.ds(0, DIM2), :]
    mine = place[0] & 1
    copies = []

    def put(row, value, at=0):
        for side in range(2):
            low, high = max(at, side * LANES), min(at + value.shape[1], (side + 1) * LANES)
            if low < high:
                piece = value[:, low - at : high - at]
                cols = pl.ds(low - side * LANES, high - low)
                packed[side, pl.ds(row, value.shape[0]), cols] = piece

    def send(chunk, kept, sent):
        start, size = CHUNKS[chunk]
        rows_of = pl.ds(start, size)
        for n, (side, out) in enumerate(((mine, kept), (1 - mine, sent))):
            copy = pltpu.make_async_copy(
                packed.at[side, rows_of, :], out, semaphores.at[2 * chunk + n]
            )
            copy.start()
            copies.append(copy)

    row = CHUNKS[1][0]
    for start in range(0, 2 * DIM1, PANEL):
        put(row, dot_nt(x1[...], g1[pl.ds(start, PANEL), :]))
        row += DIM1
    send(1, kept1, sent1)

    row = 0
    for start in range(0, DIM0, PANEL):
        size = min(PANEL, DIM0 - start)
        put(row, dot_nt(x0[...], g0[pl.ds(start, size), :]))
        if size < PANEL:
            put(row, proj[...], size)
        row += DIM0
    send(0, kept0, sent0)

    row = CHUNKS[2][0]
    for start in range(0, 2 * DIM2, PANEL):
        size = min(PANEL, 2 * DIM2 - start)
        put(row, dot_nt(x2[...], g2[pl.ds(start, size), :]))
        row += DIM2
    row -= DIM2
    edge_ch = feats.shape[1]
    edge_grad = lax.dot_general(
        feats[...], pre_grad, (((0,), (1,)), ((), ())), preferred_element_type=f32
    )
    put(row, edge_grad[:, :LANES], LANES)
    put(row + edge_ch, edge_grad[:, LANES:], LANES)
    wide_dot = jnp.transpose(jnp.broadcast_to(dot_grad, (HEADS * ALPHA, LANES)))
    spare = DIM2 - 2 * edge_ch
    tail = iota((spare, LANES), 0)
    first = jnp.broadcast_to(wide_dot[:1, :LANES], (spare, LANES))
    second = jnp.broadcast_to(wide_dot[:1, LANES:], (spare, LANES))
    put(row + 2 * edge_ch, jnp.where(tail == 0, first, jnp.where(tail == 1, second, 0.0)), LANES)
    row += DIM2
    put(row, dot_nt(x0[pl.ds(0, CH), :], pre_grad))
    send(2, kept2, sent2)
    for copy in copies:
        copy.wait()


CHUNKS = ((0, 2 * DIM0), (2 * DIM0, 3 * DIM1), (2 * DIM0 + 3 * DIM1, 3 * DIM2 + CH))
PACKED_ROWS = sum(size for start, size in CHUNKS)


def halves_of(place, mine, other):
    first = (place[0] & 1) == 0
    left, right = mine[...].astype(f32), other[...].astype(f32)
    return jnp.where(first, left, right), jnp.where(first, right, left)


def unpack_zero_kernel(place, mine, other, zero, proj):
    left, right = halves_of(place, mine, other)
    zero[:, pl.ds(0, LANES)] = left[:DIM0].astype(bf16)
    zero[:, pl.ds(LANES, LANES)] = right[:DIM0].astype(bf16)
    zero[:, pl.ds(2 * LANES, LANES)] = left[DIM0:].astype(bf16)
    zero[:, pl.ds(3 * LANES, DIM0 - 3 * LANES)] = right[DIM0:, : DIM0 - 3 * LANES].astype(bf16)
    for degree in range(LMAX + 1):
        start = DIM0 + degree * CH
        proj[degree] = right[start : start + CH, DIM0 - 3 * LANES :].astype(bf16)


def unpack_one_kernel(place, mine, other, one):
    left, right = halves_of(place, mine, other)
    for n in range(2 * DIM1 // LANES):
        panel = (left, right)[n % 2][(n // 2) * DIM1 : (n // 2 + 1) * DIM1]
        per = DIM1 // LANES
        one[n // per, :, pl.ds((n % per) * LANES, LANES)] = panel.astype(bf16)


def unpack_two_kernel(place, mine, other, two, alpha_in, alpha_edge, alpha_dot):
    left, right = halves_of(place, mine, other)
    panels = [(left, right)[n % 2][(n // 2) * DIM2 : (n // 2 + 1) * DIM2] for n in range(5)]
    whole = jnp.concatenate(panels, axis=1)
    two[0] = whole[:, :DIM2].astype(bf16)
    two[1] = whole[:, DIM2:].astype(bf16)
    edge_ch = alpha_edge.shape[0]
    rest = right[2 * DIM2 : 3 * DIM2]
    alpha_edge[:, pl.ds(0, LANES)] = rest[:edge_ch].astype(bf16)
    alpha_edge[:, pl.ds(LANES, LANES)] = rest[edge_ch : 2 * edge_ch].astype(bf16)
    alpha_dot[...] = rest[2 * edge_ch : 2 * edge_ch + 2].astype(bf16)
    alpha_in[:, pl.ds(0, LANES)] = left[3 * DIM2 :].astype(bf16)
    alpha_in[:, pl.ds(LANES, LANES)] = right[3 * DIM2 :].astype(bf16)


def source_kernel(
    source_slot, lists, rot, g0, g1, g2, pre_grad, wzero, wone, wtwo, ain,
    *rest,
):
    sums_out, d0, d1, d2, terms = rest[-5:]
    edges = source_slot.shape[1]
    slots = sums_out.shape[0] * sums_out.shape[1]
    d0[...] = dot_nn(wzero[...], g0[...])
    d0[pl.ds(0, CH), :] += dot_nn(ain[...], pre_grad[...])
    for out, weight, value in ((d1, wone, g1[...]), (d2, wtwo, g2[...])):
        out[...] = dot_nn(weight[0], value) - swapped_halves(dot_nn(weight[1], value), edges)

    def load(degree, order, half):
        ref, row, second = frame_place(degree, order, (d0, d1, d2))
        return ref[pl.ds(row, CH), lane_at(half, edges, second)]

    terms[pl.ds(FLAT, COLS - FLAT), :] = jnp.zeros((COLS - FLAT, 2 * edges), bf16)
    from_frame(load, rot, edges, store_terms(terms, edges))
    slot_sums(terms, mask_to(one_hot_rows(source_slot, slots), bf16), sums_out)
    put_rows(sums_out, pl.ds(COLS, LANES), lists[...])


def make_collect(lanes_total):
    def collect_kernel(place, *rest):
        arrivals = rest[:lanes_total]
        out, rows = rest[lanes_total:]
        atoms = out.shape[0]
        total = rows.shape[0]
        collect_rows(place, arrivals, rows)
        index = rows[:, pl.ds(COLS, LANES)][:, 1:2]
        picked = mask_to(iota((total, atoms), 1).astype(f32) == index, bf16)
        twice = jnp.concatenate([picked, picked], axis=0)
        for block in range(BLOCKS):
            cols = block_cols(block)
            high, low = split_two(rows[:, cols])
            out[:, cols] = dot_tn(twice, jnp.concatenate([high, low], axis=0)).astype(bf16)

    return collect_kernel


vmem = pl.BlockSpec(memory_space=pltpu.VMEM)
smem = pl.BlockSpec(memory_space=pltpu.SMEM)
anywhere = pl.BlockSpec(memory_space=pl.ANY)


def call(kernel, outs, scratch, *args, scalars=0, apart=0, after=(), work=4):
    specs = [smem if n < scalars else vmem for n in range(len(args))] + [anywhere] * len(after)
    out_specs = [vmem if n < len(outs) - apart else anywhere for n in range(len(outs))]
    shapes = [pltpu.VMEM(*entry) if isinstance(entry, tuple) else entry for entry in scratch]
    moved = sum(int(np.prod(a.shape)) * a.dtype.itemsize for a in args)
    return pl.pallas_call(
        kernel,
        out_shape=[jax.ShapeDtypeStruct(shape, kind) for shape, kind in outs],
        in_specs=specs,
        out_specs=out_specs,
        scratch_shapes=shapes,
        compiler_params=pltpu.CompilerParams(vmem_limit_bytes=VMEM_LIMIT),
        cost_estimate=pl.CostEstimate(
            flops=work * 10**9, bytes_accessed=moved, transcendentals=0
        ),
    )(*args, *after)


def swap(value, axis, bit):
    size = lax.axis_size(axis)
    return lax.ppermute(value, axis, [(i, i ^ (1 << bit)) for i in range(size)])


def bits_of(axis):
    return (lax.axis_size(axis) - 1).bit_length()


def gather_lanes(value):
    held = {0: value}
    for bit in reversed(range(bits_of("edge"))):
        held.update({k | (1 << bit): swap(v, "edge", bit) for k, v in list(held.items())})
    return [held[k] for k in range(len(held))]


def own_bit(axis, bit):
    return (lax.axis_index(axis) >> bit) & 1


def sum_all(current):
    steps = [("edge", n) for n in range(1, bits_of("edge"))]
    steps += [("graph", n) for n in range(bits_of("graph"))]
    for axis, bit in steps:
        mine = own_bit(axis, bit)
        parts = current.reshape(2, current.shape[0] // 2, -1)
        other = swap(lax.dynamic_index_in_dim(parts, 1 - mine, 0, False), axis, bit)
        current = lax.dynamic_index_in_dim(parts, mine, 0, False) + other
    current = current.astype(bf16)
    for axis, bit in reversed(steps):
        mine = own_bit(axis, bit)
        other = swap(current, axis, bit)
        current = jnp.concatenate(
            [jnp.where(mine == 0, current, other), jnp.where(mine == 0, other, current)], axis=0
        )
    return current, swap(current, "edge", 0)


def shards(
    atom_embed, out_cotangent, send_rows, recv_rows, source_slot, target_slot, rotation,
    edge_feats, edge_bias, conv_zero, conv_one, conv_two, alpha_in, alpha_edge, alpha_dot,
    out_proj,
):
    peers = lax.axis_size("graph")
    lanes_total = lax.axis_size("edge")
    atoms = atom_embed.shape[0]
    edges = rotation.shape[0]
    cap = send_rows.shape[3]
    slots = peers * cap
    place = lax.axis_index("edge").astype(jnp.int32).reshape(1)

    def exchange(value):
        return lax.all_to_all(value, "graph", split_axis=0, concat_axis=0, tiled=True)

    (outgoing,) = call(
        outgoing_kernel, [((peers, cap, WIDE), bf16)], [],
        send_rows, recv_rows, atom_embed.reshape(atoms, FLAT),
        scalars=2, work=1,
    )
    table = exchange(outgoing)

    source_row = source_slot.reshape(1, edges)
    target_row = target_slot.reshape(1, edges)
    rot = rotation.T.astype(f32)
    bias = edge_bias.T
    adot = alpha_dot.astype(f32).reshape(-1, 1)
    cot = out_cotangent.reshape(atoms, FLAT)

    sums, x0, x1, x2, v0, v1, v2, pre, logits, lists = call(
        forward_kernel,
        [
            ((peers, cap, WIDE), f32),
            ((DIM0, edges), bf16),
            ((DIM1, 2 * edges), bf16),
            ((DIM2, 2 * edges), bf16),
            ((DIM0, edges), f32),
            ((DIM1, 2 * edges), f32),
            ((DIM2, 2 * edges), f32),
            ((HEADS * ALPHA, edges), f32),
            ((8, edges), f32),
            ((slots, LANES), f32),
        ],
        [
            ((slots, WIDE), f32),
            ((FLAT, edges), f32),
            ((8, edges), f32),
            ((COLS, 2 * edges), bf16),
        ],
        table, source_row, target_row, rot, edge_feats, bias,
        conv_zero.T, jnp.swapaxes(conv_one, 1, 2), jnp.swapaxes(conv_two, 1, 2),
        alpha_in.T, alpha_edge.T, adot,
        work=8,
    )

    arrivals = gather_lanes(exchange(sums))
    total = lanes_total * slots
    agg_low, back = call(
        make_finish(lanes_total),
        [((atoms, FLAT), bf16), ((peers, cap, WIDE), bf16)],
        [((total, WIDE), f32), ((2 * total, COLS), bf16), ((atoms, FLAT), bf16)],
        place, cot, out_proj, *arrivals,
        scalars=1,
    )
    out, proj = call(
        make_project(lanes_total),
        [((atoms, FLAT), bf16), (((LMAX + 1) * CH, CH), f32)],
        [],
        agg_low, cot, out_proj,
    )

    halves = [((size, LANES), f32) for start, size in CHUNKS for _ in range(2)]
    g0, g1, g2, pre_grad, *halves = call(
        gradient_kernel,
        [
            ((DIM0, edges), bf16),
            ((DIM1, 2 * edges), bf16),
            ((DIM2, 2 * edges), bf16),
            ((HEADS * ALPHA, edges), bf16),
        ]
        + halves,
        [
            ((slots, WIDE), f32),
            ((COLS, edges), f32),
            ((8, edges), f32),
            ((2 * DIM1, 2 * edges), bf16),
            ((2 * DIM2, 2 * edges), bf16),
            ((2, PACKED_ROWS, LANES), f32),
            pltpu.SemaphoreType.DMA((len(halves),)),
        ],
        place, exchange(back), target_row, rot, edge_feats,
        x0, x1, x2, v0, v1, v2, pre, logits, adot, proj,
        scalars=1, apart=len(halves), work=8,
    )
    currents = [
        halves[2 * n] + swap(halves[2 * n + 1], "edge", 0) for n in range(len(CHUNKS))
    ]
    (source_sums,) = call(
        source_kernel,
        [((peers, cap, WIDE), f32)],
        [
            ((DIM0, edges), f32),
            ((DIM1, 2 * edges), f32),
            ((DIM2, 2 * edges), f32),
            ((COLS, 2 * edges), bf16),
        ],
        source_row, lists, rot, g0, g1, g2, pre_grad, conv_zero, conv_one, conv_two, alpha_in,
        after=currents, work=6,
    )
    (embed,) = call(
        make_collect(lanes_total),
        [((atoms, FLAT), bf16)],
        [((total, WIDE), f32)],
        place, *gather_lanes(exchange(source_sums)),
        scalars=1,
    )

    pairs = [sum_all(current) for current in currents]
    zero, proj_grad = call(
        unpack_zero_kernel,
        [((DIM0, DIM0), bf16), ((LMAX + 1, CH, CH), bf16)],
        [], place, *pairs[0], scalars=1, work=1,
    )
    (one,) = call(
        unpack_one_kernel, [((2, DIM1, DIM1), bf16)], [], place, *pairs[1], scalars=1, work=1
    )
    two, grad_in, grad_edge, grad_dot = call(
        unpack_two_kernel,
        [
            ((2, DIM2, DIM2), bf16),
            (alpha_in.shape, bf16),
            (alpha_edge.shape, bf16),
            ((2, LANES), bf16),
        ],
        [], place, *pairs[2], scalars=1, work=1,
    )

    def shaped(rows):
        return rows.reshape(atoms, COEFFS, CH)

    return (
        shaped(out), shaped(embed), zero, one, two, grad_in, grad_edge, grad_dot.reshape(-1),
        proj_grad,
    )


def solution(mesh):
    in_specs = (
        P(("groups", "graph"), None, None),
        P(("groups", "graph"), None, None),
        P(("groups", "graph"), None, "edge", None),
        P(("groups", "graph"), None, "edge", None),
        P(("groups", "graph", "edge")),
        P(("groups", "graph", "edge")),
        P(("groups", "graph", "edge"), None),
        P(("groups", "graph", "edge"), None),
        P(("groups", "graph", "edge"), None),
        P(),
        P(),
        P(),
        P(),
        P(),
        P(),
        P(),
    )
    out_specs = (
        P(("groups", "graph"), None, None),
        P(("groups", "graph"), None, None),
        P("groups", None),
        P("groups", None, None),
        P("groups", None, None),
        P("groups", None),
        P("groups", None),
        P("groups"),
        P("groups", None, None),
    )
    return jax.shard_map(shards, mesh=mesh, in_specs=in_specs, out_specs=out_specs, check_vma=False)
```

```python
import jax
import jax.numpy as jnp
import numpy as np
from jax import lax
from jax.experimental import pallas as pl
from jax.experimental.pallas import tpu as pltpu
from jax.sharding import PartitionSpec as P

LMAX = 6
MMAX = 2
CH = 64
HEADS = 4
VAL = 16
ALPHA = 64
COEFFS = (LMAX + 1) * (LMAX + 1)
FLAT = COEFFS * CH
LANES = 128
BLOCKS = (FLAT + LANES - 1) // LANES
COLS = BLOCKS * LANES
WIDE = COLS + LANES
TABLE = 2 * COLS + LANES
PEAK_AT, DOT_AT, NAME_AT = HEADS, 2 * HEADS, 3 * HEADS
DIM0 = (LMAX + 1) * CH
DIM1 = LMAX * CH
DIM2 = (LMAX - 1) * CH
PANEL = 256

leak_slope = 0.2
floor_value = -1e30
bf16 = jnp.bfloat16
f32 = jnp.float32

VMEM_LIMIT = 56 * 1024 * 1024


def degree_blocks():
    result = []
    offset = 0
    for degree in range(LMAX + 1):
        centre = min(degree, MMAX)
        row_total = 2 * centre + 1
        col_total = 2 * degree + 1
        result.append((degree, centre, row_total, col_total, offset))
        offset += row_total * col_total
    return result


def degree_of(coeff):
    return int(np.sqrt(coeff))


def dot_nn(left, right):
    return jnp.dot(left, right, preferred_element_type=f32)


def dot_nt(left, right):
    return lax.dot_general(left, right, (((1,), (1,)), ((), ())), preferred_element_type=f32)


def dot_tn(left, right):
    return lax.dot_general(left, right, (((0,), (0,)), ((), ())), preferred_element_type=f32)


def iota(shape, dim):
    return lax.broadcasted_iota(jnp.int32, shape, dim)


def split_two(value):
    high = value.astype(bf16)
    return high, (value - high.astype(f32)).astype(bf16)


def to_frame(source, rot, edges, emit):
    def body(half, carry):
        lanes = pl.ds(pl.multiple_of(half * LANES, LANES), LANES)
        for degree, centre, row_total, col_total, offset in degree_blocks():
            sums = [None] * row_total
            for j in range(col_total):
                column = source[pl.ds((degree * degree + j) * CH, CH), lanes]
                for i in range(row_total):
                    term = rot[pl.ds(offset + i * col_total + j, 1), lanes] * column
                    sums[i] = term if j == 0 else sums[i] + term
            for i in range(row_total):
                emit(degree, i - centre, half, sums[i])
        return carry

    lax.fori_loop(0, edges // LANES, body, 0)


def from_frame(load, rot, edges, emit):
    def body(half, carry):
        lanes = pl.ds(pl.multiple_of(half * LANES, LANES), LANES)
        for degree, centre, row_total, col_total, offset in degree_blocks():
            rows = [load(degree, i - centre, half) for i in range(row_total)]
            for j in range(col_total):
                total = None
                for i in range(row_total):
                    term = rot[pl.ds(offset + i * col_total + j, 1), lanes] * rows[i]
                    total = term if i == 0 else total + term
                emit(degree * degree + j, half, total)
        return carry

    lax.fori_loop(0, edges // LANES, body, 0)


def lane_at(half, edges, second):
    return pl.ds(pl.multiple_of(half * LANES + (edges if second else 0), LANES), LANES)


def frame_place(degree, order, refs):
    if order == 0:
        return refs[0], degree * CH, False
    which = abs(order)
    return refs[which], (degree - which) * CH, order < 0


def spread_heads(rows):
    return jnp.concatenate(
        [jnp.broadcast_to(row, (VAL, row.shape[1])) for row in rows], axis=0
    )


def one_hot_rows(slot_ref, slots):
    edges = slot_ref.shape[1]
    return iota((slots, edges), 0) == slot_ref[...]


def mask_to(mask, dtype):
    return jnp.where(mask, 1.0, 0.0).astype(dtype)


def stack_table(table_ref, rows_ref):
    peers, cap, width = table_ref.shape
    for start in range(0, peers * cap, 8):
        parts = [table_ref[g].astype(f32) for g in range(start // cap, (start + 8) // cap)]
        rows_ref[pl.ds(start, 8), :] = jnp.concatenate(parts, axis=0)


def put_rows(out_ref, cols, value):
    peers, cap = out_ref.shape[0], out_ref.shape[1]
    for g in range(peers):
        out_ref[g, :, cols] = value[g * cap : (g + 1) * cap].astype(out_ref.dtype)


def slot_sums(terms, one_hot, out_ref, factor=None):
    both = jnp.concatenate([one_hot, one_hot], axis=1)
    products = 0.0
    for start in range(0, COLS, PANEL):
        size = min(PANEL, COLS - start)
        sums = dot_nt(both, terms[pl.ds(start, size), :])
        put_rows(out_ref, pl.ds(start, size), sums)
        if factor is None:
            continue
        for at in range(0, size, LANES):
            width = min(LANES, FLAT - start - at)
            product = sums[:, at : at + width] * factor[:, pl.ds(start + at, width)]
            if width < LANES:
                product = jnp.concatenate([product, jnp.zeros_like(product)], axis=1)
            products = products + product
    return products


def store_terms(terms, edges):
    def emit(coeff, half, value):
        high, low = split_two(value)
        rows = pl.ds(coeff * CH, CH)
        terms[rows, lane_at(half, edges, False)] = high
        terms[rows, lane_at(half, edges, True)] = low

    return emit


def listed_rows(list_ref, shape):
    peers, cap = list_ref.shape[1], list_ref.shape[3]
    row = iota(shape, 0)
    result = jnp.zeros(shape, jnp.int32)
    for slot in range(peers * cap):
        result = jnp.where(row == slot, list_ref[0, slot // cap, 0, slot % cap], result)
    return result


def put_coeffs(out, first, coeff_rows):
    for block in range(BLOCKS):
        left = coeff_rows(2 * block)
        right = coeff_rows(2 * block + 1) if 2 * block + 1 < COEFFS else jnp.zeros_like(left)
        put_rows(out, pl.ds(first + block * LANES, LANES), jnp.concatenate([left, right], axis=1))


def outgoing_kernel(place, send, recv, embed, cot, out):
    atoms = embed.shape[1]
    slots = out.shape[0] * out.shape[1]
    sent = listed_rows(send, (slots, LANES))
    received = listed_rows(recv, (slots, LANES))
    for first, listed, values in ((0, sent, embed), (COLS, received, cot)):
        picked = mask_to(iota((slots, atoms), 1) == listed[:, :atoms], bf16)
        put_coeffs(out, first, lambda k: dot_nn(picked, values[k]))
    lane = iota((slots, LANES), 1)
    side = jnp.where(lane == 0, received, jnp.where(lane == 1, sent, 0))
    put_rows(out, pl.ds(2 * COLS, LANES), side.astype(f32))


def swapped_halves(value, edges):
    return jnp.concatenate([-value[:, edges:], value[:, :edges]], axis=1)


def make_forward(atoms):
    def forward_kernel(
        table, source_slot, target_slot, rot, feats, bias, wzero, wone, wtwo, ain, aedge, adot,
        out_proj,
        sums_out, stats_out, x0, x1, x2, v0, v1, v2, pre_out, logit_out, lists_out, agg_grad,
        rows, gathered, weights, terms,
    ):
        edges = source_slot.shape[1]
        slots = table.shape[0] * table.shape[1]
        stack_table(table, rows)
        picked = mask_to(one_hot_rows(source_slot, slots), bf16)
        gathered[...] = dot_tn(rows[:, pl.ds(0, FLAT)].astype(bf16), picked)
        lists = rows[:, pl.ds(2 * COLS, LANES)]
        lists_out[...] = lists
        for degree in range(LMAX + 1):
            ids = range(degree * degree, (degree + 1) * (degree + 1))
            cot = jnp.concatenate([rows[:, pl.ds(COLS + k * CH, CH)] for k in ids], axis=0)
            grad = dot_nt(cot.astype(bf16), out_proj[degree])
            for n, k in enumerate(ids):
                agg_grad[:, pl.ds(k * CH, CH)] = grad[n * slots : (n + 1) * slots]

        def emit(degree, order, half, value):
            ref, row, second = frame_place(degree, order, (x0, x1, x2))
            ref[pl.ds(row, CH), lane_at(half, edges, second)] = value.astype(bf16)

        to_frame(gathered, rot, edges, emit)

        pre = dot_nn(ain[...], x0[pl.ds(0, CH), :]) + dot_nt(aedge[...], feats[...])
        pre_out[...] = pre
        hidden = jnp.where(pre > 0, pre, leak_slope * pre) * adot[...]
        aims = one_hot_rows(target_slot, slots)
        lane = iota((slots, LANES), 1)
        peer = iota((slots, 1), 0) // table.shape[1]
        name = lists[:, :1] + (peer * atoms).astype(f32)
        side = jnp.where(lane == NAME_AT, name, 0.0)
        for h in range(HEADS):
            logit = jnp.sum(hidden[h * ALPHA : (h + 1) * ALPHA], axis=0, keepdims=True)
            logit = logit + bias[pl.ds(h, 1), :]
            logit_out[pl.ds(h, 1), :] = logit
            peak = jnp.max(jnp.where(aims, logit, floor_value), axis=1, keepdims=True)
            of_edge = jnp.sum(jnp.where(aims, peak, 0.0), axis=0, keepdims=True)
            weight = jnp.exp(logit - of_edge)
            weights[pl.ds(h, 1), :] = weight
            den = jnp.sum(jnp.where(aims, weight, 0.0), axis=1, keepdims=True)
            side = jnp.where(lane == h, den, jnp.where(lane == PEAK_AT + h, peak, side))

        v0[...] = dot_nn(wzero[...], x0[...])
        for out, weight, value in ((v1, wone, x1[...]), (v2, wtwo, x2[...])):
            out[...] = dot_nn(weight[0], value) + swapped_halves(dot_nn(weight[1], value), edges)

        def load(degree, order, half):
            ref, row, second = frame_place(degree, order, (v0, v1, v2))
            return ref[pl.ds(row, CH), lane_at(half, edges, second)]

        store = store_terms(terms, edges)

        def weigh(coeff, half, value):
            lanes = lane_at(half, edges, False)
            spread = spread_heads([weights[pl.ds(h, 1), lanes] for h in range(HEADS)])
            store(coeff, half, value * spread)

        terms[pl.ds(FLAT, COLS - FLAT), :] = jnp.zeros((COLS - FLAT, 2 * edges), bf16)
        from_frame(load, rot, edges, weigh)
        dots = slot_sums(terms, mask_to(aims, bf16), sums_out, agg_grad)
        head = (lane % CH) // VAL
        for h in range(HEADS):
            dot = jnp.sum(jnp.where(head == h, dots, 0.0), axis=1, keepdims=True)
            side = jnp.where(lane == DOT_AT + h, dot, side)
        put_rows(sums_out, pl.ds(COLS, LANES), side)

        def copy_to(n, carry):
            stats_out[n] = side
            return carry

        lax.fori_loop(0, stats_out.shape[0], copy_to, 0)

    return forward_kernel


def lane_heads(values, shape):
    head = (iota(shape, 1) % CH) // VAL
    result = jnp.broadcast_to(values[0], shape)
    for h in range(1, HEADS):
        result = jnp.where(head == h, values[h], result)
    return result


def collect_rows(place, arrivals, rows_ref):
    for k, arrival in enumerate(arrivals):
        peers, cap, width = arrival.shape
        base = (place[0] ^ k) * (peers * cap)
        for start in range(0, peers * cap, 8):
            parts = [arrival[g] for g in range(start // cap, (start + 8) // cap)]
            at = pl.ds(pl.multiple_of(base + start, 8), 8)
            rows_ref[at, :] = jnp.concatenate(parts, axis=0)


def block_cols(block):
    return pl.ds(block * LANES, min(LANES, FLAT - block * LANES))


def make_finish(lanes_total):
    def finish_kernel(place, cot, out_proj, *rest):
        arrivals = rest[:lanes_total]
        out, proj, rows, terms, agg_low = rest[lanes_total:]
        atoms = cot.shape[1]
        total = rows.shape[0]
        collect_rows(place, arrivals, rows)
        side = rows[:, pl.ds(COLS, LANES)]
        owner = (place[1] * atoms).astype(f32)
        names = iota((total, atoms), 1).astype(f32) + owner == side[:, NAME_AT : NAME_AT + 1]
        eye = iota((atoms, atoms), 0) == iota((atoms, atoms), 1)
        scales, dens = [], []
        for h in range(HEADS):
            peak_rows = side[:, PEAK_AT + h : PEAK_AT + h + 1]
            peak = jnp.max(jnp.where(names, peak_rows, floor_value), axis=0, keepdims=True)
            of_row = jnp.sum(jnp.where(names, peak, 0.0), axis=1, keepdims=True)
            scale = jnp.exp(peak_rows - of_row)
            scaled_den = side[:, h : h + 1] * scale
            den = jnp.sum(jnp.where(names, scaled_den, 0.0), axis=0, keepdims=True)
            scales.append(scale)
            dens.append(jnp.sum(jnp.where(eye, den, 0.0), axis=1, keepdims=True))
        scale_full = lane_heads(scales, (total, LANES))
        den_full = lane_heads(dens, (atoms, LANES))
        picked = mask_to(names, bf16)
        twice = jnp.concatenate([picked, picked], axis=0)
        for block in range(BLOCKS):
            cols = pl.ds(block * LANES, LANES)
            high, low = split_two(rows[:, cols] * scale_full)
            terms[pl.ds(0, total), cols] = high
            terms[pl.ds(total, total), cols] = low
        for block in range(BLOCKS):
            cols = pl.ds(block * LANES, LANES)
            agg = (dot_tn(twice, terms[:, cols]) / den_full).astype(bf16)
            agg_low[2 * block] = agg[:, :CH]
            if 2 * block + 1 < COEFFS:
                agg_low[2 * block + 1] = agg[:, CH:]
        for degree in range(LMAX + 1):
            ids = pl.ds(degree * degree, 2 * degree + 1)
            stacked = ((2 * degree + 1) * atoms, CH)
            left = agg_low[ids].reshape(stacked)
            right = cot[ids].reshape(stacked)
            value = dot_nn(left, out_proj[degree]).astype(bf16)
            out[ids] = value.reshape((2 * degree + 1, atoms, CH))
            proj[pl.ds(degree * CH, CH), :] = dot_tn(left, right)

    return finish_kernel


def combine_stats(stats, own):
    blocks, slots = stats.shape[0], stats.shape[1]
    chunk = max(1, PANEL // slots)
    name = own[:, NAME_AT : NAME_AT + 1]

    def part(at):
        turned = jnp.transpose(stats[pl.ds(at * chunk, chunk)].reshape(chunk * slots, LANES))
        same = name == turned[NAME_AT : NAME_AT + 1]
        result = []
        for h in range(HEADS):
            peaks = turned[PEAK_AT + h : PEAK_AT + h + 1]
            peak = jnp.max(jnp.where(same, peaks, floor_value), axis=1, keepdims=True)
            scale = jnp.where(same, jnp.exp(jnp.where(same, peaks - peak, 0.0)), 0.0)
            den = jnp.sum(turned[h : h + 1] * scale, axis=1, keepdims=True)
            dot = jnp.sum(turned[DOT_AT + h : DOT_AT + h + 1] * scale, axis=1, keepdims=True)
            result += [peak, den, dot]
        return tuple(result)

    def step(at, held):
        fresh = part(at)
        result = []
        for h in range(HEADS):
            peak, den, dot = held[3 * h : 3 * h + 3]
            new_peak, new_den, new_dot = fresh[3 * h : 3 * h + 3]
            most = jnp.maximum(peak, new_peak)
            old, new = jnp.exp(peak - most), jnp.exp(new_peak - most)
            result += [most, den * old + new_den * new, dot * old + new_dot * new]
        return tuple(result)

    held = part(0)
    if blocks > chunk:
        held = lax.fori_loop(1, blocks // chunk, step, held)
    return [held[3 * h : 3 * h + 3] for h in range(HEADS)]


def gradient_kernel(
    place, stats, own, agg_grad, target_slot, rot, feats,
    x0, x1, x2, v0, v1, v2, pre, logits, adot,
    g0, top1, top2, pre_grad_out, kept0, sent0, kept1, sent1,
    num_grad, spread_grad, weights, g1, g2, packed, semaphores,
):
    edges = target_slot.shape[1]
    slots = agg_grad.shape[0]
    aims = one_hot_rows(target_slot, slots)
    combined = combine_stats(stats, own[...])
    den_grads = []
    for h, (peak, den, dot) in enumerate(combined):
        of_edge = jnp.sum(jnp.where(aims, peak, 0.0), axis=0, keepdims=True)
        weights[pl.ds(h, 1), :] = jnp.exp(logits[pl.ds(h, 1), :] - of_edge)
        den_grad = (-(dot / den) / den).astype(bf16).astype(f32)
        den_grads.append(jnp.sum(jnp.where(aims, den_grad, 0.0), axis=0, keepdims=True))
    den_full = lane_heads([den for peak, den, dot in combined], (slots, LANES))
    for block in range(BLOCKS):
        cols = block_cols(block)
        num_grad[:, cols] = (agg_grad[:, cols] / den_full[:, : cols.size]).astype(bf16)
    spread_grad[...] = dot_tn(num_grad[...], mask_to(aims, bf16))

    state = {}

    def emit(degree, order, half, value):
        lanes = lane_at(half, edges, False)
        ref, row, second = frame_place(degree, order, (v0, v1, v2))
        product = value * ref[pl.ds(row, CH), lane_at(half, edges, second)]
        if degree == 0:
            state["sum"] = product
            state["spread"] = spread_heads([weights[pl.ds(h, 1), lanes] for h in range(HEADS)])
        else:
            state["sum"] = state["sum"] + product
        grad = (value * state["spread"]).astype(bf16)
        ref, row, second = frame_place(degree, order, (g0, g1, g2))
        ref[pl.ds(row, CH), lane_at(half, edges, second)] = grad
        if order != 0:
            swapped = grad if order < 0 else -grad
            below = row + (DIM1 if abs(order) == 1 else DIM2)
            ref[pl.ds(below, CH), lane_at(half, edges, not second)] = swapped
        if degree == LMAX and order == MMAX:
            for h in range(HEADS):
                part = state["sum"][h * VAL : (h + 1) * VAL]
                weights[pl.ds(HEADS + h, 1), lanes] = jnp.sum(part, axis=0, keepdims=True)

    to_frame(spread_grad, rot, edges, emit)

    hidden = jnp.where(pre[...] > 0, pre[...], leak_slope * pre[...])
    logit_grads = [
        weights[pl.ds(h, 1), :] * (weights[pl.ds(HEADS + h, 1), :] + den_grads[h])
        for h in range(HEADS)
    ]
    tall = jnp.concatenate(
        [jnp.broadcast_to(row, (ALPHA, edges)) for row in logit_grads], axis=0
    )
    slope = jnp.where(pre[...] > 0, 1.0, leak_slope)
    pre_grad = (tall * adot[...] * slope).astype(bf16)
    pre_grad_out[...] = pre_grad
    dot_grad = jnp.sum(tall * hidden, axis=1, keepdims=True)

    top1[...] = g1[pl.ds(0, DIM1), :]
    top2[...] = g2[pl.ds(0, DIM2), :]
    mine = place[0] & 1
    copies = []

    def put(row, value, at=0):
        for side in range(2):
            low, high = max(at, side * LANES), min(at + value.shape[1], (side + 1) * LANES)
            if low < high:
                piece = value[:, low - at : high - at]
                cols = pl.ds(low - side * LANES, high - low)
                packed[side, pl.ds(row, value.shape[0]), cols] = piece

    def send(chunk, kept, sent):
        start, size = CHUNKS[chunk]
        rows_of = pl.ds(start, size)
        for n, (side, out) in enumerate(((mine, kept), (1 - mine, sent))):
            copy = pltpu.make_async_copy(
                packed.at[side, rows_of, :], out, semaphores.at[2 * chunk + n]
            )
            copy.start()
            copies.append(copy)

    row = 0
    for left, right, dim in ((x1, g1, DIM1), (x2, g2, DIM2)):
        for start in range(0, 2 * dim, PANEL):
            size = min(PANEL, 2 * dim - start)
            put(row, dot_nt(left[...], right[pl.ds(start, size), :]))
            row += dim
    row -= DIM2
    edge_ch = feats.shape[1]
    edge_grad = lax.dot_general(
        feats[...], pre_grad, (((0,), (1,)), ((), ())), preferred_element_type=f32
    )
    put(row, edge_grad[:, :LANES], LANES)
    put(row + edge_ch, edge_grad[:, LANES:], LANES)
    wide_dot = jnp.transpose(jnp.broadcast_to(dot_grad, (HEADS * ALPHA, LANES)))
    spare = DIM2 - 2 * edge_ch
    tail = iota((spare, LANES), 0)
    first = jnp.broadcast_to(wide_dot[:1, :LANES], (spare, LANES))
    second = jnp.broadcast_to(wide_dot[:1, LANES:], (spare, LANES))
    put(row + 2 * edge_ch, jnp.where(tail == 0, first, jnp.where(tail == 1, second, 0.0)), LANES)
    row += DIM2
    put(row, dot_nt(x0[pl.ds(0, CH), :], pre_grad))
    send(0, kept0, sent0)

    row = CHUNKS[1][0]
    for start in range(0, DIM0, PANEL):
        size = min(PANEL, DIM0 - start)
        put(row, dot_nt(x0[...], g0[pl.ds(start, size), :]))
        if size < PANEL:
            put(row, jnp.zeros((DIM0, PANEL - size), f32), size)
        row += DIM0
    send(1, kept1, sent1)
    for copy in copies:
        copy.wait()


CHUNKS = ((0, 3 * DIM1 + 3 * DIM2 + CH), (3 * DIM1 + 3 * DIM2 + CH, 2 * DIM0))
PACKED_ROWS = sum(size for start, size in CHUNKS)


def halves_of(place, mine, other):
    first = (place[0] & 1) == 0
    left, right = mine[...].astype(f32), other[...].astype(f32)
    return jnp.where(first, left, right), jnp.where(first, right, left)


def unpack_zero_kernel(place, mine, other, zero):
    left, right = halves_of(place, mine, other)
    zero[:, pl.ds(0, LANES)] = left[:DIM0].astype(bf16)
    zero[:, pl.ds(LANES, LANES)] = right[:DIM0].astype(bf16)
    zero[:, pl.ds(2 * LANES, LANES)] = left[DIM0:].astype(bf16)
    zero[:, pl.ds(3 * LANES, DIM0 - 3 * LANES)] = right[DIM0:, : DIM0 - 3 * LANES].astype(bf16)


def unpack_rest_kernel(place, mine, other, one, two, alpha_in, alpha_edge, alpha_dot):
    left, right = halves_of(place, mine, other)
    for n in range(2 * DIM1 // LANES):
        panel = (left, right)[n % 2][(n // 2) * DIM1 : (n // 2 + 1) * DIM1]
        per = DIM1 // LANES
        one[n // per, :, pl.ds((n % per) * LANES, LANES)] = panel.astype(bf16)
    left, right = left[3 * DIM1 :], right[3 * DIM1 :]
    panels = [(left, right)[n % 2][(n // 2) * DIM2 : (n // 2 + 1) * DIM2] for n in range(5)]
    whole = jnp.concatenate(panels, axis=1)
    two[0] = whole[:, :DIM2].astype(bf16)
    two[1] = whole[:, DIM2:].astype(bf16)
    edge_ch = alpha_edge.shape[0]
    rest = right[2 * DIM2 : 3 * DIM2]
    alpha_edge[:, pl.ds(0, LANES)] = rest[:edge_ch].astype(bf16)
    alpha_edge[:, pl.ds(LANES, LANES)] = rest[edge_ch : 2 * edge_ch].astype(bf16)
    alpha_dot[...] = rest[2 * edge_ch : 2 * edge_ch + 2].astype(bf16)
    alpha_in[:, pl.ds(0, LANES)] = left[3 * DIM2 :].astype(bf16)
    alpha_in[:, pl.ds(LANES, LANES)] = right[3 * DIM2 :].astype(bf16)


def source_kernel(
    source_slot, lists, rot, g0, g1, g2, pre_grad, wzero, wone, wtwo, ain,
    *rest,
):
    sums_out, d0, d1, d2, terms = rest[-5:]
    edges = source_slot.shape[1]
    slots = sums_out.shape[0] * sums_out.shape[1]
    d0[...] = dot_nn(wzero[...], g0[...])
    d0[pl.ds(0, CH), :] += dot_nn(ain[...], pre_grad[...])
    for out, weight, value in ((d1, wone, g1[...]), (d2, wtwo, g2[...])):
        out[...] = dot_nn(weight[0], value) - swapped_halves(dot_nn(weight[1], value), edges)

    def load(degree, order, half):
        ref, row, second = frame_place(degree, order, (d0, d1, d2))
        return ref[pl.ds(row, CH), lane_at(half, edges, second)]

    terms[pl.ds(FLAT, COLS - FLAT), :] = jnp.zeros((COLS - FLAT, 2 * edges), bf16)
    from_frame(load, rot, edges, store_terms(terms, edges))
    slot_sums(terms, mask_to(one_hot_rows(source_slot, slots), bf16), sums_out)
    put_rows(sums_out, pl.ds(COLS, LANES), lists[...])


def make_collect(lanes_total):
    def collect_kernel(place, *rest):
        arrivals = rest[:lanes_total]
        out, rows = rest[lanes_total:]
        atoms = out.shape[1]
        total = rows.shape[0]
        collect_rows(place, arrivals, rows)
        index = rows[:, pl.ds(COLS, LANES)][:, 1:2]
        picked = mask_to(iota((total, atoms), 1).astype(f32) == index, bf16)
        twice = jnp.concatenate([picked, picked], axis=0)
        for block in range(BLOCKS):
            high, low = split_two(rows[:, pl.ds(block * LANES, LANES)])
            sums = dot_tn(twice, jnp.concatenate([high, low], axis=0)).astype(bf16)
            out[2 * block] = sums[:, :CH]
            if 2 * block + 1 < COEFFS:
                out[2 * block + 1] = sums[:, CH:]

    return collect_kernel


vmem = pl.BlockSpec(memory_space=pltpu.VMEM)
smem = pl.BlockSpec(memory_space=pltpu.SMEM)
anywhere = pl.BlockSpec(memory_space=pl.ANY)


def call(kernel, outs, scratch, *args, scalars=0, apart=0, after=(), work=4):
    specs = [smem if n < scalars else vmem for n in range(len(args))] + [anywhere] * len(after)
    out_specs = [vmem if n < len(outs) - apart else anywhere for n in range(len(outs))]
    shapes = [pltpu.VMEM(*entry) if isinstance(entry, tuple) else entry for entry in scratch]
    moved = sum(int(np.prod(a.shape)) * a.dtype.itemsize for a in args)
    return pl.pallas_call(
        kernel,
        out_shape=[jax.ShapeDtypeStruct(shape, kind) for shape, kind in outs],
        in_specs=specs,
        out_specs=out_specs,
        scratch_shapes=shapes,
        compiler_params=pltpu.CompilerParams(vmem_limit_bytes=VMEM_LIMIT),
        cost_estimate=pl.CostEstimate(
            flops=work * 10**9, bytes_accessed=moved, transcendentals=0
        ),
    )(*args, *after)


def swap(value, axis, bit):
    size = lax.axis_size(axis)
    return lax.ppermute(value, axis, [(i, i ^ (1 << bit)) for i in range(size)])


def bits_of(axis):
    return (lax.axis_size(axis) - 1).bit_length()


def gather_lanes(value):
    held = {0: value}
    for bit in reversed(range(bits_of("edge"))):
        held.update({k | (1 << bit): swap(v, "edge", bit) for k, v in list(held.items())})
    return [held[k] for k in range(len(held))]


def own_bit(axis, bit):
    return (lax.axis_index(axis) >> bit) & 1


def sum_all(current, first):
    steps = [("edge", n) for n in range(1, bits_of("edge"))]
    steps += [("graph", n) for n in range(bits_of("graph"))]
    steps.sort(key=lambda step: step[0] != first)
    for axis, bit in steps:
        mine = own_bit(axis, bit)
        parts = current.reshape(2, current.shape[0] // 2, -1)
        other = swap(lax.dynamic_index_in_dim(parts, 1 - mine, 0, False), axis, bit)
        current = lax.dynamic_index_in_dim(parts, mine, 0, False) + other
    current = current.astype(bf16)
    for axis, bit in reversed(steps):
        mine = own_bit(axis, bit)
        other = swap(current, axis, bit)
        current = jnp.concatenate(
            [jnp.where(mine == 0, current, other), jnp.where(mine == 0, other, current)], axis=0
        )
    return current, swap(current, "edge", 0)


def shards(
    atom_embed, out_cotangent, send_rows, recv_rows, source_slot, target_slot, rotation,
    edge_feats, edge_bias, conv_zero, conv_one, conv_two, alpha_in, alpha_edge, alpha_dot,
    out_proj,
):
    peers = lax.axis_size("graph")
    lanes_total = lax.axis_size("edge")
    atoms = atom_embed.shape[0]
    edges = rotation.shape[0]
    cap = send_rows.shape[3]
    slots = peers * cap
    own_place = [lax.axis_index("edge"), lax.axis_index("graph")]
    place = jnp.stack(own_place).astype(jnp.int32)
    blocks = peers * lanes_total

    def exchange(value):
        return lax.all_to_all(value, "graph", split_axis=0, concat_axis=0, tiled=True)

    cot = jnp.transpose(out_cotangent, (1, 0, 2))
    (outgoing,) = call(
        outgoing_kernel, [((peers, cap, TABLE), bf16)], [],
        place, send_rows, recv_rows, jnp.transpose(atom_embed, (1, 0, 2)), cot,
        scalars=3, work=2,
    )
    table = exchange(outgoing)

    source_row = source_slot.reshape(1, edges)
    target_row = target_slot.reshape(1, edges)
    rot = rotation.T.astype(f32)
    bias = edge_bias.T
    adot = alpha_dot.astype(f32).reshape(-1, 1)

    sums, stats, x0, x1, x2, v0, v1, v2, pre, logits, lists, agg_grad = call(
        make_forward(atoms),
        [
            ((peers, cap, WIDE), f32),
            ((blocks, slots, LANES), f32),
            ((DIM0, edges), bf16),
            ((DIM1, 2 * edges), bf16),
            ((DIM2, 2 * edges), bf16),
            ((DIM0, edges), f32),
            ((DIM1, 2 * edges), f32),
            ((DIM2, 2 * edges), f32),
            ((HEADS * ALPHA, edges), f32),
            ((8, edges), f32),
            ((slots, LANES), f32),
            ((slots, FLAT), f32),
        ],
        [
            ((slots, TABLE), f32),
            ((FLAT, edges), f32),
            ((8, edges), f32),
            ((COLS, 2 * edges), bf16),
        ],
        table, source_row, target_row, rot, edge_feats, bias,
        conv_zero.T, jnp.swapaxes(conv_one, 1, 2), jnp.swapaxes(conv_two, 1, 2),
        alpha_in.T, alpha_edge.T, adot, out_proj,
        work=8,
    )
    own_stats = stats[0]
    all_stats = lax.all_to_all(stats, ("graph", "edge"), split_axis=0, concat_axis=0, tiled=True)

    halves = [((size, LANES), f32) for start, size in CHUNKS for _ in range(2)]
    g0, g1, g2, pre_grad, *halves = call(
        gradient_kernel,
        [
            ((DIM0, edges), bf16),
            ((DIM1, 2 * edges), bf16),
            ((DIM2, 2 * edges), bf16),
            ((HEADS * ALPHA, edges), bf16),
        ]
        + halves,
        [
            ((slots, FLAT), bf16),
            ((FLAT, edges), f32),
            ((8, edges), f32),
            ((2 * DIM1, 2 * edges), bf16),
            ((2 * DIM2, 2 * edges), bf16),
            ((2, PACKED_ROWS, LANES), f32),
            pltpu.SemaphoreType.DMA((len(halves),)),
        ],
        place, all_stats, own_stats, agg_grad, target_row, rot, edge_feats,
        x0, x1, x2, v0, v1, v2, pre, logits, adot,
        scalars=1, apart=len(halves), work=8,
    )
    currents = [
        halves[2 * n] + swap(halves[2 * n + 1], "edge", 0) for n in range(len(CHUNKS))
    ]

    total = lanes_total * slots
    (source_sums,) = call(
        source_kernel,
        [((peers, cap, WIDE), f32)],
        [
            ((DIM0, edges), f32),
            ((DIM1, 2 * edges), f32),
            ((DIM2, 2 * edges), f32),
            ((COLS, 2 * edges), bf16),
        ],
        source_row, lists, rot, g0, g1, g2, pre_grad, conv_zero, conv_one, conv_two, alpha_in,
        after=currents, work=6,
    )
    out, proj = call(
        make_finish(lanes_total),
        [((COEFFS, atoms, CH), bf16), (((LMAX + 1) * CH, CH), f32)],
        [((total, WIDE), f32), ((2 * total, COLS), bf16), ((COEFFS, atoms, CH), bf16)],
        place, cot, out_proj, *gather_lanes(exchange(sums)),
        scalars=1,
    )
    for bit in range(bits_of("graph")):
        proj = proj + swap(proj, "graph", bit)
    (embed,) = call(
        make_collect(lanes_total),
        [((COEFFS, atoms, CH), bf16)],
        [((total, WIDE), f32)],
        place, *gather_lanes(exchange(source_sums)),
        scalars=1,
    )

    rest_pair = sum_all(currents[0], "edge")
    zero_pair = sum_all(currents[1], "graph")
    (zero,) = call(
        unpack_zero_kernel, [((DIM0, DIM0), bf16)], [], place, *zero_pair, scalars=1, work=1
    )
    one, two, grad_in, grad_edge, grad_dot = call(
        unpack_rest_kernel,
        [
            ((2, DIM1, DIM1), bf16),
            ((2, DIM2, DIM2), bf16),
            (alpha_in.shape, bf16),
            (alpha_edge.shape, bf16),
            ((2, LANES), bf16),
        ],
        [], place, *rest_pair, scalars=1, work=1,
    )

    def shaped(value):
        return jnp.transpose(value, (1, 0, 2))

    return (
        shaped(out), shaped(embed), zero, one, two, grad_in, grad_edge, grad_dot.reshape(-1),
        proj.astype(bf16).reshape(LMAX + 1, CH, CH),
    )


def solution(mesh):
    in_specs = (
        P(("groups", "graph"), None, None),
        P(("groups", "graph"), None, None),
        P(("groups", "graph"), None, "edge", None),
        P(("groups", "graph"), None, "edge", None),
        P(("groups", "graph", "edge")),
        P(("groups", "graph", "edge")),
        P(("groups", "graph", "edge"), None),
        P(("groups", "graph", "edge"), None),
        P(("groups", "graph", "edge"), None),
        P(),
        P(),
        P(),
        P(),
        P(),
        P(),
        P(),
    )
    out_specs = (
        P(("groups", "graph"), None, None),
        P(("groups", "graph"), None, None),
        P("groups", None),
        P("groups", None, None),
        P("groups", None, None),
        P("groups", None),
        P("groups", None),
        P("groups"),
        P("groups", None, None),
    )
    return jax.shard_map(shards, mesh=mesh, in_specs=in_specs, out_specs=out_specs, check_vma=False)
```

```python
import jax
import jax.numpy as jnp
import numpy as np
from jax import lax
from jax.experimental import pallas as pl
from jax.experimental.pallas import tpu as pltpu
from jax.sharding import PartitionSpec as P

LMAX = 6
MMAX = 2
CH = 64
HEADS = 4
VAL = 16
ALPHA = 64
COEFFS = (LMAX + 1) * (LMAX + 1)
FLAT = COEFFS * CH
LANES = 128
BLOCKS = (FLAT + LANES - 1) // LANES
COLS = BLOCKS * LANES
WIDE = COLS + LANES
TABLE = 2 * COLS + LANES
PEAK_AT, DOT_AT, NAME_AT = HEADS, 2 * HEADS, 3 * HEADS
STATS = 16
DIM0 = (LMAX + 1) * CH
DIM1 = LMAX * CH
DIM2 = (LMAX - 1) * CH
PANEL = 256

leak_slope = 0.2
floor_value = -1e30
bf16 = jnp.bfloat16
f32 = jnp.float32

VMEM_LIMIT = 56 * 1024 * 1024


def degree_blocks():
    result = []
    offset = 0
    for degree in range(LMAX + 1):
        centre = min(degree, MMAX)
        row_total = 2 * centre + 1
        col_total = 2 * degree + 1
        result.append((degree, centre, row_total, col_total, offset))
        offset += row_total * col_total
    return result


def degree_of(coeff):
    return int(np.sqrt(coeff))


def dot_nn(left, right):
    return jnp.dot(left, right, preferred_element_type=f32)


def dot_nt(left, right):
    return lax.dot_general(left, right, (((1,), (1,)), ((), ())), preferred_element_type=f32)


def dot_tn(left, right):
    return lax.dot_general(left, right, (((0,), (0,)), ((), ())), preferred_element_type=f32)


def iota(shape, dim):
    return lax.broadcasted_iota(jnp.int32, shape, dim)


def split_two(value):
    high = value.astype(bf16)
    return high, (value - high.astype(f32)).astype(bf16)


def to_frame(source, rot, edges, emit):
    def body(half, carry):
        lanes = pl.ds(pl.multiple_of(half * LANES, LANES), LANES)
        for degree, centre, row_total, col_total, offset in degree_blocks():
            sums = [None] * row_total
            for j in range(col_total):
                column = source[pl.ds((degree * degree + j) * CH, CH), lanes]
                for i in range(row_total):
                    term = rot[pl.ds(offset + i * col_total + j, 1), lanes] * column
                    sums[i] = term if j == 0 else sums[i] + term
            for i in range(row_total):
                emit(degree, i - centre, half, sums[i])
        return carry

    lax.fori_loop(0, edges // LANES, body, 0)


def from_frame(load, rot, edges, emit):
    def body(half, carry):
        lanes = pl.ds(pl.multiple_of(half * LANES, LANES), LANES)
        for degree, centre, row_total, col_total, offset in degree_blocks():
            rows = [load(degree, i - centre, half) for i in range(row_total)]
            for j in range(col_total):
                total = None
                for i in range(row_total):
                    term = rot[pl.ds(offset + i * col_total + j, 1), lanes] * rows[i]
                    total = term if i == 0 else total + term
                emit(degree * degree + j, half, total)
        return carry

    lax.fori_loop(0, edges // LANES, body, 0)


def lane_at(half, edges, second):
    return pl.ds(pl.multiple_of(half * LANES + (edges if second else 0), LANES), LANES)


def frame_place(degree, order, refs):
    if order == 0:
        return refs[0], degree * CH, False
    which = abs(order)
    return refs[which], (degree - which) * CH, order < 0


def spread_heads(rows):
    return jnp.concatenate(
        [jnp.broadcast_to(row, (VAL, row.shape[1])) for row in rows], axis=0
    )


def one_hot_rows(slot_ref, slots):
    edges = slot_ref.shape[1]
    return iota((slots, edges), 0) == slot_ref[...]


def mask_to(mask, dtype):
    return jnp.where(mask, 1.0, 0.0).astype(dtype)


def stack_table(table_ref, rows_ref):
    peers, cap, width = table_ref.shape
    for start in range(0, peers * cap, 8):
        parts = [table_ref[g].astype(f32) for g in range(start // cap, (start + 8) // cap)]
        rows_ref[pl.ds(start, 8), :] = jnp.concatenate(parts, axis=0)


def put_rows(out_ref, cols, value):
    peers, cap = out_ref.shape[0], out_ref.shape[1]
    for g in range(peers):
        out_ref[g, :, cols] = value[g * cap : (g + 1) * cap].astype(out_ref.dtype)


def slot_sums(terms, one_hot, out_ref, factor=None):
    both = jnp.concatenate([one_hot, one_hot], axis=1)
    products = 0.0
    for start in range(0, COLS, PANEL):
        size = min(PANEL, COLS - start)
        sums = dot_nt(both, terms[pl.ds(start, size), :])
        put_rows(out_ref, pl.ds(start, size), sums)
        if factor is None:
            continue
        for at in range(0, size, LANES):
            width = min(LANES, FLAT - start - at)
            product = sums[:, at : at + width] * factor[:, pl.ds(start + at, width)]
            if width < LANES:
                product = jnp.concatenate([product, jnp.zeros_like(product)], axis=1)
            products = products + product
    return products


def store_terms(terms, edges):
    def emit(coeff, half, value):
        high, low = split_two(value)
        rows = pl.ds(coeff * CH, CH)
        terms[rows, lane_at(half, edges, False)] = high
        terms[rows, lane_at(half, edges, True)] = low

    return emit


def listed_rows(list_ref, shape):
    peers, cap = list_ref.shape[1], list_ref.shape[3]
    row = iota(shape, 0)
    result = jnp.zeros(shape, jnp.int32)
    for slot in range(peers * cap):
        result = jnp.where(row == slot, list_ref[0, slot // cap, 0, slot % cap], result)
    return result


def put_coeffs(out, first, coeff_rows):
    for block in range(BLOCKS):
        left = coeff_rows(2 * block)
        right = coeff_rows(2 * block + 1) if 2 * block + 1 < COEFFS else jnp.zeros_like(left)
        put_rows(out, pl.ds(first + block * LANES, LANES), jnp.concatenate([left, right], axis=1))


def outgoing_kernel(send, recv, embed, cot, out):
    atoms = embed.shape[1]
    slots = out.shape[0] * out.shape[1]
    sent = listed_rows(send, (slots, LANES))
    received = listed_rows(recv, (slots, LANES))
    for first, listed, values in ((0, sent, embed), (COLS, received, cot)):
        picked = mask_to(iota((slots, atoms), 1) == listed[:, :atoms], bf16)
        put_coeffs(out, first, lambda k: dot_nn(picked, values[k]))
    lane = iota((slots, LANES), 1)
    side = jnp.where(lane == 0, received, jnp.where(lane == 1, sent, 0))
    put_rows(out, pl.ds(2 * COLS, LANES), side.astype(f32))


def swapped_halves(value, edges):
    return jnp.concatenate([-value[:, edges:], value[:, :edges]], axis=1)


def make_forward(atoms):
    def forward_kernel(
        table, source_slot, target_slot, rotation, feats, bias, wzero_at, wone_at, wtwo_at,
        ain, aedge, adot, out_proj,
        sums_out, stats_out, x0_at, x1_at, x2_at, v0_at, v1_at, v2_at, pre_at, logit_out,
        lists_out, agg_grad, rot, own_out,
        rows, gathered, weights, terms, wzero, wone, wtwo, x0, x1, x2, v0, v1, v2, pre_out,
        semaphores,
    ):
        copies = []

        def move(source, target):
            copy = pltpu.make_async_copy(source, target, semaphores.at[len(copies)])
            copy.start()
            copies.append(copy)

        move(wzero_at, wzero)
        move(wone_at, wone)
        move(wtwo_at, wtwo)
        rot[...] = jnp.transpose(rotation[...].astype(f32))
        edges = source_slot.shape[1]
        slots = table.shape[0] * table.shape[1]
        stack_table(table, rows)
        picked = mask_to(one_hot_rows(source_slot, slots), bf16)
        gathered[...] = dot_tn(rows[:, pl.ds(0, FLAT)].astype(bf16), picked)
        lists = rows[:, pl.ds(2 * COLS, LANES)]
        lists_out[...] = lists
        for degree in range(LMAX + 1):
            ids = range(degree * degree, (degree + 1) * (degree + 1))
            cot = jnp.concatenate([rows[:, pl.ds(COLS + k * CH, CH)] for k in ids], axis=0)
            grad = dot_nt(cot.astype(bf16), out_proj[degree])
            for n, k in enumerate(ids):
                agg_grad[:, pl.ds(k * CH, CH)] = grad[n * slots : (n + 1) * slots]

        def emit(degree, order, half, value):
            ref, row, second = frame_place(degree, order, (x0, x1, x2))
            ref[pl.ds(row, CH), lane_at(half, edges, second)] = value.astype(bf16)

        to_frame(gathered, rot, edges, emit)
        for source, target in ((x0, x0_at), (x1, x1_at), (x2, x2_at)):
            move(source, target)

        pre = dot_tn(ain[...], x0[pl.ds(0, CH), :]) + lax.dot_general(
            aedge[...], feats[...], (((0,), (1,)), ((), ())), preferred_element_type=f32
        )
        pre_out[...] = pre
        move(pre_out, pre_at)
        hidden = jnp.where(pre > 0, pre, leak_slope * pre) * turned_column(adot[...].astype(f32))
        aims = one_hot_rows(target_slot, slots)
        lane = iota((slots, LANES), 1)
        peer = iota((slots, 1), 0) // table.shape[1]
        name = lists[:, :1] + (peer * atoms).astype(f32)
        side = jnp.where(lane == NAME_AT, name, 0.0)
        for h in range(HEADS):
            logit = jnp.sum(hidden[h * ALPHA : (h + 1) * ALPHA], axis=0, keepdims=True)
            logit = logit + bias[pl.ds(h, 1), :]
            logit_out[pl.ds(h, 1), :] = logit
            peak = jnp.max(jnp.where(aims, logit, floor_value), axis=1, keepdims=True)
            of_edge = jnp.sum(jnp.where(aims, peak, 0.0), axis=0, keepdims=True)
            weight = jnp.exp(logit - of_edge)
            weights[pl.ds(h, 1), :] = weight
            den = jnp.sum(jnp.where(aims, weight, 0.0), axis=1, keepdims=True)
            side = jnp.where(lane == h, den, jnp.where(lane == PEAK_AT + h, peak, side))

        for copy in copies[:3]:
            copy.wait()
        v0[...] = dot_tn(wzero[...], x0[...])
        for out, weight, value in ((v1, wone, x1[...]), (v2, wtwo, x2[...])):
            out[...] = dot_tn(weight[0], value) + swapped_halves(dot_tn(weight[1], value), edges)
        for source, target in ((v0, v0_at), (v1, v1_at), (v2, v2_at)):
            move(source, target)

        def load(degree, order, half):
            ref, row, second = frame_place(degree, order, (v0, v1, v2))
            return ref[pl.ds(row, CH), lane_at(half, edges, second)]

        store = store_terms(terms, edges)

        def weigh(coeff, half, value):
            lanes = lane_at(half, edges, False)
            spread = spread_heads([weights[pl.ds(h, 1), lanes] for h in range(HEADS)])
            store(coeff, half, value * spread)

        terms[pl.ds(FLAT, COLS - FLAT), :] = jnp.zeros((COLS - FLAT, 2 * edges), bf16)
        from_frame(load, rot, edges, weigh)
        dots = slot_sums(terms, mask_to(aims, bf16), sums_out, agg_grad)
        head = (lane % CH) // VAL
        for h in range(HEADS):
            dot = jnp.sum(jnp.where(head == h, dots, 0.0), axis=1, keepdims=True)
            side = jnp.where(lane == DOT_AT + h, dot, side)
        put_rows(sums_out, pl.ds(COLS, LANES), side)
        own_out[...] = side
        spread = jnp.concatenate([side[:, :STATS]] * (LANES // STATS), axis=1)
        spread = jnp.where(lane // STATS == iota((slots, LANES), 0) % 8, spread, 0.0)
        packed = jnp.sum(spread.reshape(slots // 8, 8, LANES), axis=1)

        def copy_to(n, carry):
            stats_out[n] = packed
            return carry

        lax.fori_loop(0, stats_out.shape[0], copy_to, 0)
        for copy in copies[3:]:
            copy.wait()

    return forward_kernel


def lane_heads(values, shape):
    head = (iota(shape, 1) % CH) // VAL
    result = jnp.broadcast_to(values[0], shape)
    for h in range(1, HEADS):
        result = jnp.where(head == h, values[h], result)
    return result


def collect_rows(arrivals, rows_ref):
    own = lax.axis_index("edge")
    for k, arrival in enumerate(arrivals):
        peers, cap, width = arrival.shape
        base = (own ^ k) * (peers * cap)
        for start in range(0, peers * cap, 8):
            parts = [arrival[g] for g in range(start // cap, (start + 8) // cap)]
            at = pl.ds(pl.multiple_of(base + start, 8), 8)
            rows_ref[at, :] = jnp.concatenate(parts, axis=0)


def block_cols(block):
    return pl.ds(block * LANES, min(LANES, FLAT - block * LANES))


def make_finish(lanes_total):
    def finish_kernel(cot, out_proj, *rest):
        arrivals = rest[:lanes_total]
        out, proj, rows, terms, agg_low = rest[lanes_total:]
        atoms = cot.shape[1]
        total = rows.shape[0]
        collect_rows(arrivals, rows)
        side = rows[:, pl.ds(COLS, LANES)]
        owner = (lax.axis_index("graph") * atoms).astype(f32)
        names = iota((total, atoms), 1).astype(f32) + owner == side[:, NAME_AT : NAME_AT + 1]
        eye = iota((atoms, atoms), 0) == iota((atoms, atoms), 1)
        scales, dens = [], []
        for h in range(HEADS):
            peak_rows = side[:, PEAK_AT + h : PEAK_AT + h + 1]
            peak = jnp.max(jnp.where(names, peak_rows, floor_value), axis=0, keepdims=True)
            of_row = jnp.sum(jnp.where(names, peak, 0.0), axis=1, keepdims=True)
            scale = jnp.exp(peak_rows - of_row)
            scaled_den = side[:, h : h + 1] * scale
            den = jnp.sum(jnp.where(names, scaled_den, 0.0), axis=0, keepdims=True)
            scales.append(scale)
            dens.append(jnp.sum(jnp.where(eye, den, 0.0), axis=1, keepdims=True))
        scale_full = lane_heads(scales, (total, LANES))
        den_full = lane_heads(dens, (atoms, LANES))
        picked = mask_to(names, bf16)
        twice = jnp.concatenate([picked, picked], axis=0)
        for block in range(BLOCKS):
            cols = pl.ds(block * LANES, LANES)
            high, low = split_two(rows[:, cols] * scale_full)
            terms[pl.ds(0, total), cols] = high
            terms[pl.ds(total, total), cols] = low
        for block in range(BLOCKS):
            cols = pl.ds(block * LANES, LANES)
            agg = (dot_tn(twice, terms[:, cols]) / den_full).astype(bf16)
            agg_low[2 * block] = agg[:, :CH]
            if 2 * block + 1 < COEFFS:
                agg_low[2 * block + 1] = agg[:, CH:]
        for degree in range(LMAX + 1):
            ids = pl.ds(degree * degree, 2 * degree + 1)
            stacked = ((2 * degree + 1) * atoms, CH)
            left = agg_low[ids].reshape(stacked)
            right = cot[ids].reshape(stacked)
            value = dot_nn(left, out_proj[degree]).astype(bf16)
            out[ids] = value.reshape((2 * degree + 1, atoms, CH))
            at = (pl.ds(degree // 2 * CH, CH), pl.ds(degree % 2 * CH, CH))
            proj[at] = dot_tn(left, right)
        proj[pl.ds(LMAX // 2 * CH, CH), pl.ds(CH, CH)] = jnp.zeros((CH, CH), f32)

    return finish_kernel


def combine_stats(stats, own):
    blocks, slots = stats.shape[0], stats.shape[1] * 8
    chunk = max(1, PANEL // slots)
    name = own[:, NAME_AT : NAME_AT + 1]

    def part(at):
        part_rows = jnp.concatenate([stats[at * chunk + n] for n in range(chunk)], axis=0)
        entries = [part_rows[:, n : n + STATS] for n in range(0, LANES, STATS)]
        turned = jnp.transpose(jnp.concatenate(entries, axis=0))
        same = name == turned[NAME_AT : NAME_AT + 1]
        result = []
        for h in range(HEADS):
            peaks = turned[PEAK_AT + h : PEAK_AT + h + 1]
            peak = jnp.max(jnp.where(same, peaks, floor_value), axis=1, keepdims=True)
            scale = jnp.where(same, jnp.exp(jnp.where(same, peaks - peak, 0.0)), 0.0)
            den = jnp.sum(turned[h : h + 1] * scale, axis=1, keepdims=True)
            dot = jnp.sum(turned[DOT_AT + h : DOT_AT + h + 1] * scale, axis=1, keepdims=True)
            result += [peak, den, dot]
        return tuple(result)

    def step(at, held):
        fresh = part(at)
        result = []
        for h in range(HEADS):
            peak, den, dot = held[3 * h : 3 * h + 3]
            new_peak, new_den, new_dot = fresh[3 * h : 3 * h + 3]
            most = jnp.maximum(peak, new_peak)
            old, new = jnp.exp(peak - most), jnp.exp(new_peak - most)
            result += [most, den * old + new_den * new, dot * old + new_dot * new]
        return tuple(result)

    held = part(0)
    if blocks > chunk:
        held = lax.fori_loop(1, blocks // chunk, step, held)
    return [held[3 * h : 3 * h + 3] for h in range(HEADS)]


def gradient_kernel(
    stats, own, agg_grad, target_slot, rot, feats,
    x0_at, x1_at, x2_at, v0_at, v1_at, v2_at, pre, logits, adot,
    g0, top1, top2, pre_grad_out, kept0, sent0, kept1, sent1,
    num_grad, spread_grad, weights, g1, g2, packed, x0, x1, x2, v0, v1, v2, semaphores,
):
    loads = []
    for source, target in (
        (v0_at, v0), (v1_at, v1), (v2_at, v2), (x0_at, x0), (x1_at, x1), (x2_at, x2)
    ):
        load = pltpu.make_async_copy(source, target, semaphores.at[4 + len(loads)])
        load.start()
        loads.append(load)
    edges = target_slot.shape[1]
    slots = agg_grad.shape[0]
    aims = one_hot_rows(target_slot, slots)
    combined = combine_stats(stats, own[...])
    den_grads = []
    for h, (peak, den, dot) in enumerate(combined):
        of_edge = jnp.sum(jnp.where(aims, peak, 0.0), axis=0, keepdims=True)
        weights[pl.ds(h, 1), :] = jnp.exp(logits[pl.ds(h, 1), :] - of_edge)
        den_grad = (-(dot / den) / den).astype(bf16).astype(f32)
        den_grads.append(jnp.sum(jnp.where(aims, den_grad, 0.0), axis=0, keepdims=True))
    den_full = lane_heads([den for peak, den, dot in combined], (slots, LANES))
    for block in range(BLOCKS):
        cols = block_cols(block)
        num_grad[:, cols] = (agg_grad[:, cols] / den_full[:, : cols.size]).astype(bf16)
    spread_grad[...] = dot_tn(num_grad[...], mask_to(aims, bf16))

    state = {}

    def emit(degree, order, half, value):
        lanes = lane_at(half, edges, False)
        ref, row, second = frame_place(degree, order, (v0, v1, v2))
        product = value * ref[pl.ds(row, CH), lane_at(half, edges, second)]
        if degree == 0:
            state["sum"] = product
            state["spread"] = spread_heads([weights[pl.ds(h, 1), lanes] for h in range(HEADS)])
        else:
            state["sum"] = state["sum"] + product
        grad = (value * state["spread"]).astype(bf16)
        ref, row, second = frame_place(degree, order, (g0, g1, g2))
        ref[pl.ds(row, CH), lane_at(half, edges, second)] = grad
        if order != 0:
            swapped = grad if order < 0 else -grad
            below = row + (DIM1 if abs(order) == 1 else DIM2)
            ref[pl.ds(below, CH), lane_at(half, edges, not second)] = swapped
        if degree == LMAX and order == MMAX:
            for h in range(HEADS):
                part = state["sum"][h * VAL : (h + 1) * VAL]
                weights[pl.ds(HEADS + h, 1), lanes] = jnp.sum(part, axis=0, keepdims=True)

    for load in loads:
        load.wait()
    to_frame(spread_grad, rot, edges, emit)

    hidden = jnp.where(pre[...] > 0, pre[...], leak_slope * pre[...])
    logit_grads = [
        weights[pl.ds(h, 1), :] * (weights[pl.ds(HEADS + h, 1), :] + den_grads[h])
        for h in range(HEADS)
    ]
    tall = jnp.concatenate(
        [jnp.broadcast_to(row, (ALPHA, edges)) for row in logit_grads], axis=0
    )
    slope = jnp.where(pre[...] > 0, 1.0, leak_slope)
    pre_grad = (tall * turned_column(adot[...].astype(f32)) * slope).astype(bf16)
    pre_grad_out[...] = pre_grad
    dot_grad = jnp.sum(tall * hidden, axis=1, keepdims=True)

    top1[...] = g1[pl.ds(0, DIM1), :]
    top2[...] = g2[pl.ds(0, DIM2), :]
    mine = lax.axis_index("edge") & 1
    copies = []

    def put(row, value, at=0):
        for side in range(2):
            low, high = max(at, side * LANES), min(at + value.shape[1], (side + 1) * LANES)
            if low < high:
                piece = value[:, low - at : high - at]
                cols = pl.ds(low - side * LANES, high - low)
                packed[side, pl.ds(row, value.shape[0]), cols] = piece

    def send(chunk, kept, sent):
        start, size = CHUNKS[chunk]
        rows_of = pl.ds(start, size)
        for n, (side, out) in enumerate(((mine, kept), (1 - mine, sent))):
            copy = pltpu.make_async_copy(
                packed.at[side, rows_of, :], out, semaphores.at[2 * chunk + n]
            )
            copy.start()
            copies.append(copy)

    row = 0
    for left, right, dim in ((x1, g1, DIM1), (x2, g2, DIM2)):
        for start in range(0, 2 * dim, PANEL):
            size = min(PANEL, 2 * dim - start)
            put(row, dot_nt(left[...], right[pl.ds(start, size), :]))
            row += dim
    row -= DIM2
    edge_ch = feats.shape[1]
    edge_grad = lax.dot_general(
        feats[...], pre_grad, (((0,), (1,)), ((), ())), preferred_element_type=f32
    )
    put(row, edge_grad[:, :LANES], LANES)
    put(row + edge_ch, edge_grad[:, LANES:], LANES)
    wide_dot = jnp.transpose(jnp.broadcast_to(dot_grad, (HEADS * ALPHA, LANES)))
    spare = DIM2 - 2 * edge_ch
    tail = iota((spare, LANES), 0)
    first = jnp.broadcast_to(wide_dot[:1, :LANES], (spare, LANES))
    second = jnp.broadcast_to(wide_dot[:1, LANES:], (spare, LANES))
    put(row + 2 * edge_ch, jnp.where(tail == 0, first, jnp.where(tail == 1, second, 0.0)), LANES)
    row += DIM2
    put(row, dot_nt(x0[pl.ds(0, CH), :], pre_grad))
    send(0, kept0, sent0)

    row = CHUNKS[1][0]
    for start in range(0, DIM0, PANEL):
        size = min(PANEL, DIM0 - start)
        put(row, dot_nt(x0[...], g0[pl.ds(start, size), :]))
        if size < PANEL:
            put(row, jnp.zeros((DIM0, PANEL - size), f32), size)
        row += DIM0
    send(1, kept1, sent1)
    for copy in copies:
        copy.wait()


CHUNKS = ((0, 3 * DIM1 + 3 * DIM2 + CH), (3 * DIM1 + 3 * DIM2 + CH, 2 * DIM0))
PACKED_ROWS = sum(size for start, size in CHUNKS)


def halves_of(mine, other):
    first = (lax.axis_index("edge") & 1) == 0
    left, right = mine[...].astype(f32), other[...].astype(f32)
    return jnp.where(first, left, right), jnp.where(first, right, left)


def unpack_zero_kernel(mine, other, zero):
    left, right = halves_of(mine, other)
    zero[:, pl.ds(0, LANES)] = left[:DIM0].astype(bf16)
    zero[:, pl.ds(LANES, LANES)] = right[:DIM0].astype(bf16)
    zero[:, pl.ds(2 * LANES, LANES)] = left[DIM0:].astype(bf16)
    zero[:, pl.ds(3 * LANES, DIM0 - 3 * LANES)] = right[DIM0:, : DIM0 - 3 * LANES].astype(bf16)


def unpack_rest_kernel(mine, other, one, two, alpha_in, alpha_edge, alpha_dot):
    left, right = halves_of(mine, other)
    for n in range(2 * DIM1 // LANES):
        panel = (left, right)[n % 2][(n // 2) * DIM1 : (n // 2 + 1) * DIM1]
        per = DIM1 // LANES
        one[n // per, :, pl.ds((n % per) * LANES, LANES)] = panel.astype(bf16)
    left, right = left[3 * DIM1 :], right[3 * DIM1 :]
    panels = [(left, right)[n % 2][(n // 2) * DIM2 : (n // 2 + 1) * DIM2] for n in range(5)]
    whole = jnp.concatenate(panels, axis=1)
    two[0] = whole[:, :DIM2].astype(bf16)
    two[1] = whole[:, DIM2:].astype(bf16)
    edge_ch = alpha_edge.shape[0]
    rest = right[2 * DIM2 : 3 * DIM2]
    alpha_edge[:, pl.ds(0, LANES)] = rest[:edge_ch].astype(bf16)
    alpha_edge[:, pl.ds(LANES, LANES)] = rest[edge_ch : 2 * edge_ch].astype(bf16)
    alpha_dot[...] = rest[2 * edge_ch : 2 * edge_ch + 2].astype(bf16)
    alpha_in[:, pl.ds(0, LANES)] = left[3 * DIM2 :].astype(bf16)
    alpha_in[:, pl.ds(LANES, LANES)] = right[3 * DIM2 :].astype(bf16)


def source_kernel(
    source_slot, lists, rot, g0, g1, g2, pre_grad, wzero, wone, wtwo, ain,
    *rest,
):
    sums_out, d0, d1, d2, terms = rest[-5:]
    edges = source_slot.shape[1]
    slots = sums_out.shape[0] * sums_out.shape[1]
    d0[...] = dot_nn(wzero[...], g0[...])
    d0[pl.ds(0, CH), :] += dot_nn(ain[...], pre_grad[...])
    for out, weight, value in ((d1, wone, g1[...]), (d2, wtwo, g2[...])):
        out[...] = dot_nn(weight[0], value) - swapped_halves(dot_nn(weight[1], value), edges)

    def load(degree, order, half):
        ref, row, second = frame_place(degree, order, (d0, d1, d2))
        return ref[pl.ds(row, CH), lane_at(half, edges, second)]

    terms[pl.ds(FLAT, COLS - FLAT), :] = jnp.zeros((COLS - FLAT, 2 * edges), bf16)
    from_frame(load, rot, edges, store_terms(terms, edges))
    slot_sums(terms, mask_to(one_hot_rows(source_slot, slots), bf16), sums_out)
    put_rows(sums_out, pl.ds(COLS, LANES), lists[...])


def make_collect(lanes_total):
    def collect_kernel(*rest):
        arrivals = rest[:lanes_total]
        out, rows = rest[lanes_total:]
        atoms = out.shape[1]
        total = rows.shape[0]
        collect_rows(arrivals, rows)
        index = rows[:, pl.ds(COLS, LANES)][:, 1:2]
        picked = mask_to(iota((total, atoms), 1).astype(f32) == index, bf16)
        twice = jnp.concatenate([picked, picked], axis=0)
        for block in range(BLOCKS):
            high, low = split_two(rows[:, pl.ds(block * LANES, LANES)])
            sums = dot_tn(twice, jnp.concatenate([high, low], axis=0)).astype(bf16)
            out[2 * block] = sums[:, :CH]
            if 2 * block + 1 < COEFFS:
                out[2 * block + 1] = sums[:, CH:]

    return collect_kernel


vmem = pl.BlockSpec(memory_space=pltpu.VMEM)
smem = pl.BlockSpec(memory_space=pltpu.SMEM)
anywhere = pl.BlockSpec(memory_space=pl.ANY)


def call(kernel, outs, scratch, *args, scalars=0, far=(), apart=(), after=(), work=4):
    specs = [smem if n < scalars else anywhere if n in far else vmem for n in range(len(args))]
    specs += [anywhere] * len(after)
    out_specs = [anywhere if n in apart else vmem for n in range(len(outs))]
    shapes = [pltpu.VMEM(*entry) if isinstance(entry, tuple) else entry for entry in scratch]
    moved = sum(int(np.prod(a.shape)) * a.dtype.itemsize for a in args)
    return pl.pallas_call(
        kernel,
        out_shape=[jax.ShapeDtypeStruct(shape, kind) for shape, kind in outs],
        in_specs=specs,
        out_specs=out_specs,
        scratch_shapes=shapes,
        compiler_params=pltpu.CompilerParams(vmem_limit_bytes=VMEM_LIMIT),
        cost_estimate=pl.CostEstimate(
            flops=work * 10**9, bytes_accessed=moved, transcendentals=0
        ),
    )(*args, *after)


def tie(value, *earlier):
    return lax.optimization_barrier((value, *earlier))[0]


def turned_column(row):
    return jnp.transpose(jnp.broadcast_to(row, (8, row.shape[1])))[:, :1]


def swap(value, axis, bit):
    size = lax.axis_size(axis)
    return lax.ppermute(value, axis, [(i, i ^ (1 << bit)) for i in range(size)])


def bits_of(axis):
    return (lax.axis_size(axis) - 1).bit_length()


def gather_lanes(value):
    held = {0: value}
    for bit in reversed(range(bits_of("edge"))):
        held.update({k | (1 << bit): swap(v, "edge", bit) for k, v in list(held.items())})
    return [held[k] for k in range(len(held))]


def own_bit(axis, bit):
    return (lax.axis_index(axis) >> bit) & 1


def sum_all(current, first, earlier=()):
    steps = [("edge", n) for n in range(1, bits_of("edge"))]
    steps += [("graph", n) for n in range(bits_of("graph"))]
    steps.sort(key=lambda step: step[0] != first)
    for axis, bit in steps:
        mine = own_bit(axis, bit)
        parts = current.reshape(2, current.shape[0] // 2, -1)
        other = swap(lax.dynamic_index_in_dim(parts, 1 - mine, 0, False), axis, bit)
        if earlier:
            other, earlier = tie(other, *earlier), ()
        current = lax.dynamic_index_in_dim(parts, mine, 0, False) + other
    current = current.astype(bf16)
    for axis, bit in reversed(steps):
        mine = own_bit(axis, bit)
        other = swap(current, axis, bit)
        current = jnp.concatenate(
            [jnp.where(mine == 0, current, other), jnp.where(mine == 0, other, current)], axis=0
        )
    return current, swap(current, "edge", 0)


def shards(
    atom_embed, out_cotangent, send_rows, recv_rows, source_slot, target_slot, rotation,
    edge_feats, edge_bias, conv_zero, conv_one, conv_two, alpha_in, alpha_edge, alpha_dot,
    out_proj,
):
    peers = lax.axis_size("graph")
    lanes_total = lax.axis_size("edge")
    atoms = atom_embed.shape[0]
    edges = rotation.shape[0]
    cap = send_rows.shape[3]
    slots = peers * cap
    blocks = peers * lanes_total

    def exchange(value):
        return lax.all_to_all(value, "graph", split_axis=0, concat_axis=0, tiled=True)

    cot = jnp.transpose(out_cotangent, (1, 0, 2))
    (outgoing,) = call(
        outgoing_kernel, [((peers, cap, TABLE), bf16)], [],
        send_rows, recv_rows, jnp.transpose(atom_embed, (1, 0, 2)), cot,
        scalars=2, work=2,
    )
    table = exchange(outgoing)

    source_row = source_slot.reshape(1, edges)
    target_row = target_slot.reshape(1, edges)
    bias = edge_bias.T
    adot = alpha_dot.reshape(1, -1)

    frames = [
        ((DIM0, edges), bf16),
        ((DIM1, 2 * edges), bf16),
        ((DIM2, 2 * edges), bf16),
        ((DIM0, edges), f32),
        ((DIM1, 2 * edges), f32),
        ((DIM2, 2 * edges), f32),
    ]
    pre_shape = ((HEADS * ALPHA, edges), f32)
    sums, stats, x0, x1, x2, v0, v1, v2, pre, logits, lists, agg_grad, rot, own_stats = call(
        make_forward(atoms),
        [((peers, cap, WIDE), f32), ((blocks, slots // 8, LANES), f32)]
        + frames
        + [
            pre_shape,
            ((8, edges), f32),
            ((slots, LANES), f32),
            ((slots, FLAT), f32),
            ((rotation.shape[1], edges), f32),
            ((slots, LANES), f32),
        ],
        [
            ((slots, TABLE), f32),
            ((FLAT, edges), f32),
            ((8, edges), f32),
            ((COLS, 2 * edges), bf16),
            (conv_zero.shape, bf16),
            (conv_one.shape, bf16),
            (conv_two.shape, bf16),
        ]
        + frames
        + [pre_shape, pltpu.SemaphoreType.DMA((10,))],
        table, source_row, target_row, rotation, edge_feats, bias,
        conv_zero, conv_one, conv_two, alpha_in, alpha_edge, adot, out_proj,
        far=(6, 7, 8), apart=range(2, 9), work=8,
    )
    all_stats = lax.all_to_all(stats, ("graph", "edge"), split_axis=0, concat_axis=0, tiled=True)

    halves = [((size, LANES), f32) for start, size in CHUNKS for _ in range(2)]
    g0, g1, g2, pre_grad, *halves = call(
        gradient_kernel,
        [
            ((DIM0, edges), bf16),
            ((DIM1, 2 * edges), bf16),
            ((DIM2, 2 * edges), bf16),
            ((HEADS * ALPHA, edges), bf16),
        ]
        + halves,
        [
            ((slots, FLAT), bf16),
            ((FLAT, edges), f32),
            ((8, edges), f32),
            ((2 * DIM1, 2 * edges), bf16),
            ((2 * DIM2, 2 * edges), bf16),
            ((2, PACKED_ROWS, LANES), f32),
        ]
        + frames
        + [pltpu.SemaphoreType.DMA((10,))],
        all_stats, own_stats, agg_grad, target_row, rot, edge_feats,
        x0, x1, x2, v0, v1, v2, pre, logits, adot,
        far=range(6, 12), apart=range(4, 8), work=8,
    )
    currents = [
        halves[2 * n] + swap(halves[2 * n + 1], "edge", 0) for n in range(len(CHUNKS))
    ]

    total = lanes_total * slots
    (source_sums,) = call(
        source_kernel,
        [((peers, cap, WIDE), f32)],
        [
            ((DIM0, edges), f32),
            ((DIM1, 2 * edges), f32),
            ((DIM2, 2 * edges), f32),
            ((COLS, 2 * edges), bf16),
        ],
        source_row, lists, rot, g0, g1, g2, pre_grad, conv_zero, conv_one, conv_two, alpha_in,
        after=currents, work=6,
    )
    returned = exchange(source_sums)
    out, proj = call(
        make_finish(lanes_total),
        [((COEFFS, atoms, CH), bf16), (((LMAX // 2 + 1) * CH, LANES), f32)],
        [((total, WIDE), f32), ((2 * total, COLS), bf16), ((COEFFS, atoms, CH), bf16)],
        cot, out_proj, *gather_lanes(tie(exchange(tie(sums, halves[1])), source_sums)),
    )
    for bit in range(bits_of("graph")):
        proj = proj + swap(proj, "graph", bit)
    (embed,) = call(
        make_collect(lanes_total),
        [((COEFFS, atoms, CH), bf16)],
        [((total, WIDE), f32)],
        *gather_lanes(returned),
    )

    rest_pair = sum_all(currents[0], "edge", [source_sums])
    zero_pair = sum_all(currents[1], "graph")
    (zero,) = call(
        unpack_zero_kernel, [((DIM0, DIM0), bf16)], [], *zero_pair, work=1
    )
    one, two, grad_in, grad_edge, grad_dot = call(
        unpack_rest_kernel,
        [
            ((2, DIM1, DIM1), bf16),
            ((2, DIM2, DIM2), bf16),
            (alpha_in.shape, bf16),
            (alpha_edge.shape, bf16),
            ((2, LANES), bf16),
        ],
        [], *rest_pair, work=1,
    )

    def shaped(value):
        return jnp.transpose(value, (1, 0, 2))

    return (
        shaped(out), shaped(embed), zero, one, two, grad_in, grad_edge, grad_dot.reshape(-1),
        jnp.swapaxes(proj.astype(bf16).reshape(-1, CH, 2, CH), 1, 2).reshape(-1, CH, CH)[: LMAX + 1],
    )


def solution(mesh):
    in_specs = (
        P(("groups", "graph"), None, None),
        P(("groups", "graph"), None, None),
        P(("groups", "graph"), None, "edge", None),
        P(("groups", "graph"), None, "edge", None),
        P(("groups", "graph", "edge")),
        P(("groups", "graph", "edge")),
        P(("groups", "graph", "edge"), None),
        P(("groups", "graph", "edge"), None),
        P(("groups", "graph", "edge"), None),
        P(),
        P(),
        P(),
        P(),
        P(),
        P(),
        P(),
    )
    out_specs = (
        P(("groups", "graph"), None, None),
        P(("groups", "graph"), None, None),
        P("groups", None),
        P("groups", None, None),
        P("groups", None, None),
        P("groups", None),
        P("groups", None),
        P("groups"),
        P("groups", None, None),
    )
    return jax.shard_map(shards, mesh=mesh, in_specs=in_specs, out_specs=out_specs, check_vma=False)
```

```python
import jax
import jax.numpy as jnp
import numpy as np
from jax import lax
from jax.experimental import pallas as pl
from jax.experimental.pallas import tpu as pltpu
from jax.sharding import PartitionSpec as P

LMAX = 6
MMAX = 2
CH = 64
HEADS = 4
VAL = 16
ALPHA = 64
COEFFS = (LMAX + 1) * (LMAX + 1)
FLAT = COEFFS * CH
LANES = 128
BLOCKS = (FLAT + LANES - 1) // LANES
COLS = BLOCKS * LANES
WIDE = COLS + LANES
TABLE = 2 * COLS + LANES
PEAK_AT, DOT_AT, NAME_AT = HEADS, 2 * HEADS, 3 * HEADS
STATS = 16
DIM0 = (LMAX + 1) * CH
DIM1 = LMAX * CH
DIM2 = (LMAX - 1) * CH
PANEL = 256

leak_slope = 0.2
floor_value = -1e30
bf16 = jnp.bfloat16
f32 = jnp.float32

VMEM_LIMIT = 56 * 1024 * 1024


def degree_blocks():
    result = []
    offset = 0
    for degree in range(LMAX + 1):
        centre = min(degree, MMAX)
        row_total = 2 * centre + 1
        col_total = 2 * degree + 1
        result.append((degree, centre, row_total, col_total, offset))
        offset += row_total * col_total
    return result


def degree_of(coeff):
    return int(np.sqrt(coeff))


def dot_nn(left, right):
    return jnp.dot(left, right, preferred_element_type=f32)


def dot_nt(left, right):
    return lax.dot_general(left, right, (((1,), (1,)), ((), ())), preferred_element_type=f32)


def dot_tn(left, right):
    return lax.dot_general(left, right, (((0,), (0,)), ((), ())), preferred_element_type=f32)


def iota(shape, dim):
    return lax.broadcasted_iota(jnp.int32, shape, dim)


def split_two(value):
    high = value.astype(bf16)
    return high, (value - high.astype(f32)).astype(bf16)


def to_frame(source, rot, edges, emit):
    for half in range(edges // LANES):
        lanes = pl.ds(half * LANES, LANES)
        for degree, centre, row_total, col_total, offset in degree_blocks():
            sums = [None] * row_total
            for j in range(col_total):
                column = source[pl.ds((degree * degree + j) * CH, CH), lanes]
                for i in range(row_total):
                    term = rot[pl.ds(offset + i * col_total + j, 1), lanes] * column
                    sums[i] = term if j == 0 else sums[i] + term
            for i in range(row_total):
                emit(degree, i - centre, half, sums[i])


def from_frame(load, rot, edges, emit):
    for half in range(edges // LANES):
        lanes = pl.ds(half * LANES, LANES)
        for degree, centre, row_total, col_total, offset in degree_blocks():
            rows = [load(degree, i - centre, half) for i in range(row_total)]
            for j in range(col_total):
                total = None
                for i in range(row_total):
                    term = rot[pl.ds(offset + i * col_total + j, 1), lanes] * rows[i]
                    total = term if i == 0 else total + term
                emit(degree * degree + j, half, total)


def lane_at(half, edges, second):
    return pl.ds(half * LANES + (edges if second else 0), LANES)


def frame_place(degree, order, refs):
    if order == 0:
        return refs[0], degree * CH, False
    which = abs(order)
    return refs[which], (degree - which) * CH, order < 0


def spread_heads(rows):
    return jnp.concatenate(
        [jnp.broadcast_to(row, (VAL, row.shape[1])) for row in rows], axis=0
    )


def is_direct(peers):
    return peers <= 4


def flip_of(peers):
    return lax.axis_index("graph") if is_direct(peers) else 0


def one_hot_rows(slot_ref, peers, slots):
    edges = slot_ref.shape[1]
    first = flip_of(peers) * (slots // peers)
    return jnp.bitwise_xor(iota((slots, edges), 0), first) == slot_ref[...]


def mask_to(mask, dtype):
    return jnp.where(mask, 1.0, 0.0).astype(dtype)


def stack_table(tables, rows_ref):
    cap = tables[0].shape[0]
    per = 8 // cap
    for n in range(0, len(tables), per):
        parts = [table[...].astype(f32) for table in tables[n : n + per]]
        rows_ref[pl.ds(n * cap, 8), :] = jnp.concatenate(parts, axis=0)


def put_rows(out_ref, cols, value):
    peers, cap = out_ref.shape[0], out_ref.shape[1]
    flip = flip_of(peers)
    for n in range(peers):
        place = jnp.bitwise_xor(flip, n) if is_direct(peers) else n
        out_ref[place, :, cols] = value[n * cap : (n + 1) * cap].astype(out_ref.dtype)


def slot_sums(terms, one_hot, out_ref, factor=None):
    both = jnp.concatenate([one_hot, one_hot], axis=1)
    products = 0.0
    for start in range(0, COLS, PANEL):
        size = min(PANEL, COLS - start)
        sums = dot_nt(both, terms[pl.ds(start, size), :])
        put_rows(out_ref, pl.ds(start, size), sums)
        if factor is None:
            continue
        for at in range(0, size, LANES):
            width = min(LANES, FLAT - start - at)
            product = sums[:, at : at + width] * factor[:, pl.ds(start + at, width)]
            if width < LANES:
                product = jnp.concatenate([product, jnp.zeros_like(product)], axis=1)
            products = products + product
    return products


def store_terms(terms, edges):
    def emit(coeff, half, value):
        high, low = split_two(value)
        rows = pl.ds(coeff * CH, CH)
        terms[rows, lane_at(half, edges, False)] = high
        terms[rows, lane_at(half, edges, True)] = low

    return emit


def listed_rows(list_ref, shape):
    peers, cap = list_ref.shape[1], list_ref.shape[3]
    flip = flip_of(peers)
    row = iota(shape, 0)
    result = jnp.zeros(shape, jnp.int32)
    for slot in range(peers * cap):
        owner = jnp.bitwise_xor(flip, slot // cap) if is_direct(peers) else slot // cap
        result = jnp.where(row == slot, list_ref[0, owner, 0, slot % cap], result)
    return result


def put_coeffs(outs, first, coeff_rows):
    for block in range(BLOCKS):
        left = coeff_rows(2 * block)
        right = coeff_rows(2 * block + 1) if 2 * block + 1 < COEFFS else jnp.zeros_like(left)
        put_pieces(outs, first + block * LANES, jnp.concatenate([left, right], axis=1))


def put_pieces(outs, first, value):
    cap = outs[0].shape[0]
    for n, out in enumerate(outs):
        out[:, pl.ds(first, LANES)] = value[n * cap : (n + 1) * cap].astype(out.dtype)


def outgoing_kernel(send, recv, embed, cot, *outs):
    atoms = embed.shape[1]
    slots = send.shape[1] * send.shape[3]
    sent = listed_rows(send, (slots, LANES))
    received = listed_rows(recv, (slots, LANES))
    for first, listed, values in ((0, sent, embed), (COLS, received, cot)):
        picked = mask_to(iota((slots, atoms), 1) == listed[:, :atoms], bf16)
        put_coeffs(outs, first, lambda k: dot_nn(picked, values[k]))
    lane = iota((slots, LANES), 1)
    side = jnp.where(lane == 0, received, jnp.where(lane == 1, sent, 0))
    put_pieces(outs, 2 * COLS, side.astype(f32))


def swapped_halves(value, edges):
    return jnp.concatenate([-value[:, edges:], value[:, :edges]], axis=1)


def make_forward(atoms, peers):
    def forward_kernel(
        source_slot, target_slot, rotation, feats, bias, wzero_at, wone_at, wtwo_at,
        ain, aedge, adot, out_proj, *rest,
    ):
        tables, rest = rest[:peers], rest[peers:]
        (
        sums_out, stats_out, x0_at, x1_at, x2_at, v0_at, v1_at, v2_at, pre_at, logit_out,
        lists_out, agg_grad, rot, own_out,
        rows, gathered, weights, terms, wzero, wone, wtwo, x0, x1, x2, v0, v1, v2, pre_out,
        semaphores,
        ) = rest
        copies = []

        def move(source, target):
            copy = pltpu.make_async_copy(source, target, semaphores.at[len(copies)])
            copy.start()
            copies.append(copy)

        move(wzero_at, wzero)
        move(wone_at, wone)
        move(wtwo_at, wtwo)
        rot[...] = jnp.transpose(rotation[...].astype(f32))
        edges = source_slot.shape[1]
        cap = tables[0].shape[0]
        slots = peers * cap
        stack_table(tables, rows)
        picked = mask_to(one_hot_rows(source_slot, peers, slots), bf16)
        for degree in range(LMAX + 1):
            ids = pl.ds(degree * degree * CH, (2 * degree + 1) * CH)
            gathered[ids, :] = dot_tn(rows[:, ids].astype(bf16), picked)
        lists = rows[:, pl.ds(2 * COLS, LANES)]
        lists_out[...] = lists
        for degree in range(LMAX + 1):
            ids = range(degree * degree, (degree + 1) * (degree + 1))
            cot = jnp.concatenate([rows[:, pl.ds(COLS + k * CH, CH)] for k in ids], axis=0)
            grad = dot_nt(cot.astype(bf16), out_proj[degree])
            for n, k in enumerate(ids):
                agg_grad[:, pl.ds(k * CH, CH)] = grad[n * slots : (n + 1) * slots]

        def emit(degree, order, half, value):
            ref, row, second = frame_place(degree, order, (x0, x1, x2))
            ref[pl.ds(row, CH), lane_at(half, edges, second)] = value.astype(bf16)

        to_frame(gathered, rot, edges, emit)
        for source, target in ((x0, x0_at), (x1, x1_at), (x2, x2_at)):
            move(source, target)

        pre = dot_tn(ain[...], x0[pl.ds(0, CH), :]) + lax.dot_general(
            aedge[...], feats[...], (((0,), (1,)), ((), ())), preferred_element_type=f32
        )
        pre_out[...] = pre
        move(pre_out, pre_at)
        hidden = jnp.where(pre > 0, pre, leak_slope * pre) * turned_column(adot[...].astype(f32))
        aims = one_hot_rows(target_slot, peers, slots)
        lane = iota((slots, LANES), 1)
        peer = jnp.bitwise_xor(iota((slots, 1), 0) // cap, flip_of(peers))
        name = lists[:, :1] + (peer * atoms).astype(f32)
        side = jnp.where(lane == NAME_AT, name, 0.0)
        for h in range(HEADS):
            logit = jnp.sum(hidden[h * ALPHA : (h + 1) * ALPHA], axis=0, keepdims=True)
            logit = logit + bias[pl.ds(h, 1), :]
            logit_out[pl.ds(h, 1), :] = logit
            peak = jnp.max(jnp.where(aims, logit, floor_value), axis=1, keepdims=True)
            of_edge = jnp.sum(jnp.where(aims, peak, 0.0), axis=0, keepdims=True)
            weight = jnp.exp(logit - of_edge)
            weights[pl.ds(h, 1), :] = weight
            den = jnp.sum(jnp.where(aims, weight, 0.0), axis=1, keepdims=True)
            side = jnp.where(lane == h, den, jnp.where(lane == PEAK_AT + h, peak, side))

        for copy in copies[:3]:
            copy.wait()
        v0[...] = dot_tn(wzero[...], x0[...])
        for out, weight, value in ((v1, wone, x1[...]), (v2, wtwo, x2[...])):
            out[...] = dot_tn(weight[0], value) + swapped_halves(dot_tn(weight[1], value), edges)
        for source, target in ((v0, v0_at), (v1, v1_at), (v2, v2_at)):
            move(source, target)

        def load(degree, order, half):
            ref, row, second = frame_place(degree, order, (v0, v1, v2))
            return ref[pl.ds(row, CH), lane_at(half, edges, second)]

        store = store_terms(terms, edges)

        def weigh(coeff, half, value):
            lanes = lane_at(half, edges, False)
            spread = spread_heads([weights[pl.ds(h, 1), lanes] for h in range(HEADS)])
            store(coeff, half, value * spread)

        terms[pl.ds(FLAT, COLS - FLAT), :] = jnp.zeros((COLS - FLAT, 2 * edges), bf16)
        from_frame(load, rot, edges, weigh)
        dots = slot_sums(terms, mask_to(aims, bf16), sums_out, agg_grad)
        head = (lane % CH) // VAL
        for h in range(HEADS):
            dot = jnp.sum(jnp.where(head == h, dots, 0.0), axis=1, keepdims=True)
            side = jnp.where(lane == DOT_AT + h, dot, side)
        put_rows(sums_out, pl.ds(COLS, LANES), side)
        own_out[...] = side
        spread = jnp.concatenate([side[:, :STATS]] * (LANES // STATS), axis=1)
        spread = jnp.where(lane // STATS == iota((slots, LANES), 0) % 8, spread, 0.0)
        packed = jnp.sum(spread.reshape(slots // 8, 8, LANES), axis=1)

        stats_out[...] = packed
        for copy in copies[3:]:
            copy.wait()

    return forward_kernel


def lane_heads(values, shape):
    head = (iota(shape, 1) % CH) // VAL
    result = jnp.broadcast_to(values[0], shape)
    for h in range(1, HEADS):
        result = jnp.where(head == h, values[h], result)
    return result


def collect_rows(arrivals, rows_ref):
    own = lax.axis_index("edge")
    for k, arrival in enumerate(arrivals):
        peers, cap, width = arrival.shape
        base = (own ^ k) * (peers * cap)
        for start in range(0, peers * cap, 8):
            parts = [arrival[g] for g in range(start // cap, (start + 8) // cap)]
            at = pl.ds(pl.multiple_of(base + start, 8), 8)
            rows_ref[at, :] = jnp.concatenate(parts, axis=0)


def block_cols(block):
    return pl.ds(block * LANES, min(LANES, FLAT - block * LANES))


def make_finish(lanes_total):
    def finish_kernel(cot, out_proj, *rest):
        arrivals = rest[:lanes_total]
        out, proj, rows, terms, agg_low = rest[lanes_total:]
        atoms = cot.shape[1]
        total = rows.shape[0]
        collect_rows(arrivals, rows)
        side = rows[:, pl.ds(COLS, LANES)]
        owner = (lax.axis_index("graph") * atoms).astype(f32)
        names = iota((total, atoms), 1).astype(f32) + owner == side[:, NAME_AT : NAME_AT + 1]
        eye = iota((atoms, atoms), 0) == iota((atoms, atoms), 1)
        scales, dens = [], []
        for h in range(HEADS):
            peak_rows = side[:, PEAK_AT + h : PEAK_AT + h + 1]
            peak = jnp.max(jnp.where(names, peak_rows, floor_value), axis=0, keepdims=True)
            of_row = jnp.sum(jnp.where(names, peak, 0.0), axis=1, keepdims=True)
            scale = jnp.exp(peak_rows - of_row)
            scaled_den = side[:, h : h + 1] * scale
            den = jnp.sum(jnp.where(names, scaled_den, 0.0), axis=0, keepdims=True)
            scales.append(scale)
            dens.append(jnp.sum(jnp.where(eye, den, 0.0), axis=1, keepdims=True))
        scale_full = lane_heads(scales, (total, LANES))
        den_full = lane_heads(dens, (atoms, LANES))
        picked = mask_to(names, bf16)
        twice = jnp.concatenate([picked, picked], axis=0)
        for block in range(BLOCKS):
            cols = pl.ds(block * LANES, LANES)
            high, low = split_two(rows[:, cols] * scale_full)
            terms[pl.ds(0, total), cols] = high
            terms[pl.ds(total, total), cols] = low
        for block in range(BLOCKS):
            cols = pl.ds(block * LANES, LANES)
            agg = (dot_tn(twice, terms[:, cols]) / den_full).astype(bf16)
            agg_low[2 * block] = agg[:, :CH]
            if 2 * block + 1 < COEFFS:
                agg_low[2 * block + 1] = agg[:, CH:]
        for degree in range(LMAX + 1):
            ids = pl.ds(degree * degree, 2 * degree + 1)
            stacked = ((2 * degree + 1) * atoms, CH)
            left = agg_low[ids].reshape(stacked)
            right = cot[ids].reshape(stacked)
            value = dot_nn(left, out_proj[degree]).astype(bf16)
            out[ids] = value.reshape((2 * degree + 1, atoms, CH))
            at = (pl.ds(degree // 2 * CH, CH), pl.ds(degree % 2 * CH, CH))
            proj[at] = dot_tn(left, right)
        proj[pl.ds(LMAX // 2 * CH, CH), pl.ds(CH, CH)] = jnp.zeros((CH, CH), f32)

    return finish_kernel


def combine_stats(stats, own):
    chunk = 32
    name = own[:, NAME_AT : NAME_AT + 1]

    def part(part_rows):
        entries = [part_rows[:, n : n + STATS] for n in range(0, LANES, STATS)]
        turned = jnp.transpose(jnp.concatenate(entries, axis=0))
        same = name == turned[NAME_AT : NAME_AT + 1]
        result = []
        for h in range(HEADS):
            peaks = turned[PEAK_AT + h : PEAK_AT + h + 1]
            peak = jnp.max(jnp.where(same, peaks, floor_value), axis=1, keepdims=True)
            scale = jnp.where(same, jnp.exp(jnp.where(same, peaks - peak, 0.0)), 0.0)
            den = jnp.sum(turned[h : h + 1] * scale, axis=1, keepdims=True)
            dot = jnp.sum(turned[DOT_AT + h : DOT_AT + h + 1] * scale, axis=1, keepdims=True)
            result += [peak, den, dot]
        return tuple(result)

    def step(at, held):
        fresh = part(stats[0][pl.ds(pl.multiple_of(at * chunk, chunk), chunk), :])
        result = []
        for h in range(HEADS):
            peak, den, dot = held[3 * h : 3 * h + 3]
            new_peak, new_den, new_dot = fresh[3 * h : 3 * h + 3]
            most = jnp.maximum(peak, new_peak)
            old, new = jnp.exp(peak - most), jnp.exp(new_peak - most)
            result += [most, den * old + new_den * new, dot * old + new_dot * new]
        return tuple(result)

    if len(stats) > 1:
        held = part(jnp.concatenate([rows[...] for rows in stats], axis=0))
    else:
        held = part(stats[0][pl.ds(0, chunk), :])
        held = lax.fori_loop(1, stats[0].shape[0] // chunk, step, held)
    return [held[3 * h : 3 * h + 3] for h in range(HEADS)]


def make_gradient(peers, parts):
    def kernel(*refs):
        gradient_kernel(peers, refs[:parts], *refs[parts:])

    return kernel


def gradient_kernel(
    peers, stats, own, agg_grad, target_slot, rot, feats,
    x0_at, x1_at, x2_at, v0_at, v1_at, v2_at, pre, logits, adot,
    g0, top1, top2, pre_grad_out, kept0, sent0, kept1, sent1,
    num_grad, spread_grad, weights, g1, g2, packed, x0, x1, x2, v0, v1, v2, semaphores,
):
    loads = []
    for source, target in (
        (v0_at, v0), (v1_at, v1), (v2_at, v2), (x0_at, x0), (x1_at, x1), (x2_at, x2)
    ):
        load = pltpu.make_async_copy(source, target, semaphores.at[4 + len(loads)])
        load.start()
        loads.append(load)
    edges = target_slot.shape[1]
    slots = agg_grad.shape[0]
    aims = one_hot_rows(target_slot, peers, slots)
    combined = combine_stats(stats, own[...])
    den_grads = []
    for h, (peak, den, dot) in enumerate(combined):
        of_edge = jnp.sum(jnp.where(aims, peak, 0.0), axis=0, keepdims=True)
        weights[pl.ds(h, 1), :] = jnp.exp(logits[pl.ds(h, 1), :] - of_edge)
        den_grad = (-(dot / den) / den).astype(bf16).astype(f32)
        den_grads.append(jnp.sum(jnp.where(aims, den_grad, 0.0), axis=0, keepdims=True))
    den_full = lane_heads([den for peak, den, dot in combined], (slots, LANES))
    for block in range(BLOCKS):
        cols = block_cols(block)
        num_grad[:, cols] = (agg_grad[:, cols] / den_full[:, : cols.size]).astype(bf16)
    picked = mask_to(aims, bf16)
    for degree in range(LMAX + 1):
        ids = pl.ds(degree * degree * CH, (2 * degree + 1) * CH)
        spread_grad[ids, :] = dot_tn(num_grad[:, ids], picked)

    state = {}

    def emit(degree, order, half, value):
        lanes = lane_at(half, edges, False)
        ref, row, second = frame_place(degree, order, (v0, v1, v2))
        product = value * ref[pl.ds(row, CH), lane_at(half, edges, second)]
        if degree == 0:
            state["sum"] = product
            state["spread"] = spread_heads([weights[pl.ds(h, 1), lanes] for h in range(HEADS)])
        else:
            state["sum"] = state["sum"] + product
        grad = (value * state["spread"]).astype(bf16)
        ref, row, second = frame_place(degree, order, (g0, g1, g2))
        ref[pl.ds(row, CH), lane_at(half, edges, second)] = grad
        if order != 0:
            swapped = grad if order < 0 else -grad
            below = row + (DIM1 if abs(order) == 1 else DIM2)
            ref[pl.ds(below, CH), lane_at(half, edges, not second)] = swapped
        if degree == LMAX and order == MMAX:
            for h in range(HEADS):
                part = state["sum"][h * VAL : (h + 1) * VAL]
                weights[pl.ds(HEADS + h, 1), lanes] = jnp.sum(part, axis=0, keepdims=True)

    for load in loads:
        load.wait()
    to_frame(spread_grad, rot, edges, emit)

    hidden = jnp.where(pre[...] > 0, pre[...], leak_slope * pre[...])
    logit_grads = [
        weights[pl.ds(h, 1), :] * (weights[pl.ds(HEADS + h, 1), :] + den_grads[h])
        for h in range(HEADS)
    ]
    tall = jnp.concatenate(
        [jnp.broadcast_to(row, (ALPHA, edges)) for row in logit_grads], axis=0
    )
    slope = jnp.where(pre[...] > 0, 1.0, leak_slope)
    pre_grad = (tall * turned_column(adot[...].astype(f32)) * slope).astype(bf16)
    pre_grad_out[...] = pre_grad
    dot_grad = jnp.sum(tall * hidden, axis=1, keepdims=True)

    top1[...] = g1[pl.ds(0, DIM1), :]
    top2[...] = g2[pl.ds(0, DIM2), :]
    mine = lax.axis_index("edge") & 1
    copies = []

    def put(row, value, at=0):
        for side in range(2):
            low, high = max(at, side * LANES), min(at + value.shape[1], (side + 1) * LANES)
            if low < high:
                piece = value[:, low - at : high - at]
                cols = pl.ds(low - side * LANES, high - low)
                packed[side, pl.ds(row, value.shape[0]), cols] = piece

    def send(chunk, kept, sent):
        start, size = CHUNKS[chunk]
        rows_of = pl.ds(start, size)
        for n, (side, out) in enumerate(((mine, kept), (1 - mine, sent))):
            copy = pltpu.make_async_copy(
                packed.at[side, rows_of, :], out, semaphores.at[2 * chunk + n]
            )
            copy.start()
            copies.append(copy)

    row = 0
    for left, right, dim in ((x1, g1, DIM1), (x2, g2, DIM2)):
        for start in range(0, 2 * dim, PANEL):
            size = min(PANEL, 2 * dim - start)
            put(row, dot_nt(left[...], right[pl.ds(start, size), :]))
            row += dim
    row -= DIM2
    edge_ch = feats.shape[1]
    edge_grad = lax.dot_general(
        feats[...], pre_grad, (((0,), (1,)), ((), ())), preferred_element_type=f32
    )
    put(row, edge_grad[:, :LANES], LANES)
    put(row + edge_ch, edge_grad[:, LANES:], LANES)
    wide_dot = jnp.transpose(jnp.broadcast_to(dot_grad, (HEADS * ALPHA, LANES)))
    spare = DIM2 - 2 * edge_ch
    tail = iota((spare, LANES), 0)
    first = jnp.broadcast_to(wide_dot[:1, :LANES], (spare, LANES))
    second = jnp.broadcast_to(wide_dot[:1, LANES:], (spare, LANES))
    put(row + 2 * edge_ch, jnp.where(tail == 0, first, jnp.where(tail == 1, second, 0.0)), LANES)
    row += DIM2
    put(row, dot_nt(x0[pl.ds(0, CH), :], pre_grad))
    send(0, kept0, sent0)

    row = CHUNKS[1][0]
    for start in range(0, DIM0, PANEL):
        size = min(PANEL, DIM0 - start)
        put(row, dot_nt(x0[...], g0[pl.ds(start, size), :]))
        if size < PANEL:
            put(row, jnp.zeros((DIM0, PANEL - size), f32), size)
        row += DIM0
    send(1, kept1, sent1)
    for copy in copies:
        copy.wait()


CHUNKS = ((0, 3 * DIM1 + 3 * DIM2 + CH), (3 * DIM1 + 3 * DIM2 + CH, 2 * DIM0))
PACKED_ROWS = sum(size for start, size in CHUNKS)


def halves_of(mine, other):
    first = (lax.axis_index("edge") & 1) == 0
    left, right = mine[...].astype(f32), other[...].astype(f32)
    return jnp.where(first, left, right), jnp.where(first, right, left)


def unpack_zero_kernel(mine, other, zero):
    left, right = halves_of(mine, other)
    zero[:, pl.ds(0, LANES)] = left[:DIM0].astype(bf16)
    zero[:, pl.ds(LANES, LANES)] = right[:DIM0].astype(bf16)
    zero[:, pl.ds(2 * LANES, LANES)] = left[DIM0:].astype(bf16)
    zero[:, pl.ds(3 * LANES, DIM0 - 3 * LANES)] = right[DIM0:, : DIM0 - 3 * LANES].astype(bf16)


def unpack_rest_kernel(mine, other, one, two, alpha_in, alpha_edge, alpha_dot):
    left, right = halves_of(mine, other)
    for n in range(2 * DIM1 // LANES):
        panel = (left, right)[n % 2][(n // 2) * DIM1 : (n // 2 + 1) * DIM1]
        per = DIM1 // LANES
        one[n // per, :, pl.ds((n % per) * LANES, LANES)] = panel.astype(bf16)
    left, right = left[3 * DIM1 :], right[3 * DIM1 :]
    panels = [(left, right)[n % 2][(n // 2) * DIM2 : (n // 2 + 1) * DIM2] for n in range(5)]
    whole = jnp.concatenate(panels, axis=1)
    two[0] = whole[:, :DIM2].astype(bf16)
    two[1] = whole[:, DIM2:].astype(bf16)
    edge_ch = alpha_edge.shape[0]
    rest = right[2 * DIM2 : 3 * DIM2]
    alpha_edge[:, pl.ds(0, LANES)] = rest[:edge_ch].astype(bf16)
    alpha_edge[:, pl.ds(LANES, LANES)] = rest[edge_ch : 2 * edge_ch].astype(bf16)
    alpha_dot[...] = rest[2 * edge_ch : 2 * edge_ch + 2].astype(bf16)
    alpha_in[:, pl.ds(0, LANES)] = left[3 * DIM2 :].astype(bf16)
    alpha_in[:, pl.ds(LANES, LANES)] = right[3 * DIM2 :].astype(bf16)


def source_kernel(
    source_slot, lists, rot, g0, g1, g2, pre_grad, wzero, wone, wtwo, ain,
    *rest,
):
    sums_out, d0, d1, d2, terms = rest[-5:]
    edges = source_slot.shape[1]
    slots = sums_out.shape[0] * sums_out.shape[1]
    d0[...] = dot_nn(wzero[...], g0[...])
    d0[pl.ds(0, CH), :] += dot_nn(ain[...], pre_grad[...])
    for out, weight, value in ((d1, wone, g1[...]), (d2, wtwo, g2[...])):
        out[...] = dot_nn(weight[0], value) - swapped_halves(dot_nn(weight[1], value), edges)

    def load(degree, order, half):
        ref, row, second = frame_place(degree, order, (d0, d1, d2))
        return ref[pl.ds(row, CH), lane_at(half, edges, second)]

    terms[pl.ds(FLAT, COLS - FLAT), :] = jnp.zeros((COLS - FLAT, 2 * edges), bf16)
    from_frame(load, rot, edges, store_terms(terms, edges))
    slot_sums(terms, mask_to(one_hot_rows(source_slot, sums_out.shape[0], slots), bf16), sums_out)
    put_rows(sums_out, pl.ds(COLS, LANES), lists[...])


def make_collect(lanes_total):
    def collect_kernel(*rest):
        arrivals = rest[:lanes_total]
        out, rows = rest[lanes_total:]
        atoms = out.shape[1]
        total = rows.shape[0]
        collect_rows(arrivals, rows)
        index = rows[:, pl.ds(COLS, LANES)][:, 1:2]
        picked = mask_to(iota((total, atoms), 1).astype(f32) == index, bf16)
        twice = jnp.concatenate([picked, picked], axis=0)
        for block in range(BLOCKS):
            high, low = split_two(rows[:, pl.ds(block * LANES, LANES)])
            sums = dot_tn(twice, jnp.concatenate([high, low], axis=0)).astype(bf16)
            out[2 * block] = sums[:, :CH]
            if 2 * block + 1 < COEFFS:
                out[2 * block + 1] = sums[:, CH:]

    return collect_kernel


vmem = pl.BlockSpec(memory_space=pltpu.VMEM)
smem = pl.BlockSpec(memory_space=pltpu.SMEM)
anywhere = pl.BlockSpec(memory_space=pl.ANY)


def call(kernel, outs, scratch, *args, scalars=0, far=(), apart=(), after=(), work=4):
    specs = [smem if n < scalars else anywhere if n in far else vmem for n in range(len(args))]
    specs += [anywhere] * len(after)
    out_specs = [anywhere if n in apart else vmem for n in range(len(outs))]
    shapes = [pltpu.VMEM(*entry) if isinstance(entry, tuple) else entry for entry in scratch]
    moved = sum(int(np.prod(a.shape)) * a.dtype.itemsize for a in args)
    return pl.pallas_call(
        kernel,
        out_shape=[jax.ShapeDtypeStruct(shape, kind) for shape, kind in outs],
        in_specs=specs,
        out_specs=out_specs,
        scratch_shapes=shapes,
        compiler_params=pltpu.CompilerParams(vmem_limit_bytes=VMEM_LIMIT),
        cost_estimate=pl.CostEstimate(
            flops=work * 10**9, bytes_accessed=moved, transcendentals=0
        ),
    )(*args, *after)


class Order:
    def __init__(self):
        self.last = None

    def hold(self, value):
        if self.last is None:
            return value
        return lax.optimization_barrier((value, self.last))[0]

    def mark(self, value):
        self.last = value
        return value


def turned_column(row):
    return jnp.transpose(jnp.broadcast_to(row, (8, row.shape[1])))[:, :1]


def swap(value, axis, bit):
    size = lax.axis_size(axis)
    return lax.ppermute(value, axis, [(i, i ^ (1 << bit)) for i in range(size)])


def bits_of(axis):
    return (lax.axis_size(axis) - 1).bit_length()


def gather_lanes(value):
    held = {0: value}
    for bit in reversed(range(bits_of("edge"))):
        held.update({k | (1 << bit): swap(v, "edge", bit) for k, v in list(held.items())})
    return [held[k] for k in range(len(held))]


def own_bit(axis, bit):
    return (lax.axis_index(axis) >> bit) & 1


def sum_all(kept, sent, first, order):
    steps = [("edge", n) for n in range(1, bits_of("edge"))]
    steps += [("graph", n) for n in range(bits_of("graph"))]
    steps.sort(key=lambda step: step[0] != first)
    other = swap(sent, "edge", 0)
    yield
    current = kept + order.hold(other)
    for axis, bit in steps:
        mine = own_bit(axis, bit)
        parts = current.reshape(2, current.shape[0] // 2, -1)
        sent = order.mark(lax.dynamic_index_in_dim(parts, 1 - mine, 0, False))
        other = swap(sent, axis, bit)
        yield
        current = lax.dynamic_index_in_dim(parts, mine, 0, False) + order.hold(other)
    current = order.mark(current.astype(bf16))
    for axis, bit in reversed(steps):
        mine = own_bit(axis, bit)
        other = swap(current, axis, bit)
        yield
        other = order.hold(other)
        current = order.mark(
            jnp.concatenate(
                [jnp.where(mine == 0, current, other), jnp.where(mine == 0, other, current)],
                axis=0,
            )
        )
    other = swap(current, "edge", 0)
    yield
    return current, other


def finish_steps(chain):
    while True:
        try:
            next(chain)
        except StopIteration as end:
            return end.value


def shards(
    atom_embed, out_cotangent, send_rows, recv_rows, source_slot, target_slot, rotation,
    edge_feats, edge_bias, conv_zero, conv_one, conv_two, alpha_in, alpha_edge, alpha_dot,
    out_proj,
):
    peers = lax.axis_size("graph")
    lanes_total = lax.axis_size("edge")
    atoms = atom_embed.shape[0]
    edges = rotation.shape[0]
    cap = send_rows.shape[3]
    slots = peers * cap
    blocks = peers * lanes_total
    direct = is_direct(peers)
    order = Order()

    def exchange(value):
        return lax.all_to_all(value, "graph", split_axis=0, concat_axis=0, tiled=True)

    cot = jnp.transpose(out_cotangent, (1, 0, 2))
    outgoing = call(
        outgoing_kernel, [((cap, TABLE), bf16)] * peers, [],
        send_rows, recv_rows, jnp.transpose(atom_embed, (1, 0, 2)), cot,
        scalars=2, work=2,
    )
    if direct:
        tables = [outgoing[0]] + [
            lax.ppermute(outgoing[k], "graph", [(i, i ^ k) for i in range(peers)])
            for k in range(1, peers)
        ]
    else:
        tables = list(exchange(jnp.stack(outgoing)))

    source_row = source_slot.reshape(1, edges)
    target_row = target_slot.reshape(1, edges)
    bias = edge_bias.T
    adot = alpha_dot.reshape(1, -1)

    frames = [
        ((DIM0, edges), bf16),
        ((DIM1, 2 * edges), bf16),
        ((DIM2, 2 * edges), bf16),
        ((DIM0, edges), f32),
        ((DIM1, 2 * edges), f32),
        ((DIM2, 2 * edges), f32),
    ]
    pre_shape = ((HEADS * ALPHA, edges), f32)
    sums, stats, x0, x1, x2, v0, v1, v2, pre, logits, lists, agg_grad, rot, own_stats = call(
        make_forward(atoms, peers),
        [((peers, cap, WIDE), f32), ((slots // 8, LANES), f32)]
        + frames
        + [
            pre_shape,
            ((8, edges), f32),
            ((slots, LANES), f32),
            ((slots, FLAT), f32),
            ((rotation.shape[1], edges), f32),
            ((slots, LANES), f32),
        ],
        [
            ((slots, TABLE), f32),
            ((FLAT, edges), f32),
            ((8, edges), f32),
            ((COLS, 2 * edges), bf16),
            (conv_zero.shape, bf16),
            (conv_one.shape, bf16),
            (conv_two.shape, bf16),
        ]
        + frames
        + [pre_shape, pltpu.SemaphoreType.DMA((10,))],
        source_row, target_row, rotation, edge_feats, bias,
        conv_zero, conv_one, conv_two, alpha_in, alpha_edge, adot, out_proj, *tables,
        far=(5, 6, 7), apart=range(2, 9), work=8,
    )
    if direct:
        lanes_stats = [stats] + [
            lax.ppermute(stats, "edge", [(i, i ^ k) for i in range(lanes_total)])
            for k in range(1, lanes_total)
        ]
        graph_stats = jnp.concatenate(lanes_stats, axis=0)
        all_stats = [graph_stats] + [
            lax.ppermute(graph_stats, "graph", [(i, i ^ k) for i in range(peers)])
            for k in range(1, peers)
        ]
    else:
        all_stats = [lax.all_gather(stats, ("graph", "edge"), tiled=True)]
    messages = exchange(sums)

    halves = [((size, LANES), f32) for start, size in CHUNKS for _ in range(2)]
    g0, g1, g2, pre_grad, *halves = call(
        make_gradient(peers, len(all_stats)),
        [
            ((DIM0, edges), bf16),
            ((DIM1, 2 * edges), bf16),
            ((DIM2, 2 * edges), bf16),
            ((HEADS * ALPHA, edges), bf16),
        ]
        + halves,
        [
            ((slots, FLAT), bf16),
            ((FLAT, edges), f32),
            ((8, edges), f32),
            ((2 * DIM1, 2 * edges), bf16),
            ((2 * DIM2, 2 * edges), bf16),
            ((2, PACKED_ROWS, LANES), f32),
        ]
        + frames
        + [pltpu.SemaphoreType.DMA((10,))],
        *all_stats, own_stats, agg_grad, target_row, rot, edge_feats,
        x0, x1, x2, v0, v1, v2, pre, logits, adot,
        far=range(len(all_stats) + 5, len(all_stats) + 11), apart=range(4, 8), work=8,
    )

    total = lanes_total * slots
    order.mark(halves[0])
    message_rows = gather_lanes(order.hold(messages))
    zero_steps = sum_all(halves[2], halves[3], "graph", order)
    rest_steps = sum_all(halves[0], halves[1], "edge", order)
    next(zero_steps)
    next(rest_steps)
    next(zero_steps)
    next(rest_steps)
    (source_sums,) = call(
        source_kernel,
        [((peers, cap, WIDE), f32)],
        [
            ((DIM0, edges), f32),
            ((DIM1, 2 * edges), f32),
            ((DIM2, 2 * edges), f32),
            ((COLS, 2 * edges), bf16),
        ],
        source_row, lists, rot, g0, g1, g2, order.hold(pre_grad),
        conv_zero, conv_one, conv_two, alpha_in,
        work=6,
    )
    order.mark(source_sums)
    returned = exchange(source_sums)
    next(zero_steps)
    out, proj = call(
        make_finish(lanes_total),
        [((COEFFS, atoms, CH), bf16), (((LMAX // 2 + 1) * CH, LANES), f32)],
        [((total, WIDE), f32), ((2 * total, COLS), bf16), ((COEFFS, atoms, CH), bf16)],
        order.hold(cot), out_proj, *message_rows,
    )
    order.mark(proj)
    next(rest_steps)
    next(zero_steps)
    source_rows = gather_lanes(order.hold(returned))
    next(zero_steps)
    next(rest_steps)
    next(zero_steps)
    (embed,) = call(
        make_collect(lanes_total),
        [((COEFFS, atoms, CH), bf16)],
        [((total, WIDE), f32)],
        order.hold(source_rows[0]), *source_rows[1:],
    )
    order.mark(embed)
    next(rest_steps)
    next(zero_steps)
    for bit in range(bits_of("graph")):
        proj = proj + order.hold(swap(proj, "graph", bit))
        order.mark(proj)
        next(rest_steps)
    zero_pair = finish_steps(zero_steps)
    (zero,) = call(
        unpack_zero_kernel, [((DIM0, DIM0), bf16)], [], order.hold(zero_pair[0]), zero_pair[1],
        work=1,
    )
    order.mark(zero)
    rest_pair = finish_steps(rest_steps)
    one, two, grad_in, grad_edge, grad_dot = call(
        unpack_rest_kernel,
        [
            ((2, DIM1, DIM1), bf16),
            ((2, DIM2, DIM2), bf16),
            (alpha_in.shape, bf16),
            (alpha_edge.shape, bf16),
            ((2, LANES), bf16),
        ],
        [], order.hold(rest_pair[0]), rest_pair[1], work=1,
    )

    def shaped(value):
        return jnp.transpose(value, (1, 0, 2))

    return (
        shaped(out), shaped(embed), zero, one, two, grad_in, grad_edge, grad_dot.reshape(-1),
        jnp.swapaxes(proj.astype(bf16).reshape(-1, CH, 2, CH), 1, 2).reshape(-1, CH, CH)[: LMAX + 1],
    )


def solution(mesh):
    in_specs = (
        P(("groups", "graph"), None, None),
        P(("groups", "graph"), None, None),
        P(("groups", "graph"), None, "edge", None),
        P(("groups", "graph"), None, "edge", None),
        P(("groups", "graph", "edge")),
        P(("groups", "graph", "edge")),
        P(("groups", "graph", "edge"), None),
        P(("groups", "graph", "edge"), None),
        P(("groups", "graph", "edge"), None),
        P(),
        P(),
        P(),
        P(),
        P(),
        P(),
        P(),
    )
    out_specs = (
        P(("groups", "graph"), None, None),
        P(("groups", "graph"), None, None),
        P("groups", None),
        P("groups", None, None),
        P("groups", None, None),
        P("groups", None),
        P("groups", None),
        P("groups"),
        P("groups", None, None),
    )
    return jax.shard_map(shards, mesh=mesh, in_specs=in_specs, out_specs=out_specs, check_vma=False)
```

```python
import jax
import jax.numpy as jnp
import numpy as np
from jax import lax
from jax.experimental import pallas as pl
from jax.experimental.pallas import tpu as pltpu
from jax.sharding import PartitionSpec as P

LMAX = 6
MMAX = 2
CH = 64
HEADS = 4
VAL = 16
ALPHA = 64
COEFFS = (LMAX + 1) * (LMAX + 1)
FLAT = COEFFS * CH
LANES = 128
BLOCKS = (FLAT + LANES - 1) // LANES
COLS = BLOCKS * LANES
WIDE = COLS + LANES
TABLE = 2 * COLS + LANES
PEAK_AT, DOT_AT, NAME_AT = HEADS, 2 * HEADS, 3 * HEADS
STATS = 16
DIM0 = (LMAX + 1) * CH
DIM1 = LMAX * CH
DIM2 = (LMAX - 1) * CH
PANEL = 256

leak_slope = 0.2
floor_value = -1e30
bf16 = jnp.bfloat16
f32 = jnp.float32

VMEM_LIMIT = 56 * 1024 * 1024


def degree_blocks():
    result = []
    offset = 0
    for degree in range(LMAX + 1):
        centre = min(degree, MMAX)
        row_total = 2 * centre + 1
        col_total = 2 * degree + 1
        result.append((degree, centre, row_total, col_total, offset))
        offset += row_total * col_total
    return result


def degree_of(coeff):
    return int(np.sqrt(coeff))


def dot_nn(left, right):
    return jnp.dot(left, right, preferred_element_type=f32)


def dot_nt(left, right):
    return lax.dot_general(left, right, (((1,), (1,)), ((), ())), preferred_element_type=f32)


def dot_tn(left, right):
    return lax.dot_general(left, right, (((0,), (0,)), ((), ())), preferred_element_type=f32)


def iota(shape, dim):
    return lax.broadcasted_iota(jnp.int32, shape, dim)


def split_two(value):
    high = value.astype(bf16)
    return high, (value - high.astype(f32)).astype(bf16)


def to_frame(source, rot, edges, emit):
    for half in range(edges // LANES):
        lanes = pl.ds(half * LANES, LANES)
        for degree, centre, row_total, col_total, offset in degree_blocks():
            sums = [None] * row_total
            for j in range(col_total):
                column = source[pl.ds((degree * degree + j) * CH, CH), lanes]
                for i in range(row_total):
                    term = rot[pl.ds(offset + i * col_total + j, 1), lanes] * column
                    sums[i] = term if j == 0 else sums[i] + term
            for i in range(row_total):
                emit(degree, i - centre, half, sums[i])


def from_frame(load, rot, edges, emit):
    for half in range(edges // LANES):
        lanes = pl.ds(half * LANES, LANES)
        for degree, centre, row_total, col_total, offset in degree_blocks():
            rows = [load(degree, i - centre, half) for i in range(row_total)]
            for j in range(col_total):
                total = None
                for i in range(row_total):
                    term = rot[pl.ds(offset + i * col_total + j, 1), lanes] * rows[i]
                    total = term if i == 0 else total + term
                emit(degree * degree + j, half, total)


def lane_at(half, edges, second):
    return pl.ds(half * LANES + (edges if second else 0), LANES)


def frame_place(degree, order, refs):
    if order == 0:
        return refs[0], degree * CH, False
    which = abs(order)
    return refs[which], (degree - which) * CH, order < 0


def spread_heads(rows):
    return jnp.concatenate(
        [jnp.broadcast_to(row, (VAL, row.shape[1])) for row in rows], axis=0
    )


def is_direct(peers):
    return peers <= 4


def flip_of(peers):
    return lax.axis_index("graph") if is_direct(peers) else 0


def one_hot_rows(slot_ref, peers, slots):
    edges = slot_ref.shape[1]
    first = flip_of(peers) * (slots // peers)
    return jnp.bitwise_xor(iota((slots, edges), 0), first) == slot_ref[...]


def mask_to(mask, dtype):
    return jnp.where(mask, 1.0, 0.0).astype(dtype)


def stack_table(tables, rows_ref):
    cap = tables[0].shape[0]
    per = 8 // cap
    for n in range(0, len(tables), per):
        parts = [table[...].astype(f32) for table in tables[n : n + per]]
        rows_ref[pl.ds(n * cap, 8), :] = jnp.concatenate(parts, axis=0)


def put_rows(out_ref, cols, value):
    peers, cap = out_ref.shape[0], out_ref.shape[1]
    flip = flip_of(peers)
    for n in range(peers):
        place = jnp.bitwise_xor(flip, n) if is_direct(peers) else n
        out_ref[place, :, cols] = value[n * cap : (n + 1) * cap].astype(out_ref.dtype)


def slot_sums(terms, one_hot, out_ref, factor=None):
    both = jnp.concatenate([one_hot, one_hot], axis=1)
    products = 0.0
    for start in range(0, COLS, PANEL):
        size = min(PANEL, COLS - start)
        sums = dot_nt(both, terms[pl.ds(start, size), :])
        put_rows(out_ref, pl.ds(start, size), sums)
        if factor is None:
            continue
        for at in range(0, size, LANES):
            width = min(LANES, FLAT - start - at)
            product = sums[:, at : at + width] * factor[:, pl.ds(start + at, width)]
            if width < LANES:
                product = jnp.concatenate([product, jnp.zeros_like(product)], axis=1)
            products = products + product
    return products


def store_terms(terms, edges):
    def emit(coeff, half, value):
        high, low = split_two(value)
        rows = pl.ds(coeff * CH, CH)
        terms[rows, lane_at(half, edges, False)] = high
        terms[rows, lane_at(half, edges, True)] = low

    return emit


def listed_rows(list_ref, shape):
    peers, cap = list_ref.shape[1], list_ref.shape[3]
    flip = flip_of(peers)
    row = iota(shape, 0)
    result = jnp.zeros(shape, jnp.int32)
    for slot in range(peers * cap):
        owner = jnp.bitwise_xor(flip, slot // cap) if is_direct(peers) else slot // cap
        result = jnp.where(row == slot, list_ref[0, owner, 0, slot % cap], result)
    return result


def put_coeffs(outs, first, coeff_rows):
    for block in range(BLOCKS):
        left = coeff_rows(2 * block)
        right = coeff_rows(2 * block + 1) if 2 * block + 1 < COEFFS else jnp.zeros_like(left)
        put_pieces(outs, first + block * LANES, jnp.concatenate([left, right], axis=1))


def put_pieces(outs, first, value):
    cap = outs[0].shape[0]
    for n, out in enumerate(outs):
        out[:, pl.ds(first, LANES)] = value[n * cap : (n + 1) * cap].astype(out.dtype)


def outgoing_kernel(send, recv, embed, cot, *outs):
    atoms = embed.shape[1]
    slots = send.shape[1] * send.shape[3]
    sent = listed_rows(send, (slots, LANES))
    received = listed_rows(recv, (slots, LANES))
    for first, listed, values in ((0, sent, embed), (COLS, received, cot)):
        picked = mask_to(iota((slots, atoms), 1) == listed[:, :atoms], bf16)
        put_coeffs(outs, first, lambda k: dot_nn(picked, values[k]))
    lane = iota((slots, LANES), 1)
    side = jnp.where(lane == 0, received, jnp.where(lane == 1, sent, 0))
    put_pieces(outs, 2 * COLS, side.astype(f32))


def swapped_halves(value, edges):
    return jnp.concatenate([-value[:, edges:], value[:, :edges]], axis=1)


def make_forward(atoms, peers):
    def forward_kernel(
        source_slot, target_slot, rotation, feats, bias, wzero_at, wone_at, wtwo_at,
        ain, aedge, adot, out_proj, *rest,
    ):
        tables, rest = rest[:peers], rest[peers:]
        (
        sums_out, stats_out, x0_at, x1_at, x2_at, v0_at, v1_at, v2_at, pre_at, logit_out,
        lists_out, agg_grad, rot, own_out,
        rows, gathered, weights, terms, wzero, wone, wtwo, x0, x1, x2, v0, v1, v2, pre_out,
        semaphores,
        ) = rest
        copies = []

        def move(source, target):
            copy = pltpu.make_async_copy(source, target, semaphores.at[len(copies)])
            copy.start()
            copies.append(copy)

        move(wzero_at, wzero)
        move(wone_at, wone)
        move(wtwo_at, wtwo)
        rot[...] = jnp.transpose(rotation[...].astype(f32))
        edges = source_slot.shape[1]
        cap = tables[0].shape[0]
        slots = peers * cap
        stack_table(tables, rows)
        picked = mask_to(one_hot_rows(source_slot, peers, slots), bf16)
        for degree in range(LMAX + 1):
            ids = pl.ds(degree * degree * CH, (2 * degree + 1) * CH)
            gathered[ids, :] = dot_tn(rows[:, ids].astype(bf16), picked)
        lists = rows[:, pl.ds(2 * COLS, LANES)]
        lists_out[...] = lists
        for degree in range(LMAX + 1):
            ids = range(degree * degree, (degree + 1) * (degree + 1))
            cot = jnp.concatenate([rows[:, pl.ds(COLS + k * CH, CH)] for k in ids], axis=0)
            grad = dot_nt(cot.astype(bf16), out_proj[degree])
            for n, k in enumerate(ids):
                agg_grad[:, pl.ds(k * CH, CH)] = grad[n * slots : (n + 1) * slots]

        def emit(degree, order, half, value):
            ref, row, second = frame_place(degree, order, (x0, x1, x2))
            ref[pl.ds(row, CH), lane_at(half, edges, second)] = value.astype(bf16)

        to_frame(gathered, rot, edges, emit)
        for source, target in ((x0, x0_at), (x1, x1_at), (x2, x2_at)):
            move(source, target)

        pre = dot_tn(ain[...], x0[pl.ds(0, CH), :]) + lax.dot_general(
            aedge[...], feats[...], (((0,), (1,)), ((), ())), preferred_element_type=f32
        )
        pre_out[...] = pre
        move(pre_out, pre_at)
        hidden = jnp.where(pre > 0, pre, leak_slope * pre) * turned_column(adot[...].astype(f32))
        aims = one_hot_rows(target_slot, peers, slots)
        lane = iota((slots, LANES), 1)
        peer = jnp.bitwise_xor(iota((slots, 1), 0) // cap, flip_of(peers))
        name = lists[:, :1] + (peer * atoms).astype(f32)
        side = jnp.where(lane == NAME_AT, name, 0.0)
        for h in range(HEADS):
            logit = jnp.sum(hidden[h * ALPHA : (h + 1) * ALPHA], axis=0, keepdims=True)
            logit = logit + bias[pl.ds(h, 1), :]
            logit_out[pl.ds(h, 1), :] = logit
            peak = jnp.max(jnp.where(aims, logit, floor_value), axis=1, keepdims=True)
            of_edge = jnp.sum(jnp.where(aims, peak, 0.0), axis=0, keepdims=True)
            weight = jnp.exp(logit - of_edge)
            weights[pl.ds(h, 1), :] = weight
            den = jnp.sum(jnp.where(aims, weight, 0.0), axis=1, keepdims=True)
            side = jnp.where(lane == h, den, jnp.where(lane == PEAK_AT + h, peak, side))

        for copy in copies[:3]:
            copy.wait()
        v0[...] = dot_tn(wzero[...], x0[...])
        for out, weight, value in ((v1, wone, x1[...]), (v2, wtwo, x2[...])):
            out[...] = dot_tn(weight[0], value) + swapped_halves(dot_tn(weight[1], value), edges)
        for source, target in ((v0, v0_at), (v1, v1_at), (v2, v2_at)):
            move(source, target)

        def load(degree, order, half):
            ref, row, second = frame_place(degree, order, (v0, v1, v2))
            return ref[pl.ds(row, CH), lane_at(half, edges, second)]

        store = store_terms(terms, edges)

        def weigh(coeff, half, value):
            lanes = lane_at(half, edges, False)
            spread = spread_heads([weights[pl.ds(h, 1), lanes] for h in range(HEADS)])
            store(coeff, half, value * spread)

        terms[pl.ds(FLAT, COLS - FLAT), :] = jnp.zeros((COLS - FLAT, 2 * edges), bf16)
        from_frame(load, rot, edges, weigh)
        dots = slot_sums(terms, mask_to(aims, bf16), sums_out, agg_grad)
        head = (lane % CH) // VAL
        for h in range(HEADS):
            dot = jnp.sum(jnp.where(head == h, dots, 0.0), axis=1, keepdims=True)
            side = jnp.where(lane == DOT_AT + h, dot, side)
        put_rows(sums_out, pl.ds(COLS, LANES), side)
        own_out[...] = side
        spread = jnp.concatenate([side[:, :STATS]] * (LANES // STATS), axis=1)
        spread = jnp.where(lane // STATS == iota((slots, LANES), 0) % 8, spread, 0.0)
        packed = jnp.sum(spread.reshape(slots // 8, 8, LANES), axis=1)

        stats_out[...] = packed
        for copy in copies[3:]:
            copy.wait()

    return forward_kernel


def lane_heads(values, shape):
    head = (iota(shape, 1) % CH) // VAL
    result = jnp.broadcast_to(values[0], shape)
    for h in range(1, HEADS):
        result = jnp.where(head == h, values[h], result)
    return result


def collect_rows(arrivals, rows_ref):
    own = lax.axis_index("edge")
    for k, arrival in enumerate(arrivals):
        peers, cap, width = arrival.shape
        base = (own ^ k) * (peers * cap)
        for start in range(0, peers * cap, 8):
            parts = [arrival[g] for g in range(start // cap, (start + 8) // cap)]
            at = pl.ds(pl.multiple_of(base + start, 8), 8)
            rows_ref[at, :] = jnp.concatenate(parts, axis=0)


def block_cols(block):
    return pl.ds(block * LANES, min(LANES, FLAT - block * LANES))


def make_finish(lanes_total):
    def finish_kernel(cot, out_proj, *rest):
        arrivals = rest[:lanes_total]
        out, proj, rows, terms, agg_low = rest[lanes_total:]
        atoms = cot.shape[1]
        total = rows.shape[0]
        collect_rows(arrivals, rows)
        side = rows[:, pl.ds(COLS, LANES)]
        owner = (lax.axis_index("graph") * atoms).astype(f32)
        names = iota((total, atoms), 1).astype(f32) + owner == side[:, NAME_AT : NAME_AT + 1]
        eye = iota((atoms, atoms), 0) == iota((atoms, atoms), 1)
        scales, dens = [], []
        for h in range(HEADS):
            peak_rows = side[:, PEAK_AT + h : PEAK_AT + h + 1]
            peak = jnp.max(jnp.where(names, peak_rows, floor_value), axis=0, keepdims=True)
            of_row = jnp.sum(jnp.where(names, peak, 0.0), axis=1, keepdims=True)
            scale = jnp.exp(peak_rows - of_row)
            scaled_den = side[:, h : h + 1] * scale
            den = jnp.sum(jnp.where(names, scaled_den, 0.0), axis=0, keepdims=True)
            scales.append(scale)
            dens.append(jnp.sum(jnp.where(eye, den, 0.0), axis=1, keepdims=True))
        scale_full = lane_heads(scales, (total, LANES))
        den_full = lane_heads(dens, (atoms, LANES))
        picked = mask_to(names, bf16)
        twice = jnp.concatenate([picked, picked], axis=0)
        for block in range(BLOCKS):
            cols = pl.ds(block * LANES, LANES)
            high, low = split_two(rows[:, cols] * scale_full)
            terms[pl.ds(0, total), cols] = high
            terms[pl.ds(total, total), cols] = low
        for block in range(BLOCKS):
            cols = pl.ds(block * LANES, LANES)
            agg = (dot_tn(twice, terms[:, cols]) / den_full).astype(bf16)
            agg_low[2 * block] = agg[:, :CH]
            if 2 * block + 1 < COEFFS:
                agg_low[2 * block + 1] = agg[:, CH:]
        for degree in range(LMAX + 1):
            ids = pl.ds(degree * degree, 2 * degree + 1)
            stacked = ((2 * degree + 1) * atoms, CH)
            left = agg_low[ids].reshape(stacked)
            right = cot[ids].reshape(stacked)
            value = dot_nn(left, out_proj[degree]).astype(bf16)
            out[ids] = value.reshape((2 * degree + 1, atoms, CH))
            at = (pl.ds(degree // 2 * CH, CH), pl.ds(degree % 2 * CH, CH))
            proj[at] = dot_tn(left, right)
        proj[pl.ds(LMAX // 2 * CH, CH), pl.ds(CH, CH)] = jnp.zeros((CH, CH), f32)

    return finish_kernel


def combine_stats(stats, own):
    chunk = 32
    name = own[:, NAME_AT : NAME_AT + 1]

    def part(part_rows):
        entries = [part_rows[:, n : n + STATS] for n in range(0, LANES, STATS)]
        turned = jnp.transpose(jnp.concatenate(entries, axis=0))
        same = name == turned[NAME_AT : NAME_AT + 1]
        result = []
        for h in range(HEADS):
            peaks = turned[PEAK_AT + h : PEAK_AT + h + 1]
            peak = jnp.max(jnp.where(same, peaks, floor_value), axis=1, keepdims=True)
            scale = jnp.where(same, jnp.exp(jnp.where(same, peaks - peak, 0.0)), 0.0)
            den = jnp.sum(turned[h : h + 1] * scale, axis=1, keepdims=True)
            dot = jnp.sum(turned[DOT_AT + h : DOT_AT + h + 1] * scale, axis=1, keepdims=True)
            result += [peak, den, dot]
        return tuple(result)

    def step(at, held):
        fresh = part(stats[0][pl.ds(pl.multiple_of(at * chunk, chunk), chunk), :])
        result = []
        for h in range(HEADS):
            peak, den, dot = held[3 * h : 3 * h + 3]
            new_peak, new_den, new_dot = fresh[3 * h : 3 * h + 3]
            most = jnp.maximum(peak, new_peak)
            old, new = jnp.exp(peak - most), jnp.exp(new_peak - most)
            result += [most, den * old + new_den * new, dot * old + new_dot * new]
        return tuple(result)

    if len(stats) > 1:
        held = part(jnp.concatenate([rows[...] for rows in stats], axis=0))
    else:
        held = part(stats[0][pl.ds(0, chunk), :])
        held = lax.fori_loop(1, stats[0].shape[0] // chunk, step, held)
    return [held[3 * h : 3 * h + 3] for h in range(HEADS)]


def make_gradient(peers, parts):
    def kernel(*refs):
        gradient_kernel(peers, refs[:parts], *refs[parts:])

    return kernel


def gradient_kernel(
    peers, stats, own, agg_grad, target_slot, rot, feats,
    x0_at, x1_at, x2_at, v0_at, v1_at, v2_at, pre, logits, adot,
    g0, top1, top2, pre_grad_out, kept0, sent0, kept1, sent1,
    num_grad, spread_grad, weights, g1, g2, packed, x0, x1, x2, v0, v1, v2, semaphores,
):
    loads = []
    for source, target in (
        (v0_at, v0), (v1_at, v1), (v2_at, v2), (x0_at, x0), (x1_at, x1), (x2_at, x2)
    ):
        load = pltpu.make_async_copy(source, target, semaphores.at[4 + len(loads)])
        load.start()
        loads.append(load)
    edges = target_slot.shape[1]
    slots = agg_grad.shape[0]
    aims = one_hot_rows(target_slot, peers, slots)
    combined = combine_stats(stats, own[...])
    den_grads = []
    for h, (peak, den, dot) in enumerate(combined):
        of_edge = jnp.sum(jnp.where(aims, peak, 0.0), axis=0, keepdims=True)
        weights[pl.ds(h, 1), :] = jnp.exp(logits[pl.ds(h, 1), :] - of_edge)
        den_grad = (-(dot / den) / den).astype(bf16).astype(f32)
        den_grads.append(jnp.sum(jnp.where(aims, den_grad, 0.0), axis=0, keepdims=True))
    den_full = lane_heads([den for peak, den, dot in combined], (slots, LANES))
    for block in range(BLOCKS):
        cols = block_cols(block)
        num_grad[:, cols] = (agg_grad[:, cols] / den_full[:, : cols.size]).astype(bf16)
    picked = mask_to(aims, bf16)
    for degree in range(LMAX + 1):
        ids = pl.ds(degree * degree * CH, (2 * degree + 1) * CH)
        spread_grad[ids, :] = dot_tn(num_grad[:, ids], picked)

    state = {}

    def emit(degree, order, half, value):
        lanes = lane_at(half, edges, False)
        ref, row, second = frame_place(degree, order, (v0, v1, v2))
        product = value * ref[pl.ds(row, CH), lane_at(half, edges, second)]
        if degree == 0:
            state["sum"] = product
            state["spread"] = spread_heads([weights[pl.ds(h, 1), lanes] for h in range(HEADS)])
        else:
            state["sum"] = state["sum"] + product
        grad = (value * state["spread"]).astype(bf16)
        ref, row, second = frame_place(degree, order, (g0, g1, g2))
        ref[pl.ds(row, CH), lane_at(half, edges, second)] = grad
        if order != 0:
            swapped = grad if order < 0 else -grad
            below = row + (DIM1 if abs(order) == 1 else DIM2)
            ref[pl.ds(below, CH), lane_at(half, edges, not second)] = swapped
        if degree == LMAX and order == MMAX:
            for h in range(HEADS):
                part = state["sum"][h * VAL : (h + 1) * VAL]
                weights[pl.ds(HEADS + h, 1), lanes] = jnp.sum(part, axis=0, keepdims=True)

    for load in loads:
        load.wait()
    to_frame(spread_grad, rot, edges, emit)

    hidden = jnp.where(pre[...] > 0, pre[...], leak_slope * pre[...])
    logit_grads = [
        weights[pl.ds(h, 1), :] * (weights[pl.ds(HEADS + h, 1), :] + den_grads[h])
        for h in range(HEADS)
    ]
    tall = jnp.concatenate(
        [jnp.broadcast_to(row, (ALPHA, edges)) for row in logit_grads], axis=0
    )
    slope = jnp.where(pre[...] > 0, 1.0, leak_slope)
    pre_grad = (tall * turned_column(adot[...].astype(f32)) * slope).astype(bf16)
    pre_grad_out[...] = pre_grad
    dot_grad = jnp.sum(tall * hidden, axis=1, keepdims=True)

    top1[...] = g1[pl.ds(0, DIM1), :]
    top2[...] = g2[pl.ds(0, DIM2), :]
    mine = lax.axis_index("edge") & 1
    copies = []

    def put(row, value, at=0):
        for side in range(2):
            low, high = max(at, side * LANES), min(at + value.shape[1], (side + 1) * LANES)
            if low < high:
                piece = value[:, low - at : high - at]
                cols = pl.ds(low - side * LANES, high - low)
                packed[side, pl.ds(row, value.shape[0]), cols] = piece

    def send(chunk, kept, sent):
        start, size = CHUNKS[chunk]
        rows_of = pl.ds(start, size)
        for n, (side, out) in enumerate(((mine, kept), (1 - mine, sent))):
            copy = pltpu.make_async_copy(
                packed.at[side, rows_of, :], out, semaphores.at[2 * chunk + n]
            )
            copy.start()
            copies.append(copy)

    row = 0
    for left, right, dim in ((x1, g1, DIM1), (x2, g2, DIM2)):
        for start in range(0, 2 * dim, PANEL):
            size = min(PANEL, 2 * dim - start)
            put(row, dot_nt(left[...], right[pl.ds(start, size), :]))
            row += dim
    row -= DIM2
    edge_ch = feats.shape[1]
    edge_grad = lax.dot_general(
        feats[...], pre_grad, (((0,), (1,)), ((), ())), preferred_element_type=f32
    )
    put(row, edge_grad[:, :LANES], LANES)
    put(row + edge_ch, edge_grad[:, LANES:], LANES)
    wide_dot = jnp.transpose(jnp.broadcast_to(dot_grad, (HEADS * ALPHA, LANES)))
    spare = DIM2 - 2 * edge_ch
    tail = iota((spare, LANES), 0)
    first = jnp.broadcast_to(wide_dot[:1, :LANES], (spare, LANES))
    second = jnp.broadcast_to(wide_dot[:1, LANES:], (spare, LANES))
    put(row + 2 * edge_ch, jnp.where(tail == 0, first, jnp.where(tail == 1, second, 0.0)), LANES)
    row += DIM2
    put(row, dot_nt(x0[pl.ds(0, CH), :], pre_grad))
    send(0, kept0, sent0)

    row = CHUNKS[1][0]
    for start in range(0, DIM0, PANEL):
        size = min(PANEL, DIM0 - start)
        put(row, dot_nt(x0[...], g0[pl.ds(start, size), :]))
        if size < PANEL:
            put(row, jnp.zeros((DIM0, PANEL - size), f32), size)
        row += DIM0
    send(1, kept1, sent1)
    for copy in copies:
        copy.wait()


PROJ_ROWS = (LMAX // 2 + 1) * CH
CHUNKS = ((0, 3 * DIM1 + 3 * DIM2 + CH), (3 * DIM1 + 3 * DIM2 + CH, 2 * DIM0))
PACKED_ROWS = sum(size for start, size in CHUNKS)


def halves_of(mine, other):
    first = (lax.axis_index("edge") & 1) == 0
    left, right = mine[...].astype(f32), other[...].astype(f32)
    return jnp.where(first, left, right), jnp.where(first, right, left)


def unpack_zero_kernel(mine, other, zero):
    left, right = halves_of(mine, other)
    zero[:, pl.ds(0, LANES)] = left[:DIM0].astype(bf16)
    zero[:, pl.ds(LANES, LANES)] = right[:DIM0].astype(bf16)
    zero[:, pl.ds(2 * LANES, LANES)] = left[DIM0:].astype(bf16)
    zero[:, pl.ds(3 * LANES, DIM0 - 3 * LANES)] = right[DIM0:, : DIM0 - 3 * LANES].astype(bf16)


def make_unpack_rest(lanes_total):
    def unpack_rest_kernel(mine, other, one, two, alpha_in, alpha_edge, alpha_dot, proj):
        left, right = halves_of(mine, other)
        parts = lanes_total // 2
        late = PROJ_ROWS // lanes_total
        size = left.shape[0] // parts - late
        tail = jnp.concatenate(
            [
                value[n * (size + late) + size : (n + 1) * (size + late)]
                for value in (left, right)
                for n in range(parts)
            ],
            axis=0,
        )
        for degree in range(LMAX + 1):
            piece = tail[degree // 2 * CH : (degree // 2 + 1) * CH]
            proj[degree] = piece[:, degree % 2 * CH : (degree % 2 + 1) * CH].astype(bf16)
        left, right = (
            jnp.concatenate(
                [value[n * (size + late) : n * (size + late) + size] for n in range(parts)], axis=0
            )
            for value in (left, right)
        )
        unpack_rest(left, right, one, two, alpha_in, alpha_edge, alpha_dot)

    return unpack_rest_kernel


def unpack_rest(left, right, one, two, alpha_in, alpha_edge, alpha_dot):
    for n in range(2 * DIM1 // LANES):
        panel = (left, right)[n % 2][(n // 2) * DIM1 : (n // 2 + 1) * DIM1]
        per = DIM1 // LANES
        one[n // per, :, pl.ds((n % per) * LANES, LANES)] = panel.astype(bf16)
    left, right = left[3 * DIM1 :], right[3 * DIM1 :]
    panels = [(left, right)[n % 2][(n // 2) * DIM2 : (n // 2 + 1) * DIM2] for n in range(5)]
    whole = jnp.concatenate(panels, axis=1)
    two[0] = whole[:, :DIM2].astype(bf16)
    two[1] = whole[:, DIM2:].astype(bf16)
    edge_ch = alpha_edge.shape[0]
    rest = right[2 * DIM2 : 3 * DIM2]
    alpha_edge[:, pl.ds(0, LANES)] = rest[:edge_ch].astype(bf16)
    alpha_edge[:, pl.ds(LANES, LANES)] = rest[edge_ch : 2 * edge_ch].astype(bf16)
    alpha_dot[...] = rest[2 * edge_ch : 2 * edge_ch + 2].astype(bf16)
    alpha_in[:, pl.ds(0, LANES)] = left[3 * DIM2 :].astype(bf16)
    alpha_in[:, pl.ds(LANES, LANES)] = right[3 * DIM2 :].astype(bf16)


def source_kernel(
    source_slot, lists, rot, g0, g1, g2, pre_grad, wzero, wone, wtwo, ain,
    *rest,
):
    sums_out, d0, d1, d2, terms = rest[-5:]
    edges = source_slot.shape[1]
    slots = sums_out.shape[0] * sums_out.shape[1]
    d0[...] = dot_nn(wzero[...], g0[...])
    d0[pl.ds(0, CH), :] += dot_nn(ain[...], pre_grad[...])
    for out, weight, value in ((d1, wone, g1[...]), (d2, wtwo, g2[...])):
        out[...] = dot_nn(weight[0], value) - swapped_halves(dot_nn(weight[1], value), edges)

    def load(degree, order, half):
        ref, row, second = frame_place(degree, order, (d0, d1, d2))
        return ref[pl.ds(row, CH), lane_at(half, edges, second)]

    terms[pl.ds(FLAT, COLS - FLAT), :] = jnp.zeros((COLS - FLAT, 2 * edges), bf16)
    from_frame(load, rot, edges, store_terms(terms, edges))
    slot_sums(terms, mask_to(one_hot_rows(source_slot, sums_out.shape[0], slots), bf16), sums_out)
    put_rows(sums_out, pl.ds(COLS, LANES), lists[...])


def make_collect(lanes_total):
    def collect_kernel(*rest):
        arrivals = rest[:lanes_total]
        out, rows = rest[lanes_total:]
        atoms = out.shape[1]
        total = rows.shape[0]
        collect_rows(arrivals, rows)
        index = rows[:, pl.ds(COLS, LANES)][:, 1:2]
        picked = mask_to(iota((total, atoms), 1).astype(f32) == index, bf16)
        twice = jnp.concatenate([picked, picked], axis=0)
        for block in range(BLOCKS):
            high, low = split_two(rows[:, pl.ds(block * LANES, LANES)])
            sums = dot_tn(twice, jnp.concatenate([high, low], axis=0)).astype(bf16)
            out[2 * block] = sums[:, :CH]
            if 2 * block + 1 < COEFFS:
                out[2 * block + 1] = sums[:, CH:]

    return collect_kernel


vmem = pl.BlockSpec(memory_space=pltpu.VMEM)
smem = pl.BlockSpec(memory_space=pltpu.SMEM)
anywhere = pl.BlockSpec(memory_space=pl.ANY)


def call(kernel, outs, scratch, *args, scalars=0, far=(), apart=(), after=()):
    specs = [smem if n < scalars else anywhere if n in far else vmem for n in range(len(args))]
    specs += [anywhere] * len(after)
    out_specs = [anywhere if n in apart else vmem for n in range(len(outs))]
    shapes = [pltpu.VMEM(*entry) if isinstance(entry, tuple) else entry for entry in scratch]
    return pl.pallas_call(
        kernel,
        out_shape=[jax.ShapeDtypeStruct(shape, kind) for shape, kind in outs],
        in_specs=specs,
        out_specs=out_specs,
        scratch_shapes=shapes,
        compiler_params=pltpu.CompilerParams(vmem_limit_bytes=VMEM_LIMIT),
        cost_estimate=pl.CostEstimate(flops=1, bytes_accessed=1, transcendentals=0),
    )(*args, *after)


class Order:
    def __init__(self):
        self.last = None

    def hold(self, value):
        if self.last is None:
            return value
        return lax.optimization_barrier((value, self.last))[0]

    def mark(self, value):
        self.last = value
        return value


def turned_column(row):
    return jnp.transpose(jnp.broadcast_to(row, (8, row.shape[1])))[:, :1]


def swap(value, axis, bit):
    size = lax.axis_size(axis)
    return lax.ppermute(value, axis, [(i, i ^ (1 << bit)) for i in range(size)])


def bits_of(axis):
    return (lax.axis_size(axis) - 1).bit_length()


def gather_lanes(value):
    held = {0: value}
    for bit in reversed(range(bits_of("edge"))):
        held.update({k | (1 << bit): swap(v, "edge", bit) for k, v in list(held.items())})
    return [held[k] for k in range(len(held))]


def own_bit(axis, bit):
    return (lax.axis_index(axis) >> bit) & 1


def sum_all(kept, sent, first, order, late=None):
    steps = [("edge", n) for n in range(1, bits_of("edge"))]
    steps += [("graph", n) for n in range(bits_of("graph"))]
    steps.sort(key=lambda step: step[0] != first)
    other = swap(sent, "edge", 0)
    yield
    current = kept + order.hold(other)
    for n, (axis, bit) in enumerate(steps):
        if late is not None and n == bits_of("edge") - 1:
            current = jnp.concatenate([current, late[0]], axis=0)
        mine = own_bit(axis, bit)
        parts = current.reshape(2, current.shape[0] // 2, -1)
        sent = order.mark(lax.dynamic_index_in_dim(parts, 1 - mine, 0, False))
        other = swap(sent, axis, bit)
        yield
        current = lax.dynamic_index_in_dim(parts, mine, 0, False) + order.hold(other)
    current = order.mark(current.astype(bf16))
    for axis, bit in reversed(steps):
        mine = own_bit(axis, bit)
        other = swap(current, axis, bit)
        yield
        other = order.hold(other)
        current = order.mark(
            jnp.concatenate(
                [jnp.where(mine == 0, current, other), jnp.where(mine == 0, other, current)],
                axis=0,
            )
        )
    other = swap(current, "edge", 0)
    yield
    return current, other


def finish_steps(chain):
    while True:
        try:
            next(chain)
        except StopIteration as end:
            return end.value


def shards(
    atom_embed, out_cotangent, send_rows, recv_rows, source_slot, target_slot, rotation,
    edge_feats, edge_bias, conv_zero, conv_one, conv_two, alpha_in, alpha_edge, alpha_dot,
    out_proj,
):
    peers = lax.axis_size("graph")
    lanes_total = lax.axis_size("edge")
    atoms = atom_embed.shape[0]
    edges = rotation.shape[0]
    cap = send_rows.shape[3]
    slots = peers * cap
    blocks = peers * lanes_total
    direct = is_direct(peers)
    order = Order()

    def exchange(value):
        return lax.all_to_all(value, "graph", split_axis=0, concat_axis=0, tiled=True)

    cot = jnp.transpose(out_cotangent, (1, 0, 2))
    outgoing = call(
        outgoing_kernel, [((cap, TABLE), bf16)] * peers, [],
        send_rows, recv_rows, jnp.transpose(atom_embed, (1, 0, 2)), cot,
        scalars=2
    )
    if direct:
        tables = [outgoing[0]] + [
            lax.ppermute(outgoing[k], "graph", [(i, i ^ k) for i in range(peers)])
            for k in range(1, peers)
        ]
    else:
        tables = list(exchange(jnp.stack(outgoing)))

    source_row = source_slot.reshape(1, edges)
    target_row = target_slot.reshape(1, edges)
    bias = edge_bias.T
    adot = alpha_dot.reshape(1, -1)

    frames = [
        ((DIM0, edges), bf16),
        ((DIM1, 2 * edges), bf16),
        ((DIM2, 2 * edges), bf16),
        ((DIM0, edges), f32),
        ((DIM1, 2 * edges), f32),
        ((DIM2, 2 * edges), f32),
    ]
    pre_shape = ((HEADS * ALPHA, edges), f32)
    sums, stats, x0, x1, x2, v0, v1, v2, pre, logits, lists, agg_grad, rot, own_stats = call(
        make_forward(atoms, peers),
        [((peers, cap, WIDE), f32), ((slots // 8, LANES), f32)]
        + frames
        + [
            pre_shape,
            ((8, edges), f32),
            ((slots, LANES), f32),
            ((slots, FLAT), f32),
            ((rotation.shape[1], edges), f32),
            ((slots, LANES), f32),
        ],
        [
            ((slots, TABLE), f32),
            ((FLAT, edges), f32),
            ((8, edges), f32),
            ((COLS, 2 * edges), bf16),
            (conv_zero.shape, bf16),
            (conv_one.shape, bf16),
            (conv_two.shape, bf16),
        ]
        + frames
        + [pre_shape, pltpu.SemaphoreType.DMA((10,))],
        source_row, target_row, rotation, edge_feats, bias,
        conv_zero, conv_one, conv_two, alpha_in, alpha_edge, adot, out_proj, *tables,
        far=(5, 6, 7), apart=range(2, 9)
    )
    if direct:
        lanes_stats = [stats] + [
            lax.ppermute(stats, "edge", [(i, i ^ k) for i in range(lanes_total)])
            for k in range(1, lanes_total)
        ]
        graph_stats = jnp.concatenate(lanes_stats, axis=0)
        all_stats = [graph_stats] + [
            lax.ppermute(graph_stats, "graph", [(i, i ^ k) for i in range(peers)])
            for k in range(1, peers)
        ]
    else:
        all_stats = [lax.all_gather(stats, ("graph", "edge"), tiled=True)]
    messages = exchange(sums)
    order.mark(messages)
    message_rows = gather_lanes(messages)

    halves = [((size, LANES), f32) for start, size in CHUNKS for _ in range(2)]
    g0, g1, g2, pre_grad, *halves = call(
        make_gradient(peers, len(all_stats)),
        [
            ((DIM0, edges), bf16),
            ((DIM1, 2 * edges), bf16),
            ((DIM2, 2 * edges), bf16),
            ((HEADS * ALPHA, edges), bf16),
        ]
        + halves,
        [
            ((slots, FLAT), bf16),
            ((FLAT, edges), f32),
            ((8, edges), f32),
            ((2 * DIM1, 2 * edges), bf16),
            ((2 * DIM2, 2 * edges), bf16),
            ((2, PACKED_ROWS, LANES), f32),
        ]
        + frames
        + [pltpu.SemaphoreType.DMA((10,))],
        *all_stats, order.hold(own_stats), agg_grad, target_row, rot, edge_feats,
        x0, x1, x2, v0, v1, v2, pre, logits, adot,
        far=range(len(all_stats) + 5, len(all_stats) + 11), apart=range(4, 8)
    )

    total = lanes_total * slots
    order.mark(halves[0])
    message_rows = [order.hold(message_rows[0])] + message_rows[1:]
    late = []
    rest_steps = sum_all(halves[0], halves[1], "edge", order, late)
    zero_steps = sum_all(halves[2], halves[3], "graph", order)
    next(rest_steps)
    next(zero_steps)
    next(rest_steps)
    next(zero_steps)
    (source_sums,) = call(
        source_kernel,
        [((peers, cap, WIDE), f32)],
        [
            ((DIM0, edges), f32),
            ((DIM1, 2 * edges), f32),
            ((DIM2, 2 * edges), f32),
            ((COLS, 2 * edges), bf16),
        ],
        source_row, lists, rot, g0, g1, g2, order.hold(pre_grad),
        conv_zero, conv_one, conv_two, alpha_in
    )
    order.mark(source_sums)
    returned = exchange(source_sums)
    next(zero_steps)
    out, proj = call(
        make_finish(lanes_total),
        [((COEFFS, atoms, CH), bf16), ((PROJ_ROWS, LANES), f32)],
        [((total, WIDE), f32), ((2 * total, COLS), bf16), ((COEFFS, atoms, CH), bf16)],
        order.hold(cot), out_proj, *message_rows,
    )
    order.mark(proj)
    lane = lax.axis_index("edge")
    late_rows = PROJ_ROWS // lanes_total
    place = ((lane & 1) * (lanes_total // 2) + (lane >> 1)) * late_rows
    late.append(lax.dynamic_slice_in_dim(proj, place, late_rows, 0))
    for _ in range(bits_of("edge") - 1):
        next(rest_steps)
    next(zero_steps)
    source_rows = gather_lanes(order.hold(returned))
    next(zero_steps)
    next(rest_steps)
    next(zero_steps)
    (embed,) = call(
        make_collect(lanes_total),
        [((COEFFS, atoms, CH), bf16)],
        [((total, WIDE), f32)],
        order.hold(source_rows[0]), *source_rows[1:],
    )
    order.mark(embed)
    next(rest_steps)
    next(zero_steps)
    next(rest_steps)
    next(zero_steps)
    next(rest_steps)
    zero_pair = finish_steps(zero_steps)
    (zero,) = call(
        unpack_zero_kernel, [((DIM0, DIM0), bf16)], [], order.hold(zero_pair[0]), zero_pair[1]
    )
    order.mark(zero)
    rest_pair = finish_steps(rest_steps)
    one, two, grad_in, grad_edge, grad_dot, grad_proj = call(
        make_unpack_rest(lanes_total),
        [
            ((2, DIM1, DIM1), bf16),
            ((2, DIM2, DIM2), bf16),
            (alpha_in.shape, bf16),
            (alpha_edge.shape, bf16),
            ((2, LANES), bf16),
            (out_proj.shape, bf16),
        ],
        [], order.hold(rest_pair[0]), rest_pair[1]
    )

    def shaped(value):
        return jnp.transpose(value, (1, 0, 2))

    return (
        shaped(out), shaped(embed), zero, one, two, grad_in, grad_edge, grad_dot.reshape(-1),
        grad_proj,
    )


def solution(mesh):
    in_specs = (
        P(("groups", "graph"), None, None),
        P(("groups", "graph"), None, None),
        P(("groups", "graph"), None, "edge", None),
        P(("groups", "graph"), None, "edge", None),
        P(("groups", "graph", "edge")),
        P(("groups", "graph", "edge")),
        P(("groups", "graph", "edge"), None),
        P(("groups", "graph", "edge"), None),
        P(("groups", "graph", "edge"), None),
        P(),
        P(),
        P(),
        P(),
        P(),
        P(),
        P(),
    )
    out_specs = (
        P(("groups", "graph"), None, None),
        P(("groups", "graph"), None, None),
        P("groups", None),
        P("groups", None, None),
        P("groups", None, None),
        P("groups", None),
        P("groups", None),
        P("groups"),
        P("groups", None, None),
    )
    return jax.shard_map(shards, mesh=mesh, in_specs=in_specs, out_specs=out_specs, check_vma=False)
```

```python
import jax
import jax.numpy as jnp
import numpy as np
from jax import lax
from jax.experimental import pallas as pl
from jax.experimental.pallas import tpu as pltpu
from jax.sharding import PartitionSpec as P

LMAX = 6
MMAX = 2
CH = 64
HEADS = 4
VAL = 16
ALPHA = 64
COEFFS = (LMAX + 1) * (LMAX + 1)
FLAT = COEFFS * CH
LANES = 128
BLOCKS = (FLAT + LANES - 1) // LANES
COLS = BLOCKS * LANES
WIDE = COLS + LANES
TABLE = 2 * COLS + LANES
PEAK_AT, DOT_AT, NAME_AT = HEADS, 2 * HEADS, 3 * HEADS
STATS = 16
DIM0 = (LMAX + 1) * CH
DIM1 = LMAX * CH
DIM2 = (LMAX - 1) * CH
PANEL = 256

leak_slope = 0.2
floor_value = -1e30
bf16 = jnp.bfloat16
f32 = jnp.float32

VMEM_LIMIT = 56 * 1024 * 1024


def degree_blocks():
    result = []
    offset = 0
    for degree in range(LMAX + 1):
        centre = min(degree, MMAX)
        row_total = 2 * centre + 1
        col_total = 2 * degree + 1
        result.append((degree, centre, row_total, col_total, offset))
        offset += row_total * col_total
    return result


def degree_of(coeff):
    return int(np.sqrt(coeff))


def dot_nn(left, right):
    return jnp.dot(left, right, preferred_element_type=f32)


def dot_nt(left, right):
    return lax.dot_general(left, right, (((1,), (1,)), ((), ())), preferred_element_type=f32)


def dot_tn(left, right):
    return lax.dot_general(left, right, (((0,), (0,)), ((), ())), preferred_element_type=f32)


def iota(shape, dim):
    return lax.broadcasted_iota(jnp.int32, shape, dim)


def split_two(value):
    high = value.astype(bf16)
    return high, (value - high.astype(f32)).astype(bf16)


def to_frame(source, rot, edges, emit):
    for half in range(edges // LANES):
        lanes = pl.ds(half * LANES, LANES)
        for degree, centre, row_total, col_total, offset in degree_blocks():
            sums = [None] * row_total
            for j in range(col_total):
                column = source[pl.ds((degree * degree + j) * CH, CH), lanes]
                for i in range(row_total):
                    term = rot[pl.ds(offset + i * col_total + j, 1), lanes] * column
                    sums[i] = term if j == 0 else sums[i] + term
            for i in range(row_total):
                emit(degree, i - centre, half, sums[i])


def from_frame(load, rot, edges, emit):
    for half in range(edges // LANES):
        lanes = pl.ds(half * LANES, LANES)
        for degree, centre, row_total, col_total, offset in degree_blocks():
            rows = [load(degree, i - centre, half) for i in range(row_total)]
            for j in range(col_total):
                total = None
                for i in range(row_total):
                    term = rot[pl.ds(offset + i * col_total + j, 1), lanes] * rows[i]
                    total = term if i == 0 else total + term
                emit(degree * degree + j, half, total)


def lane_at(half, edges, second):
    return pl.ds(half * LANES + (edges if second else 0), LANES)


def frame_place(degree, order, refs):
    if order == 0:
        return refs[0], degree * CH, False
    which = abs(order)
    return refs[which], (degree - which) * CH, order < 0


def spread_heads(rows):
    return jnp.concatenate(
        [jnp.broadcast_to(row, (VAL, row.shape[1])) for row in rows], axis=0
    )


def is_direct(peers):
    return peers <= 4


def flip_of(peers):
    return lax.axis_index("graph") if is_direct(peers) else 0


def one_hot_rows(slot_ref, peers, slots):
    edges = slot_ref.shape[1]
    first = flip_of(peers) * (slots // peers)
    return jnp.bitwise_xor(iota((slots, edges), 0), first) == slot_ref[...]


def mask_to(mask, dtype):
    return jnp.where(mask, 1.0, 0.0).astype(dtype)


def stack_table(tables, rows_ref):
    cap = tables[0].shape[0]
    per = 8 // cap
    for n in range(0, len(tables), per):
        parts = [table[...].astype(f32) for table in tables[n : n + per]]
        rows_ref[pl.ds(n * cap, 8), :] = jnp.concatenate(parts, axis=0)


def put_rows(out_ref, cols, value):
    peers, cap = out_ref.shape[0], out_ref.shape[1]
    flip = flip_of(peers)
    for n in range(peers):
        place = jnp.bitwise_xor(flip, n) if is_direct(peers) else n
        out_ref[place, :, cols] = value[n * cap : (n + 1) * cap].astype(out_ref.dtype)


def slot_sums(terms, one_hot, out_ref, factor=None):
    both = jnp.concatenate([one_hot, one_hot], axis=1)
    products = 0.0
    for start in range(0, COLS, PANEL):
        size = min(PANEL, COLS - start)
        sums = dot_nt(both, terms[pl.ds(start, size), :])
        put_rows(out_ref, pl.ds(start, size), sums)
        if factor is None:
            continue
        for at in range(0, size, LANES):
            width = min(LANES, FLAT - start - at)
            product = sums[:, at : at + width] * factor[:, pl.ds(start + at, width)]
            if width < LANES:
                product = jnp.concatenate([product, jnp.zeros_like(product)], axis=1)
            products = products + product
    return products


def store_terms(terms, edges):
    def emit(coeff, half, value):
        high, low = split_two(value)
        rows = pl.ds(coeff * CH, CH)
        terms[rows, lane_at(half, edges, False)] = high
        terms[rows, lane_at(half, edges, True)] = low

    return emit


def listed_rows(list_ref, shape):
    peers, cap = list_ref.shape[1], list_ref.shape[3]
    flip = flip_of(peers)
    row = iota(shape, 0)
    result = jnp.zeros(shape, jnp.int32)
    for slot in range(peers * cap):
        owner = jnp.bitwise_xor(flip, slot // cap) if is_direct(peers) else slot // cap
        result = jnp.where(row == slot, list_ref[0, owner, 0, slot % cap], result)
    return result


def put_coeffs(outs, first, coeff_rows):
    for block in range(BLOCKS):
        left = coeff_rows(2 * block)
        right = coeff_rows(2 * block + 1) if 2 * block + 1 < COEFFS else jnp.zeros_like(left)
        put_pieces(outs, first + block * LANES, jnp.concatenate([left, right], axis=1))


def put_pieces(outs, first, value):
    cap = outs[0].shape[0]
    for n, out in enumerate(outs):
        out[:, pl.ds(first, LANES)] = value[n * cap : (n + 1) * cap].astype(out.dtype)


def outgoing_kernel(send, recv, embed, cot, *outs):
    atoms = embed.shape[1]
    slots = send.shape[1] * send.shape[3]
    sent = listed_rows(send, (slots, LANES))
    received = listed_rows(recv, (slots, LANES))
    for first, listed, values in ((0, sent, embed), (COLS, received, cot)):
        picked = mask_to(iota((slots, atoms), 1) == listed[:, :atoms], bf16)
        put_coeffs(outs, first, lambda k: dot_nn(picked, values[k]))
    lane = iota((slots, LANES), 1)
    side = jnp.where(lane == 0, received, jnp.where(lane == 1, sent, 0))
    put_pieces(outs, 2 * COLS, side.astype(f32))


def swapped_halves(value, edges):
    return jnp.concatenate([-value[:, edges:], value[:, :edges]], axis=1)


def make_forward(atoms, peers):
    def forward_kernel(
        source_slot, target_slot, rotation, feats, bias, wzero_at, wone_at, wtwo_at,
        ain, aedge, adot, out_proj, *rest,
    ):
        tables, rest = rest[:peers], rest[peers:]
        (
        sums_out, stats_out, x0_at, x1_at, x2_at, v0_at, v1_at, v2_at, pre_at, logit_out,
        lists_out, agg_grad, rot, own_out,
        rows, gathered, weights, terms, wzero, wone, wtwo, x0, x1, x2, v0, v1, v2, pre_out,
        semaphores,
        ) = rest
        copies = []

        def move(source, target):
            copy = pltpu.make_async_copy(source, target, semaphores.at[len(copies)])
            copy.start()
            copies.append(copy)

        move(wzero_at, wzero)
        move(wone_at, wone)
        move(wtwo_at, wtwo)
        rot[...] = jnp.transpose(rotation[...].astype(f32))
        edges = source_slot.shape[1]
        cap = tables[0].shape[0]
        slots = peers * cap
        stack_table(tables, rows)
        picked = mask_to(one_hot_rows(source_slot, peers, slots), bf16)
        for degree in range(LMAX + 1):
            ids = pl.ds(degree * degree * CH, (2 * degree + 1) * CH)
            gathered[ids, :] = dot_tn(rows[:, ids].astype(bf16), picked)
        lists = rows[:, pl.ds(2 * COLS, LANES)]
        lists_out[...] = lists
        for degree in range(LMAX + 1):
            ids = range(degree * degree, (degree + 1) * (degree + 1))
            cot = jnp.concatenate([rows[:, pl.ds(COLS + k * CH, CH)] for k in ids], axis=0)
            grad = dot_nt(cot.astype(bf16), out_proj[degree])
            for n, k in enumerate(ids):
                agg_grad[:, pl.ds(k * CH, CH)] = grad[n * slots : (n + 1) * slots]

        def emit(degree, order, half, value):
            ref, row, second = frame_place(degree, order, (x0, x1, x2))
            ref[pl.ds(row, CH), lane_at(half, edges, second)] = value.astype(bf16)

        to_frame(gathered, rot, edges, emit)
        for source, target in ((x0, x0_at), (x1, x1_at), (x2, x2_at)):
            move(source, target)

        pre = dot_tn(ain[...], x0[pl.ds(0, CH), :]) + lax.dot_general(
            aedge[...], feats[...], (((0,), (1,)), ((), ())), preferred_element_type=f32
        )
        pre_out[...] = pre
        move(pre_out, pre_at)
        hidden = jnp.where(pre > 0, pre, leak_slope * pre) * turned_column(adot[...].astype(f32))
        aims = one_hot_rows(target_slot, peers, slots)
        lane = iota((slots, LANES), 1)
        peer = jnp.bitwise_xor(iota((slots, 1), 0) // cap, flip_of(peers))
        name = lists[:, :1] + (peer * atoms).astype(f32)
        side = jnp.where(lane == NAME_AT, name, 0.0)
        for h in range(HEADS):
            logit = jnp.sum(hidden[h * ALPHA : (h + 1) * ALPHA], axis=0, keepdims=True)
            logit = logit + bias[pl.ds(h, 1), :]
            logit_out[pl.ds(h, 1), :] = logit
            peak = jnp.max(jnp.where(aims, logit, floor_value), axis=1, keepdims=True)
            of_edge = jnp.sum(jnp.where(aims, peak, 0.0), axis=0, keepdims=True)
            weight = jnp.exp(logit - of_edge)
            weights[pl.ds(h, 1), :] = weight
            den = jnp.sum(jnp.where(aims, weight, 0.0), axis=1, keepdims=True)
            side = jnp.where(lane == h, den, jnp.where(lane == PEAK_AT + h, peak, side))

        for copy in copies[:3]:
            copy.wait()
        v0[...] = dot_tn(wzero[...], x0[...])
        for out, weight, value in ((v1, wone, x1[...]), (v2, wtwo, x2[...])):
            out[...] = dot_tn(weight[0], value) + swapped_halves(dot_tn(weight[1], value), edges)
        for source, target in ((v0, v0_at), (v1, v1_at), (v2, v2_at)):
            move(source, target)

        def load(degree, order, half):
            ref, row, second = frame_place(degree, order, (v0, v1, v2))
            return ref[pl.ds(row, CH), lane_at(half, edges, second)]

        store = store_terms(terms, edges)

        def weigh(coeff, half, value):
            lanes = lane_at(half, edges, False)
            spread = spread_heads([weights[pl.ds(h, 1), lanes] for h in range(HEADS)])
            store(coeff, half, value * spread)

        terms[pl.ds(FLAT, COLS - FLAT), :] = jnp.zeros((COLS - FLAT, 2 * edges), bf16)
        from_frame(load, rot, edges, weigh)
        dots = slot_sums(terms, mask_to(aims, bf16), sums_out, agg_grad)
        head = (lane % CH) // VAL
        for h in range(HEADS):
            dot = jnp.sum(jnp.where(head == h, dots, 0.0), axis=1, keepdims=True)
            side = jnp.where(lane == DOT_AT + h, dot, side)
        put_rows(sums_out, pl.ds(COLS, LANES), side)
        own_out[...] = side
        spread = jnp.concatenate([side[:, :STATS]] * (LANES // STATS), axis=1)
        spread = jnp.where(lane // STATS == iota((slots, LANES), 0) % 8, spread, 0.0)
        packed = jnp.sum(spread.reshape(slots // 8, 8, LANES), axis=1)

        stats_out[...] = packed
        for copy in copies[3:]:
            copy.wait()

    return forward_kernel


def lane_heads(values, shape):
    head = (iota(shape, 1) % CH) // VAL
    result = jnp.broadcast_to(values[0], shape)
    for h in range(1, HEADS):
        result = jnp.where(head == h, values[h], result)
    return result


def collect_rows(arrived, rows_ref):
    cap = arrived.shape[1]
    for start in range(0, arrived.shape[0] * cap, 8):
        parts = [arrived[n] for n in range(start // cap, (start + 8) // cap)]
        rows_ref[pl.ds(start, 8), :] = jnp.concatenate(parts, axis=0)


def block_cols(block):
    return pl.ds(block * LANES, min(LANES, FLAT - block * LANES))


def finish_kernel(cot, out_proj, arrived, out, proj, rows, terms, agg_low):
    atoms = cot.shape[1]
    total = rows.shape[0]
    collect_rows(arrived, rows)
    side = rows[:, pl.ds(COLS, LANES)]
    owner = (lax.axis_index("graph") * atoms).astype(f32)
    names = iota((total, atoms), 1).astype(f32) + owner == side[:, NAME_AT : NAME_AT + 1]
    eye = iota((atoms, atoms), 0) == iota((atoms, atoms), 1)
    scales, dens = [], []
    for h in range(HEADS):
        peak_rows = side[:, PEAK_AT + h : PEAK_AT + h + 1]
        peak = jnp.max(jnp.where(names, peak_rows, floor_value), axis=0, keepdims=True)
        of_row = jnp.sum(jnp.where(names, peak, 0.0), axis=1, keepdims=True)
        scale = jnp.exp(peak_rows - of_row)
        scaled_den = side[:, h : h + 1] * scale
        den = jnp.sum(jnp.where(names, scaled_den, 0.0), axis=0, keepdims=True)
        scales.append(scale)
        dens.append(jnp.sum(jnp.where(eye, den, 0.0), axis=1, keepdims=True))
    scale_full = lane_heads(scales, (total, LANES))
    den_full = lane_heads(dens, (atoms, LANES))
    picked = mask_to(names, bf16)
    twice = jnp.concatenate([picked, picked], axis=0)
    for block in range(BLOCKS):
        cols = pl.ds(block * LANES, LANES)
        high, low = split_two(rows[:, cols] * scale_full)
        terms[pl.ds(0, total), cols] = high
        terms[pl.ds(total, total), cols] = low
    for block in range(BLOCKS):
        cols = pl.ds(block * LANES, LANES)
        agg = (dot_tn(twice, terms[:, cols]) / den_full).astype(bf16)
        agg_low[2 * block] = agg[:, :CH]
        if 2 * block + 1 < COEFFS:
            agg_low[2 * block + 1] = agg[:, CH:]
    for degree in range(LMAX + 1):
        ids = pl.ds(degree * degree, 2 * degree + 1)
        stacked = ((2 * degree + 1) * atoms, CH)
        left = agg_low[ids].reshape(stacked)
        right = cot[ids].reshape(stacked)
        value = dot_nn(left, out_proj[degree]).astype(bf16)
        out[ids] = value.reshape((2 * degree + 1, atoms, CH))
        at = (pl.ds(degree // 2 * CH, CH), pl.ds(degree % 2 * CH, CH))
        proj[at] = dot_tn(left, right)
    proj[pl.ds(LMAX // 2 * CH, CH), pl.ds(CH, CH)] = jnp.zeros((CH, CH), f32)


def combine_stats(stats, own):
    chunk = 32
    name = own[:, NAME_AT : NAME_AT + 1]

    def part(part_rows):
        entries = [part_rows[:, n : n + STATS] for n in range(0, LANES, STATS)]
        turned = jnp.transpose(jnp.concatenate(entries, axis=0))
        same = name == turned[NAME_AT : NAME_AT + 1]
        result = []
        for h in range(HEADS):
            peaks = turned[PEAK_AT + h : PEAK_AT + h + 1]
            peak = jnp.max(jnp.where(same, peaks, floor_value), axis=1, keepdims=True)
            scale = jnp.where(same, jnp.exp(jnp.where(same, peaks - peak, 0.0)), 0.0)
            den = jnp.sum(turned[h : h + 1] * scale, axis=1, keepdims=True)
            dot = jnp.sum(turned[DOT_AT + h : DOT_AT + h + 1] * scale, axis=1, keepdims=True)
            result += [peak, den, dot]
        return tuple(result)

    def step(at, held):
        fresh = part(stats[pl.ds(pl.multiple_of(at * chunk, chunk), chunk), :])
        result = []
        for h in range(HEADS):
            peak, den, dot = held[3 * h : 3 * h + 3]
            new_peak, new_den, new_dot = fresh[3 * h : 3 * h + 3]
            most = jnp.maximum(peak, new_peak)
            old, new = jnp.exp(peak - most), jnp.exp(new_peak - most)
            result += [most, den * old + new_den * new, dot * old + new_dot * new]
        return tuple(result)

    held = part(stats[pl.ds(0, chunk), :])
    if stats.shape[0] > chunk:
        held = lax.fori_loop(1, stats.shape[0] // chunk, step, held)
    return [held[3 * h : 3 * h + 3] for h in range(HEADS)]


def make_gradient(peers):
    def kernel(*refs):
        gradient_kernel(peers, *refs)

    return kernel


def gradient_kernel(
    peers, stats, own, agg_grad, target_slot, rot, feats,
    x0_at, x1_at, x2_at, v0_at, v1_at, v2_at, pre, logits, adot,
    g0, top1, top2, pre_grad_out, kept0, sent0, kept1, sent1,
    num_grad, spread_grad, weights, g1, g2, packed, x0, x1, x2, v0, v1, v2, semaphores,
):
    loads = []
    for source, target in (
        (v0_at, v0), (v1_at, v1), (v2_at, v2), (x0_at, x0), (x1_at, x1), (x2_at, x2)
    ):
        load = pltpu.make_async_copy(source, target, semaphores.at[4 + len(loads)])
        load.start()
        loads.append(load)
    edges = target_slot.shape[1]
    slots = agg_grad.shape[0]
    aims = one_hot_rows(target_slot, peers, slots)
    combined = combine_stats(stats, own[...])
    den_grads = []
    for h, (peak, den, dot) in enumerate(combined):
        of_edge = jnp.sum(jnp.where(aims, peak, 0.0), axis=0, keepdims=True)
        weights[pl.ds(h, 1), :] = jnp.exp(logits[pl.ds(h, 1), :] - of_edge)
        den_grad = (-(dot / den) / den).astype(bf16).astype(f32)
        den_grads.append(jnp.sum(jnp.where(aims, den_grad, 0.0), axis=0, keepdims=True))
    den_full = lane_heads([den for peak, den, dot in combined], (slots, LANES))
    for block in range(BLOCKS):
        cols = block_cols(block)
        num_grad[:, cols] = (agg_grad[:, cols] / den_full[:, : cols.size]).astype(bf16)
    picked = mask_to(aims, bf16)
    for degree in range(LMAX + 1):
        ids = pl.ds(degree * degree * CH, (2 * degree + 1) * CH)
        spread_grad[ids, :] = dot_tn(num_grad[:, ids], picked)

    state = {}

    def emit(degree, order, half, value):
        lanes = lane_at(half, edges, False)
        ref, row, second = frame_place(degree, order, (v0, v1, v2))
        product = value * ref[pl.ds(row, CH), lane_at(half, edges, second)]
        if degree == 0:
            state["sum"] = product
            state["spread"] = spread_heads([weights[pl.ds(h, 1), lanes] for h in range(HEADS)])
        else:
            state["sum"] = state["sum"] + product
        grad = (value * state["spread"]).astype(bf16)
        ref, row, second = frame_place(degree, order, (g0, g1, g2))
        ref[pl.ds(row, CH), lane_at(half, edges, second)] = grad
        if order != 0:
            swapped = grad if order < 0 else -grad
            below = row + (DIM1 if abs(order) == 1 else DIM2)
            ref[pl.ds(below, CH), lane_at(half, edges, not second)] = swapped
        if degree == LMAX and order == MMAX:
            for h in range(HEADS):
                part = state["sum"][h * VAL : (h + 1) * VAL]
                weights[pl.ds(HEADS + h, 1), lanes] = jnp.sum(part, axis=0, keepdims=True)

    for load in loads:
        load.wait()
    to_frame(spread_grad, rot, edges, emit)

    hidden = jnp.where(pre[...] > 0, pre[...], leak_slope * pre[...])
    logit_grads = [
        weights[pl.ds(h, 1), :] * (weights[pl.ds(HEADS + h, 1), :] + den_grads[h])
        for h in range(HEADS)
    ]
    tall = jnp.concatenate(
        [jnp.broadcast_to(row, (ALPHA, edges)) for row in logit_grads], axis=0
    )
    slope = jnp.where(pre[...] > 0, 1.0, leak_slope)
    pre_grad = (tall * turned_column(adot[...].astype(f32)) * slope).astype(bf16)
    pre_grad_out[...] = pre_grad
    dot_grad = jnp.sum(tall * hidden, axis=1, keepdims=True)

    top1[...] = g1[pl.ds(0, DIM1), :]
    top2[...] = g2[pl.ds(0, DIM2), :]
    mine = lax.axis_index("edge") & 1
    copies = []

    def put(row, value, at=0):
        for side in range(2):
            low, high = max(at, side * LANES), min(at + value.shape[1], (side + 1) * LANES)
            if low < high:
                piece = value[:, low - at : high - at]
                cols = pl.ds(low - side * LANES, high - low)
                packed[side, pl.ds(row, value.shape[0]), cols] = piece

    def send(chunk, kept, sent):
        start, size = CHUNKS[chunk]
        rows_of = pl.ds(start, size)
        for n, (side, out) in enumerate(((mine, kept), (1 - mine, sent))):
            copy = pltpu.make_async_copy(
                packed.at[side, rows_of, :], out, semaphores.at[2 * chunk + n]
            )
            copy.start()
            copies.append(copy)

    row = 0
    for left, right, dim in ((x1, g1, DIM1), (x2, g2, DIM2)):
        for start in range(0, 2 * dim, PANEL):
            size = min(PANEL, 2 * dim - start)
            put(row, dot_nt(left[...], right[pl.ds(start, size), :]))
            row += dim
    row -= DIM2
    edge_ch = feats.shape[1]
    edge_grad = lax.dot_general(
        feats[...], pre_grad, (((0,), (1,)), ((), ())), preferred_element_type=f32
    )
    put(row, edge_grad[:, :LANES], LANES)
    put(row + edge_ch, edge_grad[:, LANES:], LANES)
    wide_dot = jnp.transpose(jnp.broadcast_to(dot_grad, (HEADS * ALPHA, LANES)))
    spare = DIM2 - 2 * edge_ch
    tail = iota((spare, LANES), 0)
    first = jnp.broadcast_to(wide_dot[:1, :LANES], (spare, LANES))
    second = jnp.broadcast_to(wide_dot[:1, LANES:], (spare, LANES))
    put(row + 2 * edge_ch, jnp.where(tail == 0, first, jnp.where(tail == 1, second, 0.0)), LANES)
    row += DIM2
    put(row, dot_nt(x0[pl.ds(0, CH), :], pre_grad))
    send(0, kept0, sent0)

    row = CHUNKS[1][0]
    for start in range(0, DIM0, PANEL):
        size = min(PANEL, DIM0 - start)
        put(row, dot_nt(x0[...], g0[pl.ds(start, size), :]))
        if size < PANEL:
            put(row, jnp.zeros((DIM0, PANEL - size), f32), size)
        row += DIM0
    send(1, kept1, sent1)
    for copy in copies:
        copy.wait()


PROJ_ROWS = (LMAX // 2 + 1) * CH
CHUNKS = ((0, 3 * DIM1 + 3 * DIM2 + CH), (3 * DIM1 + 3 * DIM2 + CH, 2 * DIM0))
PACKED_ROWS = sum(size for start, size in CHUNKS)


def reversed_bits(value, count):
    return sum(((value >> n) & 1) << (count - 1 - n) for n in range(count))


def make_unpack(lanes_total, peers):
    def unpack_kernel(shares, zero, one, two, alpha_in, alpha_edge, alpha_dot, proj):
        cols = lanes_total // 2
        col_bits, peer_bits = (cols - 1).bit_length(), (peers - 1).bit_length()
        late = PROJ_ROWS // lanes_total
        first_rows = (CHUNKS[0][1] // cols + late) // peers
        share = shares.shape[1]
        main, zeros, tail = [], [], []
        for core in range(2):
            parts, zero_parts = [], {}
            for col in range(cols):
                col_of = reversed_bits(col, col_bits)
                rows = []
                for at in range(peers):
                    peer = reversed_bits(at, peer_bits)
                    value = shares[(col_of * 2 + core) * peers + peer].astype(f32)
                    rows.append(value[:first_rows])
                    zero_parts[at * cols + col] = value[first_rows:share]
                rows = jnp.concatenate(rows, axis=0)
                parts.append(rows[: CHUNKS[0][1] // cols])
                tail.append((core * cols + col_of, rows[CHUNKS[0][1] // cols :]))
            main.append(jnp.concatenate(parts, axis=0))
            zeros.append(jnp.concatenate([zero_parts[n] for n in sorted(zero_parts)], axis=0))
        tail = jnp.concatenate([rows for place, rows in sorted(tail, key=lambda e: e[0])], axis=0)
        for degree in range(LMAX + 1):
            piece = tail[degree // 2 * CH : (degree // 2 + 1) * CH]
            proj[degree] = piece[:, degree % 2 * CH : (degree % 2 + 1) * CH].astype(bf16)
        left, right = zeros
        zero[:, pl.ds(0, LANES)] = left[:DIM0].astype(bf16)
        zero[:, pl.ds(LANES, LANES)] = right[:DIM0].astype(bf16)
        zero[:, pl.ds(2 * LANES, LANES)] = left[DIM0:].astype(bf16)
        zero[:, pl.ds(3 * LANES, DIM0 - 3 * LANES)] = right[DIM0:, : DIM0 - 3 * LANES].astype(bf16)
        unpack_rest(*main, one, two, alpha_in, alpha_edge, alpha_dot)

    return unpack_kernel


def unpack_rest(left, right, one, two, alpha_in, alpha_edge, alpha_dot):
    for n in range(2 * DIM1 // LANES):
        panel = (left, right)[n % 2][(n // 2) * DIM1 : (n // 2 + 1) * DIM1]
        per = DIM1 // LANES
        one[n // per, :, pl.ds((n % per) * LANES, LANES)] = panel.astype(bf16)
    left, right = left[3 * DIM1 :], right[3 * DIM1 :]
    panels = [(left, right)[n % 2][(n // 2) * DIM2 : (n // 2 + 1) * DIM2] for n in range(5)]
    whole = jnp.concatenate(panels, axis=1)
    two[0] = whole[:, :DIM2].astype(bf16)
    two[1] = whole[:, DIM2:].astype(bf16)
    edge_ch = alpha_edge.shape[0]
    rest = right[2 * DIM2 : 3 * DIM2]
    alpha_edge[:, pl.ds(0, LANES)] = rest[:edge_ch].astype(bf16)
    alpha_edge[:, pl.ds(LANES, LANES)] = rest[edge_ch : 2 * edge_ch].astype(bf16)
    alpha_dot[...] = rest[2 * edge_ch : 2 * edge_ch + 2].astype(bf16)
    alpha_in[:, pl.ds(0, LANES)] = left[3 * DIM2 :].astype(bf16)
    alpha_in[:, pl.ds(LANES, LANES)] = right[3 * DIM2 :].astype(bf16)


def source_kernel(
    source_slot, lists, rot, g0, g1, g2, pre_grad, wzero, wone, wtwo, ain,
    *rest,
):
    sums_out, d0, d1, d2, terms = rest[-5:]
    edges = source_slot.shape[1]
    slots = sums_out.shape[0] * sums_out.shape[1]
    d0[...] = dot_nn(wzero[...], g0[...])
    d0[pl.ds(0, CH), :] += dot_nn(ain[...], pre_grad[...])
    for out, weight, value in ((d1, wone, g1[...]), (d2, wtwo, g2[...])):
        out[...] = dot_nn(weight[0], value) - swapped_halves(dot_nn(weight[1], value), edges)

    def load(degree, order, half):
        ref, row, second = frame_place(degree, order, (d0, d1, d2))
        return ref[pl.ds(row, CH), lane_at(half, edges, second)]

    terms[pl.ds(FLAT, COLS - FLAT), :] = jnp.zeros((COLS - FLAT, 2 * edges), bf16)
    from_frame(load, rot, edges, store_terms(terms, edges))
    slot_sums(terms, mask_to(one_hot_rows(source_slot, sums_out.shape[0], slots), bf16), sums_out)
    put_rows(sums_out, pl.ds(COLS, LANES), lists[...])


def collect_kernel(arrived, out, rows):
    atoms = out.shape[1]
    total = rows.shape[0]
    collect_rows(arrived, rows)
    index = rows[:, pl.ds(COLS, LANES)][:, 1:2]
    picked = mask_to(iota((total, atoms), 1).astype(f32) == index, bf16)
    twice = jnp.concatenate([picked, picked], axis=0)
    for block in range(BLOCKS):
        high, low = split_two(rows[:, pl.ds(block * LANES, LANES)])
        sums = dot_tn(twice, jnp.concatenate([high, low], axis=0)).astype(bf16)
        out[2 * block] = sums[:, :CH]
        if 2 * block + 1 < COEFFS:
            out[2 * block + 1] = sums[:, CH:]


vmem = pl.BlockSpec(memory_space=pltpu.VMEM)
smem = pl.BlockSpec(memory_space=pltpu.SMEM)
anywhere = pl.BlockSpec(memory_space=pl.ANY)


def call(kernel, outs, scratch, *args, scalars=0, far=(), apart=(), after=()):
    specs = [smem if n < scalars else anywhere if n in far else vmem for n in range(len(args))]
    specs += [anywhere] * len(after)
    out_specs = [anywhere if n in apart else vmem for n in range(len(outs))]
    shapes = [pltpu.VMEM(*entry) if isinstance(entry, tuple) else entry for entry in scratch]
    return pl.pallas_call(
        kernel,
        out_shape=[jax.ShapeDtypeStruct(shape, kind) for shape, kind in outs],
        in_specs=specs,
        out_specs=out_specs,
        scratch_shapes=shapes,
        compiler_params=pltpu.CompilerParams(vmem_limit_bytes=VMEM_LIMIT),
        cost_estimate=pl.CostEstimate(flops=1, bytes_accessed=1, transcendentals=0),
    )(*args, *after)


class Order:
    def __init__(self):
        self.last = None

    def hold(self, value):
        if self.last is None:
            return value
        return lax.optimization_barrier((value, self.last))[0]

    def mark(self, value):
        self.last = value
        return value


def turned_column(row):
    return jnp.transpose(jnp.broadcast_to(row, (8, row.shape[1])))[:, :1]


def swap(value, axis, bit):
    size = lax.axis_size(axis)
    return lax.ppermute(value, axis, [(i, i ^ (1 << bit)) for i in range(size)])


def bits_of(axis):
    return (lax.axis_size(axis) - 1).bit_length()


def own_bit(axis, bit):
    return (lax.axis_index(axis) >> bit) & 1


def sum_all(kept, sent, first, order, late=None):
    steps = [("edge", n) for n in range(1, bits_of("edge"))]
    steps += [("graph", n) for n in range(bits_of("graph"))]
    steps.sort(key=lambda step: step[0] != first)
    other = swap(sent, "edge", 0)
    yield
    current = kept + order.hold(other)
    for n, (axis, bit) in enumerate(steps):
        if late is not None and n == bits_of("edge") - 1:
            current = jnp.concatenate([current, late[0]], axis=0)
        mine = own_bit(axis, bit)
        parts = current.reshape(2, current.shape[0] // 2, -1)
        sent = order.mark(lax.dynamic_index_in_dim(parts, 1 - mine, 0, False))
        other = swap(sent, axis, bit)
        yield
        current = lax.dynamic_index_in_dim(parts, mine, 0, False) + order.hold(other)
    return order.mark(current.astype(bf16))


def finish_steps(chain):
    while True:
        try:
            next(chain)
        except StopIteration as end:
            return end.value


def shards(
    atom_embed, out_cotangent, send_rows, recv_rows, source_slot, target_slot, rotation,
    edge_feats, edge_bias, conv_zero, conv_one, conv_two, alpha_in, alpha_edge, alpha_dot,
    out_proj,
):
    peers = lax.axis_size("graph")
    lanes_total = lax.axis_size("edge")
    atoms = atom_embed.shape[0]
    edges = rotation.shape[0]
    cap = send_rows.shape[3]
    slots = peers * cap
    blocks = peers * lanes_total
    direct = is_direct(peers)
    order = Order()

    def exchange(value):
        return lax.all_to_all(value, "graph", split_axis=0, concat_axis=0, tiled=True)

    cot = jnp.transpose(out_cotangent, (1, 0, 2))
    outgoing = call(
        outgoing_kernel, [((cap, TABLE), bf16)] * peers, [],
        send_rows, recv_rows, jnp.transpose(atom_embed, (1, 0, 2)), cot,
        scalars=2
    )
    if direct:
        tables = [outgoing[0]] + [
            lax.ppermute(outgoing[k], "graph", [(i, i ^ k) for i in range(peers)])
            for k in range(1, peers)
        ]
    else:
        tables = list(exchange(jnp.stack(outgoing)))

    source_row = source_slot.reshape(1, edges)
    target_row = target_slot.reshape(1, edges)
    bias = edge_bias.T
    adot = alpha_dot.reshape(1, -1)

    frames = [
        ((DIM0, edges), bf16),
        ((DIM1, 2 * edges), bf16),
        ((DIM2, 2 * edges), bf16),
        ((DIM0, edges), f32),
        ((DIM1, 2 * edges), f32),
        ((DIM2, 2 * edges), f32),
    ]
    pre_shape = ((HEADS * ALPHA, edges), f32)
    sums, stats, x0, x1, x2, v0, v1, v2, pre, logits, lists, agg_grad, rot, own_stats = call(
        make_forward(atoms, peers),
        [((peers, cap, WIDE), f32), ((slots // 8, LANES), f32)]
        + frames
        + [
            pre_shape,
            ((8, edges), f32),
            ((slots, LANES), f32),
            ((slots, FLAT), f32),
            ((rotation.shape[1], edges), f32),
            ((slots, LANES), f32),
        ],
        [
            ((slots, TABLE), f32),
            ((FLAT, edges), f32),
            ((8, edges), f32),
            ((COLS, 2 * edges), bf16),
            (conv_zero.shape, bf16),
            (conv_one.shape, bf16),
            (conv_two.shape, bf16),
        ]
        + frames
        + [pre_shape, pltpu.SemaphoreType.DMA((10,))],
        source_row, target_row, rotation, edge_feats, bias,
        conv_zero, conv_one, conv_two, alpha_in, alpha_edge, adot, out_proj, *tables,
        far=(5, 6, 7), apart=range(2, 9)
    )
    all_stats = lax.all_gather(stats, ("graph", "edge"), tiled=True)
    messages = exchange(sums)
    message_rows = lax.all_gather(messages, "edge", tiled=True)

    halves = [((size, LANES), f32) for start, size in CHUNKS for _ in range(2)]
    g0, g1, g2, pre_grad, *halves = call(
        make_gradient(peers),
        [
            ((DIM0, edges), bf16),
            ((DIM1, 2 * edges), bf16),
            ((DIM2, 2 * edges), bf16),
            ((HEADS * ALPHA, edges), bf16),
        ]
        + halves,
        [
            ((slots, FLAT), bf16),
            ((FLAT, edges), f32),
            ((8, edges), f32),
            ((2 * DIM1, 2 * edges), bf16),
            ((2 * DIM2, 2 * edges), bf16),
            ((2, PACKED_ROWS, LANES), f32),
        ]
        + frames
        + [pltpu.SemaphoreType.DMA((10,))],
        all_stats, own_stats, agg_grad, target_row, rot, edge_feats,
        x0, x1, x2, v0, v1, v2, pre, logits, adot,
        far=range(6, 12), apart=range(4, 8)
    )

    total = lanes_total * slots
    order.mark(halves[0])
    late = []
    rest_steps = sum_all(halves[0], halves[1], "edge", order, late)
    zero_steps = sum_all(halves[2], halves[3], "graph", order)
    next(rest_steps)
    next(zero_steps)
    next(rest_steps)
    next(zero_steps)
    (source_sums,) = call(
        source_kernel,
        [((peers, cap, WIDE), f32)],
        [
            ((DIM0, edges), f32),
            ((DIM1, 2 * edges), f32),
            ((DIM2, 2 * edges), f32),
            ((COLS, 2 * edges), bf16),
        ],
        source_row, lists, rot, g0, g1, g2, order.hold(pre_grad),
        conv_zero, conv_one, conv_two, alpha_in
    )
    order.mark(source_sums)
    returned = exchange(source_sums)
    next(zero_steps)
    out, proj = call(
        finish_kernel,
        [((COEFFS, atoms, CH), bf16), ((PROJ_ROWS, LANES), f32)],
        [((total, WIDE), f32), ((2 * total, COLS), bf16), ((COEFFS, atoms, CH), bf16)],
        order.hold(cot), out_proj, message_rows,
    )
    order.mark(proj)
    lane = lax.axis_index("edge")
    late_rows = PROJ_ROWS // lanes_total
    place = ((lane & 1) * (lanes_total // 2) + (lane >> 1)) * late_rows
    late.append(lax.dynamic_slice_in_dim(proj, place, late_rows, 0))
    for _ in range(bits_of("edge") - 1):
        next(rest_steps)
    next(zero_steps)
    source_rows = lax.all_gather(returned, "edge", tiled=True)
    next(rest_steps)
    zero_share = finish_steps(zero_steps)
    share = jnp.concatenate([finish_steps(rest_steps), zero_share], axis=0)
    shares = lax.all_gather(share, ("edge", "graph"))
    (embed,) = call(
        collect_kernel,
        [((COEFFS, atoms, CH), bf16)],
        [((total, WIDE), f32)],
        order.hold(source_rows),
    )
    zero, one, two, grad_in, grad_edge, grad_dot, grad_proj = call(
        make_unpack(lanes_total, peers),
        [
            ((DIM0, DIM0), bf16),
            ((2, DIM1, DIM1), bf16),
            ((2, DIM2, DIM2), bf16),
            (alpha_in.shape, bf16),
            (alpha_edge.shape, bf16),
            ((2, LANES), bf16),
            (out_proj.shape, bf16),
        ],
        [],
        shares.reshape(blocks, -1, LANES),
    )

    def shaped(value):
        return jnp.transpose(value, (1, 0, 2))

    return (
        shaped(out), shaped(embed), zero, one, two, grad_in, grad_edge, grad_dot.reshape(-1),
        grad_proj,
    )


def solution(mesh):
    in_specs = (
        P(("groups", "graph"), None, None),
        P(("groups", "graph"), None, None),
        P(("groups", "graph"), None, "edge", None),
        P(("groups", "graph"), None, "edge", None),
        P(("groups", "graph", "edge")),
        P(("groups", "graph", "edge")),
        P(("groups", "graph", "edge"), None),
        P(("groups", "graph", "edge"), None),
        P(("groups", "graph", "edge"), None),
        P(),
        P(),
        P(),
        P(),
        P(),
        P(),
        P(),
    )
    out_specs = (
        P(("groups", "graph"), None, None),
        P(("groups", "graph"), None, None),
        P("groups", None),
        P("groups", None, None),
        P("groups", None, None),
        P("groups", None),
        P("groups", None),
        P("groups"),
        P("groups", None, None),
    )
    return jax.shard_map(shards, mesh=mesh, in_specs=in_specs, out_specs=out_specs, check_vma=False)
```

```python
import jax
import jax.numpy as jnp
import numpy as np
from jax import lax
from jax.experimental import pallas as pl
from jax.experimental.pallas import tpu as pltpu
from jax.sharding import PartitionSpec as P

LMAX = 6
MMAX = 2
CH = 64
HEADS = 4
VAL = 16
ALPHA = 64
COEFFS = (LMAX + 1) * (LMAX + 1)
FLAT = COEFFS * CH
LANES = 128
BLOCKS = (FLAT + LANES - 1) // LANES
COLS = BLOCKS * LANES
WIDE = COLS + LANES
TABLE = 2 * COLS + LANES
PEAK_AT, DOT_AT, NAME_AT = HEADS, 2 * HEADS, 3 * HEADS
STATS = 16
DIM0 = (LMAX + 1) * CH
DIM1 = LMAX * CH
DIM2 = (LMAX - 1) * CH
PANEL = 256

leak_slope = 0.2
floor_value = -1e30
bf16 = jnp.bfloat16
f32 = jnp.float32

VMEM_LIMIT = 56 * 1024 * 1024


def degree_blocks():
    result = []
    offset = 0
    for degree in range(LMAX + 1):
        centre = min(degree, MMAX)
        row_total = 2 * centre + 1
        col_total = 2 * degree + 1
        result.append((degree, centre, row_total, col_total, offset))
        offset += row_total * col_total
    return result


def degree_of(coeff):
    return int(np.sqrt(coeff))


def dot_nn(left, right):
    return jnp.dot(left, right, preferred_element_type=f32)


def dot_nt(left, right):
    return lax.dot_general(left, right, (((1,), (1,)), ((), ())), preferred_element_type=f32)


def dot_tn(left, right):
    return lax.dot_general(left, right, (((0,), (0,)), ((), ())), preferred_element_type=f32)


def iota(shape, dim):
    return lax.broadcasted_iota(jnp.int32, shape, dim)


def split_two(value):
    high = value.astype(bf16)
    return high, (value - high.astype(f32)).astype(bf16)


def to_frame(source, rot, edges, emit):
    for half in range(edges // LANES):
        lanes = pl.ds(half * LANES, LANES)
        for degree, centre, row_total, col_total, offset in degree_blocks():
            sums = [None] * row_total
            for j in range(col_total):
                column = source[pl.ds((degree * degree + j) * CH, CH), lanes]
                for i in range(row_total):
                    term = rot[pl.ds(offset + i * col_total + j, 1), lanes] * column
                    sums[i] = term if j == 0 else sums[i] + term
            for i in range(row_total):
                emit(degree, i - centre, half, sums[i])


def from_frame(load, rot, edges, emit):
    for half in range(edges // LANES):
        lanes = pl.ds(half * LANES, LANES)
        for degree, centre, row_total, col_total, offset in degree_blocks():
            rows = [load(degree, i - centre, half) for i in range(row_total)]
            for j in range(col_total):
                total = None
                for i in range(row_total):
                    term = rot[pl.ds(offset + i * col_total + j, 1), lanes] * rows[i]
                    total = term if i == 0 else total + term
                emit(degree * degree + j, half, total)


def lane_at(half, edges, second):
    return pl.ds(half * LANES + (edges if second else 0), LANES)


def frame_place(degree, order, refs):
    if order == 0:
        return refs[0], degree * CH, False
    which = abs(order)
    return refs[which], (degree - which) * CH, order < 0


def spread_heads(rows):
    return jnp.concatenate(
        [jnp.broadcast_to(row, (VAL, row.shape[1])) for row in rows], axis=0
    )


def is_direct(peers):
    return peers <= 4


def flip_of(peers):
    return lax.axis_index("graph") if is_direct(peers) else 0


def one_hot_rows(slot_ref, peers, slots):
    edges = slot_ref.shape[1]
    first = flip_of(peers) * (slots // peers)
    return jnp.bitwise_xor(iota((slots, edges), 0), first) == slot_ref[...]


def mask_to(mask, dtype):
    return jnp.where(mask, 1.0, 0.0).astype(dtype)


def stack_table(tables, rows_ref):
    cap = tables[0].shape[0]
    per = 8 // cap
    for n in range(0, len(tables), per):
        parts = [table[...].astype(f32) for table in tables[n : n + per]]
        rows_ref[pl.ds(n * cap, 8), :] = jnp.concatenate(parts, axis=0)


def put_rows(out_ref, cols, value):
    peers, cap = out_ref.shape[0], out_ref.shape[1]
    flip = flip_of(peers)
    for n in range(peers):
        place = jnp.bitwise_xor(flip, n) if is_direct(peers) else n
        out_ref[place, :, cols] = value[n * cap : (n + 1) * cap].astype(out_ref.dtype)


def slot_sums(terms, one_hot, out_ref, factor=None):
    both = jnp.concatenate([one_hot, one_hot], axis=1)
    products = 0.0
    for start in range(0, COLS, PANEL):
        size = min(PANEL, COLS - start)
        sums = dot_nt(both, terms[pl.ds(start, size), :])
        put_rows(out_ref, pl.ds(start, size), sums)
        if factor is None:
            continue
        for at in range(0, size, LANES):
            width = min(LANES, FLAT - start - at)
            product = sums[:, at : at + width] * factor[:, pl.ds(start + at, width)]
            if width < LANES:
                product = jnp.concatenate([product, jnp.zeros_like(product)], axis=1)
            products = products + product
    return products


def store_terms(terms, edges):
    def emit(coeff, half, value):
        high, low = split_two(value)
        rows = pl.ds(coeff * CH, CH)
        terms[rows, lane_at(half, edges, False)] = high
        terms[rows, lane_at(half, edges, True)] = low

    return emit


def listed_rows(list_ref, shape):
    peers, cap = list_ref.shape[1], list_ref.shape[3]
    flip = flip_of(peers)
    row = iota(shape, 0)
    result = jnp.zeros(shape, jnp.int32)
    for slot in range(peers * cap):
        owner = jnp.bitwise_xor(flip, slot // cap) if is_direct(peers) else slot // cap
        result = jnp.where(row == slot, list_ref[0, owner, 0, slot % cap], result)
    return result


def put_coeffs(outs, first, coeff_rows):
    for block in range(BLOCKS):
        left = coeff_rows(2 * block)
        right = coeff_rows(2 * block + 1) if 2 * block + 1 < COEFFS else jnp.zeros_like(left)
        put_pieces(outs, first + block * LANES, jnp.concatenate([left, right], axis=1))


def put_pieces(outs, first, value):
    cap = outs[0].shape[0]
    for n, out in enumerate(outs):
        out[:, pl.ds(first, LANES)] = value[n * cap : (n + 1) * cap].astype(out.dtype)


def outgoing_kernel(send, recv, embed, cot, *outs):
    atoms = embed.shape[1]
    slots = send.shape[1] * send.shape[3]
    sent = listed_rows(send, (slots, LANES))
    received = listed_rows(recv, (slots, LANES))
    for first, listed, values in ((0, sent, embed), (COLS, received, cot)):
        picked = mask_to(iota((slots, atoms), 1) == listed[:, :atoms], bf16)
        put_coeffs(outs, first, lambda k: dot_nn(picked, values[k]))
    lane = iota((slots, LANES), 1)
    side = jnp.where(lane == 0, received, jnp.where(lane == 1, sent, 0))
    put_pieces(outs, 2 * COLS, side.astype(f32))


def swapped_halves(value, edges):
    return jnp.concatenate([-value[:, edges:], value[:, :edges]], axis=1)


def make_forward(atoms, peers):
    def forward_kernel(
        source_slot, target_slot, rotation, feats, bias, wzero_at, wone_at, wtwo_at,
        ain, aedge, adot, out_proj, *rest,
    ):
        tables, rest = rest[:peers], rest[peers:]
        (
        sums_out, stats_out, x0_at, x1_at, x2_at, v0_at, v1_at, v2_at, pre_at, logit_out,
        lists_out, agg_grad, rot, own_out,
        rows, gathered, weights, terms, wzero, wone, wtwo, x0, x1, x2, v0, v1, v2, pre_out,
        semaphores,
        ) = rest
        copies = []

        def move(source, target):
            copy = pltpu.make_async_copy(source, target, semaphores.at[len(copies)])
            copy.start()
            copies.append(copy)

        move(wzero_at, wzero)
        move(wone_at, wone)
        move(wtwo_at, wtwo)
        rot[...] = jnp.transpose(rotation[...].astype(f32))
        edges = source_slot.shape[1]
        cap = tables[0].shape[0]
        slots = peers * cap
        stack_table(tables, rows)
        picked = mask_to(one_hot_rows(source_slot, peers, slots), bf16)
        for degree in range(LMAX + 1):
            ids = pl.ds(degree * degree * CH, (2 * degree + 1) * CH)
            gathered[ids, :] = dot_tn(rows[:, ids].astype(bf16), picked)
        lists = rows[:, pl.ds(2 * COLS, LANES)]
        lists_out[...] = lists
        for degree in range(LMAX + 1):
            ids = range(degree * degree, (degree + 1) * (degree + 1))
            cot = jnp.concatenate([rows[:, pl.ds(COLS + k * CH, CH)] for k in ids], axis=0)
            grad = dot_nt(cot.astype(bf16), out_proj[degree])
            for n, k in enumerate(ids):
                agg_grad[:, pl.ds(k * CH, CH)] = grad[n * slots : (n + 1) * slots]

        def emit(degree, order, half, value):
            ref, row, second = frame_place(degree, order, (x0, x1, x2))
            ref[pl.ds(row, CH), lane_at(half, edges, second)] = value.astype(bf16)

        to_frame(gathered, rot, edges, emit)
        for source, target in ((x0, x0_at), (x1, x1_at), (x2, x2_at)):
            move(source, target)

        pre = dot_tn(ain[...], x0[pl.ds(0, CH), :]) + lax.dot_general(
            aedge[...], feats[...], (((0,), (1,)), ((), ())), preferred_element_type=f32
        )
        pre_out[...] = pre
        move(pre_out, pre_at)
        hidden = jnp.where(pre > 0, pre, leak_slope * pre) * turned_column(adot[...].astype(f32))
        aims = one_hot_rows(target_slot, peers, slots)
        lane = iota((slots, LANES), 1)
        peer = jnp.bitwise_xor(iota((slots, 1), 0) // cap, flip_of(peers))
        name = lists[:, :1] + (peer * atoms).astype(f32)
        side = jnp.where(lane == NAME_AT, name, 0.0)
        for h in range(HEADS):
            logit = jnp.sum(hidden[h * ALPHA : (h + 1) * ALPHA], axis=0, keepdims=True)
            logit = logit + bias[pl.ds(h, 1), :]
            logit_out[pl.ds(h, 1), :] = logit
            peak = jnp.max(jnp.where(aims, logit, floor_value), axis=1, keepdims=True)
            of_edge = jnp.sum(jnp.where(aims, peak, 0.0), axis=0, keepdims=True)
            weight = jnp.exp(logit - of_edge)
            weights[pl.ds(h, 1), :] = weight
            den = jnp.sum(jnp.where(aims, weight, 0.0), axis=1, keepdims=True)
            side = jnp.where(lane == h, den, jnp.where(lane == PEAK_AT + h, peak, side))

        for copy in copies[:3]:
            copy.wait()
        v0[...] = dot_tn(wzero[...], x0[...])
        for out, weight, value in ((v1, wone, x1[...]), (v2, wtwo, x2[...])):
            out[...] = dot_tn(weight[0], value) + swapped_halves(dot_tn(weight[1], value), edges)
        for source, target in ((v0, v0_at), (v1, v1_at), (v2, v2_at)):
            move(source, target)

        def load(degree, order, half):
            ref, row, second = frame_place(degree, order, (v0, v1, v2))
            return ref[pl.ds(row, CH), lane_at(half, edges, second)]

        store = store_terms(terms, edges)

        def weigh(coeff, half, value):
            lanes = lane_at(half, edges, False)
            spread = spread_heads([weights[pl.ds(h, 1), lanes] for h in range(HEADS)])
            store(coeff, half, value * spread)

        terms[pl.ds(FLAT, COLS - FLAT), :] = jnp.zeros((COLS - FLAT, 2 * edges), bf16)
        from_frame(load, rot, edges, weigh)
        dots = slot_sums(terms, mask_to(aims, bf16), sums_out, agg_grad)
        head = (lane % CH) // VAL
        for h in range(HEADS):
            dot = jnp.sum(jnp.where(head == h, dots, 0.0), axis=1, keepdims=True)
            side = jnp.where(lane == DOT_AT + h, dot, side)
        put_rows(sums_out, pl.ds(COLS, LANES), side)
        own_out[...] = side
        spread = jnp.concatenate([side[:, :STATS]] * (LANES // STATS), axis=1)
        spread = jnp.where(lane // STATS == iota((slots, LANES), 0) % 8, spread, 0.0)
        packed = jnp.sum(spread.reshape(slots // 8, 8, LANES), axis=1)

        stats_out[...] = packed
        for copy in copies[3:]:
            copy.wait()

    return forward_kernel


def lane_heads(values, shape):
    head = (iota(shape, 1) % CH) // VAL
    result = jnp.broadcast_to(values[0], shape)
    for h in range(1, HEADS):
        result = jnp.where(head == h, values[h], result)
    return result


def collect_rows(arrivals, rows_ref):
    own = lax.axis_index("edge")
    for k, arrival in enumerate(arrivals):
        peers, cap, width = arrival.shape
        base = (own ^ k) * (peers * cap)
        for start in range(0, peers * cap, 8):
            parts = [arrival[g] for g in range(start // cap, (start + 8) // cap)]
            at = pl.ds(pl.multiple_of(base + start, 8), 8)
            rows_ref[at, :] = jnp.concatenate(parts, axis=0)


def block_cols(block):
    return pl.ds(block * LANES, min(LANES, FLAT - block * LANES))


def make_finish(lanes_total):
    def finish_kernel(cot, out_proj, *rest):
        arrivals = rest[:lanes_total]
        out, proj, rows, terms, agg_low = rest[lanes_total:]
        atoms = cot.shape[1]
        total = rows.shape[0]
        collect_rows(arrivals, rows)
        side = rows[:, pl.ds(COLS, LANES)]
        owner = (lax.axis_index("graph") * atoms).astype(f32)
        names = iota((total, atoms), 1).astype(f32) + owner == side[:, NAME_AT : NAME_AT + 1]
        eye = iota((atoms, atoms), 0) == iota((atoms, atoms), 1)
        scales, dens = [], []
        for h in range(HEADS):
            peak_rows = side[:, PEAK_AT + h : PEAK_AT + h + 1]
            peak = jnp.max(jnp.where(names, peak_rows, floor_value), axis=0, keepdims=True)
            of_row = jnp.sum(jnp.where(names, peak, 0.0), axis=1, keepdims=True)
            scale = jnp.exp(peak_rows - of_row)
            scaled_den = side[:, h : h + 1] * scale
            den = jnp.sum(jnp.where(names, scaled_den, 0.0), axis=0, keepdims=True)
            scales.append(scale)
            dens.append(jnp.sum(jnp.where(eye, den, 0.0), axis=1, keepdims=True))
        scale_full = lane_heads(scales, (total, LANES))
        den_full = lane_heads(dens, (atoms, LANES))
        picked = mask_to(names, bf16)
        twice = jnp.concatenate([picked, picked], axis=0)
        for block in range(BLOCKS):
            cols = pl.ds(block * LANES, LANES)
            high, low = split_two(rows[:, cols] * scale_full)
            terms[pl.ds(0, total), cols] = high
            terms[pl.ds(total, total), cols] = low
        for block in range(BLOCKS):
            cols = pl.ds(block * LANES, LANES)
            agg = (dot_tn(twice, terms[:, cols]) / den_full).astype(bf16)
            agg_low[2 * block] = agg[:, :CH]
            if 2 * block + 1 < COEFFS:
                agg_low[2 * block + 1] = agg[:, CH:]
        for degree in range(LMAX + 1):
            ids = pl.ds(degree * degree, 2 * degree + 1)
            stacked = ((2 * degree + 1) * atoms, CH)
            left = agg_low[ids].reshape(stacked)
            right = cot[ids].reshape(stacked)
            value = dot_nn(left, out_proj[degree]).astype(bf16)
            out[ids] = value.reshape((2 * degree + 1, atoms, CH))
            at = (pl.ds(degree // 2 * CH, CH), pl.ds(degree % 2 * CH, CH))
            proj[at] = dot_tn(left, right)
        proj[pl.ds(LMAX // 2 * CH, CH), pl.ds(CH, CH)] = jnp.zeros((CH, CH), f32)

    return finish_kernel


def combine_stats(stats, own):
    chunk = 32
    name = own[:, NAME_AT : NAME_AT + 1]

    def part(part_rows):
        entries = [part_rows[:, n : n + STATS] for n in range(0, LANES, STATS)]
        turned = jnp.transpose(jnp.concatenate(entries, axis=0))
        same = name == turned[NAME_AT : NAME_AT + 1]
        result = []
        for h in range(HEADS):
            peaks = turned[PEAK_AT + h : PEAK_AT + h + 1]
            peak = jnp.max(jnp.where(same, peaks, floor_value), axis=1, keepdims=True)
            scale = jnp.where(same, jnp.exp(jnp.where(same, peaks - peak, 0.0)), 0.0)
            den = jnp.sum(turned[h : h + 1] * scale, axis=1, keepdims=True)
            dot = jnp.sum(turned[DOT_AT + h : DOT_AT + h + 1] * scale, axis=1, keepdims=True)
            result += [peak, den, dot]
        return tuple(result)

    def step(at, held):
        fresh = part(stats[0][pl.ds(pl.multiple_of(at * chunk, chunk), chunk), :])
        result = []
        for h in range(HEADS):
            peak, den, dot = held[3 * h : 3 * h + 3]
            new_peak, new_den, new_dot = fresh[3 * h : 3 * h + 3]
            most = jnp.maximum(peak, new_peak)
            old, new = jnp.exp(peak - most), jnp.exp(new_peak - most)
            result += [most, den * old + new_den * new, dot * old + new_dot * new]
        return tuple(result)

    if len(stats) > 1:
        held = part(jnp.concatenate([rows[...] for rows in stats], axis=0))
    else:
        held = part(stats[0][pl.ds(0, chunk), :])
        held = lax.fori_loop(1, stats[0].shape[0] // chunk, step, held)
    return [held[3 * h : 3 * h + 3] for h in range(HEADS)]


def make_gradient(peers, parts):
    def kernel(*refs):
        gradient_kernel(peers, refs[:parts], *refs[parts:])

    return kernel


def gradient_kernel(
    peers, stats, own, agg_grad, target_slot, rot, feats,
    x0_at, x1_at, x2_at, v0_at, v1_at, v2_at, pre, logits, adot,
    g0, top1, top2, pre_grad_out, kept0, sent0, kept1, sent1,
    num_grad, spread_grad, weights, g1, g2, packed, x0, x1, x2, v0, v1, v2, semaphores,
):
    loads = []
    for source, target in (
        (v0_at, v0), (v1_at, v1), (v2_at, v2), (x0_at, x0), (x1_at, x1), (x2_at, x2)
    ):
        load = pltpu.make_async_copy(source, target, semaphores.at[4 + len(loads)])
        load.start()
        loads.append(load)
    edges = target_slot.shape[1]
    slots = agg_grad.shape[0]
    aims = one_hot_rows(target_slot, peers, slots)
    combined = combine_stats(stats, own[...])
    den_grads = []
    for h, (peak, den, dot) in enumerate(combined):
        of_edge = jnp.sum(jnp.where(aims, peak, 0.0), axis=0, keepdims=True)
        weights[pl.ds(h, 1), :] = jnp.exp(logits[pl.ds(h, 1), :] - of_edge)
        den_grad = (-(dot / den) / den).astype(bf16).astype(f32)
        den_grads.append(jnp.sum(jnp.where(aims, den_grad, 0.0), axis=0, keepdims=True))
    den_full = lane_heads([den for peak, den, dot in combined], (slots, LANES))
    for block in range(BLOCKS):
        cols = block_cols(block)
        num_grad[:, cols] = (agg_grad[:, cols] / den_full[:, : cols.size]).astype(bf16)
    picked = mask_to(aims, bf16)
    for degree in range(LMAX + 1):
        ids = pl.ds(degree * degree * CH, (2 * degree + 1) * CH)
        spread_grad[ids, :] = dot_tn(num_grad[:, ids], picked)

    state = {}

    def emit(degree, order, half, value):
        lanes = lane_at(half, edges, False)
        ref, row, second = frame_place(degree, order, (v0, v1, v2))
        product = value * ref[pl.ds(row, CH), lane_at(half, edges, second)]
        if degree == 0:
            state["sum"] = product
            state["spread"] = spread_heads([weights[pl.ds(h, 1), lanes] for h in range(HEADS)])
        else:
            state["sum"] = state["sum"] + product
        grad = (value * state["spread"]).astype(bf16)
        ref, row, second = frame_place(degree, order, (g0, g1, g2))
        ref[pl.ds(row, CH), lane_at(half, edges, second)] = grad
        if order != 0:
            swapped = grad if order < 0 else -grad
            below = row + (DIM1 if abs(order) == 1 else DIM2)
            ref[pl.ds(below, CH), lane_at(half, edges, not second)] = swapped
        if degree == LMAX and order == MMAX:
            for h in range(HEADS):
                part = state["sum"][h * VAL : (h + 1) * VAL]
                weights[pl.ds(HEADS + h, 1), lanes] = jnp.sum(part, axis=0, keepdims=True)

    for load in loads:
        load.wait()
    to_frame(spread_grad, rot, edges, emit)

    hidden = jnp.where(pre[...] > 0, pre[...], leak_slope * pre[...])
    logit_grads = [
        weights[pl.ds(h, 1), :] * (weights[pl.ds(HEADS + h, 1), :] + den_grads[h])
        for h in range(HEADS)
    ]
    tall = jnp.concatenate(
        [jnp.broadcast_to(row, (ALPHA, edges)) for row in logit_grads], axis=0
    )
    slope = jnp.where(pre[...] > 0, 1.0, leak_slope)
    pre_grad = (tall * turned_column(adot[...].astype(f32)) * slope).astype(bf16)
    pre_grad_out[...] = pre_grad
    dot_grad = jnp.sum(tall * hidden, axis=1, keepdims=True)

    top1[...] = g1[pl.ds(0, DIM1), :]
    top2[...] = g2[pl.ds(0, DIM2), :]
    mine = lax.axis_index("edge") & 1
    copies = []

    def put(row, value, at=0):
        for side in range(2):
            low, high = max(at, side * LANES), min(at + value.shape[1], (side + 1) * LANES)
            if low < high:
                piece = value[:, low - at : high - at]
                cols = pl.ds(low - side * LANES, high - low)
                packed[side, pl.ds(row, value.shape[0]), cols] = piece

    def send(chunk, kept, sent):
        start, size = CHUNKS[chunk]
        rows_of = pl.ds(start, size)
        for n, (side, out) in enumerate(((mine, kept), (1 - mine, sent))):
            copy = pltpu.make_async_copy(
                packed.at[side, rows_of, :], out, semaphores.at[2 * chunk + n]
            )
            copy.start()
            copies.append(copy)

    row = 0
    for left, right, dim in ((x1, g1, DIM1), (x2, g2, DIM2)):
        for start in range(0, 2 * dim, PANEL):
            size = min(PANEL, 2 * dim - start)
            put(row, dot_nt(left[...], right[pl.ds(start, size), :]))
            row += dim
    row -= DIM2
    edge_ch = feats.shape[1]
    edge_grad = lax.dot_general(
        feats[...], pre_grad, (((0,), (1,)), ((), ())), preferred_element_type=f32
    )
    put(row, edge_grad[:, :LANES], LANES)
    put(row + edge_ch, edge_grad[:, LANES:], LANES)
    wide_dot = jnp.transpose(jnp.broadcast_to(dot_grad, (HEADS * ALPHA, LANES)))
    spare = DIM2 - 2 * edge_ch
    tail = iota((spare, LANES), 0)
    first = jnp.broadcast_to(wide_dot[:1, :LANES], (spare, LANES))
    second = jnp.broadcast_to(wide_dot[:1, LANES:], (spare, LANES))
    put(row + 2 * edge_ch, jnp.where(tail == 0, first, jnp.where(tail == 1, second, 0.0)), LANES)
    row += DIM2
    put(row, dot_nt(x0[pl.ds(0, CH), :], pre_grad))
    send(0, kept0, sent0)

    row = CHUNKS[1][0]
    for start in range(0, DIM0, PANEL):
        size = min(PANEL, DIM0 - start)
        put(row, dot_nt(x0[...], g0[pl.ds(start, size), :]))
        if size < PANEL:
            put(row, jnp.zeros((DIM0, PANEL - size), f32), size)
        row += DIM0
    send(1, kept1, sent1)
    for copy in copies:
        copy.wait()


PROJ_ROWS = (LMAX // 2 + 1) * CH
CHUNKS = ((0, 3 * DIM1 + 3 * DIM2 + CH), (3 * DIM1 + 3 * DIM2 + CH, 2 * DIM0))
PACKED_ROWS = sum(size for start, size in CHUNKS)


def halves_of(mine, other):
    first = (lax.axis_index("edge") & 1) == 0
    left, right = mine[...].astype(f32), other[...].astype(f32)
    return jnp.where(first, left, right), jnp.where(first, right, left)


def reversed_bits(value, count):
    return sum(((value >> n) & 1) << (count - 1 - n) for n in range(count))


def make_unpack(lanes_total, peers):
    def unpack_kernel(mine, other, zero, one, two, alpha_in, alpha_edge, alpha_dot, proj):
        cols = lanes_total // 2
        col_bits = (cols - 1).bit_length()
        late = PROJ_ROWS // lanes_total
        own_rows = CHUNKS[0][1] // cols
        first_rows = (own_rows + late) // peers
        share = first_rows + CHUNKS[1][1] // (cols * peers)
        main, zeros, tail = [], [], {}
        for core, value in enumerate(halves_of(mine, other)):
            parts, zero_parts = [], {}
            for col in range(cols):
                rows = []
                for peer in range(peers):
                    start = (col * peers + peer) * share
                    rows.append(value[start : start + first_rows])
                    zero_parts[peer * cols + col] = value[start + first_rows : start + share]
                rows = jnp.concatenate(rows, axis=0)
                parts.append(rows[:own_rows])
                tail[core * cols + reversed_bits(col, col_bits)] = rows[own_rows:]
            main.append(jnp.concatenate(parts, axis=0))
            zeros.append(jnp.concatenate([zero_parts[n] for n in sorted(zero_parts)], axis=0))
        tail = jnp.concatenate([tail[n] for n in sorted(tail)], axis=0)
        for degree in range(LMAX + 1):
            piece = tail[degree // 2 * CH : (degree // 2 + 1) * CH]
            proj[degree] = piece[:, degree % 2 * CH : (degree % 2 + 1) * CH].astype(bf16)
        left, right = zeros
        zero[:, pl.ds(0, LANES)] = left[:DIM0].astype(bf16)
        zero[:, pl.ds(LANES, LANES)] = right[:DIM0].astype(bf16)
        zero[:, pl.ds(2 * LANES, LANES)] = left[DIM0:].astype(bf16)
        zero[:, pl.ds(3 * LANES, DIM0 - 3 * LANES)] = right[DIM0:, : DIM0 - 3 * LANES].astype(bf16)
        unpack_rest(*main, one, two, alpha_in, alpha_edge, alpha_dot)

    return unpack_kernel


def unpack_rest(left, right, one, two, alpha_in, alpha_edge, alpha_dot):
    for n in range(2 * DIM1 // LANES):
        panel = (left, right)[n % 2][(n // 2) * DIM1 : (n // 2 + 1) * DIM1]
        per = DIM1 // LANES
        one[n // per, :, pl.ds((n % per) * LANES, LANES)] = panel.astype(bf16)
    left, right = left[3 * DIM1 :], right[3 * DIM1 :]
    panels = [(left, right)[n % 2][(n // 2) * DIM2 : (n // 2 + 1) * DIM2] for n in range(5)]
    whole = jnp.concatenate(panels, axis=1)
    two[0] = whole[:, :DIM2].astype(bf16)
    two[1] = whole[:, DIM2:].astype(bf16)
    edge_ch = alpha_edge.shape[0]
    rest = right[2 * DIM2 : 3 * DIM2]
    alpha_edge[:, pl.ds(0, LANES)] = rest[:edge_ch].astype(bf16)
    alpha_edge[:, pl.ds(LANES, LANES)] = rest[edge_ch : 2 * edge_ch].astype(bf16)
    alpha_dot[...] = rest[2 * edge_ch : 2 * edge_ch + 2].astype(bf16)
    alpha_in[:, pl.ds(0, LANES)] = left[3 * DIM2 :].astype(bf16)
    alpha_in[:, pl.ds(LANES, LANES)] = right[3 * DIM2 :].astype(bf16)


def source_kernel(
    source_slot, lists, rot, g0, g1, g2, pre_grad, wzero, wone, wtwo, ain,
    *rest,
):
    sums_out, d0, d1, d2, terms = rest[-5:]
    edges = source_slot.shape[1]
    slots = sums_out.shape[0] * sums_out.shape[1]
    d0[...] = dot_nn(wzero[...], g0[...])
    d0[pl.ds(0, CH), :] += dot_nn(ain[...], pre_grad[...])
    for out, weight, value in ((d1, wone, g1[...]), (d2, wtwo, g2[...])):
        out[...] = dot_nn(weight[0], value) - swapped_halves(dot_nn(weight[1], value), edges)

    def load(degree, order, half):
        ref, row, second = frame_place(degree, order, (d0, d1, d2))
        return ref[pl.ds(row, CH), lane_at(half, edges, second)]

    terms[pl.ds(FLAT, COLS - FLAT), :] = jnp.zeros((COLS - FLAT, 2 * edges), bf16)
    from_frame(load, rot, edges, store_terms(terms, edges))
    slot_sums(terms, mask_to(one_hot_rows(source_slot, sums_out.shape[0], slots), bf16), sums_out)
    put_rows(sums_out, pl.ds(COLS, LANES), lists[...])


def make_collect(lanes_total):
    def collect_kernel(*rest):
        arrivals = rest[:lanes_total]
        out, rows = rest[lanes_total:]
        atoms = out.shape[1]
        total = rows.shape[0]
        collect_rows(arrivals, rows)
        index = rows[:, pl.ds(COLS, LANES)][:, 1:2]
        picked = mask_to(iota((total, atoms), 1).astype(f32) == index, bf16)
        twice = jnp.concatenate([picked, picked], axis=0)
        for block in range(BLOCKS):
            high, low = split_two(rows[:, pl.ds(block * LANES, LANES)])
            sums = dot_tn(twice, jnp.concatenate([high, low], axis=0)).astype(bf16)
            out[2 * block] = sums[:, :CH]
            if 2 * block + 1 < COEFFS:
                out[2 * block + 1] = sums[:, CH:]

    return collect_kernel


vmem = pl.BlockSpec(memory_space=pltpu.VMEM)
smem = pl.BlockSpec(memory_space=pltpu.SMEM)
anywhere = pl.BlockSpec(memory_space=pl.ANY)


def call(kernel, outs, scratch, *args, scalars=0, far=(), apart=(), after=()):
    specs = [smem if n < scalars else anywhere if n in far else vmem for n in range(len(args))]
    specs += [anywhere] * len(after)
    out_specs = [anywhere if n in apart else vmem for n in range(len(outs))]
    shapes = [pltpu.VMEM(*entry) if isinstance(entry, tuple) else entry for entry in scratch]
    return pl.pallas_call(
        kernel,
        out_shape=[jax.ShapeDtypeStruct(shape, kind) for shape, kind in outs],
        in_specs=specs,
        out_specs=out_specs,
        scratch_shapes=shapes,
        compiler_params=pltpu.CompilerParams(vmem_limit_bytes=VMEM_LIMIT),
        cost_estimate=pl.CostEstimate(flops=1, bytes_accessed=1, transcendentals=0),
    )(*args, *after)


class Order:
    def __init__(self):
        self.last = None

    def hold(self, value):
        if self.last is None:
            return value
        return lax.optimization_barrier((value, self.last))[0]

    def mark(self, value):
        self.last = value
        return value


def turned_column(row):
    return jnp.transpose(jnp.broadcast_to(row, (8, row.shape[1])))[:, :1]


def swap(value, axis, bit):
    size = lax.axis_size(axis)
    return lax.ppermute(value, axis, [(i, i ^ (1 << bit)) for i in range(size)])


def bits_of(axis):
    return (lax.axis_size(axis) - 1).bit_length()


def gather_lanes(value, order):
    held = {0: value}
    for bit in reversed(range(bits_of("edge"))):
        fresh = {}
        for k, v in held.items():
            fresh[k | (1 << bit)] = swap(order.hold(v) if k else v, "edge", bit)
        held.update(fresh)
        yield
    return [held[k] for k in range(len(held))]


def own_bit(axis, bit):
    return (lax.axis_index(axis) >> bit) & 1


def share_steps(first):
    steps = [("edge", n) for n in range(1, bits_of("edge"))]
    steps += [("graph", n) for n in range(bits_of("graph"))]
    return sorted(steps, key=lambda step: step[0] != first)


def halve(kept, sent, first, order, late=None):
    other = swap(sent, "edge", 0)
    yield
    current = kept + order.hold(other)
    for n, (axis, bit) in enumerate(share_steps(first)):
        if late is not None and n == bits_of("edge") - 1:
            current = jnp.concatenate([current, late[0]], axis=0)
        mine = own_bit(axis, bit)
        parts = current.reshape(2, current.shape[0] // 2, -1)
        sent = order.mark(lax.dynamic_index_in_dim(parts, 1 - mine, 0, False))
        other = swap(sent, axis, bit)
        yield
        current = lax.dynamic_index_in_dim(parts, mine, 0, False) + order.hold(other)
    return order.mark(current.astype(bf16))


def double(current, order):
    for axis, bit in reversed(share_steps("edge")):
        mine = own_bit(axis, bit)
        other = swap(current, axis, bit)
        yield
        other = order.hold(other)
        current = order.mark(
            jnp.concatenate(
                [jnp.where(mine == 0, current, other), jnp.where(mine == 0, other, current)],
                axis=0,
            )
        )
    return current, swap(current, "edge", 0)


def finish_steps(chain):
    while True:
        try:
            next(chain)
        except StopIteration as end:
            return end.value


def shards(
    atom_embed, out_cotangent, send_rows, recv_rows, source_slot, target_slot, rotation,
    edge_feats, edge_bias, conv_zero, conv_one, conv_two, alpha_in, alpha_edge, alpha_dot,
    out_proj,
):
    peers = lax.axis_size("graph")
    lanes_total = lax.axis_size("edge")
    atoms = atom_embed.shape[0]
    edges = rotation.shape[0]
    cap = send_rows.shape[3]
    slots = peers * cap
    blocks = peers * lanes_total
    direct = is_direct(peers)
    order = Order()

    def exchange(value):
        return lax.all_to_all(value, "graph", split_axis=0, concat_axis=0, tiled=True)

    cot = jnp.transpose(out_cotangent, (1, 0, 2))
    outgoing = call(
        outgoing_kernel, [((cap, TABLE), bf16)] * peers, [],
        send_rows, recv_rows, jnp.transpose(atom_embed, (1, 0, 2)), cot,
        scalars=2
    )
    if direct:
        tables = [outgoing[0]] + [
            lax.ppermute(outgoing[k], "graph", [(i, i ^ k) for i in range(peers)])
            for k in range(1, peers)
        ]
    else:
        tables = list(exchange(jnp.stack(outgoing)))

    source_row = source_slot.reshape(1, edges)
    target_row = target_slot.reshape(1, edges)
    bias = edge_bias.T
    adot = alpha_dot.reshape(1, -1)

    frames = [
        ((DIM0, edges), bf16),
        ((DIM1, 2 * edges), bf16),
        ((DIM2, 2 * edges), bf16),
        ((DIM0, edges), f32),
        ((DIM1, 2 * edges), f32),
        ((DIM2, 2 * edges), f32),
    ]
    pre_shape = ((HEADS * ALPHA, edges), f32)
    sums, stats, x0, x1, x2, v0, v1, v2, pre, logits, lists, agg_grad, rot, own_stats = call(
        make_forward(atoms, peers),
        [((peers, cap, WIDE), f32), ((slots // 8, LANES), f32)]
        + frames
        + [
            pre_shape,
            ((8, edges), f32),
            ((slots, LANES), f32),
            ((slots, FLAT), f32),
            ((rotation.shape[1], edges), f32),
            ((slots, LANES), f32),
        ],
        [
            ((slots, TABLE), f32),
            ((FLAT, edges), f32),
            ((8, edges), f32),
            ((COLS, 2 * edges), bf16),
            (conv_zero.shape, bf16),
            (conv_one.shape, bf16),
            (conv_two.shape, bf16),
        ]
        + frames
        + [pre_shape, pltpu.SemaphoreType.DMA((10,))],
        source_row, target_row, rotation, edge_feats, bias,
        conv_zero, conv_one, conv_two, alpha_in, alpha_edge, adot, out_proj, *tables,
        far=(5, 6, 7), apart=range(2, 9)
    )
    if direct:
        lanes_stats = [stats] + [
            lax.ppermute(stats, "edge", [(i, i ^ k) for i in range(lanes_total)])
            for k in range(1, lanes_total)
        ]
        graph_stats = jnp.concatenate(lanes_stats, axis=0)
        all_stats = [graph_stats] + [
            lax.ppermute(graph_stats, "graph", [(i, i ^ k) for i in range(peers)])
            for k in range(1, peers)
        ]
    else:
        all_stats = [lax.all_gather(stats, ("graph", "edge"), tiled=True)]

    halves = [((size, LANES), f32) for start, size in CHUNKS for _ in range(2)]
    g0, g1, g2, pre_grad, *halves = call(
        make_gradient(peers, len(all_stats)),
        [
            ((DIM0, edges), bf16),
            ((DIM1, 2 * edges), bf16),
            ((DIM2, 2 * edges), bf16),
            ((HEADS * ALPHA, edges), bf16),
        ]
        + halves,
        [
            ((slots, FLAT), bf16),
            ((FLAT, edges), f32),
            ((8, edges), f32),
            ((2 * DIM1, 2 * edges), bf16),
            ((2 * DIM2, 2 * edges), bf16),
            ((2, PACKED_ROWS, LANES), f32),
        ]
        + frames
        + [pltpu.SemaphoreType.DMA((10,))],
        *all_stats, own_stats, agg_grad, target_row, rot, edge_feats,
        x0, x1, x2, v0, v1, v2, pre, logits, adot,
        far=range(len(all_stats) + 5, len(all_stats) + 11), apart=range(4, 8)
    )

    total = lanes_total * slots
    order.mark(halves[0])
    messages = exchange(order.hold(sums))
    late = []
    rest_steps = halve(halves[0], halves[1], "edge", order, late)
    zero_steps = halve(halves[2], halves[3], "graph", order)
    next(rest_steps)
    next(zero_steps)
    next(rest_steps)
    next(zero_steps)
    message_hops = gather_lanes(order.hold(messages), order)
    next(message_hops)
    (source_sums,) = call(
        source_kernel,
        [((peers, cap, WIDE), f32)],
        [
            ((DIM0, edges), f32),
            ((DIM1, 2 * edges), f32),
            ((DIM2, 2 * edges), f32),
            ((COLS, 2 * edges), bf16),
        ],
        source_row, lists, rot, g0, g1, g2, order.hold(pre_grad),
        conv_zero, conv_one, conv_two, alpha_in
    )
    order.mark(source_sums)
    returned = exchange(source_sums)
    next(zero_steps)
    message_rows = finish_steps(message_hops)
    out, proj = call(
        make_finish(lanes_total),
        [((COEFFS, atoms, CH), bf16), ((PROJ_ROWS, LANES), f32)],
        [((total, WIDE), f32), ((2 * total, COLS), bf16), ((COEFFS, atoms, CH), bf16)],
        order.hold(cot), out_proj, *message_rows,
    )
    order.mark(proj)
    lane = lax.axis_index("edge")
    late_rows = PROJ_ROWS // lanes_total
    place = ((lane & 1) * (lanes_total // 2) + (lane >> 1)) * late_rows
    late.append(lax.dynamic_slice_in_dim(proj, place, late_rows, 0))
    for _ in range(bits_of("edge") - 1):
        next(rest_steps)
    source_hops = gather_lanes(order.mark(order.hold(returned)), order)
    next(source_hops)
    next(zero_steps)
    next(rest_steps)
    zero_share = finish_steps(zero_steps)
    source_rows = finish_steps(source_hops)
    share = jnp.concatenate([finish_steps(rest_steps), zero_share], axis=0)
    doubling = double(order.mark(share), order)
    next(doubling)
    for _ in share_steps("edge")[1:]:
        next(doubling)
    (embed,) = call(
        make_collect(lanes_total),
        [((COEFFS, atoms, CH), bf16)],
        [((total, WIDE), f32)],
        order.hold(source_rows[0]), *source_rows[1:],
    )
    order.mark(embed)
    mine, other = finish_steps(doubling)
    zero, one, two, grad_in, grad_edge, grad_dot, grad_proj = call(
        make_unpack(lanes_total, peers),
        [
            ((DIM0, DIM0), bf16),
            ((2, DIM1, DIM1), bf16),
            ((2, DIM2, DIM2), bf16),
            (alpha_in.shape, bf16),
            (alpha_edge.shape, bf16),
            ((2, LANES), bf16),
            (out_proj.shape, bf16),
        ],
        [],
        mine, other,
    )

    def shaped(value):
        return jnp.transpose(value, (1, 0, 2))

    return (
        shaped(out), shaped(embed), zero, one, two, grad_in, grad_edge, grad_dot.reshape(-1),
        grad_proj,
    )


def solution(mesh):
    in_specs = (
        P(("groups", "graph"), None, None),
        P(("groups", "graph"), None, None),
        P(("groups", "graph"), None, "edge", None),
        P(("groups", "graph"), None, "edge", None),
        P(("groups", "graph", "edge")),
        P(("groups", "graph", "edge")),
        P(("groups", "graph", "edge"), None),
        P(("groups", "graph", "edge"), None),
        P(("groups", "graph", "edge"), None),
        P(),
        P(),
        P(),
        P(),
        P(),
        P(),
        P(),
    )
    out_specs = (
        P(("groups", "graph"), None, None),
        P(("groups", "graph"), None, None),
        P("groups", None),
        P("groups", None, None),
        P("groups", None, None),
        P("groups", None),
        P("groups", None),
        P("groups"),
        P("groups", None, None),
    )
    return jax.shard_map(shards, mesh=mesh, in_specs=in_specs, out_specs=out_specs, check_vma=False)
```

```python
import jax
import jax.numpy as jnp
import numpy as np
from jax import lax
from jax.experimental import pallas as pl
from jax.experimental.pallas import tpu as pltpu
from jax.sharding import PartitionSpec as P

LMAX = 6
MMAX = 2
CH = 64
HEADS = 4
VAL = 16
ALPHA = 64
COEFFS = (LMAX + 1) * (LMAX + 1)
FLAT = COEFFS * CH
LANES = 128
BLOCKS = (FLAT + LANES - 1) // LANES
COLS = BLOCKS * LANES
WIDE = COLS + LANES
TABLE = 2 * COLS + LANES
PEAK_AT, DOT_AT, NAME_AT = HEADS, 2 * HEADS, 3 * HEADS
STATS = 16
DIM0 = (LMAX + 1) * CH
DIM1 = LMAX * CH
DIM2 = (LMAX - 1) * CH
PANEL = 256

leak_slope = 0.2
floor_value = -1e30
bf16 = jnp.bfloat16
f32 = jnp.float32

VMEM_LIMIT = 56 * 1024 * 1024


def degree_blocks():
    result = []
    offset = 0
    for degree in range(LMAX + 1):
        centre = min(degree, MMAX)
        row_total = 2 * centre + 1
        col_total = 2 * degree + 1
        result.append((degree, centre, row_total, col_total, offset))
        offset += row_total * col_total
    return result


def degree_of(coeff):
    return int(np.sqrt(coeff))


def dot_nn(left, right):
    return jnp.dot(left, right, preferred_element_type=f32)


def dot_nt(left, right):
    return lax.dot_general(left, right, (((1,), (1,)), ((), ())), preferred_element_type=f32)


def dot_tn(left, right):
    return lax.dot_general(left, right, (((0,), (0,)), ((), ())), preferred_element_type=f32)


def iota(shape, dim):
    return lax.broadcasted_iota(jnp.int32, shape, dim)


def split_two(value):
    high = value.astype(bf16)
    return high, (value - high.astype(f32)).astype(bf16)


def to_frame(source, rot, edges, emit):
    for half in range(edges // LANES):
        lanes = pl.ds(half * LANES, LANES)
        for degree, centre, row_total, col_total, offset in degree_blocks():
            sums = [None] * row_total
            for j in range(col_total):
                column = source[pl.ds((degree * degree + j) * CH, CH), lanes]
                for i in range(row_total):
                    term = rot[pl.ds(offset + i * col_total + j, 1), lanes] * column
                    sums[i] = term if j == 0 else sums[i] + term
            for i in range(row_total):
                emit(degree, i - centre, half, sums[i])


def from_frame(load, rot, edges, emit):
    for half in range(edges // LANES):
        lanes = pl.ds(half * LANES, LANES)
        for degree, centre, row_total, col_total, offset in degree_blocks():
            rows = [load(degree, i - centre, half) for i in range(row_total)]
            for j in range(col_total):
                total = None
                for i in range(row_total):
                    term = rot[pl.ds(offset + i * col_total + j, 1), lanes] * rows[i]
                    total = term if i == 0 else total + term
                emit(degree * degree + j, half, total)


def lane_at(half, edges, second):
    return pl.ds(half * LANES + (edges if second else 0), LANES)


def frame_place(degree, order, refs):
    if order == 0:
        return refs[0], degree * CH, False
    which = abs(order)
    return refs[which], (degree - which) * CH, order < 0


def spread_heads(rows):
    return jnp.concatenate(
        [jnp.broadcast_to(row, (VAL, row.shape[1])) for row in rows], axis=0
    )


def is_direct(peers):
    return peers <= 4


def flip_of(peers):
    return lax.axis_index("graph") if is_direct(peers) else 0


def one_hot_rows(slot_ref, peers, slots):
    edges = slot_ref.shape[1]
    first = flip_of(peers) * (slots // peers)
    return jnp.bitwise_xor(iota((slots, edges), 0), first) == slot_ref[...]


def mask_to(mask, dtype):
    return jnp.where(mask, 1.0, 0.0).astype(dtype)


def stack_table(tables, rows_ref):
    cap = tables[0].shape[0]
    per = 8 // cap
    for n in range(0, len(tables), per):
        parts = [table[...].astype(f32) for table in tables[n : n + per]]
        rows_ref[pl.ds(n * cap, 8), :] = jnp.concatenate(parts, axis=0)


def put_rows(out_ref, cols, value):
    peers, cap = out_ref.shape[0], out_ref.shape[1]
    flip = flip_of(peers)
    for n in range(peers):
        place = jnp.bitwise_xor(flip, n) if is_direct(peers) else n
        out_ref[place, :, cols] = value[n * cap : (n + 1) * cap].astype(out_ref.dtype)


def slot_sums(terms, one_hot, out_ref, factor=None):
    both = jnp.concatenate([one_hot, one_hot], axis=1)
    products = 0.0
    for start in range(0, COLS, PANEL):
        size = min(PANEL, COLS - start)
        sums = dot_nt(both, terms[pl.ds(start, size), :])
        put_rows(out_ref, pl.ds(start, size), sums)
        if factor is None:
            continue
        for at in range(0, size, LANES):
            width = min(LANES, FLAT - start - at)
            product = sums[:, at : at + width] * factor[:, pl.ds(start + at, width)]
            if width < LANES:
                product = jnp.concatenate([product, jnp.zeros_like(product)], axis=1)
            products = products + product
    return products


def store_terms(terms, edges):
    def emit(coeff, half, value):
        high, low = split_two(value)
        rows = pl.ds(coeff * CH, CH)
        terms[rows, lane_at(half, edges, False)] = high
        terms[rows, lane_at(half, edges, True)] = low

    return emit


def listed_rows(list_ref, shape):
    peers, cap = list_ref.shape[1], list_ref.shape[3]
    flip = flip_of(peers)
    row = iota(shape, 0)
    result = jnp.zeros(shape, jnp.int32)
    for slot in range(peers * cap):
        owner = jnp.bitwise_xor(flip, slot // cap) if is_direct(peers) else slot // cap
        result = jnp.where(row == slot, list_ref[0, owner, 0, slot % cap], result)
    return result


def put_coeffs(outs, first, coeff_rows):
    for block in range(BLOCKS):
        left = coeff_rows(2 * block)
        right = coeff_rows(2 * block + 1) if 2 * block + 1 < COEFFS else jnp.zeros_like(left)
        put_pieces(outs, first + block * LANES, jnp.concatenate([left, right], axis=1))


def put_pieces(outs, first, value):
    cap = outs[0].shape[0]
    for n, out in enumerate(outs):
        out[:, pl.ds(first, LANES)] = value[n * cap : (n + 1) * cap].astype(out.dtype)


def outgoing_kernel(send, recv, embed, cot, *outs):
    atoms = embed.shape[1]
    slots = send.shape[1] * send.shape[3]
    sent = listed_rows(send, (slots, LANES))
    received = listed_rows(recv, (slots, LANES))
    for first, listed, values in ((0, sent, embed), (COLS, received, cot)):
        picked = mask_to(iota((slots, atoms), 1) == listed[:, :atoms], bf16)
        put_coeffs(outs, first, lambda k: dot_nn(picked, values[k]))
    lane = iota((slots, LANES), 1)
    side = jnp.where(lane == 0, received, jnp.where(lane == 1, sent, 0))
    put_pieces(outs, 2 * COLS, side.astype(f32))


def swapped_halves(value, edges):
    return jnp.concatenate([-value[:, edges:], value[:, :edges]], axis=1)


def make_forward(atoms, peers):
    def forward_kernel(
        source_slot, target_slot, rotation, feats, bias, wzero_at, wone_at, wtwo_at,
        ain, aedge, adot, out_proj, *rest,
    ):
        tables, rest = rest[:peers], rest[peers:]
        (
        sums_out, stats_out, x0_at, x1_at, x2_at, v0_at, v1_at, v2_at, pre_at, logit_out,
        lists_out, agg_grad, rot, own_out,
        rows, gathered, weights, terms, wzero, wone, wtwo, x0, x1, x2, v0, v1, v2, pre_out,
        semaphores,
        ) = rest
        copies = []

        def move(source, target):
            copy = pltpu.make_async_copy(source, target, semaphores.at[len(copies)])
            copy.start()
            copies.append(copy)

        move(wzero_at, wzero)
        move(wone_at, wone)
        move(wtwo_at, wtwo)
        rot[...] = jnp.transpose(rotation[...].astype(f32))
        edges = source_slot.shape[1]
        cap = tables[0].shape[0]
        slots = peers * cap
        stack_table(tables, rows)
        picked = mask_to(one_hot_rows(source_slot, peers, slots), bf16)
        for degree in range(LMAX + 1):
            ids = pl.ds(degree * degree * CH, (2 * degree + 1) * CH)
            gathered[ids, :] = dot_tn(rows[:, ids].astype(bf16), picked)
        lists = rows[:, pl.ds(2 * COLS, LANES)]
        lists_out[...] = lists
        for degree in range(LMAX + 1):
            ids = range(degree * degree, (degree + 1) * (degree + 1))
            cot = jnp.concatenate([rows[:, pl.ds(COLS + k * CH, CH)] for k in ids], axis=0)
            grad = dot_nt(cot.astype(bf16), out_proj[degree])
            for n, k in enumerate(ids):
                agg_grad[:, pl.ds(k * CH, CH)] = grad[n * slots : (n + 1) * slots]

        def emit(degree, order, half, value):
            ref, row, second = frame_place(degree, order, (x0, x1, x2))
            ref[pl.ds(row, CH), lane_at(half, edges, second)] = value.astype(bf16)

        to_frame(gathered, rot, edges, emit)
        for source, target in ((x0, x0_at), (x1, x1_at), (x2, x2_at)):
            move(source, target)

        pre = dot_tn(ain[...], x0[pl.ds(0, CH), :]) + lax.dot_general(
            aedge[...], feats[...], (((0,), (1,)), ((), ())), preferred_element_type=f32
        )
        pre_out[...] = pre
        move(pre_out, pre_at)
        hidden = jnp.where(pre > 0, pre, leak_slope * pre) * turned_column(adot[...].astype(f32))
        aims = one_hot_rows(target_slot, peers, slots)
        lane = iota((slots, LANES), 1)
        peer = jnp.bitwise_xor(iota((slots, 1), 0) // cap, flip_of(peers))
        name = lists[:, :1] + (peer * atoms).astype(f32)
        side = jnp.where(lane == NAME_AT, name, 0.0)
        for h in range(HEADS):
            logit = jnp.sum(hidden[h * ALPHA : (h + 1) * ALPHA], axis=0, keepdims=True)
            logit = logit + bias[pl.ds(h, 1), :]
            logit_out[pl.ds(h, 1), :] = logit
            peak = jnp.max(jnp.where(aims, logit, floor_value), axis=1, keepdims=True)
            of_edge = jnp.sum(jnp.where(aims, peak, 0.0), axis=0, keepdims=True)
            weight = jnp.exp(logit - of_edge)
            weights[pl.ds(h, 1), :] = weight
            den = jnp.sum(jnp.where(aims, weight, 0.0), axis=1, keepdims=True)
            side = jnp.where(lane == h, den, jnp.where(lane == PEAK_AT + h, peak, side))

        for copy in copies[:3]:
            copy.wait()
        v0[...] = dot_tn(wzero[...], x0[...])
        for out, weight, value in ((v1, wone, x1[...]), (v2, wtwo, x2[...])):
            out[...] = dot_tn(weight[0], value) + swapped_halves(dot_tn(weight[1], value), edges)
        for source, target in ((v0, v0_at), (v1, v1_at), (v2, v2_at)):
            move(source, target)

        def load(degree, order, half):
            ref, row, second = frame_place(degree, order, (v0, v1, v2))
            return ref[pl.ds(row, CH), lane_at(half, edges, second)]

        store = store_terms(terms, edges)

        def weigh(coeff, half, value):
            lanes = lane_at(half, edges, False)
            spread = spread_heads([weights[pl.ds(h, 1), lanes] for h in range(HEADS)])
            store(coeff, half, value * spread)

        terms[pl.ds(FLAT, COLS - FLAT), :] = jnp.zeros((COLS - FLAT, 2 * edges), bf16)
        from_frame(load, rot, edges, weigh)
        dots = slot_sums(terms, mask_to(aims, bf16), sums_out, agg_grad)
        head = (lane % CH) // VAL
        for h in range(HEADS):
            dot = jnp.sum(jnp.where(head == h, dots, 0.0), axis=1, keepdims=True)
            side = jnp.where(lane == DOT_AT + h, dot, side)
        put_rows(sums_out, pl.ds(COLS, LANES), side)
        own_out[...] = side
        spread = jnp.concatenate([side[:, :STATS]] * (LANES // STATS), axis=1)
        spread = jnp.where(lane // STATS == iota((slots, LANES), 0) % 8, spread, 0.0)
        packed = jnp.sum(spread.reshape(slots // 8, 8, LANES), axis=1)

        stats_out[...] = packed
        for copy in copies[3:]:
            copy.wait()

    return forward_kernel


def lane_heads(values, shape):
    head = (iota(shape, 1) % CH) // VAL
    result = jnp.broadcast_to(values[0], shape)
    for h in range(1, HEADS):
        result = jnp.where(head == h, values[h], result)
    return result


def collect_rows(arrivals, rows_ref):
    own = lax.axis_index("edge")
    for k, arrival in enumerate(arrivals):
        peers, cap, width = arrival.shape
        base = (own ^ k) * (peers * cap)
        for start in range(0, peers * cap, 8):
            parts = [arrival[g] for g in range(start // cap, (start + 8) // cap)]
            at = pl.ds(pl.multiple_of(base + start, 8), 8)
            rows_ref[at, :] = jnp.concatenate(parts, axis=0)


def block_cols(block):
    return pl.ds(block * LANES, min(LANES, FLAT - block * LANES))


def make_finish(lanes_total):
    def finish_kernel(cot, out_proj, *rest):
        arrivals = rest[:lanes_total]
        out, proj, rows, terms, agg_low = rest[lanes_total:]
        atoms = cot.shape[1]
        total = rows.shape[0]
        collect_rows(arrivals, rows)
        side = rows[:, pl.ds(COLS, LANES)]
        owner = (lax.axis_index("graph") * atoms).astype(f32)
        names = iota((total, atoms), 1).astype(f32) + owner == side[:, NAME_AT : NAME_AT + 1]
        eye = iota((atoms, atoms), 0) == iota((atoms, atoms), 1)
        scales, dens = [], []
        for h in range(HEADS):
            peak_rows = side[:, PEAK_AT + h : PEAK_AT + h + 1]
            peak = jnp.max(jnp.where(names, peak_rows, floor_value), axis=0, keepdims=True)
            of_row = jnp.sum(jnp.where(names, peak, 0.0), axis=1, keepdims=True)
            scale = jnp.exp(peak_rows - of_row)
            scaled_den = side[:, h : h + 1] * scale
            den = jnp.sum(jnp.where(names, scaled_den, 0.0), axis=0, keepdims=True)
            scales.append(scale)
            dens.append(jnp.sum(jnp.where(eye, den, 0.0), axis=1, keepdims=True))
        scale_full = lane_heads(scales, (total, LANES))
        den_full = lane_heads(dens, (atoms, LANES))
        picked = mask_to(names, bf16)
        twice = jnp.concatenate([picked, picked], axis=0)
        for block in range(BLOCKS):
            cols = pl.ds(block * LANES, LANES)
            high, low = split_two(rows[:, cols] * scale_full)
            terms[pl.ds(0, total), cols] = high
            terms[pl.ds(total, total), cols] = low
        for block in range(BLOCKS):
            cols = pl.ds(block * LANES, LANES)
            agg = (dot_tn(twice, terms[:, cols]) / den_full).astype(bf16)
            agg_low[2 * block] = agg[:, :CH]
            if 2 * block + 1 < COEFFS:
                agg_low[2 * block + 1] = agg[:, CH:]
        for degree in range(LMAX + 1):
            ids = pl.ds(degree * degree, 2 * degree + 1)
            stacked = ((2 * degree + 1) * atoms, CH)
            left = agg_low[ids].reshape(stacked)
            right = cot[ids].reshape(stacked)
            value = dot_nn(left, out_proj[degree]).astype(bf16)
            out[ids] = value.reshape((2 * degree + 1, atoms, CH))
            at = (pl.ds(degree // 2 * CH, CH), pl.ds(degree % 2 * CH, CH))
            proj[at] = dot_tn(left, right)
        proj[pl.ds(LMAX // 2 * CH, CH), pl.ds(CH, CH)] = jnp.zeros((CH, CH), f32)

    return finish_kernel


def combine_stats(stats, own):
    chunk = 32
    name = own[:, NAME_AT : NAME_AT + 1]

    def part(part_rows):
        entries = [part_rows[:, n : n + STATS] for n in range(0, LANES, STATS)]
        turned = jnp.transpose(jnp.concatenate(entries, axis=0))
        same = name == turned[NAME_AT : NAME_AT + 1]
        result = []
        for h in range(HEADS):
            peaks = turned[PEAK_AT + h : PEAK_AT + h + 1]
            peak = jnp.max(jnp.where(same, peaks, floor_value), axis=1, keepdims=True)
            scale = jnp.where(same, jnp.exp(jnp.where(same, peaks - peak, 0.0)), 0.0)
            den = jnp.sum(turned[h : h + 1] * scale, axis=1, keepdims=True)
            dot = jnp.sum(turned[DOT_AT + h : DOT_AT + h + 1] * scale, axis=1, keepdims=True)
            result += [peak, den, dot]
        return tuple(result)

    def step(at, held):
        fresh = part(stats[0][pl.ds(pl.multiple_of(at * chunk, chunk), chunk), :])
        result = []
        for h in range(HEADS):
            peak, den, dot = held[3 * h : 3 * h + 3]
            new_peak, new_den, new_dot = fresh[3 * h : 3 * h + 3]
            most = jnp.maximum(peak, new_peak)
            old, new = jnp.exp(peak - most), jnp.exp(new_peak - most)
            result += [most, den * old + new_den * new, dot * old + new_dot * new]
        return tuple(result)

    if len(stats) > 1:
        held = part(jnp.concatenate([rows[...] for rows in stats], axis=0))
    else:
        held = part(stats[0][pl.ds(0, chunk), :])
        held = lax.fori_loop(1, stats[0].shape[0] // chunk, step, held)
    return [held[3 * h : 3 * h + 3] for h in range(HEADS)]


def make_gradient(peers, parts):
    def kernel(*refs):
        gradient_kernel(peers, refs[:parts], *refs[parts:])

    return kernel


def gradient_kernel(
    peers, stats, own, agg_grad, target_slot, rot, feats,
    x0_at, x1_at, x2_at, v0_at, v1_at, v2_at, pre, logits, adot,
    g0, top1, top2, pre_grad_out, kept0, sent0, kept1, sent1,
    num_grad, spread_grad, weights, g1, g2, packed, x0, x1, x2, v0, v1, v2, semaphores,
):
    loads = []
    for source, target in (
        (v0_at, v0), (v1_at, v1), (v2_at, v2), (x0_at, x0), (x1_at, x1), (x2_at, x2)
    ):
        load = pltpu.make_async_copy(source, target, semaphores.at[4 + len(loads)])
        load.start()
        loads.append(load)
    edges = target_slot.shape[1]
    slots = agg_grad.shape[0]
    aims = one_hot_rows(target_slot, peers, slots)
    combined = combine_stats(stats, own[...])
    den_grads = []
    for h, (peak, den, dot) in enumerate(combined):
        of_edge = jnp.sum(jnp.where(aims, peak, 0.0), axis=0, keepdims=True)
        weights[pl.ds(h, 1), :] = jnp.exp(logits[pl.ds(h, 1), :] - of_edge)
        den_grad = (-(dot / den) / den).astype(bf16).astype(f32)
        den_grads.append(jnp.sum(jnp.where(aims, den_grad, 0.0), axis=0, keepdims=True))
    den_full = lane_heads([den for peak, den, dot in combined], (slots, LANES))
    for block in range(BLOCKS):
        cols = block_cols(block)
        num_grad[:, cols] = (agg_grad[:, cols] / den_full[:, : cols.size]).astype(bf16)
    picked = mask_to(aims, bf16)
    for degree in range(LMAX + 1):
        ids = pl.ds(degree * degree * CH, (2 * degree + 1) * CH)
        spread_grad[ids, :] = dot_tn(num_grad[:, ids], picked)

    state = {}

    def emit(degree, order, half, value):
        lanes = lane_at(half, edges, False)
        ref, row, second = frame_place(degree, order, (v0, v1, v2))
        product = value * ref[pl.ds(row, CH), lane_at(half, edges, second)]
        if degree == 0:
            state["sum"] = product
            state["spread"] = spread_heads([weights[pl.ds(h, 1), lanes] for h in range(HEADS)])
        else:
            state["sum"] = state["sum"] + product
        grad = (value * state["spread"]).astype(bf16)
        ref, row, second = frame_place(degree, order, (g0, g1, g2))
        ref[pl.ds(row, CH), lane_at(half, edges, second)] = grad
        if order != 0:
            swapped = grad if order < 0 else -grad
            below = row + (DIM1 if abs(order) == 1 else DIM2)
            ref[pl.ds(below, CH), lane_at(half, edges, not second)] = swapped
        if degree == LMAX and order == MMAX:
            for h in range(HEADS):
                part = state["sum"][h * VAL : (h + 1) * VAL]
                weights[pl.ds(HEADS + h, 1), lanes] = jnp.sum(part, axis=0, keepdims=True)

    for load in loads:
        load.wait()
    to_frame(spread_grad, rot, edges, emit)

    hidden = jnp.where(pre[...] > 0, pre[...], leak_slope * pre[...])
    logit_grads = [
        weights[pl.ds(h, 1), :] * (weights[pl.ds(HEADS + h, 1), :] + den_grads[h])
        for h in range(HEADS)
    ]
    tall = jnp.concatenate(
        [jnp.broadcast_to(row, (ALPHA, edges)) for row in logit_grads], axis=0
    )
    slope = jnp.where(pre[...] > 0, 1.0, leak_slope)
    pre_grad = (tall * turned_column(adot[...].astype(f32)) * slope).astype(bf16)
    pre_grad_out[...] = pre_grad
    dot_grad = jnp.sum(tall * hidden, axis=1, keepdims=True)

    top1[...] = g1[pl.ds(0, DIM1), :]
    top2[...] = g2[pl.ds(0, DIM2), :]
    mine = lax.axis_index("edge") & 1
    copies = []

    def put(row, value, at=0):
        for side in range(2):
            low, high = max(at, side * LANES), min(at + value.shape[1], (side + 1) * LANES)
            if low < high:
                piece = value[:, low - at : high - at]
                cols = pl.ds(low - side * LANES, high - low)
                packed[side, pl.ds(row, value.shape[0]), cols] = piece

    def send(chunk, kept, sent):
        start, size = CHUNKS[chunk]
        rows_of = pl.ds(start, size)
        for n, (side, out) in enumerate(((mine, kept), (1 - mine, sent))):
            copy = pltpu.make_async_copy(
                packed.at[side, rows_of, :], out, semaphores.at[2 * chunk + n]
            )
            copy.start()
            copies.append(copy)

    row = 0
    for left, right, dim in ((x1, g1, DIM1), (x2, g2, DIM2)):
        for start in range(0, 2 * dim, PANEL):
            size = min(PANEL, 2 * dim - start)
            put(row, dot_nt(left[...], right[pl.ds(start, size), :]))
            row += dim
    row -= DIM2
    edge_ch = feats.shape[1]
    edge_grad = lax.dot_general(
        feats[...], pre_grad, (((0,), (1,)), ((), ())), preferred_element_type=f32
    )
    put(row, edge_grad[:, :LANES], LANES)
    put(row + edge_ch, edge_grad[:, LANES:], LANES)
    wide_dot = jnp.transpose(jnp.broadcast_to(dot_grad, (HEADS * ALPHA, LANES)))
    spare = DIM2 - 2 * edge_ch
    tail = iota((spare, LANES), 0)
    first = jnp.broadcast_to(wide_dot[:1, :LANES], (spare, LANES))
    second = jnp.broadcast_to(wide_dot[:1, LANES:], (spare, LANES))
    put(row + 2 * edge_ch, jnp.where(tail == 0, first, jnp.where(tail == 1, second, 0.0)), LANES)
    row += DIM2
    put(row, dot_nt(x0[pl.ds(0, CH), :], pre_grad))
    send(0, kept0, sent0)

    row = CHUNKS[1][0]
    for start in range(0, DIM0, PANEL):
        size = min(PANEL, DIM0 - start)
        put(row, dot_nt(x0[...], g0[pl.ds(start, size), :]))
        if size < PANEL:
            put(row, jnp.zeros((DIM0, PANEL - size), f32), size)
        row += DIM0
    send(1, kept1, sent1)
    for copy in copies:
        copy.wait()


PROJ_ROWS = (LMAX // 2 + 1) * CH
CHUNKS = ((0, 3 * DIM1 + 3 * DIM2 + CH), (3 * DIM1 + 3 * DIM2 + CH, 2 * DIM0))
PACKED_ROWS = sum(size for start, size in CHUNKS)


def halves_of(mine, other):
    first = (lax.axis_index("edge") & 1) == 0
    left, right = mine[...].astype(f32), other[...].astype(f32)
    return jnp.where(first, left, right), jnp.where(first, right, left)


def reversed_bits(value, count):
    return sum(((value >> n) & 1) << (count - 1 - n) for n in range(count))


def make_unpack(lanes_total, peers):
    def unpack_kernel(mine, other, zero, one, two, alpha_in, alpha_edge, alpha_dot, proj):
        cols = lanes_total // 2
        col_bits = (cols - 1).bit_length()
        late = PROJ_ROWS // lanes_total
        first_rows = CHUNKS[0][1] // (cols * peers)
        share = first_rows + CHUNKS[1][1] // (cols * peers)
        main, zeros, tail = [], [], {}
        for core, value in enumerate(halves_of(mine, other)):
            parts, zero_parts = [], {}
            for col in range(cols):
                rows = []
                for peer in range(peers):
                    start = col * (peers * share + late) + peer * share
                    rows.append(value[start : start + first_rows])
                    zero_parts[peer * cols + col] = value[start + first_rows : start + share]
                parts += rows
                end = (col + 1) * (peers * share + late)
                tail[core * cols + reversed_bits(col, col_bits)] = value[end - late : end]
            main.append(jnp.concatenate(parts, axis=0))
            zeros.append(jnp.concatenate([zero_parts[n] for n in sorted(zero_parts)], axis=0))
        tail = jnp.concatenate([tail[n] for n in sorted(tail)], axis=0)
        for degree in range(LMAX + 1):
            piece = tail[degree // 2 * CH : (degree // 2 + 1) * CH]
            proj[degree] = piece[:, degree % 2 * CH : (degree % 2 + 1) * CH].astype(bf16)
        left, right = zeros
        zero[:, pl.ds(0, LANES)] = left[:DIM0].astype(bf16)
        zero[:, pl.ds(LANES, LANES)] = right[:DIM0].astype(bf16)
        zero[:, pl.ds(2 * LANES, LANES)] = left[DIM0:].astype(bf16)
        zero[:, pl.ds(3 * LANES, DIM0 - 3 * LANES)] = right[DIM0:, : DIM0 - 3 * LANES].astype(bf16)
        unpack_rest(*main, one, two, alpha_in, alpha_edge, alpha_dot)

    return unpack_kernel


def unpack_rest(left, right, one, two, alpha_in, alpha_edge, alpha_dot):
    for n in range(2 * DIM1 // LANES):
        panel = (left, right)[n % 2][(n // 2) * DIM1 : (n // 2 + 1) * DIM1]
        per = DIM1 // LANES
        one[n // per, :, pl.ds((n % per) * LANES, LANES)] = panel.astype(bf16)
    left, right = left[3 * DIM1 :], right[3 * DIM1 :]
    panels = [(left, right)[n % 2][(n // 2) * DIM2 : (n // 2 + 1) * DIM2] for n in range(5)]
    whole = jnp.concatenate(panels, axis=1)
    two[0] = whole[:, :DIM2].astype(bf16)
    two[1] = whole[:, DIM2:].astype(bf16)
    edge_ch = alpha_edge.shape[0]
    rest = right[2 * DIM2 : 3 * DIM2]
    alpha_edge[:, pl.ds(0, LANES)] = rest[:edge_ch].astype(bf16)
    alpha_edge[:, pl.ds(LANES, LANES)] = rest[edge_ch : 2 * edge_ch].astype(bf16)
    alpha_dot[...] = rest[2 * edge_ch : 2 * edge_ch + 2].astype(bf16)
    alpha_in[:, pl.ds(0, LANES)] = left[3 * DIM2 :].astype(bf16)
    alpha_in[:, pl.ds(LANES, LANES)] = right[3 * DIM2 :].astype(bf16)


def source_kernel(
    source_slot, lists, rot, g0, g1, g2, pre_grad, wzero, wone, wtwo, ain,
    *rest,
):
    sums_out, d0, d1, d2, terms = rest[-5:]
    edges = source_slot.shape[1]
    slots = sums_out.shape[0] * sums_out.shape[1]
    d0[...] = dot_nn(wzero[...], g0[...])
    d0[pl.ds(0, CH), :] += dot_nn(ain[...], pre_grad[...])
    for out, weight, value in ((d1, wone, g1[...]), (d2, wtwo, g2[...])):
        out[...] = dot_nn(weight[0], value) - swapped_halves(dot_nn(weight[1], value), edges)

    def load(degree, order, half):
        ref, row, second = frame_place(degree, order, (d0, d1, d2))
        return ref[pl.ds(row, CH), lane_at(half, edges, second)]

    terms[pl.ds(FLAT, COLS - FLAT), :] = jnp.zeros((COLS - FLAT, 2 * edges), bf16)
    from_frame(load, rot, edges, store_terms(terms, edges))
    slot_sums(terms, mask_to(one_hot_rows(source_slot, sums_out.shape[0], slots), bf16), sums_out)
    put_rows(sums_out, pl.ds(COLS, LANES), lists[...])


def make_collect(lanes_total):
    def collect_kernel(*rest):
        arrivals = rest[:lanes_total]
        out, rows = rest[lanes_total:]
        atoms = out.shape[1]
        total = rows.shape[0]
        collect_rows(arrivals, rows)
        index = rows[:, pl.ds(COLS, LANES)][:, 1:2]
        picked = mask_to(iota((total, atoms), 1).astype(f32) == index, bf16)
        twice = jnp.concatenate([picked, picked], axis=0)
        for block in range(BLOCKS):
            high, low = split_two(rows[:, pl.ds(block * LANES, LANES)])
            sums = dot_tn(twice, jnp.concatenate([high, low], axis=0)).astype(bf16)
            out[2 * block] = sums[:, :CH]
            if 2 * block + 1 < COEFFS:
                out[2 * block + 1] = sums[:, CH:]

    return collect_kernel


vmem = pl.BlockSpec(memory_space=pltpu.VMEM)
smem = pl.BlockSpec(memory_space=pltpu.SMEM)
anywhere = pl.BlockSpec(memory_space=pl.ANY)


def call(kernel, outs, scratch, *args, scalars=0, far=(), apart=(), after=()):
    specs = [smem if n < scalars else anywhere if n in far else vmem for n in range(len(args))]
    specs += [anywhere] * len(after)
    out_specs = [anywhere if n in apart else vmem for n in range(len(outs))]
    shapes = [pltpu.VMEM(*entry) if isinstance(entry, tuple) else entry for entry in scratch]
    return pl.pallas_call(
        kernel,
        out_shape=[jax.ShapeDtypeStruct(shape, kind) for shape, kind in outs],
        in_specs=specs,
        out_specs=out_specs,
        scratch_shapes=shapes,
        compiler_params=pltpu.CompilerParams(vmem_limit_bytes=VMEM_LIMIT),
        cost_estimate=pl.CostEstimate(flops=1, bytes_accessed=1, transcendentals=0),
    )(*args, *after)


class Order:
    def __init__(self):
        self.last = None

    def hold(self, value):
        if self.last is None:
            return value
        return lax.optimization_barrier((value, self.last))[0]

    def mark(self, value):
        self.last = value
        return value


def turned_column(row):
    return jnp.transpose(jnp.broadcast_to(row, (8, row.shape[1])))[:, :1]


def swap(value, axis, bit):
    size = lax.axis_size(axis)
    return lax.ppermute(value, axis, [(i, i ^ (1 << bit)) for i in range(size)])


def bits_of(axis):
    return (lax.axis_size(axis) - 1).bit_length()


def gather_lanes(value, order):
    held = {0: value}
    for bit in reversed(range(bits_of("edge"))):
        fresh = {}
        for k, v in held.items():
            fresh[k | (1 << bit)] = swap(order.hold(v) if k else v, "edge", bit)
        held.update(fresh)
        yield
    return [held[k] for k in range(len(held))]


def own_bit(axis, bit):
    return (lax.axis_index(axis) >> bit) & 1


def share_steps(first):
    steps = [("edge", n) for n in range(1, bits_of("edge"))]
    steps += [("graph", n) for n in range(bits_of("graph"))]
    return sorted(steps, key=lambda step: step[0] != first)


def halve(kept, sent, first, order):
    other = swap(sent, "edge", 0)
    yield
    current = kept + order.hold(other)
    for axis, bit in share_steps(first):
        mine = own_bit(axis, bit)
        parts = current.reshape(2, current.shape[0] // 2, -1)
        sent = order.mark(lax.dynamic_index_in_dim(parts, 1 - mine, 0, False))
        other = swap(sent, axis, bit)
        yield
        current = lax.dynamic_index_in_dim(parts, mine, 0, False) + order.hold(other)
    return order.mark(current.astype(bf16))


def double(current, late, order):
    joined = False
    for axis, bit in reversed(share_steps("edge")):
        if axis == "edge" and not joined:
            current, joined = jnp.concatenate([current, late[0]], axis=0), True
        mine = own_bit(axis, bit)
        other = swap(current, axis, bit)
        yield
        other = order.hold(other)
        current = order.mark(
            jnp.concatenate(
                [jnp.where(mine == 0, current, other), jnp.where(mine == 0, other, current)],
                axis=0,
            )
        )
    return current, swap(current, "edge", 0)


def finish_steps(chain):
    while True:
        try:
            next(chain)
        except StopIteration as end:
            return end.value


def shards(
    atom_embed, out_cotangent, send_rows, recv_rows, source_slot, target_slot, rotation,
    edge_feats, edge_bias, conv_zero, conv_one, conv_two, alpha_in, alpha_edge, alpha_dot,
    out_proj,
):
    peers = lax.axis_size("graph")
    lanes_total = lax.axis_size("edge")
    atoms = atom_embed.shape[0]
    edges = rotation.shape[0]
    cap = send_rows.shape[3]
    slots = peers * cap
    blocks = peers * lanes_total
    direct = is_direct(peers)
    order = Order()

    def exchange(value):
        return lax.all_to_all(value, "graph", split_axis=0, concat_axis=0, tiled=True)

    cot = jnp.transpose(out_cotangent, (1, 0, 2))
    outgoing = call(
        outgoing_kernel, [((cap, TABLE), bf16)] * peers, [],
        send_rows, recv_rows, jnp.transpose(atom_embed, (1, 0, 2)), cot,
        scalars=2
    )
    if direct:
        tables = [outgoing[0]] + [
            lax.ppermute(outgoing[k], "graph", [(i, i ^ k) for i in range(peers)])
            for k in range(1, peers)
        ]
    else:
        tables = list(exchange(jnp.stack(outgoing)))

    source_row = source_slot.reshape(1, edges)
    target_row = target_slot.reshape(1, edges)
    bias = edge_bias.T
    adot = alpha_dot.reshape(1, -1)

    frames = [
        ((DIM0, edges), bf16),
        ((DIM1, 2 * edges), bf16),
        ((DIM2, 2 * edges), bf16),
        ((DIM0, edges), f32),
        ((DIM1, 2 * edges), f32),
        ((DIM2, 2 * edges), f32),
    ]
    pre_shape = ((HEADS * ALPHA, edges), f32)
    sums, stats, x0, x1, x2, v0, v1, v2, pre, logits, lists, agg_grad, rot, own_stats = call(
        make_forward(atoms, peers),
        [((peers, cap, WIDE), f32), ((slots // 8, LANES), f32)]
        + frames
        + [
            pre_shape,
            ((8, edges), f32),
            ((slots, LANES), f32),
            ((slots, FLAT), f32),
            ((rotation.shape[1], edges), f32),
            ((slots, LANES), f32),
        ],
        [
            ((slots, TABLE), f32),
            ((FLAT, edges), f32),
            ((8, edges), f32),
            ((COLS, 2 * edges), bf16),
            (conv_zero.shape, bf16),
            (conv_one.shape, bf16),
            (conv_two.shape, bf16),
        ]
        + frames
        + [pre_shape, pltpu.SemaphoreType.DMA((10,))],
        source_row, target_row, rotation, edge_feats, bias,
        conv_zero, conv_one, conv_two, alpha_in, alpha_edge, adot, out_proj, *tables,
        far=(5, 6, 7), apart=range(2, 9)
    )
    if direct:
        lanes_stats = [stats] + [
            lax.ppermute(stats, "edge", [(i, i ^ k) for i in range(lanes_total)])
            for k in range(1, lanes_total)
        ]
        graph_stats = jnp.concatenate(lanes_stats, axis=0)
        all_stats = [graph_stats] + [
            lax.ppermute(graph_stats, "graph", [(i, i ^ k) for i in range(peers)])
            for k in range(1, peers)
        ]
    else:
        all_stats = [lax.all_gather(stats, ("graph", "edge"), tiled=True)]

    halves = [((size, LANES), f32) for start, size in CHUNKS for _ in range(2)]
    g0, g1, g2, pre_grad, *halves = call(
        make_gradient(peers, len(all_stats)),
        [
            ((DIM0, edges), bf16),
            ((DIM1, 2 * edges), bf16),
            ((DIM2, 2 * edges), bf16),
            ((HEADS * ALPHA, edges), bf16),
        ]
        + halves,
        [
            ((slots, FLAT), bf16),
            ((FLAT, edges), f32),
            ((8, edges), f32),
            ((2 * DIM1, 2 * edges), bf16),
            ((2 * DIM2, 2 * edges), bf16),
            ((2, PACKED_ROWS, LANES), f32),
        ]
        + frames
        + [pltpu.SemaphoreType.DMA((10,))],
        *all_stats, own_stats, agg_grad, target_row, rot, edge_feats,
        x0, x1, x2, v0, v1, v2, pre, logits, adot,
        far=range(len(all_stats) + 5, len(all_stats) + 11), apart=range(4, 8)
    )

    total = lanes_total * slots
    order.mark(halves[0])
    messages = exchange(order.hold(sums))
    rest_steps = halve(halves[0], halves[1], "edge", order)
    zero_steps = halve(halves[2], halves[3], "graph", order)
    next(rest_steps)
    next(zero_steps)
    next(rest_steps)
    next(zero_steps)
    (source_sums,) = call(
        source_kernel,
        [((peers, cap, WIDE), f32)],
        [
            ((DIM0, edges), f32),
            ((DIM1, 2 * edges), f32),
            ((DIM2, 2 * edges), f32),
            ((COLS, 2 * edges), bf16),
        ],
        source_row, lists, rot, g0, g1, g2, order.hold(pre_grad),
        conv_zero, conv_one, conv_two, alpha_in
    )
    order.mark(source_sums)
    next(zero_steps)
    returned = order.mark(order.hold(exchange(source_sums)))
    for _ in range(bits_of("edge") - 1):
        next(rest_steps)
    message_hops = gather_lanes(order.hold(messages), order)
    next(message_hops)
    next(zero_steps)
    next(rest_steps)
    message_rows = finish_steps(message_hops)
    zero_share = finish_steps(zero_steps)
    out, proj = call(
        make_finish(lanes_total),
        [((COEFFS, atoms, CH), bf16), ((PROJ_ROWS, LANES), f32)],
        [((total, WIDE), f32), ((2 * total, COLS), bf16), ((COEFFS, atoms, CH), bf16)],
        order.hold(cot), out_proj, *message_rows,
    )
    order.mark(proj)
    lane = lax.axis_index("edge")
    late_rows = PROJ_ROWS // lanes_total
    place = ((lane & 1) * (lanes_total // 2) + (lane >> 1)) * late_rows
    late = lax.dynamic_slice_in_dim(proj, place, late_rows, 0)
    share = jnp.concatenate([finish_steps(rest_steps), zero_share], axis=0)
    late_share = []
    doubling = double(order.mark(share), late_share, order)
    next(doubling)
    source_hops = gather_lanes(order.hold(returned), order)
    next(source_hops)
    for bit in range(bits_of("graph")):
        late = order.mark(late + order.hold(swap(late, "graph", bit)))
        if bit < bits_of("graph") - 1:
            next(doubling)
    late_share.append(late.astype(bf16))
    for _ in share_steps("edge")[bits_of("graph") :]:
        next(doubling)
    source_rows = finish_steps(source_hops)
    (embed,) = call(
        make_collect(lanes_total),
        [((COEFFS, atoms, CH), bf16)],
        [((total, WIDE), f32)],
        order.hold(source_rows[0]), *source_rows[1:],
    )
    order.mark(embed)
    mine, other = finish_steps(doubling)
    zero, one, two, grad_in, grad_edge, grad_dot, grad_proj = call(
        make_unpack(lanes_total, peers),
        [
            ((DIM0, DIM0), bf16),
            ((2, DIM1, DIM1), bf16),
            ((2, DIM2, DIM2), bf16),
            (alpha_in.shape, bf16),
            (alpha_edge.shape, bf16),
            ((2, LANES), bf16),
            (out_proj.shape, bf16),
        ],
        [],
        mine, other,
    )

    def shaped(value):
        return jnp.transpose(value, (1, 0, 2))

    return (
        shaped(out), shaped(embed), zero, one, two, grad_in, grad_edge, grad_dot.reshape(-1),
        grad_proj,
    )


def solution(mesh):
    in_specs = (
        P(("groups", "graph"), None, None),
        P(("groups", "graph"), None, None),
        P(("groups", "graph"), None, "edge", None),
        P(("groups", "graph"), None, "edge", None),
        P(("groups", "graph", "edge")),
        P(("groups", "graph", "edge")),
        P(("groups", "graph", "edge"), None),
        P(("groups", "graph", "edge"), None),
        P(("groups", "graph", "edge"), None),
        P(),
        P(),
        P(),
        P(),
        P(),
        P(),
        P(),
    )
    out_specs = (
        P(("groups", "graph"), None, None),
        P(("groups", "graph"), None, None),
        P("groups", None),
        P("groups", None, None),
        P("groups", None, None),
        P("groups", None),
        P("groups", None),
        P("groups"),
        P("groups", None, None),
    )
    return jax.shard_map(shards, mesh=mesh, in_specs=in_specs, out_specs=out_specs, check_vma=False)
```

```python
import jax
import jax.numpy as jnp
import numpy as np
from jax import lax
from jax.experimental import pallas as pl
from jax.experimental.pallas import tpu as pltpu
from jax.sharding import PartitionSpec as P

LMAX = 6
MMAX = 2
CH = 64
HEADS = 4
VAL = 16
ALPHA = 64
COEFFS = (LMAX + 1) * (LMAX + 1)
FLAT = COEFFS * CH
LANES = 128
BLOCKS = (FLAT + LANES - 1) // LANES
COLS = BLOCKS * LANES
WIDE = COLS + LANES
TABLE = 2 * COLS + LANES
PEAK_AT, DOT_AT, NAME_AT = HEADS, 2 * HEADS, 3 * HEADS
STATS = 16
DIM0 = (LMAX + 1) * CH
DIM1 = LMAX * CH
DIM2 = (LMAX - 1) * CH
PANEL = 256

leak_slope = 0.2
floor_value = -1e30
bf16 = jnp.bfloat16
f32 = jnp.float32

VMEM_LIMIT = 56 * 1024 * 1024


def degree_blocks():
    result = []
    offset = 0
    for degree in range(LMAX + 1):
        centre = min(degree, MMAX)
        row_total = 2 * centre + 1
        col_total = 2 * degree + 1
        result.append((degree, centre, row_total, col_total, offset))
        offset += row_total * col_total
    return result


def degree_of(coeff):
    return int(np.sqrt(coeff))


def dot_nn(left, right):
    return jnp.dot(left, right, preferred_element_type=f32)


def dot_nt(left, right):
    return lax.dot_general(left, right, (((1,), (1,)), ((), ())), preferred_element_type=f32)


def dot_tn(left, right):
    return lax.dot_general(left, right, (((0,), (0,)), ((), ())), preferred_element_type=f32)


def iota(shape, dim):
    return lax.broadcasted_iota(jnp.int32, shape, dim)


def split_two(value):
    high = value.astype(bf16)
    return high, (value - high.astype(f32)).astype(bf16)


def to_frame(source, rot, edges, emit):
    for half in range(edges // LANES):
        lanes = pl.ds(half * LANES, LANES)
        for degree, centre, row_total, col_total, offset in degree_blocks():
            sums = [None] * row_total
            for j in range(col_total):
                column = source[pl.ds((degree * degree + j) * CH, CH), lanes]
                for i in range(row_total):
                    term = rot[pl.ds(offset + i * col_total + j, 1), lanes] * column
                    sums[i] = term if j == 0 else sums[i] + term
            for i in range(row_total):
                emit(degree, i - centre, half, sums[i])


def from_frame(load, rot, edges, emit):
    for half in range(edges // LANES):
        lanes = pl.ds(half * LANES, LANES)
        for degree, centre, row_total, col_total, offset in degree_blocks():
            rows = [load(degree, i - centre, half) for i in range(row_total)]
            for j in range(col_total):
                total = None
                for i in range(row_total):
                    term = rot[pl.ds(offset + i * col_total + j, 1), lanes] * rows[i]
                    total = term if i == 0 else total + term
                emit(degree * degree + j, half, total)


def lane_at(half, edges, second):
    return pl.ds(half * LANES + (edges if second else 0), LANES)


def frame_place(degree, order, refs):
    if order == 0:
        return refs[0], degree * CH, False
    which = abs(order)
    return refs[which], (degree - which) * CH, order < 0


def spread_heads(rows):
    return jnp.concatenate(
        [jnp.broadcast_to(row, (VAL, row.shape[1])) for row in rows], axis=0
    )


def is_direct(peers):
    return peers <= 4


def flip_of(peers):
    return lax.axis_index("graph") if is_direct(peers) else 0


def one_hot_rows(slot_ref, peers, slots):
    edges = slot_ref.shape[1]
    first = flip_of(peers) * (slots // peers)
    return jnp.bitwise_xor(iota((slots, edges), 0), first) == slot_ref[...]


def mask_to(mask, dtype):
    return jnp.where(mask, 1.0, 0.0).astype(dtype)


def stack_table(tables, rows_ref):
    cap = tables[0].shape[0]
    per = 8 // cap
    for n in range(0, len(tables), per):
        parts = [table[...].astype(f32) for table in tables[n : n + per]]
        rows_ref[pl.ds(n * cap, 8), :] = jnp.concatenate(parts, axis=0)


def put_rows(out_ref, cols, value):
    peers, cap = out_ref.shape[0], out_ref.shape[1]
    for n in range(peers):
        out_ref[n, :, cols] = value[n * cap : (n + 1) * cap].astype(out_ref.dtype)


def slot_sums(terms, one_hot, out_ref, factor=None):
    both = jnp.concatenate([one_hot, one_hot], axis=1)
    products = 0.0
    for start in range(0, COLS, PANEL):
        size = min(PANEL, COLS - start)
        sums = dot_nt(both, terms[pl.ds(start, size), :])
        put_rows(out_ref, pl.ds(start, size), sums)
        if factor is None:
            continue
        for at in range(0, size, LANES):
            width = min(LANES, FLAT - start - at)
            product = sums[:, at : at + width] * factor[:, pl.ds(start + at, width)]
            if width < LANES:
                product = jnp.concatenate([product, jnp.zeros_like(product)], axis=1)
            products = products + product
    return products


def store_terms(terms, edges):
    def emit(coeff, half, value):
        high, low = split_two(value)
        rows = pl.ds(coeff * CH, CH)
        terms[rows, lane_at(half, edges, False)] = high
        terms[rows, lane_at(half, edges, True)] = low

    return emit


def listed_rows(list_ref, shape):
    peers, cap = list_ref.shape[1], list_ref.shape[3]
    flip = flip_of(peers)
    row = iota(shape, 0)
    result = jnp.zeros(shape, jnp.int32)
    for slot in range(peers * cap):
        owner = jnp.bitwise_xor(flip, slot // cap) if is_direct(peers) else slot // cap
        result = jnp.where(row == slot, list_ref[0, owner, 0, slot % cap], result)
    return result


def put_coeffs(outs, first, coeff_rows):
    for block in range(BLOCKS):
        left = coeff_rows(2 * block)
        right = coeff_rows(2 * block + 1) if 2 * block + 1 < COEFFS else jnp.zeros_like(left)
        put_pieces(outs, first + block * LANES, jnp.concatenate([left, right], axis=1))


def put_pieces(outs, first, value):
    cap = outs[0].shape[0]
    for n, out in enumerate(outs):
        out[:, pl.ds(first, LANES)] = value[n * cap : (n + 1) * cap].astype(out.dtype)


def outgoing_kernel(send, recv, embed, cot, *outs):
    atoms = embed.shape[1]
    slots = send.shape[1] * send.shape[3]
    sent = listed_rows(send, (slots, LANES))
    received = listed_rows(recv, (slots, LANES))
    for first, listed, values in ((0, sent, embed), (COLS, received, cot)):
        picked = mask_to(iota((slots, atoms), 1) == listed[:, :atoms], bf16)
        put_coeffs(outs, first, lambda k: dot_nn(picked, values[k]))
    lane = iota((slots, LANES), 1)
    side = jnp.where(lane == 0, received, jnp.where(lane == 1, sent, 0))
    put_pieces(outs, 2 * COLS, side.astype(f32))


def swapped_halves(value, edges):
    return jnp.concatenate([-value[:, edges:], value[:, :edges]], axis=1)


def make_forward(atoms, peers):
    def forward_kernel(
        source_slot, target_slot, rotation, feats, bias, wzero_at, wone_at, wtwo_at,
        ain, aedge, adot, out_proj, *rest,
    ):
        tables, rest = rest[:peers], rest[peers:]
        (
        sums_out, stats_out, x0_at, x1_at, x2_at, v0_at, v1_at, v2_at, pre_at, logit_out,
        lists_out, agg_grad, rot, own_out,
        rows, gathered, weights, terms, wzero, wone, wtwo, x0, x1, x2, v0, v1, v2, pre_out,
        semaphores,
        ) = rest
        copies = []

        def move(source, target):
            copy = pltpu.make_async_copy(source, target, semaphores.at[len(copies)])
            copy.start()
            copies.append(copy)

        move(wzero_at, wzero)
        move(wone_at, wone)
        move(wtwo_at, wtwo)
        rot[...] = jnp.transpose(rotation[...].astype(f32))
        edges = source_slot.shape[1]
        cap = tables[0].shape[0]
        slots = peers * cap
        stack_table(tables, rows)
        picked = mask_to(one_hot_rows(source_slot, peers, slots), bf16)
        for degree in range(LMAX + 1):
            ids = pl.ds(degree * degree * CH, (2 * degree + 1) * CH)
            gathered[ids, :] = dot_tn(rows[:, ids].astype(bf16), picked)
        lists = rows[:, pl.ds(2 * COLS, LANES)]
        lists_out[...] = lists
        for degree in range(LMAX + 1):
            ids = range(degree * degree, (degree + 1) * (degree + 1))
            cot = jnp.concatenate([rows[:, pl.ds(COLS + k * CH, CH)] for k in ids], axis=0)
            grad = dot_nt(cot.astype(bf16), out_proj[degree])
            for n, k in enumerate(ids):
                agg_grad[:, pl.ds(k * CH, CH)] = grad[n * slots : (n + 1) * slots]

        def emit(degree, order, half, value):
            ref, row, second = frame_place(degree, order, (x0, x1, x2))
            ref[pl.ds(row, CH), lane_at(half, edges, second)] = value.astype(bf16)

        to_frame(gathered, rot, edges, emit)
        for source, target in ((x0, x0_at), (x1, x1_at), (x2, x2_at)):
            move(source, target)

        pre = dot_tn(ain[...], x0[pl.ds(0, CH), :]) + lax.dot_general(
            aedge[...], feats[...], (((0,), (1,)), ((), ())), preferred_element_type=f32
        )
        pre_out[...] = pre
        move(pre_out, pre_at)
        hidden = jnp.where(pre > 0, pre, leak_slope * pre) * turned_column(adot[...].astype(f32))
        aims = one_hot_rows(target_slot, peers, slots)
        lane = iota((slots, LANES), 1)
        peer = jnp.bitwise_xor(iota((slots, 1), 0) // cap, flip_of(peers))
        name = lists[:, :1] + (peer * atoms).astype(f32)
        side = jnp.where(lane == NAME_AT, name, 0.0)
        for h in range(HEADS):
            logit = jnp.sum(hidden[h * ALPHA : (h + 1) * ALPHA], axis=0, keepdims=True)
            logit = logit + bias[pl.ds(h, 1), :]
            logit_out[pl.ds(h, 1), :] = logit
            peak = jnp.max(jnp.where(aims, logit, floor_value), axis=1, keepdims=True)
            of_edge = jnp.sum(jnp.where(aims, peak, 0.0), axis=0, keepdims=True)
            weight = jnp.exp(logit - of_edge)
            weights[pl.ds(h, 1), :] = weight
            den = jnp.sum(jnp.where(aims, weight, 0.0), axis=1, keepdims=True)
            side = jnp.where(lane == h, den, jnp.where(lane == PEAK_AT + h, peak, side))

        for copy in copies[:3]:
            copy.wait()
        v0[...] = dot_tn(wzero[...], x0[...])
        for out, weight, value in ((v1, wone, x1[...]), (v2, wtwo, x2[...])):
            out[...] = dot_tn(weight[0], value) + swapped_halves(dot_tn(weight[1], value), edges)
        for source, target in ((v0, v0_at), (v1, v1_at), (v2, v2_at)):
            move(source, target)

        def load(degree, order, half):
            ref, row, second = frame_place(degree, order, (v0, v1, v2))
            return ref[pl.ds(row, CH), lane_at(half, edges, second)]

        store = store_terms(terms, edges)

        def weigh(coeff, half, value):
            lanes = lane_at(half, edges, False)
            spread = spread_heads([weights[pl.ds(h, 1), lanes] for h in range(HEADS)])
            store(coeff, half, value * spread)

        terms[pl.ds(FLAT, COLS - FLAT), :] = jnp.zeros((COLS - FLAT, 2 * edges), bf16)
        from_frame(load, rot, edges, weigh)
        dots = slot_sums(terms, mask_to(aims, bf16), sums_out, agg_grad)
        head = (lane % CH) // VAL
        for h in range(HEADS):
            dot = jnp.sum(jnp.where(head == h, dots, 0.0), axis=1, keepdims=True)
            side = jnp.where(lane == DOT_AT + h, dot, side)
        put_rows(sums_out, pl.ds(COLS, LANES), side)
        own_out[...] = side
        spread = jnp.concatenate([side[:, :STATS]] * (LANES // STATS), axis=1)
        spread = jnp.where(lane // STATS == iota((slots, LANES), 0) % 8, spread, 0.0)
        packed = jnp.sum(spread.reshape(slots // 8, 8, LANES), axis=1)

        stats_out[...] = packed
        for copy in copies[3:]:
            copy.wait()

    return forward_kernel


def lane_heads(values, shape):
    head = (iota(shape, 1) % CH) // VAL
    result = jnp.broadcast_to(values[0], shape)
    for h in range(1, HEADS):
        result = jnp.where(head == h, values[h], result)
    return result


def collect_rows(arrivals, rows_ref):
    own = lax.axis_index("edge")
    for k, arrival in enumerate(arrivals):
        peers, cap, width = arrival.shape
        base = (own ^ k) * (peers * cap)
        for start in range(0, peers * cap, 8):
            parts = [arrival[g] for g in range(start // cap, (start + 8) // cap)]
            at = pl.ds(pl.multiple_of(base + start, 8), 8)
            rows_ref[at, :] = jnp.concatenate(parts, axis=0)


def block_cols(block):
    return pl.ds(block * LANES, min(LANES, FLAT - block * LANES))


def make_finish(lanes_total):
    def finish_kernel(cot, out_proj, *rest):
        arrivals = rest[:lanes_total]
        out, proj, rows, terms, agg_low = rest[lanes_total:]
        atoms = cot.shape[1]
        total = rows.shape[0]
        collect_rows(arrivals, rows)
        side = rows[:, pl.ds(COLS, LANES)]
        owner = (lax.axis_index("graph") * atoms).astype(f32)
        names = iota((total, atoms), 1).astype(f32) + owner == side[:, NAME_AT : NAME_AT + 1]
        eye = iota((atoms, atoms), 0) == iota((atoms, atoms), 1)
        scales, dens = [], []
        for h in range(HEADS):
            peak_rows = side[:, PEAK_AT + h : PEAK_AT + h + 1]
            peak = jnp.max(jnp.where(names, peak_rows, floor_value), axis=0, keepdims=True)
            of_row = jnp.sum(jnp.where(names, peak, 0.0), axis=1, keepdims=True)
            scale = jnp.exp(peak_rows - of_row)
            scaled_den = side[:, h : h + 1] * scale
            den = jnp.sum(jnp.where(names, scaled_den, 0.0), axis=0, keepdims=True)
            scales.append(scale)
            dens.append(jnp.sum(jnp.where(eye, den, 0.0), axis=1, keepdims=True))
        scale_full = lane_heads(scales, (total, LANES))
        den_full = lane_heads(dens, (atoms, LANES))
        picked = mask_to(names, bf16)
        twice = jnp.concatenate([picked, picked], axis=0)
        for block in range(BLOCKS):
            cols = pl.ds(block * LANES, LANES)
            high, low = split_two(rows[:, cols] * scale_full)
            terms[pl.ds(0, total), cols] = high
            terms[pl.ds(total, total), cols] = low
        for block in range(BLOCKS):
            cols = pl.ds(block * LANES, LANES)
            agg = (dot_tn(twice, terms[:, cols]) / den_full).astype(bf16)
            agg_low[2 * block] = agg[:, :CH]
            if 2 * block + 1 < COEFFS:
                agg_low[2 * block + 1] = agg[:, CH:]
        for degree in range(LMAX + 1):
            ids = pl.ds(degree * degree, 2 * degree + 1)
            stacked = ((2 * degree + 1) * atoms, CH)
            left = agg_low[ids].reshape(stacked)
            right = cot[ids].reshape(stacked)
            value = dot_nn(left, out_proj[degree]).astype(bf16)
            out[ids] = value.reshape((2 * degree + 1, atoms, CH))
            at = (pl.ds(degree // 2 * CH, CH), pl.ds(degree % 2 * CH, CH))
            proj[at] = dot_tn(left, right)
        proj[pl.ds(LMAX // 2 * CH, CH), pl.ds(CH, CH)] = jnp.zeros((CH, CH), f32)

    return finish_kernel


def combine_stats(stats, own):
    chunk = 32
    name = own[:, NAME_AT : NAME_AT + 1]

    def part(part_rows):
        entries = [part_rows[:, n : n + STATS] for n in range(0, LANES, STATS)]
        turned = jnp.transpose(jnp.concatenate(entries, axis=0))
        same = name == turned[NAME_AT : NAME_AT + 1]
        result = []
        for h in range(HEADS):
            peaks = turned[PEAK_AT + h : PEAK_AT + h + 1]
            peak = jnp.max(jnp.where(same, peaks, floor_value), axis=1, keepdims=True)
            scale = jnp.where(same, jnp.exp(jnp.where(same, peaks - peak, 0.0)), 0.0)
            den = jnp.sum(turned[h : h + 1] * scale, axis=1, keepdims=True)
            dot = jnp.sum(turned[DOT_AT + h : DOT_AT + h + 1] * scale, axis=1, keepdims=True)
            result += [peak, den, dot]
        return tuple(result)

    def step(at, held):
        fresh = part(stats[0][pl.ds(pl.multiple_of(at * chunk, chunk), chunk), :])
        result = []
        for h in range(HEADS):
            peak, den, dot = held[3 * h : 3 * h + 3]
            new_peak, new_den, new_dot = fresh[3 * h : 3 * h + 3]
            most = jnp.maximum(peak, new_peak)
            old, new = jnp.exp(peak - most), jnp.exp(new_peak - most)
            result += [most, den * old + new_den * new, dot * old + new_dot * new]
        return tuple(result)

    if len(stats) > 1:
        held = part(jnp.concatenate([rows[...] for rows in stats], axis=0))
    else:
        held = part(stats[0][pl.ds(0, chunk), :])
        held = lax.fori_loop(1, stats[0].shape[0] // chunk, step, held)
    return [held[3 * h : 3 * h + 3] for h in range(HEADS)]


def make_gradient(peers, parts):
    def kernel(*refs):
        gradient_kernel(peers, refs[:parts], *refs[parts:])

    return kernel


def gradient_kernel(
    peers, stats, own, agg_grad, target_slot, rot, feats,
    x0_at, x1_at, x2_at, v0_at, v1_at, v2_at, pre, logits, adot,
    g0, top1, top2, pre_grad_out, kept0, sent0, kept1, sent1,
    num_grad, spread_grad, weights, g1, g2, packed, x0, x1, x2, v0, v1, v2, semaphores,
):
    loads = []
    for source, target in (
        (v0_at, v0), (v1_at, v1), (v2_at, v2), (x0_at, x0), (x1_at, x1), (x2_at, x2)
    ):
        load = pltpu.make_async_copy(source, target, semaphores.at[4 + len(loads)])
        load.start()
        loads.append(load)
    edges = target_slot.shape[1]
    slots = agg_grad.shape[0]
    aims = one_hot_rows(target_slot, peers, slots)
    combined = combine_stats(stats, own[...])
    den_grads = []
    for h, (peak, den, dot) in enumerate(combined):
        of_edge = jnp.sum(jnp.where(aims, peak, 0.0), axis=0, keepdims=True)
        weights[pl.ds(h, 1), :] = jnp.exp(logits[pl.ds(h, 1), :] - of_edge)
        den_grad = (-(dot / den) / den).astype(bf16).astype(f32)
        den_grads.append(jnp.sum(jnp.where(aims, den_grad, 0.0), axis=0, keepdims=True))
    den_full = lane_heads([den for peak, den, dot in combined], (slots, LANES))
    for block in range(BLOCKS):
        cols = block_cols(block)
        num_grad[:, cols] = (agg_grad[:, cols] / den_full[:, : cols.size]).astype(bf16)
    picked = mask_to(aims, bf16)
    for degree in range(LMAX + 1):
        ids = pl.ds(degree * degree * CH, (2 * degree + 1) * CH)
        spread_grad[ids, :] = dot_tn(num_grad[:, ids], picked)

    state = {}

    def emit(degree, order, half, value):
        lanes = lane_at(half, edges, False)
        ref, row, second = frame_place(degree, order, (v0, v1, v2))
        product = value * ref[pl.ds(row, CH), lane_at(half, edges, second)]
        if degree == 0:
            state["sum"] = product
            state["spread"] = spread_heads([weights[pl.ds(h, 1), lanes] for h in range(HEADS)])
        else:
            state["sum"] = state["sum"] + product
        grad = (value * state["spread"]).astype(bf16)
        ref, row, second = frame_place(degree, order, (g0, g1, g2))
        ref[pl.ds(row, CH), lane_at(half, edges, second)] = grad
        if order != 0:
            swapped = grad if order < 0 else -grad
            below = row + (DIM1 if abs(order) == 1 else DIM2)
            ref[pl.ds(below, CH), lane_at(half, edges, not second)] = swapped
        if degree == LMAX and order == MMAX:
            for h in range(HEADS):
                part = state["sum"][h * VAL : (h + 1) * VAL]
                weights[pl.ds(HEADS + h, 1), lanes] = jnp.sum(part, axis=0, keepdims=True)

    for load in loads:
        load.wait()
    to_frame(spread_grad, rot, edges, emit)

    hidden = jnp.where(pre[...] > 0, pre[...], leak_slope * pre[...])
    logit_grads = [
        weights[pl.ds(h, 1), :] * (weights[pl.ds(HEADS + h, 1), :] + den_grads[h])
        for h in range(HEADS)
    ]
    tall = jnp.concatenate(
        [jnp.broadcast_to(row, (ALPHA, edges)) for row in logit_grads], axis=0
    )
    slope = jnp.where(pre[...] > 0, 1.0, leak_slope)
    pre_grad = (tall * turned_column(adot[...].astype(f32)) * slope).astype(bf16)
    pre_grad_out[...] = pre_grad
    dot_grad = jnp.sum(tall * hidden, axis=1, keepdims=True)

    top1[...] = g1[pl.ds(0, DIM1), :]
    top2[...] = g2[pl.ds(0, DIM2), :]
    mine = lax.axis_index("edge") & 1
    copies = []

    def put(row, value, at=0):
        for side in range(2):
            low, high = max(at, side * LANES), min(at + value.shape[1], (side + 1) * LANES)
            if low < high:
                piece = value[:, low - at : high - at]
                cols = pl.ds(low - side * LANES, high - low)
                packed[side, pl.ds(row, value.shape[0]), cols] = piece

    def send(chunk, kept, sent):
        start, size = CHUNKS[chunk]
        rows_of = pl.ds(start, size)
        for n, (side, out) in enumerate(((mine, kept), (1 - mine, sent))):
            copy = pltpu.make_async_copy(
                packed.at[side, rows_of, :], out, semaphores.at[2 * chunk + n]
            )
            copy.start()
            copies.append(copy)

    row = 0
    for left, right, dim in ((x1, g1, DIM1), (x2, g2, DIM2)):
        for start in range(0, 2 * dim, PANEL):
            size = min(PANEL, 2 * dim - start)
            put(row, dot_nt(left[...], right[pl.ds(start, size), :]))
            row += dim
    row -= DIM2
    edge_ch = feats.shape[1]
    edge_grad = lax.dot_general(
        feats[...], pre_grad, (((0,), (1,)), ((), ())), preferred_element_type=f32
    )
    put(row, edge_grad[:, :LANES], LANES)
    put(row + edge_ch, edge_grad[:, LANES:], LANES)
    wide_dot = jnp.transpose(jnp.broadcast_to(dot_grad, (HEADS * ALPHA, LANES)))
    spare = DIM2 - 2 * edge_ch
    tail = iota((spare, LANES), 0)
    first = jnp.broadcast_to(wide_dot[:1, :LANES], (spare, LANES))
    second = jnp.broadcast_to(wide_dot[:1, LANES:], (spare, LANES))
    put(row + 2 * edge_ch, jnp.where(tail == 0, first, jnp.where(tail == 1, second, 0.0)), LANES)
    row += DIM2
    put(row, dot_nt(x0[pl.ds(0, CH), :], pre_grad))
    send(0, kept0, sent0)

    row = CHUNKS[1][0]
    for start in range(0, DIM0, PANEL):
        size = min(PANEL, DIM0 - start)
        put(row, dot_nt(x0[...], g0[pl.ds(start, size), :]))
        if size < PANEL:
            put(row, jnp.zeros((DIM0, PANEL - size), f32), size)
        row += DIM0
    send(1, kept1, sent1)
    for copy in copies:
        copy.wait()


PROJ_ROWS = (LMAX // 2 + 1) * CH
CHUNKS = ((0, 3 * DIM1 + 3 * DIM2 + CH), (3 * DIM1 + 3 * DIM2 + CH, 2 * DIM0))
PACKED_ROWS = sum(size for start, size in CHUNKS)


def halves_of(mine, other):
    first = (lax.axis_index("edge") & 1) == 0
    left, right = mine[...].astype(f32), other[...].astype(f32)
    return jnp.where(first, left, right), jnp.where(first, right, left)


def reversed_bits(value, count):
    return sum(((value >> n) & 1) << (count - 1 - n) for n in range(count))


def make_unpack(lanes_total, peers):
    def unpack_kernel(mine, other, zero, one, two, alpha_in, alpha_edge, alpha_dot, proj):
        cols = lanes_total // 2
        col_bits = (cols - 1).bit_length()
        late = PROJ_ROWS // lanes_total
        first_rows = CHUNKS[0][1] // (cols * peers)
        share = first_rows + CHUNKS[1][1] // (cols * peers)
        main, zeros, tail = [], [], {}
        for core, value in enumerate(halves_of(mine, other)):
            parts, zero_parts = [], {}
            for col in range(cols):
                rows = []
                for peer in range(peers):
                    start = col * (peers * share + late) + peer * share
                    rows.append(value[start : start + first_rows])
                    zero_parts[peer * cols + col] = value[start + first_rows : start + share]
                parts += rows
                end = (col + 1) * (peers * share + late)
                tail[core * cols + reversed_bits(col, col_bits)] = value[end - late : end]
            main.append(jnp.concatenate(parts, axis=0))
            zeros.append(jnp.concatenate([zero_parts[n] for n in sorted(zero_parts)], axis=0))
        tail = jnp.concatenate([tail[n] for n in sorted(tail)], axis=0)
        for degree in range(LMAX + 1):
            piece = tail[degree // 2 * CH : (degree // 2 + 1) * CH]
            proj[degree] = piece[:, degree % 2 * CH : (degree % 2 + 1) * CH].astype(bf16)
        left, right = zeros
        zero[:, pl.ds(0, LANES)] = left[:DIM0].astype(bf16)
        zero[:, pl.ds(LANES, LANES)] = right[:DIM0].astype(bf16)
        zero[:, pl.ds(2 * LANES, LANES)] = left[DIM0:].astype(bf16)
        zero[:, pl.ds(3 * LANES, DIM0 - 3 * LANES)] = right[DIM0:, : DIM0 - 3 * LANES].astype(bf16)
        unpack_rest(*main, one, two, alpha_in, alpha_edge, alpha_dot)

    return unpack_kernel


def unpack_rest(left, right, one, two, alpha_in, alpha_edge, alpha_dot):
    for n in range(2 * DIM1 // LANES):
        panel = (left, right)[n % 2][(n // 2) * DIM1 : (n // 2 + 1) * DIM1]
        per = DIM1 // LANES
        one[n // per, :, pl.ds((n % per) * LANES, LANES)] = panel.astype(bf16)
    left, right = left[3 * DIM1 :], right[3 * DIM1 :]
    panels = [(left, right)[n % 2][(n // 2) * DIM2 : (n // 2 + 1) * DIM2] for n in range(5)]
    whole = jnp.concatenate(panels, axis=1)
    two[0] = whole[:, :DIM2].astype(bf16)
    two[1] = whole[:, DIM2:].astype(bf16)
    edge_ch = alpha_edge.shape[0]
    rest = right[2 * DIM2 : 3 * DIM2]
    alpha_edge[:, pl.ds(0, LANES)] = rest[:edge_ch].astype(bf16)
    alpha_edge[:, pl.ds(LANES, LANES)] = rest[edge_ch : 2 * edge_ch].astype(bf16)
    alpha_dot[...] = rest[2 * edge_ch : 2 * edge_ch + 2].astype(bf16)
    alpha_in[:, pl.ds(0, LANES)] = left[3 * DIM2 :].astype(bf16)
    alpha_in[:, pl.ds(LANES, LANES)] = right[3 * DIM2 :].astype(bf16)


def source_kernel(
    source_slot, lists, rot, g0, g1, g2, pre_grad, wzero, wone, wtwo, ain,
    *rest,
):
    sums_out, d0, d1, d2, terms = rest[-5:]
    edges = source_slot.shape[1]
    slots = sums_out.shape[0] * sums_out.shape[1]
    d0[...] = dot_nn(wzero[...], g0[...])
    d0[pl.ds(0, CH), :] += dot_nn(ain[...], pre_grad[...])
    for out, weight, value in ((d1, wone, g1[...]), (d2, wtwo, g2[...])):
        out[...] = dot_nn(weight[0], value) - swapped_halves(dot_nn(weight[1], value), edges)

    def load(degree, order, half):
        ref, row, second = frame_place(degree, order, (d0, d1, d2))
        return ref[pl.ds(row, CH), lane_at(half, edges, second)]

    terms[pl.ds(FLAT, COLS - FLAT), :] = jnp.zeros((COLS - FLAT, 2 * edges), bf16)
    from_frame(load, rot, edges, store_terms(terms, edges))
    slot_sums(terms, mask_to(one_hot_rows(source_slot, sums_out.shape[0], slots), bf16), sums_out)
    put_rows(sums_out, pl.ds(COLS, LANES), lists[...])


def make_collect(lanes_total):
    def collect_kernel(*rest):
        arrivals = rest[:lanes_total]
        out, rows = rest[lanes_total:]
        atoms = out.shape[1]
        total = rows.shape[0]
        collect_rows(arrivals, rows)
        index = rows[:, pl.ds(COLS, LANES)][:, 1:2]
        picked = mask_to(iota((total, atoms), 1).astype(f32) == index, bf16)
        twice = jnp.concatenate([picked, picked], axis=0)
        for block in range(BLOCKS):
            high, low = split_two(rows[:, pl.ds(block * LANES, LANES)])
            sums = dot_tn(twice, jnp.concatenate([high, low], axis=0)).astype(bf16)
            out[2 * block] = sums[:, :CH]
            if 2 * block + 1 < COEFFS:
                out[2 * block + 1] = sums[:, CH:]

    return collect_kernel


vmem = pl.BlockSpec(memory_space=pltpu.VMEM)
smem = pl.BlockSpec(memory_space=pltpu.SMEM)
anywhere = pl.BlockSpec(memory_space=pl.ANY)


def call(kernel, outs, scratch, *args, scalars=0, far=(), apart=(), after=()):
    specs = [smem if n < scalars else anywhere if n in far else vmem for n in range(len(args))]
    specs += [anywhere] * len(after)
    out_specs = [anywhere if n in apart else vmem for n in range(len(outs))]
    shapes = [pltpu.VMEM(*entry) if isinstance(entry, tuple) else entry for entry in scratch]
    return pl.pallas_call(
        kernel,
        out_shape=[jax.ShapeDtypeStruct(shape, kind) for shape, kind in outs],
        in_specs=specs,
        out_specs=out_specs,
        scratch_shapes=shapes,
        compiler_params=pltpu.CompilerParams(vmem_limit_bytes=VMEM_LIMIT),
        cost_estimate=pl.CostEstimate(flops=1, bytes_accessed=1, transcendentals=0),
    )(*args, *after)


class Order:
    def __init__(self):
        self.last = None

    def hold(self, value):
        if self.last is None:
            return value
        return lax.optimization_barrier((value, self.last))[0]

    def mark(self, value):
        self.last = value
        return value


def turned_column(row):
    return jnp.transpose(jnp.broadcast_to(row, (8, row.shape[1])))[:, :1]


def swap(value, axis, bit):
    size = lax.axis_size(axis)
    return lax.ppermute(value, axis, [(i, i ^ (1 << bit)) for i in range(size)])


def bits_of(axis):
    return (lax.axis_size(axis) - 1).bit_length()


def gather_lanes(value, order):
    held = {0: value}
    for bit in reversed(range(bits_of("edge"))):
        fresh = {}
        for k, v in held.items():
            fresh[k | (1 << bit)] = swap(order.hold(v) if k else v, "edge", bit)
        held.update(fresh)
        yield
    return [held[k] for k in range(len(held))]


def own_bit(axis, bit):
    return (lax.axis_index(axis) >> bit) & 1


def share_steps(first):
    steps = [("edge", n) for n in range(1, bits_of("edge"))]
    steps += [("graph", n) for n in range(bits_of("graph"))]
    return sorted(steps, key=lambda step: step[0] != first)


def halve(kept, sent, first, order):
    other = swap(sent, "edge", 0)
    yield
    current = kept + order.hold(other)
    for axis, bit in share_steps(first):
        mine = own_bit(axis, bit)
        parts = current.reshape(2, current.shape[0] // 2, -1)
        sent = order.mark(lax.dynamic_index_in_dim(parts, 1 - mine, 0, False))
        other = swap(sent, axis, bit)
        yield
        current = lax.dynamic_index_in_dim(parts, mine, 0, False) + order.hold(other)
    return order.mark(current.astype(bf16))


def double(current, late, order):
    joined = False
    for axis, bit in reversed(share_steps("edge")):
        if axis == "edge" and not joined:
            current, joined = jnp.concatenate([current, late[0]], axis=0), True
        mine = own_bit(axis, bit)
        other = swap(current, axis, bit)
        yield
        other = order.hold(other)
        current = order.mark(
            jnp.concatenate(
                [jnp.where(mine == 0, current, other), jnp.where(mine == 0, other, current)],
                axis=0,
            )
        )
    return current, swap(current, "edge", 0)


def finish_steps(chain):
    while True:
        try:
            next(chain)
        except StopIteration as end:
            return end.value


def shards(
    atom_embed, out_cotangent, send_rows, recv_rows, source_slot, target_slot, rotation,
    edge_feats, edge_bias, conv_zero, conv_one, conv_two, alpha_in, alpha_edge, alpha_dot,
    out_proj,
):
    peers = lax.axis_size("graph")
    lanes_total = lax.axis_size("edge")
    atoms = atom_embed.shape[0]
    edges = rotation.shape[0]
    cap = send_rows.shape[3]
    slots = peers * cap
    blocks = peers * lanes_total
    direct = is_direct(peers)
    order = Order()

    def pairwise(pieces):
        return [pieces[0]] + [
            lax.ppermute(pieces[k], "graph", [(i, i ^ k) for i in range(peers)])
            for k in range(1, peers)
        ]

    def exchange(value):
        if direct:
            return jnp.stack(pairwise([value[k] for k in range(peers)]))
        return lax.all_to_all(value, "graph", split_axis=0, concat_axis=0, tiled=True)

    cot = jnp.transpose(out_cotangent, (1, 0, 2))
    outgoing = call(
        outgoing_kernel, [((cap, TABLE), bf16)] * peers, [],
        send_rows, recv_rows, jnp.transpose(atom_embed, (1, 0, 2)), cot,
        scalars=2
    )
    tables = pairwise(outgoing) if direct else list(exchange(jnp.stack(outgoing)))

    source_row = source_slot.reshape(1, edges)
    target_row = target_slot.reshape(1, edges)
    bias = edge_bias.T
    adot = alpha_dot.reshape(1, -1)

    frames = [
        ((DIM0, edges), bf16),
        ((DIM1, 2 * edges), bf16),
        ((DIM2, 2 * edges), bf16),
        ((DIM0, edges), f32),
        ((DIM1, 2 * edges), f32),
        ((DIM2, 2 * edges), f32),
    ]
    pre_shape = ((HEADS * ALPHA, edges), f32)
    sums, stats, x0, x1, x2, v0, v1, v2, pre, logits, lists, agg_grad, rot, own_stats = call(
        make_forward(atoms, peers),
        [((peers, cap, WIDE), f32), ((slots // 8, LANES), f32)]
        + frames
        + [
            pre_shape,
            ((8, edges), f32),
            ((slots, LANES), f32),
            ((slots, FLAT), f32),
            ((rotation.shape[1], edges), f32),
            ((slots, LANES), f32),
        ],
        [
            ((slots, TABLE), f32),
            ((FLAT, edges), f32),
            ((8, edges), f32),
            ((COLS, 2 * edges), bf16),
            (conv_zero.shape, bf16),
            (conv_one.shape, bf16),
            (conv_two.shape, bf16),
        ]
        + frames
        + [pre_shape, pltpu.SemaphoreType.DMA((10,))],
        source_row, target_row, rotation, edge_feats, bias,
        conv_zero, conv_one, conv_two, alpha_in, alpha_edge, adot, out_proj, *tables,
        far=(5, 6, 7), apart=range(2, 9)
    )
    if direct:
        lanes_stats = [stats] + [
            lax.ppermute(stats, "edge", [(i, i ^ k) for i in range(lanes_total)])
            for k in range(1, lanes_total)
        ]
        graph_stats = jnp.concatenate(lanes_stats, axis=0)
        all_stats = [graph_stats] + [
            lax.ppermute(graph_stats, "graph", [(i, i ^ k) for i in range(peers)])
            for k in range(1, peers)
        ]
    else:
        all_stats = [lax.all_gather(stats, ("graph", "edge"), tiled=True)]

    halves = [((size, LANES), f32) for start, size in CHUNKS for _ in range(2)]
    g0, g1, g2, pre_grad, *halves = call(
        make_gradient(peers, len(all_stats)),
        [
            ((DIM0, edges), bf16),
            ((DIM1, 2 * edges), bf16),
            ((DIM2, 2 * edges), bf16),
            ((HEADS * ALPHA, edges), bf16),
        ]
        + halves,
        [
            ((slots, FLAT), bf16),
            ((FLAT, edges), f32),
            ((8, edges), f32),
            ((2 * DIM1, 2 * edges), bf16),
            ((2 * DIM2, 2 * edges), bf16),
            ((2, PACKED_ROWS, LANES), f32),
        ]
        + frames
        + [pltpu.SemaphoreType.DMA((10,))],
        *all_stats, own_stats, agg_grad, target_row, rot, edge_feats,
        x0, x1, x2, v0, v1, v2, pre, logits, adot,
        far=range(len(all_stats) + 5, len(all_stats) + 11), apart=range(4, 8)
    )

    total = lanes_total * slots
    order.mark(halves[0])
    messages = exchange(order.hold(sums))
    rest_steps = halve(halves[0], halves[1], "edge", order)
    zero_steps = halve(halves[2], halves[3], "graph", order)
    next(rest_steps)
    next(zero_steps)
    next(rest_steps)
    next(zero_steps)
    (source_sums,) = call(
        source_kernel,
        [((peers, cap, WIDE), f32)],
        [
            ((DIM0, edges), f32),
            ((DIM1, 2 * edges), f32),
            ((DIM2, 2 * edges), f32),
            ((COLS, 2 * edges), bf16),
        ],
        source_row, lists, rot, g0, g1, g2, order.hold(pre_grad),
        conv_zero, conv_one, conv_two, alpha_in
    )
    order.mark(source_sums)
    next(zero_steps)
    for _ in range(bits_of("edge") - 1):
        next(rest_steps)
    message_hops = gather_lanes(order.hold(messages), order)
    next(message_hops)
    next(zero_steps)
    returned = order.hold(exchange(source_sums))
    next(rest_steps)
    message_rows = finish_steps(message_hops)
    zero_share = finish_steps(zero_steps)
    out, proj = call(
        make_finish(lanes_total),
        [((COEFFS, atoms, CH), bf16), ((PROJ_ROWS, LANES), f32)],
        [((total, WIDE), f32), ((2 * total, COLS), bf16), ((COEFFS, atoms, CH), bf16)],
        order.hold(cot), out_proj, *message_rows,
    )
    order.mark(proj)
    lane = lax.axis_index("edge")
    late_rows = PROJ_ROWS // lanes_total
    place = ((lane & 1) * (lanes_total // 2) + (lane >> 1)) * late_rows
    late = lax.dynamic_slice_in_dim(proj, place, late_rows, 0)
    share = jnp.concatenate([finish_steps(rest_steps), zero_share], axis=0)
    late_share = []
    doubling = double(order.mark(share), late_share, order)
    next(doubling)
    source_hops = gather_lanes(order.hold(returned), order)
    next(source_hops)
    for bit in range(bits_of("graph")):
        late = order.mark(late + order.hold(swap(late, "graph", bit)))
        if bit < bits_of("graph") - 1:
            next(doubling)
    late_share.append(late.astype(bf16))
    for _ in share_steps("edge")[bits_of("graph") :]:
        next(doubling)
    source_rows = finish_steps(source_hops)
    (embed,) = call(
        make_collect(lanes_total),
        [((COEFFS, atoms, CH), bf16)],
        [((total, WIDE), f32)],
        order.hold(source_rows[0]), *source_rows[1:],
    )
    order.mark(embed)
    mine, other = finish_steps(doubling)
    zero, one, two, grad_in, grad_edge, grad_dot, grad_proj = call(
        make_unpack(lanes_total, peers),
        [
            ((DIM0, DIM0), bf16),
            ((2, DIM1, DIM1), bf16),
            ((2, DIM2, DIM2), bf16),
            (alpha_in.shape, bf16),
            (alpha_edge.shape, bf16),
            ((2, LANES), bf16),
            (out_proj.shape, bf16),
        ],
        [],
        mine, other,
    )

    def shaped(value):
        return jnp.transpose(value, (1, 0, 2))

    return (
        shaped(out), shaped(embed), zero, one, two, grad_in, grad_edge, grad_dot.reshape(-1),
        grad_proj,
    )


def solution(mesh):
    in_specs = (
        P(("groups", "graph"), None, None),
        P(("groups", "graph"), None, None),
        P(("groups", "graph"), None, "edge", None),
        P(("groups", "graph"), None, "edge", None),
        P(("groups", "graph", "edge")),
        P(("groups", "graph", "edge")),
        P(("groups", "graph", "edge"), None),
        P(("groups", "graph", "edge"), None),
        P(("groups", "graph", "edge"), None),
        P(),
        P(),
        P(),
        P(),
        P(),
        P(),
        P(),
    )
    out_specs = (
        P(("groups", "graph"), None, None),
        P(("groups", "graph"), None, None),
        P("groups", None),
        P("groups", None, None),
        P("groups", None, None),
        P("groups", None),
        P("groups", None),
        P("groups"),
        P("groups", None, None),
    )
    return jax.shard_map(shards, mesh=mesh, in_specs=in_specs, out_specs=out_specs, check_vma=False)
```

```python
import jax
import jax.numpy as jnp
import numpy as np
from jax import lax
from jax.experimental import pallas as pl
from jax.experimental.pallas import tpu as pltpu
from jax.sharding import PartitionSpec as P

LMAX = 6
MMAX = 2
CH = 64
HEADS = 4
VAL = 16
ALPHA = 64
COEFFS = (LMAX + 1) * (LMAX + 1)
FLAT = COEFFS * CH
LANES = 128
BLOCKS = (FLAT + LANES - 1) // LANES
COLS = BLOCKS * LANES
WIDE = COLS + LANES
TABLE = 2 * COLS + LANES
PEAK_AT, DOT_AT, NAME_AT = HEADS, 2 * HEADS, 3 * HEADS
STATS = 16
DIM0 = (LMAX + 1) * CH
DIM1 = LMAX * CH
DIM2 = (LMAX - 1) * CH
PANEL = 256

leak_slope = 0.2
floor_value = -1e30
bf16 = jnp.bfloat16
f32 = jnp.float32

VMEM_LIMIT = 56 * 1024 * 1024


def degree_blocks():
    result = []
    offset = 0
    for degree in range(LMAX + 1):
        centre = min(degree, MMAX)
        row_total = 2 * centre + 1
        col_total = 2 * degree + 1
        result.append((degree, centre, row_total, col_total, offset))
        offset += row_total * col_total
    return result


def degree_of(coeff):
    return int(np.sqrt(coeff))


def dot_nn(left, right):
    return jnp.dot(left, right, preferred_element_type=f32)


def dot_nt(left, right):
    return lax.dot_general(left, right, (((1,), (1,)), ((), ())), preferred_element_type=f32)


def dot_tn(left, right):
    return lax.dot_general(left, right, (((0,), (0,)), ((), ())), preferred_element_type=f32)


def iota(shape, dim):
    return lax.broadcasted_iota(jnp.int32, shape, dim)


def split_two(value):
    high = value.astype(bf16)
    return high, (value - high.astype(f32)).astype(bf16)


def to_frame(source, rot, edges, emit):
    for half in range(edges // LANES):
        lanes = pl.ds(half * LANES, LANES)
        for degree, centre, row_total, col_total, offset in degree_blocks():
            sums = [None] * row_total
            for j in range(col_total):
                column = source[pl.ds((degree * degree + j) * CH, CH), lanes]
                for i in range(row_total):
                    term = rot[pl.ds(offset + i * col_total + j, 1), lanes] * column
                    sums[i] = term if j == 0 else sums[i] + term
            for i in range(row_total):
                emit(degree, i - centre, half, sums[i])


def from_frame(load, rot, edges, emit):
    for half in range(edges // LANES):
        lanes = pl.ds(half * LANES, LANES)
        for degree, centre, row_total, col_total, offset in degree_blocks():
            rows = [load(degree, i - centre, half) for i in range(row_total)]
            for j in range(col_total):
                total = None
                for i in range(row_total):
                    term = rot[pl.ds(offset + i * col_total + j, 1), lanes] * rows[i]
                    total = term if i == 0 else total + term
                emit(degree * degree + j, half, total)


def lane_at(half, edges, second):
    return pl.ds(half * LANES + (edges if second else 0), LANES)


def frame_place(degree, order, refs):
    if order == 0:
        return refs[0], degree * CH, False
    which = abs(order)
    return refs[which], (degree - which) * CH, order < 0


def spread_heads(rows):
    return jnp.concatenate(
        [jnp.broadcast_to(row, (VAL, row.shape[1])) for row in rows], axis=0
    )


def is_direct(peers):
    return peers <= 4


def flip_of(peers):
    return lax.axis_index("graph") if is_direct(peers) else 0


def one_hot_rows(slot_ref, peers, slots):
    edges = slot_ref.shape[1]
    first = flip_of(peers) * (slots // peers)
    return jnp.bitwise_xor(iota((slots, edges), 0), first) == slot_ref[...]


def mask_to(mask, dtype):
    return jnp.where(mask, 1.0, 0.0).astype(dtype)


def stack_table(tables, rows_ref):
    cap = tables[0].shape[0]
    per = 8 // cap
    for n in range(0, len(tables), per):
        parts = [table[...].astype(f32) for table in tables[n : n + per]]
        rows_ref[pl.ds(n * cap, 8), :] = jnp.concatenate(parts, axis=0)


def put_rows(out_ref, cols, value):
    peers, cap = out_ref.shape[0], out_ref.shape[1]
    for n in range(peers):
        out_ref[n, :, cols] = value[n * cap : (n + 1) * cap].astype(out_ref.dtype)


def slot_sums(terms, one_hot, out_ref, factor=None):
    both = jnp.concatenate([one_hot, one_hot], axis=1)
    products = 0.0
    for start in range(0, COLS, PANEL):
        size = min(PANEL, COLS - start)
        sums = dot_nt(both, terms[pl.ds(start, size), :])
        put_rows(out_ref, pl.ds(start, size), sums)
        if factor is None:
            continue
        for at in range(0, size, LANES):
            width = min(LANES, FLAT - start - at)
            product = sums[:, at : at + width] * factor[:, pl.ds(start + at, width)]
            if width < LANES:
                product = jnp.concatenate([product, jnp.zeros_like(product)], axis=1)
            products = products + product
    return products


def store_terms(terms, edges):
    def emit(coeff, half, value):
        high, low = split_two(value)
        rows = pl.ds(coeff * CH, CH)
        terms[rows, lane_at(half, edges, False)] = high
        terms[rows, lane_at(half, edges, True)] = low

    return emit


def listed_rows(list_ref, shape):
    peers, cap = list_ref.shape[1], list_ref.shape[3]
    flip = flip_of(peers)
    row = iota(shape, 0)
    result = jnp.zeros(shape, jnp.int32)
    for slot in range(peers * cap):
        owner = jnp.bitwise_xor(flip, slot // cap) if is_direct(peers) else slot // cap
        result = jnp.where(row == slot, list_ref[0, owner, 0, slot % cap], result)
    return result


def put_coeffs(outs, first, coeff_rows):
    for block in range(BLOCKS):
        left = coeff_rows(2 * block)
        right = coeff_rows(2 * block + 1) if 2 * block + 1 < COEFFS else jnp.zeros_like(left)
        put_pieces(outs, first + block * LANES, jnp.concatenate([left, right], axis=1))


def put_pieces(outs, first, value):
    cap = outs[0].shape[0]
    for n, out in enumerate(outs):
        out[:, pl.ds(first, LANES)] = value[n * cap : (n + 1) * cap].astype(out.dtype)


def outgoing_kernel(send, recv, embed, cot, *outs):
    atoms = embed.shape[1]
    slots = send.shape[1] * send.shape[3]
    sent = listed_rows(send, (slots, LANES))
    received = listed_rows(recv, (slots, LANES))
    for first, listed, values in ((0, sent, embed), (COLS, received, cot)):
        picked = mask_to(iota((slots, atoms), 1) == listed[:, :atoms], bf16)
        put_coeffs(outs, first, lambda k: dot_nn(picked, values[k]))
    lane = iota((slots, LANES), 1)
    side = jnp.where(lane == 0, received, jnp.where(lane == 1, sent, 0))
    put_pieces(outs, 2 * COLS, side.astype(f32))


def swapped_halves(value, edges):
    return jnp.concatenate([-value[:, edges:], value[:, :edges]], axis=1)


def make_forward(atoms, peers):
    def forward_kernel(
        source_slot, target_slot, rotation, feats, bias, wzero_at, wone_at, wtwo_at,
        ain, aedge, adot, out_proj, *rest,
    ):
        tables, rest = rest[:peers], rest[peers:]
        (
        sums_out, stats_out, x0_at, x1_at, x2_at, v0_at, v1_at, v2_at, pre_at, logit_out,
        lists_out, agg_grad, rot, own_out,
        rows, gathered, weights, terms, wzero, wone, wtwo, x0, x1, x2, v0, v1, v2, pre_out,
        semaphores,
        ) = rest
        copies = []

        def move(source, target):
            copy = pltpu.make_async_copy(source, target, semaphores.at[len(copies)])
            copy.start()
            copies.append(copy)

        move(wzero_at, wzero)
        move(wone_at, wone)
        move(wtwo_at, wtwo)
        rot[...] = jnp.transpose(rotation[...].astype(f32))
        edges = source_slot.shape[1]
        cap = tables[0].shape[0]
        slots = peers * cap
        stack_table(tables, rows)
        picked = mask_to(one_hot_rows(source_slot, peers, slots), bf16)
        for degree in range(LMAX + 1):
            ids = pl.ds(degree * degree * CH, (2 * degree + 1) * CH)
            gathered[ids, :] = dot_tn(rows[:, ids].astype(bf16), picked)
        lists = rows[:, pl.ds(2 * COLS, LANES)]
        lists_out[...] = lists
        for degree in range(LMAX + 1):
            ids = range(degree * degree, (degree + 1) * (degree + 1))
            cot = jnp.concatenate([rows[:, pl.ds(COLS + k * CH, CH)] for k in ids], axis=0)
            grad = dot_nt(cot.astype(bf16), out_proj[degree])
            for n, k in enumerate(ids):
                agg_grad[:, pl.ds(k * CH, CH)] = grad[n * slots : (n + 1) * slots]

        def emit(degree, order, half, value):
            ref, row, second = frame_place(degree, order, (x0, x1, x2))
            ref[pl.ds(row, CH), lane_at(half, edges, second)] = value.astype(bf16)

        to_frame(gathered, rot, edges, emit)
        for source, target in ((x0, x0_at), (x1, x1_at), (x2, x2_at)):
            move(source, target)

        pre = dot_tn(ain[...], x0[pl.ds(0, CH), :]) + lax.dot_general(
            aedge[...], feats[...], (((0,), (1,)), ((), ())), preferred_element_type=f32
        )
        pre_out[...] = pre
        move(pre_out, pre_at)
        hidden = jnp.where(pre > 0, pre, leak_slope * pre) * turned_column(adot[...].astype(f32))
        aims = one_hot_rows(target_slot, peers, slots)
        lane = iota((slots, LANES), 1)
        peer = jnp.bitwise_xor(iota((slots, 1), 0) // cap, flip_of(peers))
        name = lists[:, :1] + (peer * atoms).astype(f32)
        side = jnp.where(lane == NAME_AT, name, 0.0)
        for h in range(HEADS):
            logit = jnp.sum(hidden[h * ALPHA : (h + 1) * ALPHA], axis=0, keepdims=True)
            logit = logit + bias[pl.ds(h, 1), :]
            logit_out[pl.ds(h, 1), :] = logit
            peak = jnp.max(jnp.where(aims, logit, floor_value), axis=1, keepdims=True)
            of_edge = jnp.sum(jnp.where(aims, peak, 0.0), axis=0, keepdims=True)
            weight = jnp.exp(logit - of_edge)
            weights[pl.ds(h, 1), :] = weight
            den = jnp.sum(jnp.where(aims, weight, 0.0), axis=1, keepdims=True)
            side = jnp.where(lane == h, den, jnp.where(lane == PEAK_AT + h, peak, side))

        for copy in copies[:3]:
            copy.wait()
        v0[...] = dot_tn(wzero[...], x0[...])
        for out, weight, value in ((v1, wone, x1[...]), (v2, wtwo, x2[...])):
            out[...] = dot_tn(weight[0], value) + swapped_halves(dot_tn(weight[1], value), edges)
        for source, target in ((v0, v0_at), (v1, v1_at), (v2, v2_at)):
            move(source, target)

        def load(degree, order, half):
            ref, row, second = frame_place(degree, order, (v0, v1, v2))
            return ref[pl.ds(row, CH), lane_at(half, edges, second)]

        store = store_terms(terms, edges)

        def weigh(coeff, half, value):
            lanes = lane_at(half, edges, False)
            spread = spread_heads([weights[pl.ds(h, 1), lanes] for h in range(HEADS)])
            store(coeff, half, value * spread)

        terms[pl.ds(FLAT, COLS - FLAT), :] = jnp.zeros((COLS - FLAT, 2 * edges), bf16)
        from_frame(load, rot, edges, weigh)
        dots = slot_sums(terms, mask_to(aims, bf16), sums_out, agg_grad)
        head = (lane % CH) // VAL
        for h in range(HEADS):
            dot = jnp.sum(jnp.where(head == h, dots, 0.0), axis=1, keepdims=True)
            side = jnp.where(lane == DOT_AT + h, dot, side)
        put_rows(sums_out, pl.ds(COLS, LANES), side)
        own_out[...] = side
        spread = jnp.concatenate([side[:, :STATS]] * (LANES // STATS), axis=1)
        spread = jnp.where(lane // STATS == iota((slots, LANES), 0) % 8, spread, 0.0)
        packed = jnp.sum(spread.reshape(slots // 8, 8, LANES), axis=1)

        stats_out[...] = packed
        for copy in copies[3:]:
            copy.wait()

    return forward_kernel


def lane_heads(values, shape):
    head = (iota(shape, 1) % CH) // VAL
    result = jnp.broadcast_to(values[0], shape)
    for h in range(1, HEADS):
        result = jnp.where(head == h, values[h], result)
    return result


def collect_rows(arrivals, rows_ref):
    own = lax.axis_index("edge")
    for k, arrival in enumerate(arrivals):
        peers, cap, width = arrival.shape
        base = (own ^ k) * (peers * cap)
        for start in range(0, peers * cap, 8):
            parts = [arrival[g] for g in range(start // cap, (start + 8) // cap)]
            at = pl.ds(pl.multiple_of(base + start, 8), 8)
            rows_ref[at, :] = jnp.concatenate(parts, axis=0)


def block_cols(block):
    return pl.ds(block * LANES, min(LANES, FLAT - block * LANES))


def make_finish(lanes_total):
    def finish_kernel(cot, out_proj, *rest):
        arrivals = rest[:lanes_total]
        out, proj, rows, terms, agg_low = rest[lanes_total:]
        atoms = cot.shape[1]
        total = rows.shape[0]
        collect_rows(arrivals, rows)
        side = rows[:, pl.ds(COLS, LANES)]
        owner = (lax.axis_index("graph") * atoms).astype(f32)
        names = iota((total, atoms), 1).astype(f32) + owner == side[:, NAME_AT : NAME_AT + 1]
        eye = iota((atoms, atoms), 0) == iota((atoms, atoms), 1)
        scales, dens = [], []
        for h in range(HEADS):
            peak_rows = side[:, PEAK_AT + h : PEAK_AT + h + 1]
            peak = jnp.max(jnp.where(names, peak_rows, floor_value), axis=0, keepdims=True)
            of_row = jnp.sum(jnp.where(names, peak, 0.0), axis=1, keepdims=True)
            scale = jnp.exp(peak_rows - of_row)
            scaled_den = side[:, h : h + 1] * scale
            den = jnp.sum(jnp.where(names, scaled_den, 0.0), axis=0, keepdims=True)
            scales.append(scale)
            dens.append(jnp.sum(jnp.where(eye, den, 0.0), axis=1, keepdims=True))
        scale_full = lane_heads(scales, (total, LANES))
        den_full = lane_heads(dens, (atoms, LANES))
        picked = mask_to(names, bf16)
        twice = jnp.concatenate([picked, picked], axis=0)
        for block in range(BLOCKS):
            cols = pl.ds(block * LANES, LANES)
            high, low = split_two(rows[:, cols] * scale_full)
            terms[pl.ds(0, total), cols] = high
            terms[pl.ds(total, total), cols] = low
        for block in range(BLOCKS):
            cols = pl.ds(block * LANES, LANES)
            agg = (dot_tn(twice, terms[:, cols]) / den_full).astype(bf16)
            agg_low[2 * block] = agg[:, :CH]
            if 2 * block + 1 < COEFFS:
                agg_low[2 * block + 1] = agg[:, CH:]
        for degree in range(LMAX + 1):
            ids = pl.ds(degree * degree, 2 * degree + 1)
            stacked = ((2 * degree + 1) * atoms, CH)
            left = agg_low[ids].reshape(stacked)
            right = cot[ids].reshape(stacked)
            value = dot_nn(left, out_proj[degree]).astype(bf16)
            out[ids] = value.reshape((2 * degree + 1, atoms, CH))
            at = (pl.ds(degree // 2 * CH, CH), pl.ds(degree % 2 * CH, CH))
            proj[at] = dot_tn(left, right)
        proj[pl.ds(LMAX // 2 * CH, CH), pl.ds(CH, CH)] = jnp.zeros((CH, CH), f32)

    return finish_kernel


def combine_stats(stats, own):
    chunk = 32
    name = own[:, NAME_AT : NAME_AT + 1]

    def part(part_rows):
        entries = [part_rows[:, n : n + STATS] for n in range(0, LANES, STATS)]
        turned = jnp.transpose(jnp.concatenate(entries, axis=0))
        same = name == turned[NAME_AT : NAME_AT + 1]
        result = []
        for h in range(HEADS):
            peaks = turned[PEAK_AT + h : PEAK_AT + h + 1]
            peak = jnp.max(jnp.where(same, peaks, floor_value), axis=1, keepdims=True)
            scale = jnp.where(same, jnp.exp(jnp.where(same, peaks - peak, 0.0)), 0.0)
            den = jnp.sum(turned[h : h + 1] * scale, axis=1, keepdims=True)
            dot = jnp.sum(turned[DOT_AT + h : DOT_AT + h + 1] * scale, axis=1, keepdims=True)
            result += [peak, den, dot]
        return tuple(result)

    def step(at, held):
        fresh = part(stats[0][pl.ds(pl.multiple_of(at * chunk, chunk), chunk), :])
        result = []
        for h in range(HEADS):
            peak, den, dot = held[3 * h : 3 * h + 3]
            new_peak, new_den, new_dot = fresh[3 * h : 3 * h + 3]
            most = jnp.maximum(peak, new_peak)
            old, new = jnp.exp(peak - most), jnp.exp(new_peak - most)
            result += [most, den * old + new_den * new, dot * old + new_dot * new]
        return tuple(result)

    if len(stats) > 1:
        held = part(jnp.concatenate([rows[...] for rows in stats], axis=0))
    else:
        held = part(stats[0][pl.ds(0, chunk), :])
        held = lax.fori_loop(1, stats[0].shape[0] // chunk, step, held)
    return [held[3 * h : 3 * h + 3] for h in range(HEADS)]


def make_gradient(peers, parts):
    def kernel(*refs):
        gradient_kernel(peers, refs[:parts], *refs[parts:])

    return kernel


def gradient_kernel(
    peers, stats, own, agg_grad, target_slot, rot, feats,
    x0_at, x1_at, x2_at, v0_at, v1_at, v2_at, pre, logits, adot,
    g0, top1, top2, pre_grad_out, kept0, sent0, kept1, sent1,
    num_grad, spread_grad, weights, g1, g2, packed, x0, x1, x2, v0, v1, v2, semaphores,
):
    loads = []
    for source, target in (
        (v0_at, v0), (v1_at, v1), (v2_at, v2), (x0_at, x0), (x1_at, x1), (x2_at, x2)
    ):
        load = pltpu.make_async_copy(source, target, semaphores.at[4 + len(loads)])
        load.start()
        loads.append(load)
    edges = target_slot.shape[1]
    slots = agg_grad.shape[0]
    aims = one_hot_rows(target_slot, peers, slots)
    combined = combine_stats(stats, own[...])
    den_grads = []
    for h, (peak, den, dot) in enumerate(combined):
        of_edge = jnp.sum(jnp.where(aims, peak, 0.0), axis=0, keepdims=True)
        weights[pl.ds(h, 1), :] = jnp.exp(logits[pl.ds(h, 1), :] - of_edge)
        den_grad = (-(dot / den) / den).astype(bf16).astype(f32)
        den_grads.append(jnp.sum(jnp.where(aims, den_grad, 0.0), axis=0, keepdims=True))
    den_full = lane_heads([den for peak, den, dot in combined], (slots, LANES))
    for block in range(BLOCKS):
        cols = block_cols(block)
        num_grad[:, cols] = (agg_grad[:, cols] / den_full[:, : cols.size]).astype(bf16)
    picked = mask_to(aims, bf16)
    for degree in range(LMAX + 1):
        ids = pl.ds(degree * degree * CH, (2 * degree + 1) * CH)
        spread_grad[ids, :] = dot_tn(num_grad[:, ids], picked)

    state = {}

    def emit(degree, order, half, value):
        lanes = lane_at(half, edges, False)
        ref, row, second = frame_place(degree, order, (v0, v1, v2))
        product = value * ref[pl.ds(row, CH), lane_at(half, edges, second)]
        if degree == 0:
            state["sum"] = product
            state["spread"] = spread_heads([weights[pl.ds(h, 1), lanes] for h in range(HEADS)])
        else:
            state["sum"] = state["sum"] + product
        grad = (value * state["spread"]).astype(bf16)
        ref, row, second = frame_place(degree, order, (g0, g1, g2))
        ref[pl.ds(row, CH), lane_at(half, edges, second)] = grad
        if order != 0:
            swapped = grad if order < 0 else -grad
            below = row + (DIM1 if abs(order) == 1 else DIM2)
            ref[pl.ds(below, CH), lane_at(half, edges, not second)] = swapped
        if degree == LMAX and order == MMAX:
            for h in range(HEADS):
                part = state["sum"][h * VAL : (h + 1) * VAL]
                weights[pl.ds(HEADS + h, 1), lanes] = jnp.sum(part, axis=0, keepdims=True)

    for load in loads:
        load.wait()
    to_frame(spread_grad, rot, edges, emit)

    hidden = jnp.where(pre[...] > 0, pre[...], leak_slope * pre[...])
    logit_grads = [
        weights[pl.ds(h, 1), :] * (weights[pl.ds(HEADS + h, 1), :] + den_grads[h])
        for h in range(HEADS)
    ]
    tall = jnp.concatenate(
        [jnp.broadcast_to(row, (ALPHA, edges)) for row in logit_grads], axis=0
    )
    slope = jnp.where(pre[...] > 0, 1.0, leak_slope)
    pre_grad = (tall * turned_column(adot[...].astype(f32)) * slope).astype(bf16)
    pre_grad_out[...] = pre_grad
    dot_grad = jnp.sum(tall * hidden, axis=1, keepdims=True)

    top1[...] = g1[pl.ds(0, DIM1), :]
    top2[...] = g2[pl.ds(0, DIM2), :]
    mine = lax.axis_index("edge") & 1
    copies = []

    def put(row, value, at=0):
        for side in range(2):
            low, high = max(at, side * LANES), min(at + value.shape[1], (side + 1) * LANES)
            if low < high:
                piece = value[:, low - at : high - at]
                cols = pl.ds(low - side * LANES, high - low)
                packed[side, pl.ds(row, value.shape[0]), cols] = piece

    def send(chunk, kept, sent):
        start, size = CHUNKS[chunk]
        rows_of = pl.ds(start, size)
        for n, (side, out) in enumerate(((mine, kept), (1 - mine, sent))):
            copy = pltpu.make_async_copy(
                packed.at[side, rows_of, :], out, semaphores.at[2 * chunk + n]
            )
            copy.start()
            copies.append(copy)

    row = 0
    for left, right, dim in ((x1, g1, DIM1), (x2, g2, DIM2)):
        for start in range(0, 2 * dim, PANEL):
            size = min(PANEL, 2 * dim - start)
            put(row, dot_nt(left[...], right[pl.ds(start, size), :]))
            row += dim
    row -= DIM2
    edge_ch = feats.shape[1]
    edge_grad = lax.dot_general(
        feats[...], pre_grad, (((0,), (1,)), ((), ())), preferred_element_type=f32
    )
    put(row, edge_grad[:, :LANES], LANES)
    put(row + edge_ch, edge_grad[:, LANES:], LANES)
    wide_dot = jnp.transpose(jnp.broadcast_to(dot_grad, (HEADS * ALPHA, LANES)))
    spare = DIM2 - 2 * edge_ch
    tail = iota((spare, LANES), 0)
    first = jnp.broadcast_to(wide_dot[:1, :LANES], (spare, LANES))
    second = jnp.broadcast_to(wide_dot[:1, LANES:], (spare, LANES))
    put(row + 2 * edge_ch, jnp.where(tail == 0, first, jnp.where(tail == 1, second, 0.0)), LANES)
    row += DIM2
    put(row, dot_nt(x0[pl.ds(0, CH), :], pre_grad))
    send(0, kept0, sent0)

    row = CHUNKS[1][0]
    for start in range(0, DIM0, PANEL):
        size = min(PANEL, DIM0 - start)
        put(row, dot_nt(x0[...], g0[pl.ds(start, size), :]))
        if size < PANEL:
            put(row, jnp.zeros((DIM0, PANEL - size), f32), size)
        row += DIM0
    send(1, kept1, sent1)
    for copy in copies:
        copy.wait()


PROJ_ROWS = (LMAX // 2 + 1) * CH
CHUNKS = ((0, 3 * DIM1 + 3 * DIM2 + CH), (3 * DIM1 + 3 * DIM2 + CH, 2 * DIM0))
PACKED_ROWS = sum(size for start, size in CHUNKS)


def halves_of(mine, other):
    first = (lax.axis_index("edge") & 1) == 0
    left, right = mine[...].astype(f32), other[...].astype(f32)
    return jnp.where(first, left, right), jnp.where(first, right, left)


def reversed_bits(value, count):
    return sum(((value >> n) & 1) << (count - 1 - n) for n in range(count))


def make_unpack(lanes_total, peers):
    def unpack_kernel(mine, other, zero, one, two, alpha_in, alpha_edge, alpha_dot, proj):
        cols = lanes_total // 2
        col_bits = (cols - 1).bit_length()
        late = PROJ_ROWS // lanes_total
        first_rows = CHUNKS[0][1] // (cols * peers)
        share = first_rows + CHUNKS[1][1] // (cols * peers)
        main, zeros, tail = [], [], {}
        for core, value in enumerate(halves_of(mine, other)):
            parts, zero_parts = [], {}
            for col in range(cols):
                rows = []
                for peer in range(peers):
                    start = col * (peers * share + late) + peer * share
                    rows.append(value[start : start + first_rows])
                    zero_parts[peer * cols + col] = value[start + first_rows : start + share]
                parts += rows
                end = (col + 1) * (peers * share + late)
                tail[core * cols + reversed_bits(col, col_bits)] = value[end - late : end]
            main.append(jnp.concatenate(parts, axis=0))
            zeros.append(jnp.concatenate([zero_parts[n] for n in sorted(zero_parts)], axis=0))
        tail = jnp.concatenate([tail[n] for n in sorted(tail)], axis=0)
        for degree in range(LMAX + 1):
            piece = tail[degree // 2 * CH : (degree // 2 + 1) * CH]
            proj[degree] = piece[:, degree % 2 * CH : (degree % 2 + 1) * CH].astype(bf16)
        left, right = zeros
        zero[:, pl.ds(0, LANES)] = left[:DIM0].astype(bf16)
        zero[:, pl.ds(LANES, LANES)] = right[:DIM0].astype(bf16)
        zero[:, pl.ds(2 * LANES, LANES)] = left[DIM0:].astype(bf16)
        zero[:, pl.ds(3 * LANES, DIM0 - 3 * LANES)] = right[DIM0:, : DIM0 - 3 * LANES].astype(bf16)
        unpack_rest(*main, one, two, alpha_in, alpha_edge, alpha_dot)

    return unpack_kernel


def unpack_rest(left, right, one, two, alpha_in, alpha_edge, alpha_dot):
    for n in range(2 * DIM1 // LANES):
        panel = (left, right)[n % 2][(n // 2) * DIM1 : (n // 2 + 1) * DIM1]
        per = DIM1 // LANES
        one[n // per, :, pl.ds((n % per) * LANES, LANES)] = panel.astype(bf16)
    left, right = left[3 * DIM1 :], right[3 * DIM1 :]
    panels = [(left, right)[n % 2][(n // 2) * DIM2 : (n // 2 + 1) * DIM2] for n in range(5)]
    whole = jnp.concatenate(panels, axis=1)
    two[0] = whole[:, :DIM2].astype(bf16)
    two[1] = whole[:, DIM2:].astype(bf16)
    edge_ch = alpha_edge.shape[0]
    rest = right[2 * DIM2 : 3 * DIM2]
    alpha_edge[:, pl.ds(0, LANES)] = rest[:edge_ch].astype(bf16)
    alpha_edge[:, pl.ds(LANES, LANES)] = rest[edge_ch : 2 * edge_ch].astype(bf16)
    alpha_dot[...] = rest[2 * edge_ch : 2 * edge_ch + 2].astype(bf16)
    alpha_in[:, pl.ds(0, LANES)] = left[3 * DIM2 :].astype(bf16)
    alpha_in[:, pl.ds(LANES, LANES)] = right[3 * DIM2 :].astype(bf16)


def source_kernel(
    source_slot, lists, rot, g0, g1, g2, pre_grad, wzero, wone, wtwo, ain,
    *rest,
):
    sums_out, d0, d1, d2, terms = rest[-5:]
    edges = source_slot.shape[1]
    slots = sums_out.shape[0] * sums_out.shape[1]
    d0[...] = dot_nn(wzero[...], g0[...])
    d0[pl.ds(0, CH), :] += dot_nn(ain[...], pre_grad[...])
    for out, weight, value in ((d1, wone, g1[...]), (d2, wtwo, g2[...])):
        out[...] = dot_nn(weight[0], value) - swapped_halves(dot_nn(weight[1], value), edges)

    def load(degree, order, half):
        ref, row, second = frame_place(degree, order, (d0, d1, d2))
        return ref[pl.ds(row, CH), lane_at(half, edges, second)]

    terms[pl.ds(FLAT, COLS - FLAT), :] = jnp.zeros((COLS - FLAT, 2 * edges), bf16)
    from_frame(load, rot, edges, store_terms(terms, edges))
    slot_sums(terms, mask_to(one_hot_rows(source_slot, sums_out.shape[0], slots), bf16), sums_out)
    put_rows(sums_out, pl.ds(COLS, LANES), lists[...])


def make_collect(lanes_total):
    def collect_kernel(*rest):
        arrivals = rest[:lanes_total]
        out, rows = rest[lanes_total:]
        atoms = out.shape[1]
        total = rows.shape[0]
        collect_rows(arrivals, rows)
        index = rows[:, pl.ds(COLS, LANES)][:, 1:2]
        picked = mask_to(iota((total, atoms), 1).astype(f32) == index, bf16)
        twice = jnp.concatenate([picked, picked], axis=0)
        for block in range(BLOCKS):
            high, low = split_two(rows[:, pl.ds(block * LANES, LANES)])
            sums = dot_tn(twice, jnp.concatenate([high, low], axis=0)).astype(bf16)
            out[2 * block] = sums[:, :CH]
            if 2 * block + 1 < COEFFS:
                out[2 * block + 1] = sums[:, CH:]

    return collect_kernel


vmem = pl.BlockSpec(memory_space=pltpu.VMEM)
smem = pl.BlockSpec(memory_space=pltpu.SMEM)
anywhere = pl.BlockSpec(memory_space=pl.ANY)


def call(kernel, outs, scratch, *args, scalars=0, far=(), apart=(), after=()):
    specs = [smem if n < scalars else anywhere if n in far else vmem for n in range(len(args))]
    specs += [anywhere] * len(after)
    out_specs = [anywhere if n in apart else vmem for n in range(len(outs))]
    shapes = [pltpu.VMEM(*entry) if isinstance(entry, tuple) else entry for entry in scratch]
    return pl.pallas_call(
        kernel,
        out_shape=[jax.ShapeDtypeStruct(shape, kind) for shape, kind in outs],
        in_specs=specs,
        out_specs=out_specs,
        scratch_shapes=shapes,
        compiler_params=pltpu.CompilerParams(vmem_limit_bytes=VMEM_LIMIT),
        cost_estimate=pl.CostEstimate(flops=1, bytes_accessed=1, transcendentals=0),
    )(*args, *after)


class Order:
    def __init__(self):
        self.last = None

    def hold(self, value):
        if self.last is None:
            return value
        return lax.optimization_barrier((value, self.last))[0]

    def mark(self, value):
        self.last = value
        return value


def turned_column(row):
    return jnp.transpose(jnp.broadcast_to(row, (8, row.shape[1])))[:, :1]


def swap(value, axis, bit):
    size = lax.axis_size(axis)
    return lax.ppermute(value, axis, [(i, i ^ (1 << bit)) for i in range(size)])


def bits_of(axis):
    return (lax.axis_size(axis) - 1).bit_length()


def gather_lanes(value, order):
    held = {0: value}
    for bit in reversed(range(bits_of("edge"))):
        fresh = {}
        for k, v in held.items():
            fresh[k | (1 << bit)] = swap(order.hold(v) if k else v, "edge", bit)
        held.update(fresh)
        yield
    return [held[k] for k in range(len(held))]


def own_bit(axis, bit):
    return (lax.axis_index(axis) >> bit) & 1


def share_steps(first):
    steps = [("edge", n) for n in range(1, bits_of("edge"))]
    steps += [("graph", n) for n in range(bits_of("graph"))]
    return sorted(steps, key=lambda step: step[0] != first)


def halve(kept, sent, first, order):
    other = swap(sent, "edge", 0)
    yield
    current = kept + order.hold(other)
    for axis, bit in share_steps(first):
        mine = own_bit(axis, bit)
        parts = current.reshape(2, current.shape[0] // 2, -1)
        sent = order.mark(lax.dynamic_index_in_dim(parts, 1 - mine, 0, False))
        other = swap(sent, axis, bit)
        yield
        current = lax.dynamic_index_in_dim(parts, mine, 0, False) + order.hold(other)
    return order.mark(current.astype(bf16))


def double(current, late, order):
    joined = False
    for axis, bit in reversed(share_steps("edge")):
        if axis == "edge" and not joined:
            current, joined = jnp.concatenate([current, late[0]], axis=0), True
        mine = own_bit(axis, bit)
        other = swap(current, axis, bit)
        yield
        other = order.hold(other)
        current = order.mark(
            jnp.concatenate(
                [jnp.where(mine == 0, current, other), jnp.where(mine == 0, other, current)],
                axis=0,
            )
        )
    return current, swap(current, "edge", 0)


def finish_steps(chain):
    while True:
        try:
            next(chain)
        except StopIteration as end:
            return end.value


def shards(
    atom_embed, out_cotangent, send_rows, recv_rows, source_slot, target_slot, rotation,
    edge_feats, edge_bias, conv_zero, conv_one, conv_two, alpha_in, alpha_edge, alpha_dot,
    out_proj,
):
    peers = lax.axis_size("graph")
    lanes_total = lax.axis_size("edge")
    atoms = atom_embed.shape[0]
    edges = rotation.shape[0]
    cap = send_rows.shape[3]
    slots = peers * cap
    blocks = peers * lanes_total
    direct = is_direct(peers)
    order = Order()

    def pairwise(pieces):
        return [pieces[0]] + [
            lax.ppermute(pieces[k], "graph", [(i, i ^ k) for i in range(peers)])
            for k in range(1, peers)
        ]

    def exchange(value):
        if direct:
            return jnp.stack(pairwise([value[k] for k in range(peers)]))
        return lax.all_to_all(value, "graph", split_axis=0, concat_axis=0, tiled=True)

    cot = jnp.transpose(out_cotangent, (1, 0, 2))
    outgoing = call(
        outgoing_kernel, [((cap, TABLE), bf16)] * peers, [],
        send_rows, recv_rows, jnp.transpose(atom_embed, (1, 0, 2)), cot,
        scalars=2
    )
    tables = pairwise(outgoing) if direct else list(exchange(jnp.stack(outgoing)))

    source_row = source_slot.reshape(1, edges)
    target_row = target_slot.reshape(1, edges)
    bias = edge_bias.T
    adot = alpha_dot.reshape(1, -1)

    frames = [
        ((DIM0, edges), bf16),
        ((DIM1, 2 * edges), bf16),
        ((DIM2, 2 * edges), bf16),
        ((DIM0, edges), f32),
        ((DIM1, 2 * edges), f32),
        ((DIM2, 2 * edges), f32),
    ]
    pre_shape = ((HEADS * ALPHA, edges), f32)
    sums, stats, x0, x1, x2, v0, v1, v2, pre, logits, lists, agg_grad, rot, own_stats = call(
        make_forward(atoms, peers),
        [((peers, cap, WIDE), f32), ((slots // 8, LANES), f32)]
        + frames
        + [
            pre_shape,
            ((8, edges), f32),
            ((slots, LANES), f32),
            ((slots, FLAT), f32),
            ((rotation.shape[1], edges), f32),
            ((slots, LANES), f32),
        ],
        [
            ((slots, TABLE), f32),
            ((FLAT, edges), f32),
            ((8, edges), f32),
            ((COLS, 2 * edges), bf16),
            (conv_zero.shape, bf16),
            (conv_one.shape, bf16),
            (conv_two.shape, bf16),
        ]
        + frames
        + [pre_shape, pltpu.SemaphoreType.DMA((10,))],
        source_row, target_row, rotation, edge_feats, bias,
        conv_zero, conv_one, conv_two, alpha_in, alpha_edge, adot, out_proj, *tables,
        far=(5, 6, 7), apart=range(2, 9)
    )
    if direct:
        lanes_stats = [stats] + [
            lax.ppermute(stats, "edge", [(i, i ^ k) for i in range(lanes_total)])
            for k in range(1, lanes_total)
        ]
        graph_stats = jnp.concatenate(lanes_stats, axis=0)
        all_stats = [graph_stats] + [
            lax.ppermute(graph_stats, "graph", [(i, i ^ k) for i in range(peers)])
            for k in range(1, peers)
        ]
    else:
        all_stats = [lax.all_gather(stats, ("graph", "edge"), tiled=True)]

    halves = [((size, LANES), f32) for start, size in CHUNKS for _ in range(2)]
    g0, g1, g2, pre_grad, *halves = call(
        make_gradient(peers, len(all_stats)),
        [
            ((DIM0, edges), bf16),
            ((DIM1, 2 * edges), bf16),
            ((DIM2, 2 * edges), bf16),
            ((HEADS * ALPHA, edges), bf16),
        ]
        + halves,
        [
            ((slots, FLAT), bf16),
            ((FLAT, edges), f32),
            ((8, edges), f32),
            ((2 * DIM1, 2 * edges), bf16),
            ((2 * DIM2, 2 * edges), bf16),
            ((2, PACKED_ROWS, LANES), f32),
        ]
        + frames
        + [pltpu.SemaphoreType.DMA((10,))],
        *all_stats, own_stats, agg_grad, target_row, rot, edge_feats,
        x0, x1, x2, v0, v1, v2, pre, logits, adot,
        far=range(len(all_stats) + 5, len(all_stats) + 11), apart=range(4, 8)
    )

    total = lanes_total * slots
    order.mark(halves[0])
    held_sums = order.hold(sums)
    pieces = pairwise([held_sums[k] for k in range(peers)]) if direct else [exchange(held_sums)]
    rest_steps = halve(halves[0], halves[1], "edge", order)
    zero_steps = halve(halves[2], halves[3], "graph", order)
    next(rest_steps)
    next(zero_steps)
    next(rest_steps)
    next(zero_steps)
    (source_sums,) = call(
        source_kernel,
        [((peers, cap, WIDE), f32)],
        [
            ((DIM0, edges), f32),
            ((DIM1, 2 * edges), f32),
            ((DIM2, 2 * edges), f32),
            ((COLS, 2 * edges), bf16),
        ],
        source_row, lists, rot, g0, g1, g2, order.hold(pre_grad),
        conv_zero, conv_one, conv_two, alpha_in
    )
    order.mark(source_sums)
    next(zero_steps)
    for _ in range(bits_of("edge") - 1):
        next(rest_steps)
    pieces = [order.hold(piece) for piece in pieces]
    message_hops = gather_lanes(jnp.stack(pieces) if direct else pieces[0], order)
    next(message_hops)
    next(zero_steps)
    returned = order.hold(exchange(source_sums))
    next(rest_steps)
    message_rows = finish_steps(message_hops)
    zero_share = finish_steps(zero_steps)
    out, proj = call(
        make_finish(lanes_total),
        [((COEFFS, atoms, CH), bf16), ((PROJ_ROWS, LANES), f32)],
        [((total, WIDE), f32), ((2 * total, COLS), bf16), ((COEFFS, atoms, CH), bf16)],
        order.hold(cot), out_proj, *message_rows,
    )
    order.mark(proj)
    lane = lax.axis_index("edge")
    late_rows = PROJ_ROWS // lanes_total
    place = ((lane & 1) * (lanes_total // 2) + (lane >> 1)) * late_rows
    late = lax.dynamic_slice_in_dim(proj, place, late_rows, 0)
    share = jnp.concatenate([finish_steps(rest_steps), zero_share], axis=0)
    late_share = []
    doubling = double(order.mark(share), late_share, order)
    next(doubling)
    source_hops = gather_lanes(order.hold(returned), order)
    next(source_hops)
    for bit in range(bits_of("graph")):
        late = order.mark(late + order.hold(swap(late, "graph", bit)))
        if bit < bits_of("graph") - 1:
            next(doubling)
    late_share.append(late.astype(bf16))
    for _ in share_steps("edge")[bits_of("graph") :]:
        next(doubling)
    source_rows = finish_steps(source_hops)
    (embed,) = call(
        make_collect(lanes_total),
        [((COEFFS, atoms, CH), bf16)],
        [((total, WIDE), f32)],
        order.hold(source_rows[0]), *source_rows[1:],
    )
    order.mark(embed)
    mine, other = finish_steps(doubling)
    zero, one, two, grad_in, grad_edge, grad_dot, grad_proj = call(
        make_unpack(lanes_total, peers),
        [
            ((DIM0, DIM0), bf16),
            ((2, DIM1, DIM1), bf16),
            ((2, DIM2, DIM2), bf16),
            (alpha_in.shape, bf16),
            (alpha_edge.shape, bf16),
            ((2, LANES), bf16),
            (out_proj.shape, bf16),
        ],
        [],
        mine, other,
    )

    def shaped(value):
        return jnp.transpose(value, (1, 0, 2))

    return (
        shaped(out), shaped(embed), zero, one, two, grad_in, grad_edge, grad_dot.reshape(-1),
        grad_proj,
    )


def solution(mesh):
    in_specs = (
        P(("groups", "graph"), None, None),
        P(("groups", "graph"), None, None),
        P(("groups", "graph"), None, "edge", None),
        P(("groups", "graph"), None, "edge", None),
        P(("groups", "graph", "edge")),
        P(("groups", "graph", "edge")),
        P(("groups", "graph", "edge"), None),
        P(("groups", "graph", "edge"), None),
        P(("groups", "graph", "edge"), None),
        P(),
        P(),
        P(),
        P(),
        P(),
        P(),
        P(),
    )
    out_specs = (
        P(("groups", "graph"), None, None),
        P(("groups", "graph"), None, None),
        P("groups", None),
        P("groups", None, None),
        P("groups", None, None),
        P("groups", None),
        P("groups", None),
        P("groups"),
        P("groups", None, None),
    )
    return jax.shard_map(shards, mesh=mesh, in_specs=in_specs, out_specs=out_specs, check_vma=False)
```
